32 devices in a mesh: shard: 2 (over y), context: 4 (over z), tensor: 4 (over x, core).
Axes of the slice: x: 2, y: 2, z: 4, core: 2. Of those that a mesh axis runs over, the one named last changes fastest.
Arguments:
- tokens: bfloat16 [4, 2048, 1024], P('shard', 'context'), may hold values from -6 to 6
- lengths: int32 [4], P('shard'), may hold values from 512 to 2048, as said below
- cotangent: bfloat16 [4, 2048, 1024], P('shard', 'context'), may hold values from -6 to 6
- query_weight: bfloat16 [1024, 2048], P('shard', 'tensor'), may hold values from -0.1875 to 0.1875
- key_weight: bfloat16 [1024, 1024], P('shard', 'tensor'), may hold values from -0.1875 to 0.1875
- value_weight: bfloat16 [1024, 1024], P('shard', 'tensor'), may hold values from -0.1875 to 0.1875
- out_weight: bfloat16 [2048, 1024], P('tensor', 'shard'), may hold values from -3 to 3
- gate_weight: bfloat16 [1024, 3072], P('shard', 'tensor'), may hold values from -0.1875 to 0.1875
- up_weight: bfloat16 [1024, 3072], P('shard', 'tensor'), may hold values from -0.1875 to 0.1875
- down_weight: bfloat16 [3072, 1024], P('tensor', 'shard'), may hold values from -0.109375 to 0.109375
- attention_gain: bfloat16 [1024], P('shard'), may hold values from 0.5 to 1.5
- feedforward_gain: bfloat16 [1024], P('shard'), may hold values from 0.5 to 1.5
- query_gain: bfloat16 [128], replicated, may hold values from 0.099609375 to 1.8984375
- key_gain: bfloat16 [128], replicated, may hold values from 0.099609375 to 1.8984375
Outputs:
- layer_out: bfloat16 [4, 2048, 1024], P('shard', 'context')
- tokens_grad: float32 [4, 2048, 1024], P('shard', 'context')
- query_grad: float32 [1024, 2048], P('shard', 'tensor')
- key_grad: float32 [1024, 1024], P('shard', 'tensor')
- value_grad: float32 [1024, 1024], P('shard', 'tensor')
- out_grad: float32 [2048, 1024], P('tensor', 'shard')
- gate_grad: float32 [1024, 3072], P('shard', 'tensor')
- up_grad: float32 [1024, 3072], P('shard', 'tensor')
- down_grad: float32 [3072, 1024], P('tensor', 'shard')
- attention_gain_grad: float32 [1024], P('shard')
- feedforward_gain_grad: float32 [1024], P('shard')
- query_gain_grad: float32 [128], replicated
- key_gain_grad: float32 [128], replicated
- root_means: float32 [4, 3], P('shard')
The draws below stay inside these ranges and needn't reach their ends.
Inputs may be any that keep to these rules, and one draw needn't show every extreme that they name: `lengths`: among the 2 slots of each index of shard one, drawn from the seed, holds 2048 valid positions; the others hold at most 1024.
All inputs are finite; a program needn't handle non-finite values.
Results may differ from the reference program's by a relative error of at most 0.015.
Values may be sent and summed in bfloat16 or wider, within the bound.
A program may use at most 320 MiB of HBM per device.

```python
from functools import partial
import jax
import jax.numpy as jnp
from jax import lax

D = 1024
H = 16
KV = 8
HD = 128
FF = 3072
SLOTS_DEV = 2
SEQ = 2048
SLOTS = 4


def draw_lengths(key, part):
    key = jax.random.fold_in(key, 11)
    pick_key, spread_key = jax.random.split(key)
    groups = SLOTS // SLOTS_DEV
    full_slot = jax.random.randint(pick_key, (groups, 1), 0, SLOTS_DEV)
    spread = jax.random.randint(spread_key, (groups, SLOTS_DEV), SEQ // 4, SEQ // 2 + 1)
    chosen = jnp.arange(SLOTS_DEV)[None, :] == full_slot
    return jnp.where(chosen, SEQ, spread).reshape(SLOTS).astype(jnp.int32)


def shard_levels(rng, shape, pieces, low, high):
    gain = 1.0
    for position, blocks in pieces:
        steps = jax.random.uniform(jax.random.fold_in(jax.random.fold_in(rng, 6), position), (blocks,), jnp.float32, low / len(pieces), high / len(pieces))
        gain = gain * jnp.repeat(jnp.exp(steps), shape[position] // blocks).reshape((-1,) + (1,) * (len(shape) - 1 - position))
    return gain


def gaussian(key, shape, width, most, shards=(), held_as=jnp.bfloat16):
    values = jax.random.normal(key, shape, jnp.float32) * width
    if len(shards) > 0:
        values = shard_levels(key, shape, shards, -0.22, 0.18) * values
    return jnp.clip(values, min=-most, max=most).astype(held_as)


def setup_inputs(seed: int = 0) -> dict:
    splits = jax.random.split(jax.random.key(seed), 15)
    tokens = gaussian(splits[0], (SLOTS, SEQ, D), 1.0, 6.0, ((0, 2), (1, 4)))
    lengths = draw_lengths(jax.random.fold_in(splits[14], 71), 0)
    cotangent = gaussian(splits[2], (SLOTS, SEQ, D), 1.0, 6.0, ((0, 2), (1, 4)))
    query_weight = gaussian(splits[3], (D, H * HD), D ** -0.5, 0.1875, ((0, 2), (1, 4)))
    key_weight = gaussian(splits[4], (D, KV * HD), D ** -0.5, 0.1875, ((0, 2), (1, 4)))
    value_weight = gaussian(splits[5], (D, KV * HD), D ** -0.5, 0.1875, ((0, 2), (1, 4)))
    out_weight = gaussian(splits[6], (H * HD, D), (max(H * HD // (SEQ // 4), 1)) ** -0.5, 3.0, ((0, 4), (1, 2)))
    gate_weight = gaussian(splits[7], (D, FF), D ** -0.5, 0.1875, ((0, 2), (1, 4)))
    up_weight = gaussian(splits[8], (D, FF), D ** -0.5, 0.1875, ((0, 2), (1, 4)))
    down_weight = gaussian(splits[9], (FF, D), FF ** -0.5, 0.109375, ((0, 4), (1, 2)))
    attention_gain = jnp.clip(1.0 + 0.1 * jax.random.normal(splits[10], (D,), jnp.float32), 0.5, 1.5).astype(jnp.bfloat16)
    feedforward_gain = jnp.clip(1.0 + 0.1 * jax.random.normal(splits[11], (D,), jnp.float32), 0.5, 1.5).astype(jnp.bfloat16)
    query_gain = jnp.clip(1.0 + 0.18 * jax.random.normal(splits[12], (HD,), jnp.float32), 0.099609375, 1.8984375).astype(jnp.bfloat16)
    key_gain = jnp.clip(1.0 + 0.18 * jax.random.normal(splits[13], (HD,), jnp.float32), 0.099609375, 1.8984375).astype(jnp.bfloat16)
    return {"tokens": tokens, "lengths": lengths, "cotangent": cotangent, "query_weight": query_weight, "key_weight": key_weight, "value_weight": value_weight, "out_weight": out_weight, "gate_weight": gate_weight, "up_weight": up_weight, "down_weight": down_weight, "attention_gain": attention_gain, "feedforward_gain": feedforward_gain, "query_gain": query_gain, "key_gain": key_gain}


@jax.custom_vjp
def low(v):
    return lax.optimization_barrier(v.astype(jnp.bfloat16)).astype(jnp.float32)

@jax.custom_vjp
def low_back(v):
    return v

def low_keep(v):
    return (low(v), None)

def low_pass(kept, grad):
    return (grad,)

def back_keep(v):
    return (v, None)

def back_low(kept, grad):
    return (low(grad),)
low.defvjp(low_keep, low_pass)
low_back.defvjp(back_keep, back_low)
epsilon = 1e-06
rope_base = 1000000.0
highest = lax.Precision.HIGHEST

def product(left, right):
    return jnp.dot(left, right, precision=highest, preferred_element_type=jnp.float32)

def rms_norm(values, scale_gain):
    return values * lax.rsqrt(lax.optimization_barrier(jnp.mean(values * values, axis=-1, keepdims=True)) + epsilon) * scale_gain

def rotary(values, positions):
    half_size = values.shape[-1] // 2
    exponents = jnp.arange(half_size, dtype=jnp.float32) * (2.0 / values.shape[-1])
    angles = positions.astype(jnp.float32)[:, None] * (rope_base ** (-exponents))[None, :]
    cosine = jnp.cos(angles)[:, None, :]
    sine = jnp.sin(angles)[:, None, :]
    first_half = values[..., :half_size]
    second_half = values[..., half_size:]
    return jnp.concatenate([first_half * cosine - second_half * sine, second_half * cosine + first_half * sine], axis=-1)

def attend(packed):
    queries, keys_all, values_all, length = packed
    group_size = queries.shape[1] // keys_all.shape[1]
    grouped = queries.reshape(queries.shape[0], keys_all.shape[1], group_size, queries.shape[2])
    scores = jnp.einsum('qgrd,kgd->grqk', grouped, keys_all, precision=highest)
    scores = low_back(scores * queries.shape[2] ** (-0.5))
    places = jnp.arange(queries.shape[0])
    allowed = (places[None, :] <= places[:, None]) & (places[None, :] < length)
    scores = jnp.where(allowed, scores, -1e+30)
    largest = lax.optimization_barrier(jnp.max(scores, axis=-1, keepdims=True))
    raised = jnp.exp(scores - largest)
    weights = low(raised / lax.optimization_barrier(jnp.sum(raised, axis=-1, keepdims=True)))
    mixed = jnp.einsum('grqk,kgd->qgrd', weights, values_all, precision=highest)
    return mixed.reshape(queries.shape[0], -1)

def forward(lengths, tokens, query_weight, key_weight, value_weight, out_weight, gate_weight, up_weight, down_weight, attention_gain, feedforward_gain, query_gain, key_gain):
    positions = jnp.arange(SEQ)
    first = low(rms_norm(tokens, attention_gain)).reshape(SLOTS * SEQ, D)

    def head_form(raw, head_gain, head_count):
        shaped = low_back(raw).reshape(SLOTS, SEQ, head_count, HD)
        return low(rotary(rms_norm(shaped, head_gain), positions))
    queries = head_form(product(first, query_weight), query_gain, H)
    keys_all = head_form(product(first, key_weight), key_gain, KV)
    values_all = low_back(low(product(first, value_weight))).reshape(SLOTS, SEQ, KV, HD)
    mixed = lax.map(jax.checkpoint(attend), (queries, keys_all, values_all, lengths))
    mixed = low_back(low(mixed)).reshape(SLOTS * SEQ, H * HD)
    attn_result = low_back(product(mixed, out_weight)).reshape(SLOTS, SEQ, D)
    residual = tokens + attn_result
    second = low(rms_norm(residual, feedforward_gain)).reshape(SLOTS * SEQ, D)
    gate_value = low_back(product(second, gate_weight))
    up_value = low_back(product(second, up_weight))
    hidden = low(jax.nn.silu(gate_value) * up_value)
    mlp_result = low_back(product(hidden, down_weight)).reshape(SLOTS, SEQ, D)
    return (residual + mlp_result, (attn_result, mlp_result))

def reference(tokens, lengths, cotangent, query_weight, key_weight, value_weight, out_weight, gate_weight, up_weight, down_weight, attention_gain, feedforward_gain, query_gain, key_gain):
    floats = tuple((item.astype(jnp.float32) for item in (tokens, query_weight, key_weight, value_weight, out_weight, gate_weight, up_weight, down_weight, attention_gain, feedforward_gain, query_gain, key_gain)))
    valid = (jnp.arange(SEQ)[None, :] < lengths[:, None]).astype(jnp.float32)
    layer, pull, extras = jax.vjp(partial(forward, lengths), *floats, has_aux=True)
    attn_result, mlp_result = extras
    grads = pull(cotangent.astype(jnp.float32) * valid[:, :, None])
    counted = lengths.astype(jnp.float32)[:, None] * D
    masked = valid[:, :, None]
    squares = jnp.stack([lax.optimization_barrier(jnp.sum(masked * layer * layer, axis=(1, 2))), lax.optimization_barrier(jnp.sum(masked * attn_result * attn_result, axis=(1, 2))), lax.optimization_barrier(jnp.sum(masked * mlp_result * mlp_result, axis=(1, 2)))], axis=1)
    root_means = jnp.sqrt(squares / counted)
    return (layer.astype(jnp.bfloat16), grads[0], grads[1], grads[2], grads[3], grads[4], grads[5], grads[6], grads[7], grads[8], grads[9], grads[10], grads[11], root_means)
```

```python
import functools
import math

import jax
import jax.numpy as jnp
import numpy as np
from jax import lax
from jax.experimental import pallas as pl
from jax.experimental.pallas import tpu as pltpu
from jax.sharding import PartitionSpec as P

epsilon = 1e-06
rope_base = 1000000.0
MESH = pl.DeviceIdType.MESH
f32 = jnp.float32
bf16 = jnp.bfloat16
HBM = pl.BlockSpec(memory_space=pl.ANY)
VMEM = pl.BlockSpec(memory_space=pltpu.VMEM)
SMEM = pl.BlockSpec(memory_space=pltpu.SMEM)
TILE = 256


def rows_of(index, size):
    return pl.ds(pl.multiple_of(index * size, size), size)


def dot_nt(left, right):
    return lax.dot_general(left, right, (((1,), (1,)), ((), ())), preferred_element_type=f32)


def dot_tn(left, right):
    return lax.dot_general(left, right, (((0,), (0,)), ((), ())), preferred_element_type=f32)


def dot_nn(left, right):
    return jnp.dot(left, right, preferred_element_type=f32)


def mean_square(values):
    return jnp.mean(values * values, axis=-1, keepdims=True)


def place():
    return lax.axis_index("shard"), lax.axis_index("context"), lax.axis_index("tensor")


def greet(devices, extra=0):
    barrier = pltpu.get_barrier_semaphore()
    for device in devices:
        pl.semaphore_signal(barrier, inc=1, device_id=device, device_id_type=MESH)
    return barrier


def greet_line(barrier, shard, context, tensor, count):
    @pl.when(context > 0)
    def _():
        pl.semaphore_signal(
            barrier, inc=1, device_id=(shard, context - 1, tensor), device_id_type=MESH
        )

    @pl.when(context < count - 1)
    def _():
        pl.semaphore_signal(
            barrier, inc=1, device_id=(shard, context + 1, tensor), device_id_type=MESH
        )

    return jnp.minimum(context, 1) + jnp.minimum(count - 1 - context, 1)


def remote(src, dst, send_sem, recv_sem, device):
    return pltpu.make_async_remote_copy(
        src_ref=src,
        dst_ref=dst,
        send_sem=send_sem,
        recv_sem=recv_sem,
        device_id=device,
        device_id_type=MESH,
    )


def rope_tables(length, head_size):
    half = head_size // 2
    angles = np.arange(length, dtype=np.float64)[:, None] * (
        rope_base ** (-np.arange(half, dtype=np.float64) * 2.0 / head_size)
    )
    cosine, sine = np.cos(angles), np.sin(angles)
    return (
        np.concatenate([cosine, cosine], axis=1).astype(np.float32),
        np.concatenate([-sine, sine], axis=1).astype(np.float32),
    )


def attention_forward(
    shards, contexts, order_ref, tok_ref, wq_ref, wk_ref, wv_ref, wo_ref, wg_ref, wu_ref, gain_ref,
    head_gain_ref, cos_ref, sin_ref,
    mixed_out, kv_out, qs_out, qraw_out, kraw_out, linv_out, first_out, wq_out, wk_out, wv_out,
    wo_out, wg_out, wu_out, gain_out,
    tok, first, wq, wk, wv, gains, kv, qs, qraw, kraw, acc, mixed, linv,
    load_sem, own_sem, store_sem, wsend, wrecv, kvsend, kvrecv,
):
    shard, context, tensor = place()
    slots, length, width = tok.shape
    share = wq_ref.shape[0]
    query_width = wq.shape[1]
    key_width = wk.shape[1]
    head = cos_ref.shape[1]
    heads = query_width // head
    group = query_width // key_width
    score_scale = head**-0.5 * math.log2(math.e)
    peers = [(lax.rem(shard + d, shards), context, tensor) for d in range(1, shards)]
    barrier = greet(peers)
    neighbours = greet_line(barrier, shard, context, tensor, contexts)

    load_tok = pltpu.make_async_copy(tok_ref, tok, load_sem)
    load_tok.start()
    mine = rows_of(shard, share)
    weights = [
        (gain_ref, gains, gains.at[:, mine]),
        (wk_ref, wk, wk.at[mine, :]),
        (wv_ref, wv, wv.at[mine, :]),
        (wq_ref, wq, wq.at[mine, :]),
        (wo_ref, wo_out, wo_out.at[:, mine]),
        (wg_ref, wg_out, wg_out.at[mine, :]),
        (wu_ref, wu_out, wu_out.at[mine, :]),
    ]
    own = [
        pltpu.make_async_copy(source, target, own_sem.at[w])
        for w, (source, _, target) in enumerate(weights)
    ]
    sends = [
        [
            remote(source, target, wsend.at[w, d], wrecv.at[w, d], peers[d])
            for d in range(shards - 1)
        ]
        for w, (source, _, target) in enumerate(weights)
    ]
    for copy in own:
        copy.start()
    pl.semaphore_wait(barrier, shards - 1 + neighbours)

    def send_weights(places):
        for w in places:
            for copy in sends[w]:
                copy.start()

    def have_weights(places):
        for w in places:
            for copy in sends[w]:
                copy.wait_recv()

    send_weights((0, 1, 2))
    for slot in range(slots):
        for h in range(heads):
            acc[slot, h] = jnp.zeros((length, 2 * head), f32)
    load_tok.wait()
    for w in range(4):
        own[w].wait()
    have_weights((0,))
    first_slot = order_ref[0]
    tiles = slots * length // TILE
    per_slot = length // TILE

    def norm_rows(i, _):
        slot = i // per_slot
        source = jnp.where(slot == 0, first_slot, 1 - first_slot)
        values = tok[source, rows_of(i % per_slot, TILE), :].astype(f32)
        scale = lax.rsqrt(mean_square(values) + epsilon)
        first[rows_of(i, TILE), :] = (values * scale * gains[0:1, :]).astype(bf16)
        return 0

    lax.fori_loop(0, tiles, norm_rows, 0)
    store_first = pltpu.make_async_copy(first, first_out, store_sem.at[0])
    store_first.start()
    have_weights((1, 2))
    send_weights((3, 4))

    def head_form(raw, gain, i):
        local = rows_of(i % per_slot, TILE)
        normal = raw * lax.rsqrt(mean_square(raw) + epsilon) * gain
        return normal * cos_ref[local, :] + pltpu.roll(normal, head // 2, 1) * sin_ref[local, :]

    def key_rows(i, _):
        place_rows = rows_of(i, TILE)
        local = rows_of(i % per_slot, TILE)
        slot = i // per_slot
        values = first[place_rows, :]
        raw = dot_nn(values, wk[...])
        kraw[place_rows, :] = raw.astype(bf16)
        for g in range(key_width // head):
            part = raw[:, g * head : (g + 1) * head]
            kv[context, slot, local, g * head : (g + 1) * head] = head_form(
                part, head_gain_ref[8:9, :], i
            ).astype(bf16)
        kv[context, slot, local, key_width:] = dot_nn(values, wv[...]).astype(bf16)
        return 0

    lax.fori_loop(0, tiles, key_rows, 0)

    def kv_copy(block, slot):
        return remote(
            kv.at[block, slot], kv.at[block, slot], kvsend.at[block, slot], kvrecv.at[block, slot],
            (shard, jnp.minimum(context + 1, contexts - 1), tensor),
        )

    half = contexts // 2

    def for_block(block, action):
        @pl.when(block >= 0)
        def _():
            action(block, 0)

        @pl.when((block >= 0) & (block < half))
        def _():
            action(block, 1)

    def start_up(block, slot):
        @pl.when(context < contexts - 1)
        def _():
            kv_copy(block, slot).start()

    for_block(context, start_up)
    have_weights((3,))
    send_weights((5, 6))
    store_weights = [
        pltpu.make_async_copy(source, target, store_sem.at[n])
        for n, (source, target) in enumerate(
            ((wq, wq_out), (wk, wk_out), (wv, wv_out), (gains, gain_out)), 1
        )
    ]
    for copy in store_weights:
        copy.start()

    def query_rows(i, _):
        place_rows = rows_of(i, TILE)
        raw = dot_nn(first[place_rows, :], wq[...])
        qraw[place_rows, :] = raw.astype(bf16)
        for h in range(heads):
            part = raw[:, h * head : (h + 1) * head]
            qs[place_rows, h * head : (h + 1) * head] = (
                head_form(part, head_gain_ref[0:1, :], i) * score_scale
            ).astype(bf16)
        return 0

    lax.fori_loop(0, tiles, query_rows, 0)
    store_raw = [
        pltpu.make_async_copy(source, target, store_sem.at[n])
        for n, (source, target) in enumerate(((qs, qs_out), (qraw, qraw_out), (kraw, kraw_out)), 5)
    ]
    for copy in store_raw:
        copy.start()
    short_length = order_ref[1]
    ones = jnp.ones((length, head), bf16)

    def attend(block, slot, diagonal):
        def one_head(h, _):
            columns = rows_of(h, head)
            keys = kv[block, slot, :, rows_of(h // group, head)]
            values = kv[block, slot, :, rows_of(key_width // head + h // group, head)]
            scores = dot_nt(qs[slot * length : (slot + 1) * length, columns], keys)
            raised = jnp.exp2(scores)
            spots = lax.broadcasted_iota(jnp.int32, (length, length), 1)
            if diagonal:
                lines = lax.broadcasted_iota(jnp.int32, (length, length), 0)
                raised = jnp.where(spots <= lines, raised, 0.0)
            if slot == 1:
                raised = jnp.where(spots + block * length < short_length, raised, 0.0)
            acc[slot, h] += dot_nn(
                raised.astype(bf16), jnp.concatenate([values, ones], axis=1)
            )
            return 0

        lax.fori_loop(0, heads, one_head, 0)

    for_block(context, lambda block, slot: attend(block, slot, True))

    def arrived(block, slot):
        kv_copy(block, slot).wait_recv()
        start_up(block, slot)
        attend(block, slot, False)

    for r in range(1, contexts):
        for_block(context - r, arrived)

    def finish(h, _):
        columns = rows_of(h, head)
        for slot in range(slots):
            lines = slice(slot * length, (slot + 1) * length)
            inverse = 1.0 / acc[slot, h, :, head:]
            mixed[lines, columns] = (acc[slot, h, :, :head] * inverse).astype(bf16)
            linv[lines, columns] = inverse
        return 0

    lax.fori_loop(0, heads, finish, 0)
    store_last = [
        pltpu.make_async_copy(source, target, store_sem.at[n])
        for n, (source, target) in enumerate(
            ((mixed, mixed_out), (linv, linv_out), (kv, kv_out)), 8
        )
    ]
    for copy in store_last:
        copy.start()

    def sent(block, slot):
        @pl.when(context < contexts - 1)
        def _():
            kv_copy(block, slot).wait_send()

    for r in range(contexts):
        for_block(context - r, sent)
    for w in range(4, 7):
        own[w].wait()
    have_weights((4, 5, 6))
    for copies in sends:
        for copy in copies:
            copy.wait_send()
    for copy in [store_first, *store_weights, *store_raw, *store_last]:
        copy.wait()


def call_attention_forward(
    shards, contexts, order, tokens, query_weight, key_weight, value_weight, out_weight,
    gate_weight, up_weight, gain_share, head_gains, cosine, sine,
):
    slots, length, width = tokens.shape
    rows = slots * length
    qw, kw, ff = query_weight.shape[1], key_weight.shape[1], gate_weight.shape[1]
    head = cosine.shape[1]
    heads = qw // head
    n_weights = 7
    shape = jax.ShapeDtypeStruct
    kv_shape = (contexts, slots, length, 2 * kw)
    outs = (
        shape((rows, qw), bf16), shape(kv_shape, bf16), shape((rows, qw), bf16),
        shape((rows, qw), bf16), shape((rows, kw), bf16), shape((rows, qw), f32),
        shape((rows, width), bf16), shape((width, qw), bf16), shape((width, kw), bf16),
        shape((width, kw), bf16), shape((qw, width), bf16), shape((width, ff), bf16),
        shape((width, ff), bf16), shape((16, width), f32),
    )
    return pl.pallas_call(
        functools.partial(attention_forward, shards, contexts),
        out_shape=outs,
        in_specs=[SMEM] + [HBM] * 8 + [VMEM] * 3,
        out_specs=[HBM] * len(outs),
        scratch_shapes=[
            pltpu.VMEM((slots, length, width), bf16),
            pltpu.VMEM((rows, width), bf16),
            pltpu.VMEM((width, qw), bf16),
            pltpu.VMEM((width, kw), bf16),
            pltpu.VMEM((width, kw), bf16),
            pltpu.VMEM((16, width), f32),
            pltpu.VMEM(kv_shape, bf16),
            pltpu.VMEM((rows, qw), bf16),
            pltpu.VMEM((rows, qw), bf16),
            pltpu.VMEM((rows, kw), bf16),
            pltpu.VMEM((slots, heads, length, 2 * head), f32),
            pltpu.VMEM((rows, qw), bf16),
            pltpu.VMEM((rows, qw), f32),
            pltpu.SemaphoreType.DMA,
            pltpu.SemaphoreType.DMA((n_weights,)),
            pltpu.SemaphoreType.DMA((11,)),
            pltpu.SemaphoreType.DMA((n_weights, shards - 1)),
            pltpu.SemaphoreType.DMA((n_weights, shards - 1)),
            pltpu.SemaphoreType.DMA((contexts, slots)),
            pltpu.SemaphoreType.DMA((contexts, slots)),
        ],
        compiler_params=pltpu.CompilerParams(
            collective_id=1, has_side_effects=True, vmem_limit_bytes=56 * 2**20
        ),
        name="attention_forward",
    )(
        order, tokens, query_weight, key_weight, value_weight, out_weight, gate_weight, up_weight,
        gain_share, head_gains, cosine, sine,
    )


def feed_forward(
    shards, order_ref, mixed_ref, wo_ref, tok_ref, cot_ref, gain_ref, wg_ref, wu_ref, wd_ref,
    second_out, hidden_out, gback_out, uback_out, cotin_out, spart_out, mpart_out, resid_out,
    square_out, own_tok_out,
    mixed, wo, tok, cot, gains, wg, wu, wd, second, hidden, gback, uback, cotin, spart, mpart,
    resid, square, own_tok, apart, csend, crecv, xsend, xrecv, ssend, srecv, msend, mrecv, gvalue, uvalue,
    load_sem, store_sem, wsend, wrecv, core_send, core_recv, x_send, x_recv,
):
    shard, context, tensor = place()
    slots, length, width = tok.shape
    share = wd_ref.shape[1]
    step_rows = TILE // 2
    steps = length // step_rows
    core = tensor % 2
    core_peer = (shard, context, tensor + 1 - 2 * core)
    x_peer = (shard, context, (tensor + 2) % 4)
    peers = [(lax.rem(shard + d, shards), context, tensor) for d in range(1, shards)]
    barrier = greet([core_peer, x_peer, *peers])
    loads = [
        pltpu.make_async_copy(source, target, load_sem.at[n])
        for n, (source, target) in enumerate(
            (
                (mixed_ref, mixed), (wo_ref, wo), (tok_ref, tok), (gain_ref, gains),
                (wg_ref, wg), (wu_ref, wu), (cot_ref, cot),
                (wd_ref, wd.at[:, rows_of(shard, share)]),
            )
        )
    ]
    for copy in loads:
        copy.start()
    square[...] = jnp.zeros_like(square)
    pl.semaphore_wait(barrier, shards + 1)
    wd_sends = [
        remote(wd_ref, wd.at[:, rows_of(shard, share)], wsend.at[d], wrecv.at[d], peers[d])
        for d in range(shards - 1)
    ]
    for copy in wd_sends:
        copy.start()
    for copy in loads[:2]:
        copy.wait()

    def mine(i):
        return rows_of(core * steps + i, step_rows)

    def theirs(i):
        return rows_of((1 - core) * steps + i, step_rows)

    def half(i):
        return rows_of(i, step_rows)

    def core_copy(kind, i, source, target):
        return remote(source, target, core_send.at[kind, i], core_recv.at[kind, i], core_peer)

    def attn_copy(i):
        return core_copy(0, i, csend.at[half(i), :], crecv.at[half(i), :])

    def second_copy(i):
        return core_copy(1, i, second.at[mine(i), :], second.at[mine(i), :])

    def spart_copy(i):
        return core_copy(2, i, ssend.at[half(i), :], srecv.at[half(i), :])

    def mpart_copy(i):
        return core_copy(3, i, msend.at[half(i), :], mrecv.at[half(i), :])

    def x_copy(i):
        return remote(
            xsend.at[half(i), :], xrecv.at[half(i), :], x_send.at[i], x_recv.at[i], x_peer
        )

    def project(i, _):
        @pl.when(i < steps)
        def _():
            both = jnp.concatenate([mixed[theirs(i), :], mixed[mine(i), :]], axis=0)
            result = dot_nn(both, wo[...])
            csend[half(i), :] = result[:step_rows].astype(bf16)
            attn_copy(i).start()
            apart[half(i), :] = result[step_rows:]

        @pl.when(i > 0)
        def _():
            before = i - 1
            attn_copy(before).wait_recv()
            total = apart[half(before), :] + crecv[half(before), :].astype(f32)
            xsend[half(before), :] = total.astype(bf16)
            x_copy(before).start()

        return 0

    lax.fori_loop(0, steps + 1, project, 0)
    for copy in loads[2:]:
        copy.wait()
    first_slot = order_ref[0]
    short_length = order_ref[1]
    own_source = jnp.where(core == 0, first_slot, 1 - first_slot)

    def counted(slot, i):
        spots = context * length + i * step_rows
        lines = lax.broadcasted_iota(jnp.int32, (step_rows, width), 0) + spots
        limit = jnp.where(slot == 0, 2**30, short_length)
        return lines < limit

    def cut(slot, i):
        source = jnp.where(slot == 0, first_slot, 1 - first_slot)
        values = cot[source, half(i), :].astype(f32)
        return jnp.where(counted(slot, i), values, 0.0).astype(bf16)

    def normalise(i):
        x_copy(i).wait_recv()
        attn = xsend[half(i), :].astype(f32) + xrecv[half(i), :].astype(f32)
        attn_counted = jnp.where(counted(core, i), attn, 0.0)
        square[...] += jnp.sum(
            (attn_counted * attn_counted).reshape(step_rows // 8, 8, width), axis=0
        )
        own_tok[half(i), :] = tok[own_source, half(i), :]
        residual = own_tok[half(i), :].astype(f32) + attn
        resid[half(i), :] = residual
        scale = lax.rsqrt(mean_square(residual) + epsilon)
        second[mine(i), :] = (residual * scale * gains[8:9, :]).astype(bf16)
        second_copy(i).start()
        cotin[mine(i), :] = cut(core, i)
        cotin[theirs(i), :] = cut(1 - core, i)

    def finish_parts(i):
        spart_copy(i).wait_recv()
        spart[half(i), :] = (
            spart[half(i), :].astype(f32) + srecv[half(i), :].astype(f32)
        ).astype(bf16)
        mpart_copy(i).wait_recv()
        mpart[half(i), :] = (
            mpart[half(i), :].astype(f32) + mrecv[half(i), :].astype(f32)
        ).astype(bf16)

    def backward(i):
        gate = gvalue[i % 2]
        up = uvalue[i % 2]
        sigmoid = 1.0 / (1.0 + jnp.exp(-gate))
        swish = gate * sigmoid
        slope = sigmoid + swish * (1.0 - sigmoid)
        low = (swish * up).astype(bf16)
        hidden[mine(i), :] = low[:step_rows]
        hidden[theirs(i), :] = low[step_rows:]
        inward = jnp.concatenate([cotin[mine(i), :], cotin[theirs(i), :]], axis=0)
        hidden_back = dot_nt(inward, wd[...])
        gate_low = (hidden_back * up * slope).astype(bf16)
        up_low = (hidden_back * swish).astype(bf16)
        gback[mine(i), :] = gate_low[:step_rows]
        gback[theirs(i), :] = gate_low[step_rows:]
        uback[mine(i), :] = up_low[:step_rows]
        uback[theirs(i), :] = up_low[step_rows:]
        result = dot_nt(gate_low, wg[...]) + dot_nt(up_low, wu[...])
        ssend[half(i), :] = result[step_rows:].astype(bf16)
        spart_copy(i).start()
        spart[half(i), :] = result[:step_rows].astype(bf16)
        result = dot_nn(low, wd[...])
        msend[half(i), :] = result[step_rows:].astype(bf16)
        mpart_copy(i).start()
        mpart[half(i), :] = result[:step_rows].astype(bf16)

    def forward(i):
        second_copy(i).wait_recv()
        both = jnp.concatenate([second[mine(i), :], second[theirs(i), :]], axis=0)
        gvalue[i % 2] = dot_nn(both, wg[...])
        uvalue[i % 2] = dot_nn(both, wu[...])

    def step(i, _):
        @pl.when(i < steps)
        def _():
            normalise(i)

        @pl.when(i == 1)
        def _():
            for copy in wd_sends:
                copy.wait_recv()

        @pl.when(i > 0)
        def _():
            backward(i - 1)

        @pl.when(i > 1)
        def _():
            finish_parts(i - 2)

        @pl.when(i < steps)
        def _():
            forward(i)

        return 0

    lax.fori_loop(0, steps + 1, step, 0)
    finish_parts(steps - 1)
    stores = [
        pltpu.make_async_copy(source, target, store_sem.at[n])
        for n, (source, target) in enumerate(
            (
                (second, second_out), (hidden, hidden_out), (gback, gback_out),
                (uback, uback_out), (cotin, cotin_out), (spart, spart_out), (mpart, mpart_out),
                (resid, resid_out), (square, square_out), (own_tok, own_tok_out),
            )
        )
    ]
    for copy in stores:
        copy.start()

    def drain(i, _):
        for copy in (attn_copy, second_copy, spart_copy, mpart_copy, x_copy):
            copy(i).wait_send()
        return 0

    lax.fori_loop(0, steps, drain, 0)
    for copy in wd_sends:
        copy.wait_send()
    for copy in stores:
        copy.wait()


def call_feed_forward(
    shards, order, mixed, out_weight, tokens, cotangent, gains, gate_weight, up_weight, down_weight
):
    slots, length, width = tokens.shape
    rows = slots * length
    qw = mixed.shape[1]
    ff = gate_weight.shape[1]
    steps = 2 * length // TILE
    shape = jax.ShapeDtypeStruct
    outs = (
        shape((rows, width), bf16), shape((rows, ff), bf16), shape((rows, ff), bf16),
        shape((rows, ff), bf16), shape((rows, width), bf16), shape((length, width), bf16),
        shape((length, width), bf16), shape((length, width), f32), shape((8, width), f32),
        shape((length, width), bf16),
    )
    half = pltpu.VMEM((length, width), bf16)
    return pl.pallas_call(
        functools.partial(feed_forward, shards),
        out_shape=outs,
        in_specs=[SMEM] + [HBM] * 8,
        out_specs=[HBM] * len(outs),
        scratch_shapes=[
            pltpu.VMEM((rows, qw), bf16),
            pltpu.VMEM((qw, width), bf16),
            pltpu.VMEM((slots, length, width), bf16),
            pltpu.VMEM((slots, length, width), bf16),
            pltpu.VMEM((16, width), f32),
            pltpu.VMEM((width, ff), bf16),
            pltpu.VMEM((width, ff), bf16),
            pltpu.VMEM((ff, width), bf16),
            *[pltpu.VMEM(out.shape, out.dtype) for out in outs],
            pltpu.VMEM((length, width), f32),
            *[half] * 8,
            pltpu.VMEM((2, TILE, ff), f32),
            pltpu.VMEM((2, TILE, ff), f32),
            pltpu.SemaphoreType.DMA((8,)),
            pltpu.SemaphoreType.DMA((10,)),
            pltpu.SemaphoreType.DMA((shards - 1,)),
            pltpu.SemaphoreType.DMA((shards - 1,)),
            pltpu.SemaphoreType.DMA((4, steps)),
            pltpu.SemaphoreType.DMA((4, steps)),
            pltpu.SemaphoreType.DMA((steps,)),
            pltpu.SemaphoreType.DMA((steps,)),
        ],
        compiler_params=pltpu.CompilerParams(
            collective_id=2, has_side_effects=True, vmem_limit_bytes=56 * 2**20
        ),
        name="feed_forward",
    )(
        order, mixed, out_weight, tokens, cotangent, gains, gate_weight, up_weight, down_weight
    )


def layer_backward(
    shards, contexts, order_ref, second_ref, gback_ref, uback_ref, cotin_ref, hidden_ref,
    spart_ref, mpart_ref, resid_ref, square_ref, mixed_ref, linv_ref, qs_ref, qraw_ref, kraw_ref,
    kv_ref, first_ref, wq_ref, wk_ref, wv_ref, wo_ref, gain_ref, own_tok_ref, head_gain_ref,
    cos_ref, sin_ref,
    grad_out, layer_out, tgrad_out, sums_out,
    second, gback, uback, cotin, hidden, spart, mpart, resid, square, dq, wq, wk, wv, wo, gains,
    own_tok, kv, xs, xm, outin, resback, dkv, dkv_in, fsend, frecv, fxsend, fxrecv,
    piece, ysend, yrecv, zin, ztop, sums, sums_in, sums_y, acc_gain, acc_ff, acc_head,
    acc_square,
    load_sem, kv_sem, late_sem, store_sem, x_send, x_recv, core_send, core_recv, y_send, y_recv,
    g_send, z_recv, top_recv, res_send, res_recv, d_send, d_recv, s_send, s_recv,
):
    shard, context, tensor = place()
    rows, width = second.shape
    length = resid.shape[0]
    ff = gback.shape[1]
    qw, kw = wq.shape[1], wk.shape[1]
    head = cos_ref.shape[1]
    heads, kv_heads = qw // head, kw // head
    group = heads // kv_heads
    share = piece.shape[1]
    chunk_count, chunk = piece.shape[0], piece.shape[2]
    early = ysend.shape[1]
    half_contexts = contexts // 2
    root = contexts // 2
    step_rows = TILE // 2
    steps = length // step_rows
    scale = head**-0.5
    core = tensor % 2
    core_peer = (shard, context, tensor + 1 - 2 * core)
    x_peer = (shard, context, (tensor + 2) % 4)
    peers = [(lax.rem(shard + d, shards), context, tensor) for d in range(1, shards)]
    below = (shard, jnp.maximum(context - 1, 0), tensor)
    above = (shard, jnp.minimum(context + 1, contexts - 1), tensor)
    barrier = greet([core_peer, x_peer, *peers])
    neighbours = greet_line(barrier, shard, context, tensor, contexts)

    pairs = [
        (spart_ref, spart), (second_ref, second), (gback_ref, gback), (uback_ref, uback),
        (cotin_ref, cotin), (hidden_ref, hidden), (resid_ref, resid), (gain_ref, gains),
        (wo_ref, wo), (linv_ref, dq), (mpart_ref, mpart), (square_ref, square), (wq_ref, wq),
        (wk_ref, wk), (wv_ref, wv), (own_tok_ref, own_tok),
    ]
    loads = [
        pltpu.make_async_copy(source, target, load_sem.at[n])
        for n, (source, target) in enumerate(pairs)
    ]
    for copy in loads:
        copy.start()

    def mine(i):
        return rows_of(core * steps + i, step_rows)

    def theirs(i):
        return rows_of((1 - core) * steps + i, step_rows)

    def half(i):
        return rows_of(i, step_rows)

    def xs_copy(i):
        return remote(spart.at[half(i), :], xs.at[half(i), :], x_send.at[0, i], x_recv.at[0, i], x_peer)

    def xm_copy(i):
        return remote(mpart.at[half(i), :], xm.at[half(i), :], x_send.at[1, i], x_recv.at[1, i], x_peer)

    def xf_copy(i):
        return remote(
            fxsend.at[half(i), :], fxrecv.at[half(i), :], x_send.at[2, i], x_recv.at[2, i], x_peer
        )

    def core_copy(kind, i, source, target):
        return remote(source, target, core_send.at[kind, i], core_recv.at[kind, i], core_peer)

    def outin_copy(i):
        return core_copy(0, i, outin.at[mine(i), :], outin.at[mine(i), :])

    def layer_copy(i):
        return core_copy(1, i, mpart.at[half(i), :], layer_out.at[core, half(i), :])

    def f_copy(i):
        return core_copy(2, i, fsend.at[half(i), :], frecv.at[half(i), :])

    def tgrad_copy(i):
        return core_copy(3, i, spart.at[half(i), :], tgrad_out.at[core, half(i), :])

    def layer_keep(i):
        return pltpu.make_async_copy(
            mpart.at[half(i), :], layer_out.at[core, half(i), :], store_sem.at[0, i]
        )

    def tgrad_keep(i):
        return pltpu.make_async_copy(
            spart.at[half(i), :], tgrad_out.at[core, half(i), :], store_sem.at[1, i]
        )

    def y_copy(d, k):
        return remote(
            ysend.at[d, k % early], yrecv.at[d, k], y_send.at[d, k], y_recv.at[d, k], peers[d]
        )

    def up_copy(k):
        return remote(piece.at[k], zin.at[k], g_send.at[k], z_recv.at[k], above)

    def down_copy(k):
        return remote(piece.at[k], zin.at[k], g_send.at[k], z_recv.at[k], below)

    def top_copy(k):
        return remote(piece.at[k], ztop.at[k], g_send.at[k], top_recv.at[k], below)

    def back_down_copy(k):
        return remote(zin.at[k], zin.at[k], res_send.at[0, k], res_recv.at[k], below)

    def back_up_copy(k):
        return remote(zin.at[k], zin.at[k], res_send.at[1, k], res_recv.at[k], above)

    def grad_keep(k):
        return pltpu.make_async_copy(zin.at[k], grad_out.at[k], late_sem.at[k])

    def reduce_chunk(k):
        total = piece[k].astype(f32)
        for d in range(shards - 1):
            y_copy(d, k).wait_recv()
            total = total + yrecv[d, k].astype(f32)
        piece[k] = total.astype(bf16)

        def add_in():
            piece[k] = (piece[k].astype(f32) + zin[k].astype(f32)).astype(bf16)

        @pl.when(context < root)
        def _():
            @pl.when(context > 0)
            def _():
                up_copy(k).wait_recv()
                add_in()

            up_copy(k).start()

        @pl.when(context > root)
        def _():
            @pl.when(context < contexts - 1)
            def _():
                down_copy(k).wait_recv()
                add_in()

            @pl.when(context == root + 1)
            def _():
                top_copy(k).start()

            @pl.when(context > root + 1)
            def _():
                down_copy(k).start()

        @pl.when(context == root)
        def _():
            total = piece[k].astype(f32)
            if root > 0:
                up_copy(k).wait_recv()
                total = total + zin[k].astype(f32)
            if root < contexts - 1:
                top_copy(k).wait_recv()
                total = total + ztop[k].astype(f32)
            zin[k] = total.astype(bf16)
            if root > 0:
                back_down_copy(k).start()
            if root < contexts - 1:
                back_up_copy(k).start()
            grad_keep(k).start()

    def return_chunk(k):
        @pl.when(context < root)
        def _():
            back_down_copy(k).wait_recv()

            @pl.when(context > 0)
            def _():
                back_down_copy(k).start()

            grad_keep(k).start()

        @pl.when(context > root)
        def _():
            back_up_copy(k).wait_recv()

            @pl.when(context < contexts - 1)
            def _():
                back_up_copy(k).start()

            grad_keep(k).start()

    far = max(root, contexts - 1 - root)
    from_end = jnp.where(context <= root, context, contexts - 1 - context)
    reduce_lag = jnp.where(context == root, far, from_end)
    return_lag = far + jnp.abs(context - root)
    ticks = chunk_count + far + far

    def tick(t):
        k = t - reduce_lag

        @pl.when((k >= 0) & (k < chunk_count))
        def _():
            reduce_chunk(k)

        back = t - return_lag

        @pl.when((back >= 0) & (back < chunk_count) & (context != root))
        def _():
            return_chunk(back)

    def weight_grad(left, right, columns, first_chunk, count):
        for d in range(shards - 1):
            theirs_at = rows_of(lax.rem(shard + d + 1, shards), share)
            result = dot_tn(left[:, theirs_at], right[:, columns : columns + count * chunk])
            for n in range(count):
                k = first_chunk + n
                if k >= early:
                    y_copy(d, k - early).wait_send()
                ysend[d, k % early] = result[:, n * chunk : (n + 1) * chunk].astype(bf16)
                y_copy(d, k).start()
        result = dot_tn(left[:, rows_of(shard, share)], right[:, columns : columns + count * chunk])
        for n in range(count):
            piece[first_chunk + n] = result[:, n * chunk : (n + 1) * chunk].astype(bf16)

    def block_at(slot, block):
        return block if slot == 0 else contexts + block

    def d_copy(slot, block):
        at = block_at(slot, block)
        return remote(dkv.at[at], dkv_in.at[at], d_send.at[at], d_recv.at[at], below)

    def pass_down(slot, block, count):
        at = block_at(slot, block)

        @pl.when((block <= context) & (context < count))
        def _():
            @pl.when(context < count - 1)
            def _():
                d_copy(slot, block).wait_recv()
                dkv[at] = (dkv[at].astype(f32) + dkv_in[at].astype(f32)).astype(bf16)

            @pl.when(block < context)
            def _():
                d_copy(slot, block).start()

    def kv_load(block):
        return pltpu.make_async_copy(kv_ref.at[block], kv.at[block % 2], kv_sem.at[block % 2])

    acc_gain[...] = jnp.zeros_like(acc_gain)
    acc_ff[...] = jnp.zeros_like(acc_ff)
    acc_head[...] = jnp.zeros_like(acc_head)
    acc_square[...] = jnp.zeros_like(acc_square)
    for n in range(6):
        loads[n].wait()
    pl.semaphore_wait(barrier, shards + 1 + neighbours)
    for i in range(steps):
        xs_copy(i).start()
    gate_chunks = ff // chunk
    out_chunks = qw // chunk
    query_chunk = 3 * gate_chunks + out_chunks
    weight_grad(second, gback, 0, 0, gate_chunks)
    weight_grad(second, uback, 0, gate_chunks, gate_chunks)
    weight_grad(cotin, hidden, 0, 2 * gate_chunks, gate_chunks)
    for n in range(6, len(loads)):
        loads[n].wait()
    qs, qraw, mixed = hidden.at[:, :qw], gback.at[:, :qw], uback.at[:, :qw]
    kraw = gback.at[:, qw:]
    next_pairs = [(qs_ref, qs), (qraw_ref, qraw), (mixed_ref, mixed), (kraw_ref, kraw)]
    next_loads = [
        pltpu.make_async_copy(source, target, load_sem.at[n])
        for n, (source, target) in enumerate(next_pairs)
    ]
    for copy in next_loads:
        copy.start()
    kv_load(0).start()

    def fold(values):
        return jnp.sum(values.reshape(values.shape[0] // 8, 8, values.shape[1]), axis=0)

    def norm_back(values, back, gain):
        inverse = lax.rsqrt(mean_square(values) + epsilon)
        normal = values * inverse
        scaled = back * gain
        inward = inverse * (scaled - normal * jnp.mean(normal * scaled, axis=-1, keepdims=True))
        return inward, back * normal

    def residual_step(i, _):
        xs_copy(i).wait_recv()
        back = spart[half(i), :].astype(f32) + xs[half(i), :].astype(f32)
        inward, terms = norm_back(resid[half(i), :], back, gains[8:9, :])
        acc_ff[...] += fold(terms)
        total = cotin[mine(i), :].astype(f32) + inward
        resback[half(i), :] = total
        outin[mine(i), :] = total.astype(bf16)
        outin_copy(i).start()
        tick(i)
        return 0

    lax.fori_loop(0, steps, residual_step, 0)
    tick_at = steps
    for i in range(steps):
        xm_copy(i).start()
    for i in range(steps):
        outin_copy(i).wait_recv()
    first = cotin
    first_load = pltpu.make_async_copy(first_ref, first, load_sem.at[4])
    first_load.start()
    for copy in next_loads:
        copy.wait()
    dox = second

    def mixed_step(i, _):
        at = rows_of(i, TILE)
        back = dot_nt(outin[at, :], wo[...]).astype(bf16).astype(f32)
        lanes = lax.broadcasted_iota(jnp.int32, (TILE, head), 1)
        for h in range(heads):
            columns = slice(h * head, (h + 1) * head)
            low = (back[:, columns] * dq[at, columns]).astype(bf16)
            centre = jnp.sum(
                low.astype(f32) * mixed[at, columns].astype(f32), axis=-1, keepdims=True
            )
            high = centre.astype(bf16).astype(f32)
            extra = jnp.where(lanes == 0, -high, jnp.where(lanes == 1, high - centre, 0.0))
            dox[at, 2 * h * head : (2 * h + 1) * head] = low
            dox[at, (2 * h + 1) * head : (2 * h + 2) * head] = extra.astype(bf16)
        dq[at, :] = jnp.zeros((TILE, qw), f32)
        return 0

    lax.fori_loop(0, rows // TILE, mixed_step, 0)
    tick(tick_at)
    weight_grad(outin, mixed, 0, 3 * gate_chunks, out_chunks)
    tick(tick_at + 1)
    tick_at += 2
    ones = jnp.ones((length, head), bf16)

    def block_back(slot, block, diagonal):
        lines = slice(slot * length, (slot + 1) * length)
        if diagonal:
            key_spots = lax.broadcasted_iota(jnp.int32, (length, length), 0)
            query_spots = lax.broadcasted_iota(jnp.int32, (length, length), 1)
            counted = key_spots <= query_spots

        def one_group(g, _):
            keys = kv[block % 2, slot, :, rows_of(g, head)]
            values = kv[block % 2, slot, :, rows_of(kv_heads + g, head)]
            widened = jnp.concatenate([values, ones], axis=1)
            key_back = jnp.zeros((length, head), f32)
            value_back = jnp.zeros((length, head), f32)
            for member in range(group):
                h = g * group + member
                columns = rows_of(h, head)
                queries = qs[lines, columns]
                inward = dox[lines, rows_of(h, 2 * head)]
                raised = jnp.exp2(dot_nt(keys, queries))
                if diagonal:
                    raised = jnp.where(counted, raised, 0.0)
                scores_back = (raised * dot_nt(widened, inward)).astype(bf16)
                value_back += dot_nn(raised.astype(bf16), inward[:, :head])
                key_back += dot_nn(scores_back, queries)
                dq[lines, columns] += dot_tn(scores_back, keys)
            at = block_at(slot, block)
            dkv[at, :, rows_of(g, head)] = (key_back * math.log(2.0)).astype(bf16)
            dkv[at, :, rows_of(kv_heads + g, head)] = value_back.astype(bf16)
            return 0

        lax.fori_loop(0, kv_heads, one_group, 0)

    for block in range(contexts):

        @pl.when(block <= context)
        def _():
            kv_load(block).wait()

        if block + 1 < contexts:

            @pl.when(block + 1 <= context)
            def _():
                kv_load(block + 1).start()

        for slot, count in ((0, contexts), (1, half_contexts)):
            if block < count:

                @pl.when(block == context)
                def _():
                    block_back(slot, block, True)

                @pl.when((block < context) & (context < count))
                def _():
                    block_back(slot, block, False)

                @pl.when(context == count - 1)
                def _():
                    pass_down(slot, block, count)

        if tick_at < query_chunk:
            tick(tick_at)
            tick_at += 1
    first_load.wait()

    def head_back(raw, back, gain, i):
        local = rows_of(i % (length // TILE), TILE)
        turned = back * cos_ref[local, :] - pltpu.roll(back, head // 2, 1) * sin_ref[local, :]
        return norm_back(raw.astype(f32), turned, gain)

    def query_step(i, _):
        at = rows_of(i, TILE)
        for h in range(heads):
            columns = slice(h * head, (h + 1) * head)
            inward, terms = head_back(
                qraw[at, columns], dq[at, columns] * scale, head_gain_ref[0:1, :], i
            )
            acc_head[0] += fold(terms)
            qraw[at, columns] = inward.astype(bf16)
        return 0

    lax.fori_loop(0, rows // TILE, query_step, 0)
    weight_grad(first, qraw, 0, query_chunk, out_chunks)
    tick(tick_at)
    tick_at += 1
    short_length = order_ref[1]

    def layer_step(i, _):
        xm_copy(i).wait_recv()
        xm_copy(i).wait_send()
        mlp = mpart[half(i), :].astype(f32) + xm[half(i), :].astype(f32)
        layer = resid[half(i), :] + mlp
        mpart[half(i), :] = layer.astype(bf16)
        layer_copy(i).start()
        layer_keep(i).start()
        lines = lax.broadcasted_iota(jnp.int32, (step_rows, width), 0)
        limit = jnp.where(core == 0, 2**30, short_length)
        counted = lines + (context * length + i * step_rows) < limit
        acc_square[0] += fold(jnp.where(counted, layer * layer, 0.0))
        acc_square[1] += fold(jnp.where(counted, mlp * mlp, 0.0))
        return 0

    lax.fori_loop(0, steps, layer_step, 0)
    for block in range(contexts):
        for slot, count in ((0, contexts), (1, half_contexts)):
            if block < count:

                @pl.when(context != count - 1)
                def _():
                    pass_down(slot, block, count)

        if tick_at < query_chunk + out_chunks:
            tick(tick_at)
            tick_at += 1
    vback = uback.at[:, :kw]
    per_slot = length // TILE

    def key_step(i, _):
        at = rows_of(i, TILE)
        local = rows_of(i % per_slot, TILE)
        slot = i // per_slot
        present = (slot == 0) | (context < half_contexts)
        block = jnp.where(slot == 0, context, jnp.where(present, contexts + context, 0))
        keep = jnp.where(present, 1.0, 0.0)
        for g in range(kv_heads):
            columns = slice(g * head, (g + 1) * head)
            back = dkv[block, local, columns].astype(f32) * keep
            inward, terms = head_back(kraw[at, columns], back, head_gain_ref[8:9, :], i)
            acc_head[1] += fold(terms)
            kraw[at, columns] = inward.astype(bf16)
        vback[at, :] = (dkv[block, local, kw:].astype(f32) * keep).astype(bf16)
        return 0

    lax.fori_loop(0, rows // TILE, key_step, 0)
    key_chunk = query_chunk + out_chunks
    weight_grad(first, kraw, 0, key_chunk, kw // chunk)
    weight_grad(first, vback, 0, key_chunk + kw // chunk, kw // chunk)
    fown = resid

    def first_step(i, _):
        @pl.when(i < steps)
        def _():
            both = lambda ref: jnp.concatenate([ref[theirs(i), :], ref[mine(i), :]], axis=0)
            result = dot_nt(both(qraw), wq[...])
            result += dot_nt(both(kraw), wk[...])
            result += dot_nt(both(vback), wv[...])
            fsend[half(i), :] = result[:step_rows].astype(bf16)
            f_copy(i).start()
            fown[half(i), :] = result[step_rows:]

        @pl.when(i > 0)
        def _():
            before = i - 1
            f_copy(before).wait_recv()
            total = fown[half(before), :] + frecv[half(before), :].astype(f32)
            fxsend[half(before), :] = total.astype(bf16)
            xf_copy(before).start()

        return 0

    lax.fori_loop(0, steps + 1, first_step, 0)
    for i in range(steps):
        xs_copy(i).wait_send()

    def tokens_step(i, _):
        tick(tick_at + i)
        xf_copy(i).wait_recv()
        back = fxsend[half(i), :].astype(f32) + fxrecv[half(i), :].astype(f32)
        inward, terms = norm_back(own_tok[half(i), :].astype(f32), back, gains[0:1, :])
        acc_gain[...] += fold(terms)
        spart[half(i), :] = (resback[half(i), :] + inward).astype(bf16)
        tgrad_copy(i).start()
        tgrad_keep(i).start()
        return 0

    lax.fori_loop(0, steps, tokens_step, 0)
    tick_at += steps

    def total_of(values):
        return jnp.sum(jnp.sum(values, axis=0, keepdims=True), axis=1, keepdims=True)

    lanes = lax.broadcasted_iota(jnp.int32, (1, width), 1)
    base = (shard * 2 + core) * 4
    squares = jnp.where(lanes == base, total_of(acc_square[0]), 0.0)
    squares += jnp.where(lanes == base + 1, total_of(square[...]), 0.0)
    squares += jnp.where(lanes == base + 2, total_of(acc_square[1]), 0.0)
    sums[0] = jnp.zeros((8, width), f32)
    sums[0, 0:1, :] = 0.5 * jnp.sum(acc_gain[...], axis=0, keepdims=True)
    sums[0, 1:2, :] = 0.5 * jnp.sum(acc_ff[...], axis=0, keepdims=True)
    sums[0, 2:3, :head] = jnp.sum(acc_head[0], axis=0, keepdims=True)
    sums[0, 2:3, head : 2 * head] = jnp.sum(acc_head[1], axis=0, keepdims=True)
    sums[0, 3:4, :] = 0.5 * squares

    def sum_copy(n, target, device):
        return remote(sums.at[n], target, s_send.at[n], s_recv.at[n], device)

    first_hop = sum_copy(0, sums_in.at[0], core_peer)
    first_hop.start()
    first_hop.wait_recv()
    sums[1] = sums[0] + sums_in[0]
    second_hop = sum_copy(1, sums_in.at[1], x_peer)
    second_hop.start()
    second_hop.wait_recv()
    sums[2] = sums[1] + sums_in[1]
    shard_hops = [
        remote(sums.at[2], sums_y.at[shard], s_send.at[4 + d], s_recv.at[4 + d], peers[d])
        for d in range(shards - 1)
    ]
    for copy in shard_hops:
        copy.start()
    sums_y[shard] = sums[2]
    tick(tick_at)
    tick_at += 1
    for copy in shard_hops:
        copy.wait_recv()
    total = sums_y[0]
    for s in range(1, shards):
        total = total + sums_y[s]
    sums[3] = total
    sum_down = remote(sums.at[3], sums_in.at[2], s_send.at[3], s_recv.at[2], below)
    sum_up = remote(sums.at[3], sums_in.at[2], s_send.at[3], s_recv.at[2], above)
    sum_top = remote(sums.at[3], sums_in.at[3], s_send.at[3], s_recv.at[3], below)
    last = 4 + shards - 1
    result_down = remote(sums_in.at[4], sums_in.at[4], s_send.at[last], s_recv.at[last], below)
    result_up = remote(sums_in.at[4], sums_in.at[4], s_send.at[last + 1], s_recv.at[last], above)

    def add_sums():
        sums[3] = sums[3] + sums_in[2]

    @pl.when(context < root)
    def _():
        @pl.when(context > 0)
        def _():
            sum_up.wait_recv()
            add_sums()

        sum_up.start()

    @pl.when(context > root)
    def _():
        @pl.when(context < contexts - 1)
        def _():
            sum_down.wait_recv()
            add_sums()

        @pl.when(context == root + 1)
        def _():
            sum_top.start()

        @pl.when(context > root + 1)
        def _():
            sum_down.start()

    def more_ticks(t, _):
        tick(t)
        return 0

    lax.fori_loop(tick_at, ticks, more_ticks, 0)

    @pl.when(context == root)
    def _():
        total = sums[3]
        if root > 0:
            sum_up.wait_recv()
            total = total + sums_in[2]
        if root < contexts - 1:
            sum_top.wait_recv()
            total = total + sums_in[3]
        sums_in[4] = total

    @pl.when(context != root)
    def _():
        result_down.wait_recv()

    @pl.when((context <= root) & (context > 0))
    def _():
        result_down.start()

    @pl.when((context >= root) & (context < contexts - 1))
    def _():
        result_up.start()

    sums_keep = pltpu.make_async_copy(sums_in.at[4], sums_out, store_sem.at[2, 0])
    sums_keep.start()
    first_hop.wait_send()
    second_hop.wait_send()
    for copy in shard_hops:
        copy.wait_send()

    @pl.when(context != root)
    def _():
        sum_up.wait_send()

    @pl.when((context <= root) & (context > 0))
    def _():
        result_down.wait_send()

    @pl.when((context >= root) & (context < contexts - 1))
    def _():
        result_up.wait_send()

    def drain_steps(i, _):
        for copy in (outin_copy, layer_copy, f_copy, tgrad_copy):
            copy(i).wait_send()
        layer_copy(i).wait_recv()
        tgrad_copy(i).wait_recv()
        xf_copy(i).wait_send()
        layer_keep(i).wait()
        tgrad_keep(i).wait()
        return 0

    lax.fori_loop(0, steps, drain_steps, 0)

    def drain_chunks(k, _):
        @pl.when(k >= chunk_count - early)
        def _():
            for d in range(shards - 1):
                y_copy(d, k).wait_send()

        @pl.when(context != root)
        def _():
            up_copy(k).wait_send()

        @pl.when((context <= root) & (context > 0))
        def _():
            back_down_copy(k).wait_send()

        @pl.when((context >= root) & (context < contexts - 1))
        def _():
            back_up_copy(k).wait_send()

        grad_keep(k).wait()
        return 0

    lax.fori_loop(0, chunk_count, drain_chunks, 0)
    for block in range(contexts):
        for slot, count in ((0, contexts), (1, half_contexts)):
            if block < count:

                @pl.when((block < context) & (context < count))
                def _():
                    d_copy(slot, block).wait_send()

    sums_keep.wait()


def call_layer_backward(shards, contexts, order, first_part):
    (
        second, gback, uback, cotin, hidden, spart, mpart, resid, square, mixed, linv, qs, qraw,
        kraw, kv, first, wq, wk, wv, wo, gains, own_tok, head_gains, cosine, sine,
    ) = first_part
    rows, width = second.shape
    length = resid.shape[0]
    ff, qw, kw = gback.shape[1], wq.shape[1], wk.shape[1]
    share = width // shards
    chunk = TILE
    chunk_count = (3 * ff + 2 * qw + 2 * kw) // chunk
    early = (3 * ff + qw) // chunk
    steps = 2 * length // TILE
    blocks = contexts + contexts // 2
    slots = rows // length
    shape = jax.ShapeDtypeStruct
    outs = (
        shape((chunk_count, share, chunk), bf16), shape((slots, length, width), bf16),
        shape((slots, length, width), bf16), shape((8, width), f32),
    )
    dma = pltpu.SemaphoreType.DMA

    def like(array):
        return pltpu.VMEM(array.shape, array.dtype)

    half = pltpu.VMEM((length, width), bf16)
    chunks = pltpu.VMEM((chunk_count, share, chunk), bf16)
    return pl.pallas_call(
        functools.partial(layer_backward, shards, contexts),
        out_shape=outs,
        in_specs=[SMEM] + [HBM] * 22 + [VMEM] * 3,
        out_specs=[HBM] * len(outs),
        scratch_shapes=[
            like(second), like(gback), like(uback), like(cotin), like(hidden), like(spart),
            like(mpart), like(resid), like(square), like(linv), like(wq), like(wk), like(wv),
            like(wo), like(gains), like(own_tok),
            pltpu.VMEM((2, *kv.shape[1:]), bf16),
            half, half, pltpu.VMEM((rows, width), bf16), pltpu.VMEM((length, width), f32),
            pltpu.VMEM((blocks, length, 2 * kw), bf16), pltpu.VMEM((blocks, length, 2 * kw), bf16),
            half, half, half, half,
            chunks,
            pltpu.VMEM((shards - 1, early, share, chunk), bf16),
            pltpu.VMEM((shards - 1, chunk_count, share, chunk), bf16),
            chunks, chunks,
            pltpu.VMEM((4, 8, width), f32), pltpu.VMEM((5, 8, width), f32),
            pltpu.VMEM((shards, 8, width), f32),
            pltpu.VMEM((8, width), f32), pltpu.VMEM((8, width), f32),
            pltpu.VMEM((2, 8, cosine.shape[1]), f32), pltpu.VMEM((2, 8, width), f32),
            dma((16,)), dma((2,)), dma((chunk_count,)), dma((3, steps)),
            dma((3, steps)), dma((3, steps)), dma((4, steps)), dma((4, steps)),
            dma((shards - 1, chunk_count)), dma((shards - 1, chunk_count)),
            dma((chunk_count,)), dma((chunk_count,)), dma((chunk_count,)),
            dma((2, chunk_count)), dma((chunk_count,)), dma((blocks,)), dma((blocks,)),
            dma((4 + shards + 1,)), dma((4 + shards + 1,)),
        ],
        compiler_params=pltpu.CompilerParams(
            collective_id=3, has_side_effects=True, vmem_limit_bytes=62 * 2**20
        ),
        name="layer_backward",
    )(order, *first_part)


def local(
    tokens, lengths, cotangent, query_weight, key_weight, value_weight, out_weight, gate_weight,
    up_weight, down_weight, attention_gain, feedforward_gain, query_gain, key_gain,
):
    slots, length, width = tokens.shape
    shards, contexts = lax.axis_size("shard"), lax.axis_size("context")
    shard, context, _ = place()
    head = query_gain.shape[0]
    ff, qw, kw = gate_weight.shape[1], query_weight.shape[1], key_weight.shape[1]
    first_slot = (lengths[1] > lengths[0]).astype(jnp.int32)
    order = jnp.stack([first_slot, jnp.minimum(lengths[0], lengths[1])])
    cosine, sine = (
        lax.dynamic_slice_in_dim(jnp.asarray(table), context * length, length, 0)
        for table in rope_tables(contexts * length, head)
    )

    def eight(vector):
        return jnp.broadcast_to(vector.astype(f32)[None], (8, vector.shape[0]))

    gain_share = jnp.concatenate([eight(attention_gain), eight(feedforward_gain)])
    head_gains = jnp.concatenate([eight(query_gain), eight(key_gain)])
    (mixed, kv, qs, qraw, kraw, linv, first, wq, wk, wv, wo, wg, wu, gains) = (
        call_attention_forward(
            shards, contexts, order, tokens, query_weight, key_weight, value_weight, out_weight,
            gate_weight, up_weight, gain_share, head_gains, cosine, sine,
        )
    )
    (second, hidden, gback, uback, cotin, spart, mpart, resid, square, own_tok) = (
        call_feed_forward(
            shards, order, mixed, wo, tokens, cotangent, gains, wg, wu, down_weight
        )
    )
    grads, layer, token_grads, sums = call_layer_backward(
        shards, contexts, order,
        (
            second, gback, uback, cotin, hidden, spart, mpart, resid, square, mixed, linv, qs,
            qraw, kraw, kv, first, wq, wk, wv, wo, gains, own_tok, head_gains, cosine, sine,
        ),
    )
    swapped = first_slot == 1

    def in_place(values):
        return jnp.where(swapped, values[::-1], values)

    at = 0

    def next_grad(columns):
        nonlocal at
        count = columns // TILE
        taken = grads[at : at + count].astype(f32)
        at += count
        return taken

    def straight(columns):
        return next_grad(columns).transpose(1, 0, 2).reshape(width // shards, columns)

    def turned(columns):
        return next_grad(columns).transpose(0, 2, 1).reshape(columns, width // shards)

    gate_grad, up_grad = straight(ff), straight(ff)
    down_grad, out_grad = turned(ff), turned(qw)
    query_grad, key_grad, value_grad = straight(qw), straight(kw), straight(kw)
    gain_grads = lax.dynamic_slice_in_dim(sums[:2], shard * (width // shards), width // shards, 1)
    squares = lax.dynamic_slice_in_dim(sums[3], shard * slots * 4, slots * 4, 0)
    squares = in_place(squares.reshape(slots, 4)[:, :3])
    return (
        in_place(layer),
        in_place(token_grads.astype(f32)),
        query_grad,
        key_grad,
        value_grad,
        out_grad,
        gate_grad,
        up_grad,
        down_grad,
        gain_grads[0],
        gain_grads[1],
        sums[2, :head],
        sums[2, head : 2 * head],
        jnp.sqrt(squares / (lengths.astype(f32)[:, None] * width)),
    )


def solution(mesh):
    placed = (
        P("shard", "context", None),
        P("shard"),
        P("shard", "context", None),
        P("shard", "tensor"),
        P("shard", "tensor"),
        P("shard", "tensor"),
        P("tensor", "shard"),
        P("shard", "tensor"),
        P("shard", "tensor"),
        P("tensor", "shard"),
        P("shard"),
        P("shard"),
        P(),
        P(),
    )
    return jax.shard_map(
        local,
        mesh=mesh,
        in_specs=placed,
        out_specs=(
            P("shard", "context", None),
            P("shard", "context", None),
            P("shard", "tensor"),
            P("shard", "tensor"),
            P("shard", "tensor"),
            P("tensor", "shard"),
            P("shard", "tensor"),
            P("shard", "tensor"),
            P("tensor", "shard"),
            P("shard"),
            P("shard"),
            P(),
            P(),
            P("shard", None),
        ),
        check_vma=False,
    )
```

```python
import functools
import math

import jax
import jax.numpy as jnp
import numpy as np
from jax import lax
from jax.experimental import pallas as pl
from jax.experimental.pallas import tpu as pltpu
from jax.sharding import PartitionSpec as P

epsilon = 1e-06
rope_base = 1000000.0
MESH = pl.DeviceIdType.MESH
f32 = jnp.float32
bf16 = jnp.bfloat16
HBM = pl.BlockSpec(memory_space=pl.ANY)
VMEM = pl.BlockSpec(memory_space=pltpu.VMEM)
SMEM = pl.BlockSpec(memory_space=pltpu.SMEM)
TILE = 256


def rows_of(index, size):
    return pl.ds(pl.multiple_of(index * size, size), size)


def dot_nt(left, right):
    return lax.dot_general(left, right, (((1,), (1,)), ((), ())), preferred_element_type=f32)


def dot_tn(left, right):
    return lax.dot_general(left, right, (((0,), (0,)), ((), ())), preferred_element_type=f32)


def dot_nn(left, right):
    return jnp.dot(left, right, preferred_element_type=f32)


def mean_square(values):
    return jnp.mean(values * values, axis=-1, keepdims=True)


def place():
    return lax.axis_index("shard"), lax.axis_index("context"), lax.axis_index("tensor")


def greet(devices, extra=0):
    barrier = pltpu.get_barrier_semaphore()
    for device in devices:
        pl.semaphore_signal(barrier, inc=1, device_id=device, device_id_type=MESH)
    return barrier


def greet_line(barrier, shard, context, tensor, count):
    @pl.when(context > 0)
    def _():
        pl.semaphore_signal(
            barrier, inc=1, device_id=(shard, context - 1, tensor), device_id_type=MESH
        )

    @pl.when(context < count - 1)
    def _():
        pl.semaphore_signal(
            barrier, inc=1, device_id=(shard, context + 1, tensor), device_id_type=MESH
        )

    return jnp.minimum(context, 1) + jnp.minimum(count - 1 - context, 1)


def turn(cosine, sine, start_ref, block, inside_cos_ref, inside_sin_ref):
    head = cosine.shape[1]
    start_cos, start_sin = start_ref[block, 0:1, :], start_ref[block, 8:9, :]
    signs = jnp.where(lax.broadcasted_iota(jnp.int32, (1, head), 1) < head // 2, -1.0, 1.0)
    inside_cos, inside_sin = inside_cos_ref[...], inside_sin_ref[...]
    cosine[...] = start_cos * inside_cos - start_sin * inside_sin
    sine[...] = signs * (start_sin * inside_cos + start_cos * inside_sin)


def slot_order(lengths_ref):
    one, other = lengths_ref[0], lengths_ref[1]
    return jnp.where(other > one, 1, 0), jnp.minimum(one, other)


def gather_loads(share_ref, whole_ref, target, shard, shards, axis, sems):
    size = share_ref.shape[axis]
    copies = []
    for d in range(shards):
        at = rows_of(lax.rem(shard + d, shards), size)
        index = (slice(None), at) if axis == 1 else (at, slice(None))
        source = share_ref if d == 0 else whole_ref.at[index]
        copies.append(pltpu.make_async_copy(source, target.at[index], sems.at[d]))
    return copies


def remote(src, dst, send_sem, recv_sem, device):
    return pltpu.make_async_remote_copy(
        src_ref=src,
        dst_ref=dst,
        send_sem=send_sem,
        recv_sem=recv_sem,
        device_id=device,
        device_id_type=MESH,
    )


def rope_tables(length, contexts, head_size):
    half = head_size // 2
    speeds = np.tile(rope_base ** (-np.arange(half, dtype=np.float64) * 2.0 / head_size), 2)
    inside = np.arange(length, dtype=np.float64)[:, None] * speeds
    starts = np.arange(contexts, dtype=np.float64)[:, None] * length * speeds
    rows = np.stack([np.cos(starts), np.sin(starts)], axis=1)
    rows = np.repeat(rows, 8, axis=1)
    return (
        np.cos(inside).astype(np.float32),
        np.sin(inside).astype(np.float32),
        rows.astype(np.float32),
    )


def attention_forward(
    shards, contexts, lengths_ref, tok_ref, wq_ref, wk_ref, wv_ref, wo_ref, wg_ref, gain_ref,
    head_gain_ref, inside_cos_ref, inside_sin_ref, start_ref,
    mixed_out, kv_out, qs_out, qraw_out, kraw_out, linv_out, first_out, wq_out, wk_out, wv_out,
    wo_out, wg_out, gain_out,
    tok, first, wq, wk, wv, gains, kv, qs, qraw, kraw, acc, mixed, linv, cosine, sine,
    load_sem, own_sem, store_sem, unit_sem, wsend, wrecv, z_send, z_recv, x_send, x_recv,
    core_send, core_recv,
):
    shard, context, tensor = place()
    slots, length, width = tok.shape
    share = wq_ref.shape[0]
    query_width = wq.shape[1]
    key_width = wk.shape[1]
    head = head_gain_ref.shape[1]
    heads = query_width // head
    group = query_width // key_width
    half = contexts // 2
    quarter = length // 4
    score_scale = head**-0.5 * math.log2(math.e)
    core = tensor % 2
    core_peer = (shard, context, tensor + 1 - 2 * core)
    x_peer = (shard, context, (tensor + 2) % 4)
    above = (shard, jnp.minimum(context + 1, contexts - 1), tensor)
    peers = [(lax.rem(shard + d, shards), context, tensor) for d in range(1, shards)]
    barrier = greet([core_peer, x_peer, *peers])
    neighbours = greet_line(barrier, shard, context, tensor, contexts)

    load_tok = pltpu.make_async_copy(tok_ref, tok, load_sem)
    load_tok.start()
    mine = rows_of(shard, share)
    weights = [
        (gain_ref, gains.at[:, mine]),
        (wk_ref, wk.at[mine, :]),
        (wv_ref, wv.at[mine, :]),
        (wq_ref, wq.at[mine, :]),
        (wo_ref, wo_out.at[:, mine]),
        (wg_ref, wg_out.at[mine, :]),
    ]
    own = [
        pltpu.make_async_copy(source, target, own_sem.at[w])
        for w, (source, target) in enumerate(weights[:4])
    ]
    sends = [
        [
            remote(source, target, wsend.at[w, d], wrecv.at[w, d], peers[d])
            for d in range(shards - 1)
        ]
        for w, (source, target) in enumerate(weights)
    ]
    for copy in own:
        copy.start()
    pl.semaphore_wait(barrier, shards + 1 + neighbours)

    def send_weights(*places):
        for w in places:
            for copy in sends[w]:
                copy.start()

    def have_weights(*places):
        for w in places:
            for copy in sends[w]:
                copy.wait_recv()

    send_weights(0, 1, 2)
    for slot in range(slots):
        for h in range(heads):
            acc[slot, h] = jnp.zeros((length, 2 * head), f32)
    load_tok.wait()
    for copy in own:
        copy.wait()
    have_weights(0)
    first_slot, short_length = slot_order(lengths_ref)
    per_slot = length // TILE
    tiles = slots * per_slot

    def norm_rows(i, _):
        slot = i // per_slot
        source = jnp.where(slot == 0, first_slot, 1 - first_slot)
        values = tok[source, rows_of(i % per_slot, TILE), :].astype(f32)
        scale = lax.rsqrt(mean_square(values) + epsilon)
        first[context, slot, rows_of(i % per_slot, TILE), :] = (
            values * scale * gains[0:1, :]
        ).astype(bf16)
        return 0

    lax.fori_loop(0, tiles, norm_rows, 0)

    def part(block, slot, which):
        return first.at[block, slot, rows_of(which, quarter), :]

    def z_copy(block, slot):
        rows = part(block, slot, tensor)
        return remote(rows, rows, z_send.at[block, slot], z_recv.at[block, slot], above)

    def x_copy(block, slot):
        rows = part(block, slot, tensor)
        return remote(rows, rows, x_send.at[block, slot], x_recv.at[block, slot], x_peer)

    def core_copy(kind, block, slot):
        rows = part(block, slot, tensor if kind == 0 else (tensor + 2) % 4)
        return remote(
            rows, rows, core_send.at[kind, block, slot], core_recv.at[kind, block, slot], core_peer
        )

    def unit_copies(block, slot):
        return [
            pltpu.make_async_copy(
                source.at[block, slot], target.at[block, slot], unit_sem.at[n, block, slot]
            )
            for n, (source, target) in enumerate(
                ((first, first_out), (kv, kv_out), (kraw, kraw_out))
            )
        ]

    def go_up(block, slot):
        @pl.when(context < contexts - 1)
        def _():
            z_copy(block, slot).start()

    def stage_in(block, slot):
        z_copy(block, slot).wait_recv()
        go_up(block, slot)
        x_copy(block, slot).start()
        core_copy(0, block, slot).start()

    def stage_across(block, slot):
        x_copy(block, slot).wait_recv()
        core_copy(1, block, slot).start()

    def head_form(raw, gain, local):
        normal = raw * lax.rsqrt(mean_square(raw) + epsilon) * gain
        return normal * cosine[local, :] + pltpu.roll(normal, head // 2, 1) * sine[local, :]

    def make_keys(block, slot):
        turn(cosine, sine, start_ref, block, inside_cos_ref, inside_sin_ref)

        def rows(i, _):
            local = rows_of(i, TILE)
            values = first[block, slot, local, :]
            raw = dot_nn(values, wk[...])
            kraw[block, slot, local, :] = raw.astype(bf16)
            for g in range(key_width // head):
                columns = slice(g * head, (g + 1) * head)
                kv[block, slot, local, columns] = head_form(
                    raw[:, columns], head_gain_ref[8:9, :], local
                ).astype(bf16)
            kv[block, slot, local, key_width:] = dot_nn(values, wv[...]).astype(bf16)
            return 0

        lax.fori_loop(0, per_slot, rows, 0)
        for copy in unit_copies(block, slot):
            copy.start()

    def stage_keys(block, slot):
        core_copy(0, block, slot).wait_recv()
        core_copy(1, block, slot).wait_recv()
        make_keys(block, slot)

    ones = jnp.ones((length, head), bf16)

    def attend(block, slot, diagonal):
        def one_head(h, _):
            columns = rows_of(h, head)
            keys = kv[block, slot, :, rows_of(h // group, head)]
            values = kv[block, slot, :, rows_of(key_width // head + h // group, head)]
            raised = jnp.exp2(dot_nt(qs[slot * length : (slot + 1) * length, columns], keys))
            spots = lax.broadcasted_iota(jnp.int32, (length, length), 1)
            if diagonal:
                lines = lax.broadcasted_iota(jnp.int32, (length, length), 0)
                raised = jnp.where(spots <= lines, raised, 0.0)
            if slot == 1:
                raised = jnp.where(spots + block * length < short_length, raised, 0.0)
            acc[slot, h] += dot_nn(
                raised.astype(bf16), jnp.concatenate([values, ones], axis=1)
            )
            return 0

        lax.fori_loop(0, heads, one_head, 0)

    units = [(r, slot) for r in range(1, contexts) for slot in range(slots)]

    def for_unit(n, action):
        if 0 <= n < len(units):
            back, slot = units[n]
            block = context - back

            @pl.when((block >= 0) if slot == 0 else ((block >= 0) & (block < half)))
            def _():
                action(block, slot)

    def for_own(action):
        action(context, 0)

        @pl.when(context < half)
        def _():
            action(context, 1)

    for_own(go_up)
    for_unit(0, stage_in)
    for_unit(1, stage_in)
    have_weights(1, 2)
    send_weights(3)
    make_keys(context, 0)
    make_keys(context, 1)
    for_unit(0, stage_across)
    for_unit(2, stage_in)
    for_unit(1, stage_across)
    for_unit(0, stage_keys)
    for_unit(3, stage_in)
    for_unit(2, stage_across)
    for_unit(1, stage_keys)
    have_weights(3)
    send_weights(4, 5)
    store_weights = [
        pltpu.make_async_copy(source, target, store_sem.at[n])
        for n, (source, target) in enumerate(
            ((wq, wq_out), (wk, wk_out), (wv, wv_out), (gains, gain_out))
        )
    ]
    for copy in store_weights:
        copy.start()
    turn(cosine, sine, start_ref, context, inside_cos_ref, inside_sin_ref)

    def query_rows(i, _):
        place_rows = rows_of(i, TILE)
        local = rows_of(i % per_slot, TILE)
        raw = dot_nn(first[context, i // per_slot, local, :], wq[...])
        qraw[place_rows, :] = raw.astype(bf16)
        for h in range(heads):
            columns = slice(h * head, (h + 1) * head)
            qs[place_rows, columns] = (
                head_form(raw[:, columns], head_gain_ref[0:1, :], local) * score_scale
            ).astype(bf16)
        return 0

    lax.fori_loop(0, tiles, query_rows, 0)
    store_raw = [
        pltpu.make_async_copy(source, target, store_sem.at[n])
        for n, (source, target) in enumerate(((qs, qs_out), (qraw, qraw_out)), 4)
    ]
    for copy in store_raw:
        copy.start()
    for_own(lambda block, slot: attend(block, slot, True))
    for n in range(len(units)):
        for_unit(n + 4, stage_in)
        for_unit(n + 3, stage_across)
        for_unit(n + 2, stage_keys)
        for_unit(n, lambda block, slot: attend(block, slot, False))

    def finish(h, _):
        columns = rows_of(h, head)
        for slot in range(slots):
            lines = slice(slot * length, (slot + 1) * length)
            inverse = 1.0 / acc[slot, h, :, head:]
            mixed[lines, columns] = (acc[slot, h, :, :head] * inverse).astype(bf16)
            linv[lines, columns] = inverse
        return 0

    lax.fori_loop(0, heads, finish, 0)
    store_last = [
        pltpu.make_async_copy(source, target, store_sem.at[n])
        for n, (source, target) in enumerate(((mixed, mixed_out), (linv, linv_out)), 6)
    ]
    for copy in store_last:
        copy.start()

    def sent_up(block, slot):
        @pl.when(context < contexts - 1)
        def _():
            z_copy(block, slot).wait_send()

    def unit_done(block, slot):
        sent_up(block, slot)
        x_copy(block, slot).wait_send()
        core_copy(0, block, slot).wait_send()
        core_copy(1, block, slot).wait_send()
        for copy in unit_copies(block, slot):
            copy.wait()

    for_own(sent_up)
    for slot in range(slots):
        for copy in unit_copies(context, slot):
            copy.wait()
    for n in range(len(units)):
        for_unit(n, unit_done)
    have_weights(4, 5)
    for copies in sends:
        for copy in copies:
            copy.wait_send()
    for copy in [*store_weights, *store_raw, *store_last]:
        copy.wait()


def call_attention_forward(
    shards, contexts, lengths, tokens, query_weight, key_weight, value_weight, out_weight,
    gate_weight, gain_share, head_gains, tables,
):
    slots, length, width = tokens.shape
    rows = slots * length
    qw, kw, ff = query_weight.shape[1], key_weight.shape[1], gate_weight.shape[1]
    head = head_gains.shape[1]
    heads = qw // head
    n_weights = 6
    shape = jax.ShapeDtypeStruct
    dma = pltpu.SemaphoreType.DMA
    kv_shape = (contexts, slots, length, 2 * kw)
    kraw_shape = (contexts, slots, length, kw)
    first_shape = (contexts, slots, length, width)
    outs = (
        shape((rows, qw), bf16), shape(kv_shape, bf16), shape((rows, qw), bf16),
        shape((rows, qw), bf16), shape(kraw_shape, bf16), shape((rows, qw), f32),
        shape(first_shape, bf16), shape((width, qw), bf16), shape((width, kw), bf16),
        shape((width, kw), bf16), shape((qw, width), bf16), shape((width, ff), bf16),
        shape((16, width), f32),
    )
    units = (contexts, slots)
    return pl.pallas_call(
        functools.partial(attention_forward, shards, contexts),
        out_shape=outs,
        in_specs=[SMEM] + [HBM] * 7 + [VMEM] * 4,
        out_specs=[HBM] * len(outs),
        scratch_shapes=[
            pltpu.VMEM((slots, length, width), bf16),
            pltpu.VMEM(first_shape, bf16),
            pltpu.VMEM((width, qw), bf16),
            pltpu.VMEM((width, kw), bf16),
            pltpu.VMEM((width, kw), bf16),
            pltpu.VMEM((16, width), f32),
            pltpu.VMEM(kv_shape, bf16),
            pltpu.VMEM((rows, qw), bf16),
            pltpu.VMEM((rows, qw), bf16),
            pltpu.VMEM(kraw_shape, bf16),
            pltpu.VMEM((slots, heads, length, 2 * head), f32),
            pltpu.VMEM((rows, qw), bf16),
            pltpu.VMEM((rows, qw), f32),
            pltpu.VMEM((length, head), f32),
            pltpu.VMEM((length, head), f32),
            dma, dma((4,)), dma((8,)), dma((3, *units)),
            dma((n_weights, shards - 1)), dma((n_weights, shards - 1)),
            dma(units), dma(units), dma(units), dma(units), dma((2, *units)), dma((2, *units)),
        ],
        compiler_params=pltpu.CompilerParams(
            collective_id=1, has_side_effects=True, vmem_limit_bytes=60 * 2**20
        ),
        name="attention_forward",
    )(
        lengths, tokens, query_weight, key_weight, value_weight, out_weight, gate_weight,
        gain_share, head_gains, *tables,
    )


def feed_forward(
    shards, lengths_ref, mixed_ref, wo_ref, tok_ref, cot_ref, gain_ref, wg_ref, wo_own_ref,
    wg_own_ref, wu_ref, wd_ref,
    second_out, hidden_out, gback_out, uback_out, cotin_out, spart_out, mpart_out, resid_out,
    square_out, own_tok_out,
    mixed, wo, tok, cot, gains, wg, wu, wd, second, hidden, gback, uback, cotin, spart, mpart,
    resid, square, own_tok, apart, csend, crecv, xsend, xrecv, ssend, srecv, msend, mrecv, gvalue, uvalue,
    load_sem, gather_sem, store_sem, wsend, wrecv, core_send, core_recv, x_send, x_recv,
):
    shard, context, tensor = place()
    slots, length, width = tok.shape
    share = wd_ref.shape[1]
    step_rows = TILE // 2
    steps = length // step_rows
    core = tensor % 2
    core_peer = (shard, context, tensor + 1 - 2 * core)
    x_peer = (shard, context, (tensor + 2) % 4)
    peers = [(lax.rem(shard + d, shards), context, tensor) for d in range(1, shards)]
    barrier = greet([core_peer, x_peer, *peers])
    loads = [
        pltpu.make_async_copy(source, target, load_sem.at[n])
        for n, (source, target) in enumerate(
            (
                (mixed_ref, mixed), (tok_ref, tok), (gain_ref, gains), (cot_ref, cot),
                (wu_ref, wu.at[rows_of(shard, share), :]),
                (wd_ref, wd.at[:, rows_of(shard, share)]),
            )
        )
    ]
    gathers = [
        gather_loads(own_ref, whole_ref, target, shard, shards, axis, gather_sem.at[n])
        for n, (own_ref, whole_ref, target, axis) in enumerate(
            (
                (wo_own_ref, wo_ref, wo, 1), (wg_own_ref, wg_ref, wg, 0),
            )
        )
    ]
    for copy in [loads[0], *gathers[0], *loads[1:], *gathers[1]]:
        copy.start()
    square[...] = jnp.zeros_like(square)
    pl.semaphore_wait(barrier, shards + 1)
    sends = [
        [
            remote(source, target, wsend.at[w, d], wrecv.at[w, d], peers[d])
            for d in range(shards - 1)
        ]
        for w, (source, target) in enumerate(
            (
                (wu_ref, wu.at[rows_of(shard, share), :]),
                (wd_ref, wd.at[:, rows_of(shard, share)]),
            )
        )
    ]
    for copy in sends[0]:
        copy.start()
    for copy in [loads[0], *gathers[0]]:
        copy.wait()

    def mine(i):
        return rows_of(core * steps + i, step_rows)

    def theirs(i):
        return rows_of((1 - core) * steps + i, step_rows)

    def half(i):
        return rows_of(i, step_rows)

    def core_copy(kind, i, source, target):
        return remote(source, target, core_send.at[kind, i], core_recv.at[kind, i], core_peer)

    def attn_copy(i):
        return core_copy(0, i, csend.at[half(i), :], crecv.at[half(i), :])

    def second_copy(i):
        return core_copy(1, i, second.at[mine(i), :], second.at[mine(i), :])

    def spart_copy(i):
        return core_copy(2, i, ssend.at[half(i), :], srecv.at[half(i), :])

    def mpart_copy(i):
        return core_copy(3, i, msend.at[half(i), :], mrecv.at[half(i), :])

    def x_copy(i):
        return remote(
            xsend.at[half(i), :], xrecv.at[half(i), :], x_send.at[i], x_recv.at[i], x_peer
        )

    def project(i, _):
        @pl.when(i < steps)
        def _():
            both = jnp.concatenate([mixed[theirs(i), :], mixed[mine(i), :]], axis=0)
            result = dot_nn(both, wo[...])
            csend[half(i), :] = result[:step_rows].astype(bf16)
            attn_copy(i).start()
            apart[half(i), :] = result[step_rows:]

        @pl.when(i > 0)
        def _():
            before = i - 1
            attn_copy(before).wait_recv()
            total = apart[half(before), :] + crecv[half(before), :].astype(f32)
            xsend[half(before), :] = total.astype(bf16)
            x_copy(before).start()

        return 0

    lax.fori_loop(0, steps + 1, project, 0)
    for copy in [*loads[1:], *gathers[1]]:
        copy.wait()
    first_slot, short_length = slot_order(lengths_ref)
    own_source = jnp.where(core == 0, first_slot, 1 - first_slot)

    def counted(slot, i):
        spots = context * length + i * step_rows
        lines = lax.broadcasted_iota(jnp.int32, (step_rows, width), 0) + spots
        limit = jnp.where(slot == 0, 2**30, short_length)
        return lines < limit

    def cut(slot, i):
        source = jnp.where(slot == 0, first_slot, 1 - first_slot)
        values = cot[source, half(i), :].astype(f32)
        return jnp.where(counted(slot, i), values, 0.0).astype(bf16)

    def normalise(i):
        x_copy(i).wait_recv()
        attn = xsend[half(i), :].astype(f32) + xrecv[half(i), :].astype(f32)
        attn_counted = jnp.where(counted(core, i), attn, 0.0)
        square[...] += jnp.sum(
            (attn_counted * attn_counted).reshape(step_rows // 8, 8, width), axis=0
        )
        own_tok[half(i), :] = tok[own_source, half(i), :]
        residual = own_tok[half(i), :].astype(f32) + attn
        resid[half(i), :] = residual
        scale = lax.rsqrt(mean_square(residual) + epsilon)
        second[mine(i), :] = (residual * scale * gains[8:9, :]).astype(bf16)
        second_copy(i).start()
        cotin[mine(i), :] = cut(core, i)
        cotin[theirs(i), :] = cut(1 - core, i)

    def finish_parts(i):
        spart_copy(i).wait_recv()
        spart[half(i), :] = (
            spart[half(i), :].astype(f32) + srecv[half(i), :].astype(f32)
        ).astype(bf16)
        mpart_copy(i).wait_recv()
        mpart[half(i), :] = (
            mpart[half(i), :].astype(f32) + mrecv[half(i), :].astype(f32)
        ).astype(bf16)

    def gate(i):
        second_copy(i).wait_recv()
        both = jnp.concatenate([second[mine(i), :], second[theirs(i), :]], axis=0)
        gvalue[i] = dot_nn(both, wg[...])

    def up(i):
        both = jnp.concatenate([second[mine(i), :], second[theirs(i), :]], axis=0)
        up_value = dot_nn(both, wu[...])
        gate_value = gvalue[i]
        sigmoid = 1.0 / (1.0 + jnp.exp(-gate_value))
        swish = gate_value * sigmoid
        slope = sigmoid + swish * (1.0 - sigmoid)
        low = (swish * up_value).astype(bf16)
        hidden[mine(i), :] = low[:step_rows]
        hidden[theirs(i), :] = low[step_rows:]
        gvalue[i] = up_value * slope
        uvalue[i] = swish

    def backward(i):
        inward = jnp.concatenate([cotin[mine(i), :], cotin[theirs(i), :]], axis=0)
        hidden_back = dot_nt(inward, wd[...])
        gate_low = (hidden_back * gvalue[i]).astype(bf16)
        up_low = (hidden_back * uvalue[i]).astype(bf16)
        gback[mine(i), :] = gate_low[:step_rows]
        gback[theirs(i), :] = gate_low[step_rows:]
        uback[mine(i), :] = up_low[:step_rows]
        uback[theirs(i), :] = up_low[step_rows:]
        result = dot_nt(gate_low, wg[...]) + dot_nt(up_low, wu[...])
        ssend[half(i), :] = result[step_rows:].astype(bf16)
        spart_copy(i).start()
        spart[half(i), :] = result[:step_rows].astype(bf16)
        low = jnp.concatenate([hidden[mine(i), :], hidden[theirs(i), :]], axis=0)
        result = dot_nn(low, wd[...])
        msend[half(i), :] = result[step_rows:].astype(bf16)
        mpart_copy(i).start()
        mpart[half(i), :] = result[:step_rows].astype(bf16)

    def have(weight):
        for copy in sends[weight]:
            copy.wait_recv()

    up_lag = 2

    def step(i, _):
        @pl.when(i < steps)
        def _():
            normalise(i)
            gate(i)

        @pl.when(i == up_lag)
        def _():
            have(0)
            for copy in sends[1]:
                copy.start()

        @pl.when(i >= up_lag)
        def _():
            up(i - up_lag)

        return 0

    lax.fori_loop(0, steps + up_lag, step, 0)
    have(1)

    def back_step(i, _):
        @pl.when(i < steps)
        def _():
            backward(i)

        @pl.when(i > 0)
        def _():
            finish_parts(i - 1)

        return 0

    lax.fori_loop(0, steps + 1, back_step, 0)
    stores = [
        pltpu.make_async_copy(source, target, store_sem.at[n])
        for n, (source, target) in enumerate(
            (
                (second, second_out), (hidden, hidden_out), (gback, gback_out),
                (uback, uback_out), (cotin, cotin_out), (spart, spart_out), (mpart, mpart_out),
                (resid, resid_out), (square, square_out), (own_tok, own_tok_out),
            )
        )
    ]
    for copy in stores:
        copy.start()

    def drain(i, _):
        for copy in (attn_copy, second_copy, spart_copy, mpart_copy, x_copy):
            copy(i).wait_send()
        return 0

    lax.fori_loop(0, steps, drain, 0)
    for copies in sends:
        for copy in copies:
            copy.wait_send()
    for copy in stores:
        copy.wait()


def call_feed_forward(
    shards, lengths, mixed, out_whole, tokens, cotangent, gains, gate_whole, out_weight,
    gate_weight, up_weight, down_weight,
):
    slots, length, width = tokens.shape
    rows = slots * length
    qw = mixed.shape[1]
    ff = gate_weight.shape[1]
    steps = 2 * length // TILE
    shape = jax.ShapeDtypeStruct
    outs = (
        shape((rows, width), bf16), shape((rows, ff), bf16), shape((rows, ff), bf16),
        shape((rows, ff), bf16), shape((rows, width), bf16), shape((length, width), bf16),
        shape((length, width), bf16), shape((length, width), f32), shape((8, width), f32),
        shape((length, width), bf16),
    )
    half = pltpu.VMEM((length, width), bf16)
    return pl.pallas_call(
        functools.partial(feed_forward, shards),
        out_shape=outs,
        in_specs=[SMEM] + [HBM] * 10,
        out_specs=[HBM] * len(outs),
        scratch_shapes=[
            pltpu.VMEM((rows, qw), bf16),
            pltpu.VMEM((qw, width), bf16),
            pltpu.VMEM((slots, length, width), bf16),
            pltpu.VMEM((slots, length, width), bf16),
            pltpu.VMEM((16, width), f32),
            pltpu.VMEM((width, ff), bf16),
            pltpu.VMEM((width, ff), bf16),
            pltpu.VMEM((ff, width), bf16),
            *[pltpu.VMEM(out.shape, out.dtype) for out in outs],
            pltpu.VMEM((length, width), f32),
            *[half] * 8,
            pltpu.VMEM((steps, TILE, ff), f32),
            pltpu.VMEM((steps, TILE, ff), f32),
            pltpu.SemaphoreType.DMA((6,)),
            pltpu.SemaphoreType.DMA((2, shards)),
            pltpu.SemaphoreType.DMA((10,)),
            pltpu.SemaphoreType.DMA((2, shards - 1)),
            pltpu.SemaphoreType.DMA((2, shards - 1)),
            pltpu.SemaphoreType.DMA((4, steps)),
            pltpu.SemaphoreType.DMA((4, steps)),
            pltpu.SemaphoreType.DMA((steps,)),
            pltpu.SemaphoreType.DMA((steps,)),
        ],
        compiler_params=pltpu.CompilerParams(
            collective_id=2, has_side_effects=True, vmem_limit_bytes=56 * 2**20
        ),
        name="feed_forward",
    )(
        lengths, mixed, out_whole, tokens, cotangent, gains, gate_whole, out_weight,
        gate_weight, up_weight, down_weight,
    )


def layer_backward(
    shards, contexts, lengths_ref, second_ref, gback_ref, uback_ref, cotin_ref, hidden_ref,
    spart_ref, mpart_ref, resid_ref, square_ref, mixed_ref, linv_ref, qs_ref, qraw_ref, kraw_ref,
    kv_ref, first_ref, wq_ref, wk_ref, wv_ref, wo_ref, wo_own_ref, gain_ref, own_tok_ref, head_gain_ref,
    inside_cos_ref, inside_sin_ref, start_ref,
    straight_out, turned_out, layer_out, tgrad_out, sums_out,
    second, gback, uback, cotin, hidden, spart, mpart, resid, square, dq, wq, wkv, wo, gains,
    unit_kv, unit_first, unit_kraw, unit_back, kv_grad, cosine, sine, xs, xm, outin,
    resback, part, part_core, part_x, part_z, fxrecv,
    piece, ysend, yrecv, zin, ztop, turned, sums, sums_in, sums_y, acc_gain, acc_ff, acc_head,
    acc_square,
    load_sem, gather_sem, kv_sem, late_sem, store_sem, x_send, x_recv, core_send, core_recv, y_send, y_recv,
    g_send, z_recv, top_recv, res_send, res_recv, p_send, p_recv, s_send, s_recv,
):
    shard, context, tensor = place()
    rows, width = second.shape
    length = resid.shape[0]
    ff = gback.shape[1]
    qw, kw = wq.shape[1], wkv.shape[1] // 2
    head = head_gain_ref.shape[1]
    heads, kv_heads = qw // head, kw // head
    group = heads // kv_heads
    share = piece.shape[1]
    chunk_count, chunk = piece.shape[0], piece.shape[2]
    early = ysend.shape[1]
    half_contexts = contexts // 2
    root = contexts // 2
    turn_from, turn_to = 2 * ff // chunk, (3 * ff + qw) // chunk
    step_rows = TILE // 2
    steps = length // step_rows
    scale = head**-0.5
    core = tensor % 2
    chip = tensor // 2
    quarter = length // 4
    core_peer = (shard, context, tensor + 1 - 2 * core)
    x_peer = (shard, context, (tensor + 2) % 4)
    peers = [(lax.rem(shard + d, shards), context, tensor) for d in range(1, shards)]
    below = (shard, jnp.maximum(context - 1, 0), tensor)
    above = (shard, jnp.minimum(context + 1, contexts - 1), tensor)
    barrier = greet([core_peer, x_peer, *peers])
    neighbours = greet_line(barrier, shard, context, tensor, contexts)

    pairs = [
        (spart_ref, spart), (second_ref, second), (gback_ref, gback), (uback_ref, uback),
        (cotin_ref, cotin), (hidden_ref, hidden), (resid_ref, resid), (gain_ref, gains),
        (linv_ref, dq), (mpart_ref, mpart), (square_ref, square), (wq_ref, wq),
        (wk_ref, wkv.at[:, :kw]), (wv_ref, wkv.at[:, kw:]),
    ]
    loads = [
        pltpu.make_async_copy(source, target, load_sem.at[n])
        for n, (source, target) in enumerate(pairs)
    ]
    loads += gather_loads(wo_own_ref, wo_ref, wo, shard, shards, 1, gather_sem)
    for copy in loads:
        copy.start()

    def mine(i):
        return rows_of(core * steps + i, step_rows)

    def theirs(i):
        return rows_of((1 - core) * steps + i, step_rows)

    def half(i):
        return rows_of(i, step_rows)

    def xs_copy(i):
        return remote(spart.at[half(i), :], xs.at[half(i), :], x_send.at[0, i], x_recv.at[0, i], x_peer)

    def xm_copy(i):
        return remote(mpart.at[half(i), :], xm.at[half(i), :], x_send.at[1, i], x_recv.at[1, i], x_peer)

    fsend, fxsend, frecv = part.at[0], part.at[1], xs

    def xf_copy(i):
        return remote(
            fxsend.at[half(i), :], fxrecv.at[half(i), :], x_send.at[2, i], x_recv.at[2, i], x_peer
        )

    def core_copy(kind, i, source, target):
        return remote(source, target, core_send.at[kind, i], core_recv.at[kind, i], core_peer)

    def outin_copy(i):
        return core_copy(0, i, outin.at[mine(i), :], outin.at[mine(i), :])

    def layer_copy(i):
        return core_copy(1, i, mpart.at[half(i), :], layer_out.at[core, half(i), :])

    def f_copy(i):
        return core_copy(2, i, fsend.at[half(i), :], frecv.at[half(i), :])

    def tgrad_copy(i):
        return core_copy(3, i, spart.at[half(i), :], tgrad_out.at[core, half(i), :])

    def layer_keep(i):
        return pltpu.make_async_copy(
            mpart.at[half(i), :], layer_out.at[core, half(i), :], store_sem.at[0, i]
        )

    def tgrad_keep(i):
        return pltpu.make_async_copy(
            spart.at[half(i), :], tgrad_out.at[core, half(i), :], store_sem.at[1, i]
        )

    def y_copy(d, k):
        return remote(
            ysend.at[d, k % early], yrecv.at[d, k], y_send.at[d, k], y_recv.at[d, k], peers[d]
        )

    def up_copy(k):
        return remote(piece.at[k], zin.at[k], g_send.at[k], z_recv.at[k], above)

    def down_copy(k):
        return remote(piece.at[k], zin.at[k], g_send.at[k], z_recv.at[k], below)

    def top_copy(k):
        return remote(piece.at[k], ztop.at[k], g_send.at[k], top_recv.at[k], below)

    def back_down_copy(k):
        return remote(zin.at[k], zin.at[k], res_send.at[0, k], res_recv.at[k], below)

    def back_up_copy(k):
        return remote(zin.at[k], zin.at[k], res_send.at[1, k], res_recv.at[k], above)

    def grad_copies(k):
        column = rows_of(jnp.where(k < turn_from, k, k - (turn_to - turn_from)), chunk)
        row = jnp.clip(k - turn_from, 0, turn_to - turn_from - 1)
        return (
            pltpu.make_async_copy(zin.at[k], straight_out.at[:, column], late_sem.at[k]),
            pltpu.make_async_copy(
                turned.at[row], turned_out.at[rows_of(row, chunk), :], late_sem.at[k]
            ),
        )

    def grad_keep(k, finish=False):
        straight_copy, turned_copy = grad_copies(k)
        aside = (k >= turn_from) & (k < turn_to)

        @pl.when(jnp.logical_not(aside))
        def _():
            straight_copy.wait() if finish else straight_copy.start()

        @pl.when(aside)
        def _():
            if not finish:
                turned[k - turn_from] = zin[k].astype(f32).T.astype(bf16)
            turned_copy.wait() if finish else turned_copy.start()

    def reduce_chunk(k):
        total = piece[k].astype(f32)
        for d in range(shards - 1):
            y_copy(d, k).wait_recv()
            total = total + yrecv[d, k].astype(f32)
        piece[k] = total.astype(bf16)

        def add_in():
            piece[k] = (piece[k].astype(f32) + zin[k].astype(f32)).astype(bf16)

        @pl.when(context < root)
        def _():
            @pl.when(context > 0)
            def _():
                up_copy(k).wait_recv()
                add_in()

            up_copy(k).start()

        @pl.when(context > root)
        def _():
            @pl.when(context < contexts - 1)
            def _():
                down_copy(k).wait_recv()
                add_in()

            @pl.when(context == root + 1)
            def _():
                top_copy(k).start()

            @pl.when(context > root + 1)
            def _():
                down_copy(k).start()

        @pl.when(context == root)
        def _():
            total = piece[k].astype(f32)
            if root > 0:
                up_copy(k).wait_recv()
                total = total + zin[k].astype(f32)
            if root < contexts - 1:
                top_copy(k).wait_recv()
                total = total + ztop[k].astype(f32)
            zin[k] = total.astype(bf16)
            if root > 0:
                back_down_copy(k).start()
            if root < contexts - 1:
                back_up_copy(k).start()
            grad_keep(k)

    def return_chunk(k):
        @pl.when(context < root)
        def _():
            back_down_copy(k).wait_recv()

            @pl.when(context > 0)
            def _():
                back_down_copy(k).start()

            grad_keep(k)

        @pl.when(context > root)
        def _():
            back_up_copy(k).wait_recv()

            @pl.when(context < contexts - 1)
            def _():
                back_up_copy(k).start()

            grad_keep(k)

    far = max(root, contexts - 1 - root)
    from_end = jnp.where(context <= root, context, contexts - 1 - context)
    reduce_lag = jnp.where(context == root, far, from_end)
    return_lag = far + jnp.abs(context - root)
    ticks = chunk_count + far + far

    def tick(t):
        k = t - reduce_lag

        @pl.when((k >= 0) & (k < chunk_count))
        def _():
            reduce_chunk(k)

        back = t - return_lag

        @pl.when((back >= 0) & (back < chunk_count) & (context != root))
        def _():
            return_chunk(back)

    def weight_grad(left, right, columns, first_chunk, count):
        for d in range(shards - 1):
            theirs_at = rows_of(lax.rem(shard + d + 1, shards), share)
            result = dot_tn(left[:, theirs_at], right[:, columns : columns + count * chunk])
            for n in range(count):
                k = first_chunk + n
                if k >= early:
                    y_copy(d, k - early).wait_send()
                ysend[d, k % early] = result[:, n * chunk : (n + 1) * chunk].astype(bf16)
                y_copy(d, k).start()
        result = dot_tn(left[:, rows_of(shard, share)], right[:, columns : columns + count * chunk])
        for n in range(count):
            piece[first_chunk + n] = result[:, n * chunk : (n + 1) * chunk].astype(bf16)

    def part_at(slot, block):
        return block if slot == 0 else contexts - 1 + block

    def part_core_copy(slot, block):
        at = part_at(slot, block)
        return remote(
            part.at[slot, pl.ds(0, length // 2), :], part_core.at[at], p_send.at[0, at],
            p_recv.at[0, at], core_peer,
        )

    def part_x_copy(slot, block):
        at = part_at(slot, block)
        return remote(
            part_core.at[at, rows_of(1 - chip, quarter), :], part_x.at[at], p_send.at[1, at],
            p_recv.at[1, at], x_peer,
        )

    def part_z_copy(slot, block):
        at = part_at(slot, block)
        return remote(part_x.at[at], part_z.at[at], p_send.at[2, at], p_recv.at[2, at], below)

    def part_make(slot, block):
        for q in range(4):
            result = dot_nt(unit_back[q * quarter : (q + 1) * quarter, :], wkv[...])
            place_at = jnp.where(core == q % 2, 2, 0) + q // 2
            part[slot, rows_of(place_at, quarter), :] = result.astype(bf16)
        part_core_copy(slot, block).start()

    def part_across(slot, block):
        part_core_copy(slot, block).wait_recv()
        at = part_at(slot, block)
        total = part[slot, length // 2 :, :].astype(f32) + part_core[at].astype(f32)
        part_core[at] = total.astype(bf16)
        part_x_copy(slot, block).start()
        part_core_copy(slot, block).wait_send()

    def part_down(slot, block, count):
        part_x_copy(slot, block).wait_recv()
        at = part_at(slot, block)
        total = part_core[at, rows_of(chip, quarter), :].astype(f32) + part_x[at].astype(f32)

        @pl.when(context == count - 1)
        def _():
            part_x[at] = total.astype(bf16)

        @pl.when(context < count - 1)
        def _():
            part_z_copy(slot, block).wait_recv()
            part_x[at] = (total + part_z[at].astype(f32)).astype(bf16)

        part_z_copy(slot, block).start()

    def unit_place(slot, block):
        return jnp.where(context < half_contexts, slot, block % 2)

    def unit_loads(slot, block):
        at = unit_place(slot, block)
        return [
            pltpu.make_async_copy(source.at[block, slot], target.at[at], kv_sem.at[n, at])
            for n, (source, target) in enumerate(
                ((kv_ref, unit_kv), (first_ref, unit_first), (kraw_ref, unit_kraw))
            )
        ]

    def start_unit(slot, block):
        for copy in unit_loads(slot, block):
            copy.start()

    acc_gain[...] = jnp.zeros_like(acc_gain)
    acc_ff[...] = jnp.zeros_like(acc_ff)
    acc_head[...] = jnp.zeros_like(acc_head)
    acc_square[...] = jnp.zeros_like(acc_square)
    for n in range(6):
        loads[n].wait()
    pl.semaphore_wait(barrier, shards + 1 + neighbours)
    for i in range(steps):
        xs_copy(i).start()
    gate_chunks = ff // chunk
    out_chunks = qw // chunk
    query_chunk = 3 * gate_chunks + out_chunks
    weight_grad(second, gback, 0, 0, gate_chunks)
    weight_grad(second, uback, 0, gate_chunks, gate_chunks)
    weight_grad(cotin, hidden, 0, 2 * gate_chunks, gate_chunks)
    for n in range(6, len(loads)):
        loads[n].wait()
    qs, qraw, mixed = hidden.at[:, :qw], gback.at[:, :qw], uback.at[:, :qw]
    own_kback, own_vback = gback.at[:, qw : qw + kw], uback.at[:, qw : qw + kw]
    next_pairs = [(qs_ref, qs), (qraw_ref, qraw), (mixed_ref, mixed)]
    next_loads = [
        pltpu.make_async_copy(source, target, load_sem.at[n])
        for n, (source, target) in enumerate(next_pairs)
    ]
    for copy in next_loads:
        copy.start()
    start_unit(0, 0)

    def fold(values):
        return jnp.sum(values.reshape(values.shape[0] // 8, 8, values.shape[1]), axis=0)

    def norm_back(values, back, gain):
        inverse = lax.rsqrt(mean_square(values) + epsilon)
        normal = values * inverse
        scaled = back * gain
        inward = inverse * (scaled - normal * jnp.mean(normal * scaled, axis=-1, keepdims=True))
        return inward, back * normal

    def residual_step(i, _):
        xs_copy(i).wait_recv()
        back = spart[half(i), :].astype(f32) + xs[half(i), :].astype(f32)
        inward, terms = norm_back(resid[half(i), :], back, gains[8:9, :])
        acc_ff[...] += fold(terms)
        total = cotin[mine(i), :].astype(f32) + inward
        resback[half(i), :] = total
        outin[mine(i), :] = total.astype(bf16)
        outin_copy(i).start()
        tick(i)
        return 0

    lax.fori_loop(0, steps, residual_step, 0)
    tick_at = steps
    ready = 3 * gate_chunks

    def next_tick(count=1):
        nonlocal tick_at
        for _ in range(count):
            if tick_at < ready or (ready == chunk_count and tick_at < ticks):
                tick(tick_at)
                tick_at += 1

    for i in range(steps):
        xm_copy(i).start()
    for i in range(steps):
        outin_copy(i).wait_recv()
    first = cotin
    first_loads = [
        pltpu.make_async_copy(
            first_ref.at[context, slot], first.at[slot * length : (slot + 1) * length, :],
            gather_sem.at[slot],
        )
        for slot in range(2)
    ]
    for copy in first_loads:
        copy.start()
    for copy in next_loads:
        copy.wait()
    dox = second

    def mixed_step(i, _):
        at = rows_of(i, TILE)
        back = dot_nt(outin[at, :], wo[...]).astype(bf16).astype(f32)
        lanes = lax.broadcasted_iota(jnp.int32, (TILE, head), 1)
        for h in range(heads):
            columns = slice(h * head, (h + 1) * head)
            low = (back[:, columns] * dq[at, columns]).astype(bf16)
            centre = jnp.sum(
                low.astype(f32) * mixed[at, columns].astype(f32), axis=-1, keepdims=True
            )
            high = centre.astype(bf16).astype(f32)
            extra = jnp.where(lanes == 0, -high, jnp.where(lanes == 1, high - centre, 0.0))
            dox[at, 2 * h * head : (2 * h + 1) * head] = low
            dox[at, (2 * h + 1) * head : (2 * h + 2) * head] = extra.astype(bf16)
        dq[at, :] = jnp.zeros((TILE, qw), f32)
        return 0

    lax.fori_loop(0, rows // TILE, mixed_step, 0)
    weight_grad(outin, mixed, 0, 3 * gate_chunks, out_chunks)
    ready += out_chunks
    ones = jnp.ones((length, head), bf16)

    def head_back(raw, back, gain, local):
        turned_back = back * cosine[local, :] - pltpu.roll(back, head // 2, 1) * sine[local, :]
        return norm_back(raw.astype(f32), turned_back, gain)

    kv_grad[...] = jnp.zeros_like(kv_grad)

    @pl.when(context >= half_contexts)
    def _():
        own_kback[length:, :] = jnp.zeros((length, kw), bf16)
        own_vback[length:, :] = jnp.zeros((length, kw), bf16)

    def block_back(slot, block, diagonal):
        lines = slice(slot * length, (slot + 1) * length)
        buffer = unit_place(slot, block)
        if diagonal:
            key_spots = lax.broadcasted_iota(jnp.int32, (length, length), 0)
            query_spots = lax.broadcasted_iota(jnp.int32, (length, length), 1)
            counted = key_spots <= query_spots

        def one_group(g, _):
            keys = unit_kv[buffer, :, rows_of(g, head)]
            values = unit_kv[buffer, :, rows_of(kv_heads + g, head)]
            widened = jnp.concatenate([values, ones], axis=1)
            key_back = jnp.zeros((length, head), f32)
            value_back = jnp.zeros((length, head), f32)
            for member in range(group):
                h = g * group + member
                columns = rows_of(h, head)
                queries = qs[lines, columns]
                inward = dox[lines, rows_of(h, 2 * head)]
                raised = jnp.exp2(dot_nt(keys, queries))
                if diagonal:
                    raised = jnp.where(counted, raised, 0.0)
                scores_back = (raised * dot_nt(widened, inward)).astype(bf16)
                value_back += dot_nn(raised.astype(bf16), inward[:, :head])
                key_back += dot_nn(scores_back, queries)
                dq[lines, columns] += dot_tn(scores_back, keys)
            raw_back, terms = head_back(
                unit_kraw[buffer, :, rows_of(g, head)], key_back * math.log(2.0),
                head_gain_ref[8:9, :], slice(None),
            )
            acc_head[1] += fold(terms)
            unit_back[:, rows_of(g, head)] = raw_back.astype(bf16)
            unit_back[:, rows_of(kv_heads + g, head)] = value_back.astype(bf16)
            return 0

        lax.fori_loop(0, kv_heads, one_group, 0)

        def grad_rows(n, _):
            at = rows_of(n, TILE)
            kv_grad[at, :] += dot_tn(unit_first[buffer, :, at], unit_back[...])
            return 0

        lax.fori_loop(0, width // TILE, grad_rows, 0)
        if diagonal:
            own_kback[lines, :] = unit_back[:, :kw]
            own_vback[lines, :] = unit_back[:, kw:]

    def next_units(slot, block):
        if slot == 0 and block < half_contexts:

            @pl.when(context < half_contexts)
            def _():
                start_unit(1, block)

        if block + 1 < contexts:
            more = block + 1 <= context
            if slot == 0:
                more = more & (context >= half_contexts)

            @pl.when(more)
            def _():
                start_unit(0, block + 1)

    for turn_at in range(contexts + 1):
        block, before = turn_at, turn_at - 1
        if block < contexts:
            turn(cosine, sine, start_ref, block, inside_cos_ref, inside_sin_ref)
        for slot, count in ((0, contexts), (1, half_contexts)):
            within = context < count
            if block < count:

                @pl.when((block <= context) & within)
                def _():
                    for copy in unit_loads(slot, block):
                        copy.wait()
                    next_units(slot, block)

                @pl.when((block == context) & within)
                def _():
                    block_back(slot, block, True)

                @pl.when((block < context) & within)
                def _():
                    block_back(slot, block, False)

            if 0 <= before < count - 1:

                @pl.when((before < context) & within)
                def _():
                    part_across(slot, before)

            if block < count - 1:

                @pl.when((block < context) & within)
                def _():
                    part_make(slot, block)

            gone = turn_at - 2 - (count - 1 - context)

            @pl.when((gone >= 0) & (gone < context) & within)
            def _():
                part_down(slot, gone, count)

        next_tick()
    for copy in first_loads:
        copy.wait()
    turn(cosine, sine, start_ref, context, inside_cos_ref, inside_sin_ref)

    def query_step(i, _):
        at = rows_of(i, TILE)
        local = rows_of(i % (length // TILE), TILE)
        for h in range(heads):
            columns = slice(h * head, (h + 1) * head)
            inward, terms = head_back(
                qraw[at, columns], dq[at, columns] * scale, head_gain_ref[0:1, :], local
            )
            acc_head[0] += fold(terms)
            qraw[at, columns] = inward.astype(bf16)
        return 0

    lax.fori_loop(0, rows // TILE, query_step, 0)
    weight_grad(first, qraw, 0, query_chunk, out_chunks)
    key_chunk = query_chunk + out_chunks
    for n in range(2 * kw // chunk):
        k = key_chunk + n
        columns = slice(n * chunk, (n + 1) * chunk)
        for d in range(shards - 1):
            theirs_at = rows_of(lax.rem(shard + d + 1, shards), share)
            y_copy(d, k - early).wait_send()
            ysend[d, k % early] = kv_grad[theirs_at, columns].astype(bf16)
            y_copy(d, k).start()
        piece[k] = kv_grad[rows_of(shard, share), columns].astype(bf16)
    ready = chunk_count
    next_tick()
    _, short_length = slot_order(lengths_ref)
    for i in range(steps):
        xs_copy(i).wait_send()
    tok_load = pltpu.make_async_copy(own_tok_ref, spart, load_sem.at[0])
    tok_load.start()

    def layer_step(i, _):
        xm_copy(i).wait_recv()
        xm_copy(i).wait_send()
        mlp = mpart[half(i), :].astype(f32) + xm[half(i), :].astype(f32)
        layer = resid[half(i), :] + mlp
        mpart[half(i), :] = layer.astype(bf16)
        layer_copy(i).start()
        layer_keep(i).start()
        lines = lax.broadcasted_iota(jnp.int32, (step_rows, width), 0)
        limit = jnp.where(core == 0, 2**30, short_length)
        counted = lines + (context * length + i * step_rows) < limit
        acc_square[0] += fold(jnp.where(counted, layer * layer, 0.0))
        acc_square[1] += fold(jnp.where(counted, mlp * mlp, 0.0))
        return 0

    lax.fori_loop(0, steps, layer_step, 0)
    next_tick()

    @pl.when(context < contexts - 1)
    def _():
        part_z_copy(0, jnp.minimum(context, contexts - 2)).wait_recv()

    @pl.when(context < half_contexts - 1)
    def _():
        part_z_copy(1, jnp.minimum(context, max(half_contexts - 2, 0))).wait_recv()

    fown = resid

    def first_step(i, _):
        @pl.when(i < steps)
        def _():
            both = lambda ref: jnp.concatenate([ref[theirs(i), :], ref[mine(i), :]], axis=0)
            result = dot_nt(both(qraw), wq[...])
            result += dot_nt(both(own_kback), wkv[:, :kw])
            result += dot_nt(both(own_vback), wkv[:, kw:])

            def from_above(slot):
                at = jnp.where(
                    slot == 0,
                    jnp.minimum(context, contexts - 2),
                    contexts - 1 + jnp.minimum(context, max(half_contexts - 2, 0)),
                )
                last = jnp.where(slot == 0, contexts - 1, half_contexts - 1)
                come = (i == tensor) & (context < last)
                return jnp.where(come, part_z[at].astype(f32), 0.0)

            fsend[half(i), :] = (result[:step_rows] + from_above(1 - core)).astype(bf16)
            f_copy(i).start()
            fown[half(i), :] = result[step_rows:] + from_above(core)

        @pl.when(i > 0)
        def _():
            before = i - 1
            f_copy(before).wait_recv()
            total = fown[half(before), :] + frecv[half(before), :].astype(f32)
            fxsend[half(before), :] = total.astype(bf16)
            xf_copy(before).start()

        return 0

    lax.fori_loop(0, steps + 1, first_step, 0)
    tok_load.wait()

    def tokens_step(i, _):
        xf_copy(i).wait_recv()
        back = fxsend[half(i), :].astype(f32) + fxrecv[half(i), :].astype(f32)
        inward, terms = norm_back(spart[half(i), :].astype(f32), back, gains[0:1, :])
        acc_gain[...] += fold(terms)
        spart[half(i), :] = (resback[half(i), :] + inward).astype(bf16)
        tgrad_copy(i).start()
        tgrad_keep(i).start()
        return 0

    for i in range(steps):
        next_tick()
        tokens_step(i, 0)

    def total_of(values):
        return jnp.sum(jnp.sum(values, axis=0, keepdims=True), axis=1, keepdims=True)

    lanes = lax.broadcasted_iota(jnp.int32, (1, width), 1)
    base = (shard * 2 + core) * 4
    squares = jnp.where(lanes == base, total_of(acc_square[0]), 0.0)
    squares += jnp.where(lanes == base + 1, total_of(square[...]), 0.0)
    squares += jnp.where(lanes == base + 2, total_of(acc_square[1]), 0.0)
    sums[0] = jnp.zeros((8, width), f32)
    sums[0, 0:1, :] = 0.5 * jnp.sum(acc_gain[...], axis=0, keepdims=True)
    sums[0, 1:2, :] = 0.5 * jnp.sum(acc_ff[...], axis=0, keepdims=True)
    sums[0, 2:3, :head] = jnp.sum(acc_head[0], axis=0, keepdims=True)
    sums[0, 2:3, head : 2 * head] = jnp.sum(acc_head[1], axis=0, keepdims=True)
    sums[0, 3:4, :] = 0.5 * squares

    def sum_copy(n, target, device):
        return remote(sums.at[n], target, s_send.at[n], s_recv.at[n], device)

    first_hop = sum_copy(0, sums_in.at[0], core_peer)
    first_hop.start()
    first_hop.wait_recv()
    sums[1] = sums[0] + sums_in[0]
    second_hop = sum_copy(1, sums_in.at[1], x_peer)
    second_hop.start()
    second_hop.wait_recv()
    sums[2] = sums[1] + sums_in[1]
    shard_hops = [
        remote(sums.at[2], sums_y.at[shard], s_send.at[4 + d], s_recv.at[4 + d], peers[d])
        for d in range(shards - 1)
    ]
    for copy in shard_hops:
        copy.start()
    sums_y[shard] = sums[2]
    next_tick()
    for copy in shard_hops:
        copy.wait_recv()
    total = sums_y[0]
    for s in range(1, shards):
        total = total + sums_y[s]
    sums[3] = total
    sum_down = remote(sums.at[3], sums_in.at[2], s_send.at[3], s_recv.at[2], below)
    sum_up = remote(sums.at[3], sums_in.at[2], s_send.at[3], s_recv.at[2], above)
    sum_top = remote(sums.at[3], sums_in.at[3], s_send.at[3], s_recv.at[3], below)
    last = 4 + shards - 1
    result_down = remote(sums_in.at[4], sums_in.at[4], s_send.at[last], s_recv.at[last], below)
    result_up = remote(sums_in.at[4], sums_in.at[4], s_send.at[last + 1], s_recv.at[last], above)

    def add_sums():
        sums[3] = sums[3] + sums_in[2]

    @pl.when(context < root)
    def _():
        @pl.when(context > 0)
        def _():
            sum_up.wait_recv()
            add_sums()

        sum_up.start()

    @pl.when(context > root)
    def _():
        @pl.when(context < contexts - 1)
        def _():
            sum_down.wait_recv()
            add_sums()

        @pl.when(context == root + 1)
        def _():
            sum_top.start()

        @pl.when(context > root + 1)
        def _():
            sum_down.start()

    def more_ticks(t, _):
        tick(t)
        return 0

    lax.fori_loop(tick_at, ticks, more_ticks, 0)

    @pl.when(context == root)
    def _():
        total = sums[3]
        if root > 0:
            sum_up.wait_recv()
            total = total + sums_in[2]
        if root < contexts - 1:
            sum_top.wait_recv()
            total = total + sums_in[3]
        sums_in[4] = total

    @pl.when(context != root)
    def _():
        result_down.wait_recv()

    @pl.when((context <= root) & (context > 0))
    def _():
        result_down.start()

    @pl.when((context >= root) & (context < contexts - 1))
    def _():
        result_up.start()

    sums_keep = pltpu.make_async_copy(sums_in.at[4], sums_out, store_sem.at[2, 0])
    sums_keep.start()
    first_hop.wait_send()
    second_hop.wait_send()
    for copy in shard_hops:
        copy.wait_send()

    @pl.when(context != root)
    def _():
        sum_up.wait_send()

    @pl.when((context <= root) & (context > 0))
    def _():
        result_down.wait_send()

    @pl.when((context >= root) & (context < contexts - 1))
    def _():
        result_up.wait_send()

    def drain_steps(i, _):
        for copy in (outin_copy, layer_copy, f_copy, tgrad_copy):
            copy(i).wait_send()
        layer_copy(i).wait_recv()
        tgrad_copy(i).wait_recv()
        xf_copy(i).wait_send()
        layer_keep(i).wait()
        tgrad_keep(i).wait()
        return 0

    lax.fori_loop(0, steps, drain_steps, 0)

    def drain_chunks(k, _):
        @pl.when(k >= chunk_count - early)
        def _():
            for d in range(shards - 1):
                y_copy(d, k).wait_send()

        @pl.when(context != root)
        def _():
            up_copy(k).wait_send()

        @pl.when((context <= root) & (context > 0))
        def _():
            back_down_copy(k).wait_send()

        @pl.when((context >= root) & (context < contexts - 1))
        def _():
            back_up_copy(k).wait_send()

        grad_keep(k, finish=True)
        return 0

    lax.fori_loop(0, chunk_count, drain_chunks, 0)
    for block in range(contexts - 1):
        for slot, count in ((0, contexts), (1, half_contexts)):
            if block < count - 1:

                @pl.when((block < context) & (context < count))
                def _():
                    part_x_copy(slot, block).wait_send()
                    part_z_copy(slot, block).wait_send()

    sums_keep.wait()


def call_layer_backward(shards, contexts, lengths, parts):
    (
        second, gback, uback, cotin, hidden, spart, mpart, resid, square, mixed, linv, qs, qraw,
        kraw, kv, first, wq, wk, wv, wo, out_weight, gains, own_tok, head_gains, *tables,
    ) = parts
    rows, width = second.shape
    length = resid.shape[0]
    ff, qw, kw = gback.shape[1], wq.shape[1], wk.shape[1]
    share = width // shards
    chunk = TILE
    chunk_count = (3 * ff + 2 * qw + 2 * kw) // chunk
    early = 3 * ff // chunk
    steps = 2 * length // TILE
    units = contexts - 1 + max(contexts // 2 - 1, 1)
    head = head_gains.shape[1]
    slots = rows // length
    shape = jax.ShapeDtypeStruct
    outs = (
        shape((share, 2 * ff + qw + 2 * kw), bf16), shape((ff + qw, share), bf16),
        shape((slots, length, width), bf16), shape((slots, length, width), bf16),
        shape((8, width), f32),
    )
    dma = pltpu.SemaphoreType.DMA

    def like(array):
        return pltpu.VMEM(array.shape, array.dtype)

    half = pltpu.VMEM((length, width), bf16)
    chunks = pltpu.VMEM((chunk_count, share, chunk), bf16)
    return pl.pallas_call(
        functools.partial(layer_backward, shards, contexts),
        out_shape=outs,
        in_specs=[SMEM] + [HBM] * 23 + [VMEM] * 4,
        out_specs=[HBM] * len(outs),
        scratch_shapes=[
            like(second), like(gback), like(uback), like(cotin), like(hidden), like(spart),
            like(mpart), like(resid), like(square), like(linv), like(wq),
            pltpu.VMEM((width, 2 * kw), bf16), like(wo), like(gains),
            pltpu.VMEM((2, length, 2 * kw), bf16), pltpu.VMEM((2, length, width), bf16),
            pltpu.VMEM((2, length, kw), bf16), pltpu.VMEM((length, 2 * kw), bf16),
            pltpu.VMEM((width, 2 * kw), f32),
            pltpu.VMEM((length, head), f32), pltpu.VMEM((length, head), f32),
            half, half, pltpu.VMEM((rows, width), bf16), pltpu.VMEM((length, width), f32),
            pltpu.VMEM((2, length, width), bf16),
            pltpu.VMEM((units, length // 2, width), bf16),
            pltpu.VMEM((units, length // 4, width), bf16),
            pltpu.VMEM((units, length // 4, width), bf16),
            half,
            chunks,
            pltpu.VMEM((shards - 1, early, share, chunk), bf16),
            pltpu.VMEM((shards - 1, chunk_count, share, chunk), bf16),
            chunks, chunks, pltpu.VMEM(((ff + qw) // chunk, chunk, share), bf16),
            pltpu.VMEM((4, 8, width), f32), pltpu.VMEM((5, 8, width), f32),
            pltpu.VMEM((shards, 8, width), f32),
            pltpu.VMEM((8, width), f32), pltpu.VMEM((8, width), f32),
            pltpu.VMEM((2, 8, head), f32), pltpu.VMEM((2, 8, width), f32),
            dma((15,)), dma((shards,)), dma((3, 2)), dma((chunk_count,)), dma((3, steps)),
            dma((3, steps)), dma((3, steps)), dma((4, steps)), dma((4, steps)),
            dma((shards - 1, chunk_count)), dma((shards - 1, chunk_count)),
            dma((chunk_count,)), dma((chunk_count,)), dma((chunk_count,)),
            dma((2, chunk_count)), dma((chunk_count,)), dma((3, units)), dma((3, units)),
            dma((4 + shards + 1,)), dma((4 + shards + 1,)),
        ],
        compiler_params=pltpu.CompilerParams(
            collective_id=3, has_side_effects=True, vmem_limit_bytes=63 * 2**20
        ),
        name="layer_backward",
    )(lengths, *parts)


def local(
    tokens, lengths, cotangent, query_weight, key_weight, value_weight, out_weight, gate_weight,
    up_weight, down_weight, attention_gain, feedforward_gain, query_gain, key_gain,
):
    slots, length, width = tokens.shape
    shards, contexts = lax.axis_size("shard"), lax.axis_size("context")
    shard, context, _ = place()
    head = query_gain.shape[0]
    ff, qw, kw = gate_weight.shape[1], query_weight.shape[1], key_weight.shape[1]
    tables = [jnp.asarray(table) for table in rope_tables(length, contexts, head)]

    def packed(one, other):
        upper = lax.broadcasted_iota(jnp.int32, (16, one.shape[0]), 0) < 8
        return jnp.where(upper, one.astype(f32)[None], other.astype(f32)[None])

    gain_share = packed(attention_gain, feedforward_gain)
    head_gains = packed(query_gain, key_gain)
    (mixed, kv, qs, qraw, kraw, linv, first, wq, wk, wv, wo, wg, gains) = (
        call_attention_forward(
            shards, contexts, lengths, tokens, query_weight, key_weight, value_weight, out_weight,
            gate_weight, gain_share, head_gains, tables,
        )
    )
    (second, hidden, gback, uback, cotin, spart, mpart, resid, square, own_tok) = (
        call_feed_forward(
            shards, lengths, mixed, wo, tokens, cotangent, gains, wg, out_weight, gate_weight,
            up_weight, down_weight,
        )
    )
    straight, turned, layer, token_grads, sums = call_layer_backward(
        shards, contexts, lengths,
        (
            second, gback, uback, cotin, hidden, spart, mpart, resid, square, mixed, linv, qs,
            qraw, kraw, kv, first, wq, wk, wv, wo, out_weight, gains, own_tok, head_gains, *tables,
        ),
    )
    swapped = lengths[1] > lengths[0]

    def in_place(values):
        return jnp.where(swapped, values[::-1], values)

    ends = np.cumsum([ff, ff, qw, kw])
    gate_grad, up_grad, query_grad, key_grad, value_grad = (
        part.astype(f32) for part in jnp.split(straight, ends, axis=1)
    )
    down_grad, out_grad = (part.astype(f32) for part in jnp.split(turned, [ff], axis=0))
    gain_grads = lax.dynamic_slice_in_dim(sums[:2], shard * (width // shards), width // shards, 1)
    squares = lax.dynamic_slice_in_dim(sums[3], shard * slots * 4, slots * 4, 0)
    squares = in_place(squares.reshape(slots, 4)[:, :3])
    return (
        in_place(layer),
        in_place(token_grads.astype(f32)),
        query_grad,
        key_grad,
        value_grad,
        out_grad,
        gate_grad,
        up_grad,
        down_grad,
        gain_grads[0],
        gain_grads[1],
        sums[2, :head],
        sums[2, head : 2 * head],
        jnp.sqrt(squares / (lengths.astype(f32)[:, None] * width)),
    )


def solution(mesh):
    placed = (
        P("shard", "context", None),
        P("shard"),
        P("shard", "context", None),
        P("shard", "tensor"),
        P("shard", "tensor"),
        P("shard", "tensor"),
        P("tensor", "shard"),
        P("shard", "tensor"),
        P("shard", "tensor"),
        P("tensor", "shard"),
        P("shard"),
        P("shard"),
        P(),
        P(),
    )
    return jax.shard_map(
        local,
        mesh=mesh,
        in_specs=placed,
        out_specs=(
            P("shard", "context", None),
            P("shard", "context", None),
            P("shard", "tensor"),
            P("shard", "tensor"),
            P("shard", "tensor"),
            P("tensor", "shard"),
            P("shard", "tensor"),
            P("shard", "tensor"),
            P("tensor", "shard"),
            P("shard"),
            P("shard"),
            P(),
            P(),
            P("shard", None),
        ),
        check_vma=False,
    )
```

```python
import functools
import math

import jax
import jax.numpy as jnp
import numpy as np
from jax import lax
from jax.experimental import pallas as pl
from jax.experimental.pallas import tpu as pltpu
from jax.sharding import PartitionSpec as P

epsilon = 1e-06
rope_base = 1000000.0
MESH = pl.DeviceIdType.MESH
f32 = jnp.float32
bf16 = jnp.bfloat16
HBM = pl.BlockSpec(memory_space=pl.ANY)
VMEM = pl.BlockSpec(memory_space=pltpu.VMEM)
SMEM = pl.BlockSpec(memory_space=pltpu.SMEM)
TILE = 256


def rows_of(index, size):
    if isinstance(index, int):
        return pl.ds(index * size, size)
    return pl.ds(pl.multiple_of(index * size, size), size)


def dot_nt(left, right):
    return lax.dot_general(left, right, (((1,), (1,)), ((), ())), preferred_element_type=f32)


def dot_tn(left, right):
    return lax.dot_general(left, right, (((0,), (0,)), ((), ())), preferred_element_type=f32)


def dot_nn(left, right):
    return jnp.dot(left, right, preferred_element_type=f32)


def mean_square(values):
    return jnp.mean(values * values, axis=-1, keepdims=True)


def place():
    return lax.axis_index("shard"), lax.axis_index("context"), lax.axis_index("tensor")


def greet(devices, extra=0):
    barrier = pltpu.get_barrier_semaphore()
    for device in devices:
        pl.semaphore_signal(barrier, inc=1, device_id=device, device_id_type=MESH)
    return barrier


def greet_line(barrier, shard, context, tensor, count):
    @pl.when(context > 0)
    def _():
        pl.semaphore_signal(
            barrier, inc=1, device_id=(shard, context - 1, tensor), device_id_type=MESH
        )

    @pl.when(context < count - 1)
    def _():
        pl.semaphore_signal(
            barrier, inc=1, device_id=(shard, context + 1, tensor), device_id_type=MESH
        )

    return jnp.minimum(context, 1) + jnp.minimum(count - 1 - context, 1)


def turn(cosine, sine, start_ref, block, inside_cos_ref, inside_sin_ref):
    head = cosine.shape[1]
    start_cos, start_sin = start_ref[block, 0:1, :], start_ref[block, 8:9, :]
    signs = jnp.where(lax.broadcasted_iota(jnp.int32, (1, head), 1) < head // 2, -1.0, 1.0)
    inside_cos, inside_sin = inside_cos_ref[...], inside_sin_ref[...]
    cosine[...] = start_cos * inside_cos - start_sin * inside_sin
    sine[...] = signs * (start_sin * inside_cos + start_cos * inside_sin)


def slot_order(lengths_ref):
    one, other = lengths_ref[0], lengths_ref[1]
    return jnp.where(other > one, 1, 0), jnp.minimum(one, other)


def gather_loads(share_ref, whole_ref, target, shard, shards, axis, sems):
    size = share_ref.shape[axis]
    copies = []
    for d in range(shards):
        at = rows_of(lax.rem(shard + d, shards), size)
        index = (slice(None), at) if axis == 1 else (at, slice(None))
        source = share_ref if d == 0 else whole_ref.at[index]
        copies.append(pltpu.make_async_copy(source, target.at[index], sems.at[d]))
    return copies


def remote(src, dst, send_sem, recv_sem, device):
    return pltpu.make_async_remote_copy(
        src_ref=src,
        dst_ref=dst,
        send_sem=send_sem,
        recv_sem=recv_sem,
        device_id=device,
        device_id_type=MESH,
    )


def rope_tables(length, contexts, head_size):
    half = head_size // 2
    speeds = np.tile(rope_base ** (-np.arange(half, dtype=np.float64) * 2.0 / head_size), 2)
    inside = np.arange(length, dtype=np.float64)[:, None] * speeds
    starts = np.arange(contexts, dtype=np.float64)[:, None] * length * speeds
    rows = np.stack([np.cos(starts), np.sin(starts)], axis=1)
    rows = np.repeat(rows, 8, axis=1)
    return (
        np.cos(inside).astype(np.float32),
        np.sin(inside).astype(np.float32),
        rows.astype(np.float32),
    )


def attention_forward(
    shards, contexts, lengths_ref, tok_ref, wq_ref, wk_ref, wv_ref, wo_ref, wg_ref, gain_ref,
    head_gain_ref, inside_cos_ref, inside_sin_ref, start_ref,
    mixed_out, kv_out, qs_out, qraw_out, kraw_out, linv_out, first_out, wq_out, wk_out, wv_out,
    wo_out, wg_out, gain_out,
    tok, first, wq, wk, wv, gains, kv, qs, qraw, kraw, acc, mixed, linv, cosine, sine,
    load_sem, own_sem, store_sem, unit_sem, wsend, wrecv, z_send, z_recv, x_send, x_recv,
    core_send, core_recv,
):
    shard, context, tensor = place()
    slots, length, width = tok.shape
    share = wq_ref.shape[0]
    query_width = wq.shape[1]
    key_width = wk.shape[1]
    head = head_gain_ref.shape[1]
    heads = query_width // head
    group = query_width // key_width
    half = contexts // 2
    quarter = length // 4
    score_scale = head**-0.5 * math.log2(math.e)
    core = tensor % 2
    core_peer = (shard, context, tensor + 1 - 2 * core)
    x_peer = (shard, context, (tensor + 2) % 4)
    above = (shard, jnp.minimum(context + 1, contexts - 1), tensor)
    peers = [(lax.rem(shard + d, shards), context, tensor) for d in range(1, shards)]
    barrier = greet([core_peer, x_peer, *peers])
    neighbours = greet_line(barrier, shard, context, tensor, contexts)

    load_tok = pltpu.make_async_copy(tok_ref, tok, load_sem)
    load_tok.start()
    mine = rows_of(shard, share)
    side = context % 2
    partner = (shard, context + 1 - 2 * side, tensor)
    weights = [
        (gain_ref, gains.at[:, mine]),
        (wk_ref, wk.at[mine, :]),
        (wv_ref, wv.at[mine, :]),
        (wq_ref, wq.at[mine, :]),
        (wg_ref.at[rows_of(side, share // 2), :], wg_out.at[rows_of(2 * shard + side, share // 2), :]),
        (wo_ref, wo_out.at[:, mine]),
    ]
    own = [
        pltpu.make_async_copy(source, target, own_sem.at[w])
        for w, (source, target) in enumerate(weights[:4])
    ]
    sends = [
        [
            remote(source, target, wsend.at[w, d], wrecv.at[w, d], peers[d])
            for d in range(shards - 1)
        ]
        for w, (source, target) in enumerate(weights)
    ]
    for copy in own:
        copy.start()
    pl.semaphore_wait(barrier, shards + 1 + neighbours)

    pair_copies = []
    for d in range(shards - 1):
        origin = lax.rem(shard + shards - d - 1, shards)
        rows = wg_out.at[rows_of(2 * origin + side, share // 2), :]
        pair_copies.append(remote(rows, rows, wsend.at[6, d], wrecv.at[6, d], partner))

    def send_weights(*places):
        for w in places:
            for copy in sends[w]:
                copy.start()

    def have_weights(*places):
        for w in places:
            for copy in sends[w]:
                copy.wait_recv()

    send_weights(0, 1, 2, 3, 4, 5)
    for slot in range(slots):
        for h in range(heads):
            acc[slot, h] = jnp.zeros((length, 2 * head), f32)
    load_tok.wait()
    for copy in own:
        copy.wait()
    have_weights(0)
    first_slot, short_length = slot_order(lengths_ref)
    per_slot = length // TILE
    tiles = slots * per_slot

    def norm_rows(i, _):
        slot = i // per_slot
        source = jnp.where(slot == 0, first_slot, 1 - first_slot)
        values = tok[source, rows_of(i % per_slot, TILE), :].astype(f32)
        scale = lax.rsqrt(mean_square(values) + epsilon)
        first[context, slot, rows_of(i % per_slot, TILE), :] = (
            values * scale * gains[0:1, :]
        ).astype(bf16)
        return 0

    lax.fori_loop(0, tiles, norm_rows, 0)

    def part(block, slot, which):
        return first.at[block, slot, rows_of(which, quarter), :]

    def z_copy(block, slot):
        rows = part(block, slot, tensor)
        return remote(rows, rows, z_send.at[block, slot], z_recv.at[block, slot], above)

    def x_copy(block, slot):
        rows = part(block, slot, tensor)
        return remote(rows, rows, x_send.at[block, slot], x_recv.at[block, slot], x_peer)

    def core_copy(kind, block, slot):
        rows = part(block, slot, tensor if kind == 0 else (tensor + 2) % 4)
        return remote(
            rows, rows, core_send.at[kind, block, slot], core_recv.at[kind, block, slot], core_peer
        )

    def unit_copies(block, slot):
        return [
            pltpu.make_async_copy(
                source.at[block, slot], target.at[block, slot], unit_sem.at[n, block, slot]
            )
            for n, (source, target) in enumerate(
                ((first, first_out), (kv, kv_out), (kraw, kraw_out))
            )
        ]

    def go_up(block, slot):
        @pl.when(context < contexts - 1)
        def _():
            z_copy(block, slot).start()

    def stage_in(block, slot):
        z_copy(block, slot).wait_recv()
        go_up(block, slot)
        x_copy(block, slot).start()
        core_copy(0, block, slot).start()

    def stage_across(block, slot):
        x_copy(block, slot).wait_recv()
        core_copy(1, block, slot).start()

    def head_form(raw, gain, local):
        normal = raw * lax.rsqrt(mean_square(raw) + epsilon) * gain
        return normal * cosine[local, :] + pltpu.roll(normal, head // 2, 1) * sine[local, :]

    def make_keys(block, slot):
        turn(cosine, sine, start_ref, block, inside_cos_ref, inside_sin_ref)

        def rows(i, _):
            local = rows_of(i, TILE)
            values = first[block, slot, local, :]
            raw = dot_nn(values, wk[...])
            kraw[block, slot, local, :] = raw.astype(bf16)
            for g in range(key_width // head):
                columns = slice(g * head, (g + 1) * head)
                kv[block, slot, local, columns] = head_form(
                    raw[:, columns], head_gain_ref[8:9, :], local
                ).astype(bf16)
            kv[block, slot, local, key_width:] = dot_nn(values, wv[...]).astype(bf16)
            return 0

        lax.fori_loop(0, per_slot, rows, 0)
        for copy in unit_copies(block, slot):
            copy.start()

    def stage_keys(block, slot):
        core_copy(0, block, slot).wait_recv()
        core_copy(1, block, slot).wait_recv()
        make_keys(block, slot)

    ones = jnp.ones((length, head), bf16)

    def attend(block, slot, diagonal):
        def one_head(h, _):
            columns = rows_of(h, head)
            keys = kv[block, slot, :, rows_of(h // group, head)]
            values = kv[block, slot, :, rows_of(key_width // head + h // group, head)]
            raised = jnp.exp2(dot_nt(qs[slot * length : (slot + 1) * length, columns], keys))
            spots = lax.broadcasted_iota(jnp.int32, (length, length), 1)
            if diagonal:
                lines = lax.broadcasted_iota(jnp.int32, (length, length), 0)
                raised = jnp.where(spots <= lines, raised, 0.0)
            if slot == 1:
                raised = jnp.where(spots + block * length < short_length, raised, 0.0)
            acc[slot, h] += dot_nn(
                raised.astype(bf16), jnp.concatenate([values, ones], axis=1)
            )
            return 0

        lax.fori_loop(0, heads, one_head, 0)

    units = [(r, slot) for r in range(1, contexts) for slot in range(slots)]

    def for_unit(n, action):
        if 0 <= n < len(units):
            back, slot = units[n]
            block = context - back

            @pl.when((block >= 0) if slot == 0 else ((block >= 0) & (block < half)))
            def _():
                action(block, slot)

    def for_own(action):
        action(context, 0)

        @pl.when(context < half)
        def _():
            action(context, 1)

    stores = []

    def store_all(*pairs):
        for source, target in pairs:
            copy = pltpu.make_async_copy(source, target, store_sem.at[len(stores)])
            copy.start()
            stores.append(copy)

    def make_queries():
        have_weights(3)
        store_all((wq, wq_out), (wk, wk_out), (wv, wv_out), (gains, gain_out))
        turn(cosine, sine, start_ref, context, inside_cos_ref, inside_sin_ref)

        def query_rows(i, _):
            place_rows = rows_of(i, TILE)
            local = rows_of(i % per_slot, TILE)
            raw = dot_nn(first[context, i // per_slot, local, :], wq[...])
            qraw[place_rows, :] = raw.astype(bf16)
            for h in range(heads):
                columns = slice(h * head, (h + 1) * head)
                qs[place_rows, columns] = (
                    head_form(raw[:, columns], head_gain_ref[0:1, :], local) * score_scale
                ).astype(bf16)
            return 0

        lax.fori_loop(0, tiles, query_rows, 0)
        store_all((qs, qs_out), (qraw, qraw_out))

    def pass_on():
        have_weights(4)
        for copy in pair_copies:
            copy.start()

    def attend_own():
        for_own(lambda block, slot: attend(block, slot, True))

    actions = dict(
        i=stage_in, a=stage_across, k=stage_keys,
        t=lambda block, slot: attend(block, slot, False),
    )

    def steps(*names):
        for name in names:
            for_unit(int(name[1:]), actions[name[0]])

    for_own(go_up)
    steps("i0")
    have_weights(1, 2)
    steps("i1")
    make_keys(context, 0)
    make_keys(context, 1)
    steps("i2", "i3", "a0", "a1")
    make_queries()
    steps("a2", "k0", "i4", "a3", "k1")
    attend_own()
    steps("i5", "k2", "t0", "a4", "k3")
    pass_on()
    steps("t1", "t2", "k4", "t3", "a5", "t4")
    for n in range(6, len(units)):
        steps(f"i{n}", f"k{n - 1}", f"a{n}", f"t{n - 1}")
    steps(f"k{len(units) - 1}", f"t{len(units) - 1}")

    def finish(h, _):
        columns = rows_of(h, head)
        for slot in range(slots):
            lines = slice(slot * length, (slot + 1) * length)
            inverse = 1.0 / acc[slot, h, :, head:]
            mixed[lines, columns] = (acc[slot, h, :, :head] * inverse).astype(bf16)
            linv[lines, columns] = inverse
        return 0

    lax.fori_loop(0, heads, finish, 0)
    store_all((mixed, mixed_out), (linv, linv_out))

    def sent_up(block, slot):
        @pl.when(context < contexts - 1)
        def _():
            z_copy(block, slot).wait_send()

    def unit_done(block, slot):
        sent_up(block, slot)
        x_copy(block, slot).wait_send()
        core_copy(0, block, slot).wait_send()
        core_copy(1, block, slot).wait_send()
        for copy in unit_copies(block, slot):
            copy.wait()

    for_own(sent_up)
    for slot in range(slots):
        for copy in unit_copies(context, slot):
            copy.wait()
    for n in range(len(units)):
        for_unit(n, unit_done)
    have_weights(5)
    for copy in pair_copies:
        copy.wait_recv()
        copy.wait_send()
    for copies in sends:
        for copy in copies:
            copy.wait_send()
    for copy in stores:
        copy.wait()


def call_attention_forward(
    shards, contexts, lengths, tokens, query_weight, key_weight, value_weight, out_weight,
    gate_weight, gain_share, head_gains, tables,
):
    slots, length, width = tokens.shape
    rows = slots * length
    qw, kw, ff = query_weight.shape[1], key_weight.shape[1], gate_weight.shape[1]
    head = head_gains.shape[1]
    heads = qw // head
    n_weights = 6
    shape = jax.ShapeDtypeStruct
    dma = pltpu.SemaphoreType.DMA
    kv_shape = (contexts, slots, length, 2 * kw)
    kraw_shape = (contexts, slots, length, kw)
    first_shape = (contexts, slots, length, width)
    outs = (
        shape((rows, qw), bf16), shape(kv_shape, bf16), shape((rows, qw), bf16),
        shape((rows, qw), bf16), shape(kraw_shape, bf16), shape((rows, qw), f32),
        shape(first_shape, bf16), shape((width, qw), bf16), shape((width, kw), bf16),
        shape((width, kw), bf16), shape((qw, width), bf16), shape((width, ff), bf16),
        shape((16, width), f32),
    )
    units = (contexts, slots)
    return pl.pallas_call(
        functools.partial(attention_forward, shards, contexts),
        out_shape=outs,
        in_specs=[SMEM] + [HBM] * 7 + [VMEM] * 4,
        out_specs=[HBM] * len(outs),
        scratch_shapes=[
            pltpu.VMEM((slots, length, width), bf16),
            pltpu.VMEM(first_shape, bf16),
            pltpu.VMEM((width, qw), bf16),
            pltpu.VMEM((width, kw), bf16),
            pltpu.VMEM((width, kw), bf16),
            pltpu.VMEM((16, width), f32),
            pltpu.VMEM(kv_shape, bf16),
            pltpu.VMEM((rows, qw), bf16),
            pltpu.VMEM((rows, qw), bf16),
            pltpu.VMEM(kraw_shape, bf16),
            pltpu.VMEM((slots, heads, length, 2 * head), f32),
            pltpu.VMEM((rows, qw), bf16),
            pltpu.VMEM((rows, qw), f32),
            pltpu.VMEM((length, head), f32),
            pltpu.VMEM((length, head), f32),
            dma, dma((4,)), dma((8,)), dma((3, *units)),
            dma((n_weights + 1, shards - 1)), dma((n_weights + 1, shards - 1)),
            dma(units), dma(units), dma(units), dma(units), dma((2, *units)), dma((2, *units)),
        ],
        compiler_params=pltpu.CompilerParams(
            collective_id=1, has_side_effects=True, vmem_limit_bytes=60 * 2**20
        ),
        name="attention_forward",
    )(
        lengths, tokens, query_weight, key_weight, value_weight, out_weight, gate_weight,
        gain_share, head_gains, *tables,
    )


def feed_forward(
    shards, lengths_ref, mixed_ref, wo_ref, tok_ref, cot_ref, gain_ref, wg_ref, wo_own_ref,
    wg_own_ref, wu_ref, wd_ref,
    second_out, hidden_out, gback_out, uback_out, cotin_out, spart_out, mpart_out, resid_out,
    square_out, own_tok_out,
    mixed, wo, tok, cot, gains, wg, wu, wd, second, hidden, gback, uback, cotin, spart, mpart,
    resid, square, own_tok, apart, csend, crecv, xsend, xrecv, ssend, srecv, msend, mrecv, gvalue, uvalue,
    load_sem, gather_sem, store_sem, chunk_sem, wsend, wrecv, core_send, core_recv, x_send, x_recv,
):
    shard, context, tensor = place()
    slots, length, width = tok.shape
    share = wd_ref.shape[1]
    step_rows = TILE // 2
    steps = length // step_rows
    core = tensor % 2
    core_peer = (shard, context, tensor + 1 - 2 * core)
    x_peer = (shard, context, (tensor + 2) % 4)
    peers = [(lax.rem(shard + d, shards), context, tensor) for d in range(1, shards)]
    side = context % 2
    partner = (shard, context + 1 - 2 * side, tensor)
    barrier = greet([core_peer, x_peer, partner, *peers])
    loads = [
        pltpu.make_async_copy(source, target, load_sem.at[n])
        for n, (source, target) in enumerate(
            (
                (mixed_ref, mixed), (tok_ref, tok), (gain_ref, gains), (cot_ref, cot),
                (wu_ref, wu.at[rows_of(shard, share), :]),
                (wd_ref, wd.at[:, rows_of(shard, share)]),
            )
        )
    ]
    gathers = [
        gather_loads(own_ref, whole_ref, target, shard, shards, axis, gather_sem.at[n])
        for n, (own_ref, whole_ref, target, axis) in enumerate(
            (
                (wo_own_ref, wo_ref, wo, 1), (wg_own_ref, wg_ref, wg, 0),
            )
        )
    ]
    for copy in [loads[0], *gathers[0]]:
        copy.start()
    square[...] = jnp.zeros_like(square)
    pl.semaphore_wait(barrier, shards + 2)
    def piece_of(weight, ref, origin, piece):
        if weight == 0:
            size = share // 4
            return ref.at[rows_of((0 if origin is None else 4 * origin) + piece, size), :]
        rows = rows_of(piece, wd.shape[0] // 4)
        return ref.at[rows, :] if origin is None else ref.at[rows, rows_of(origin, share)]

    sends, passes = [], []
    for n in range(4):
        weight, piece = n // 2, 2 * side + n % 2
        source, target = ((wu_ref, wu), (wd_ref, wd))[weight]
        sends.append([])
        passes.append([])
        for d in range(shards - 1):
            sends[n].append(
                remote(
                    piece_of(weight, source, None, piece), piece_of(weight, target, shard, piece),
                    wsend.at[n, d], wrecv.at[n, d], peers[d],
                )
            )
            origin = lax.rem(shard + shards - d - 1, shards)
            place_at = piece_of(weight, target, origin, piece)
            passes[n].append(
                remote(place_at, place_at, wsend.at[4 + n, d], wrecv.at[4 + n, d], partner)
            )
    for copies in sends:
        for copy in copies:
            copy.start()
    for copy in [loads[0], *gathers[0]]:
        copy.wait()
    for copy in [*loads[1:], *gathers[1]]:
        copy.start()

    def mine(i):
        return rows_of(core * steps + i, step_rows)

    def theirs(i):
        return rows_of((1 - core) * steps + i, step_rows)

    def half(i):
        return rows_of(i, step_rows)

    def core_copy(kind, i, source, target):
        return remote(source, target, core_send.at[kind, i], core_recv.at[kind, i], core_peer)

    def attn_copy(i):
        return core_copy(0, i, csend.at[half(i), :], crecv.at[half(i), :])

    def second_copy(i):
        return core_copy(1, i, second.at[mine(i), :], second.at[mine(i), :])

    def spart_copy(i):
        return core_copy(2, i, ssend.at[half(i), :], srecv.at[half(i), :])

    def mpart_copy(i):
        return core_copy(3, i, msend.at[half(i), :], mrecv.at[half(i), :])

    def x_copy(i):
        return remote(
            xsend.at[half(i), :], xrecv.at[half(i), :], x_send.at[i], x_recv.at[i], x_peer
        )

    def project(i, _):
        @pl.when(i < steps)
        def _():
            both = jnp.concatenate([mixed[theirs(i), :], mixed[mine(i), :]], axis=0)
            result = dot_nn(both, wo[...])
            csend[half(i), :] = result[:step_rows].astype(bf16)
            attn_copy(i).start()
            apart[half(i), :] = result[step_rows:]

        @pl.when(i > 0)
        def _():
            before = i - 1
            attn_copy(before).wait_recv()
            total = apart[half(before), :] + crecv[half(before), :].astype(f32)
            xsend[half(before), :] = total.astype(bf16)
            x_copy(before).start()

        return 0

    lax.fori_loop(0, steps + 1, project, 0)
    for copy in [*loads[1:], *gathers[1]]:
        copy.wait()
    first_slot, short_length = slot_order(lengths_ref)
    own_source = jnp.where(core == 0, first_slot, 1 - first_slot)

    def counted(slot, i):
        spots = context * length + i * step_rows
        lines = lax.broadcasted_iota(jnp.int32, (step_rows, width), 0) + spots
        limit = jnp.where(slot == 0, 2**30, short_length)
        return lines < limit

    def cut(slot, i):
        source = jnp.where(slot == 0, first_slot, 1 - first_slot)
        values = cot[source, half(i), :].astype(f32)
        return jnp.where(counted(slot, i), values, 0.0).astype(bf16)

    def normalise(i):
        x_copy(i).wait_recv()
        attn = xsend[half(i), :].astype(f32) + xrecv[half(i), :].astype(f32)
        attn_counted = jnp.where(counted(core, i), attn, 0.0)
        square[...] += jnp.sum(
            (attn_counted * attn_counted).reshape(step_rows // 8, 8, width), axis=0
        )
        own_tok[half(i), :] = tok[own_source, half(i), :]
        residual = own_tok[half(i), :].astype(f32) + attn
        resid[half(i), :] = residual
        scale = lax.rsqrt(mean_square(residual) + epsilon)
        second[mine(i), :] = (residual * scale * gains[8:9, :]).astype(bf16)
        second_copy(i).start()
        cotin[mine(i), :] = cut(core, i)
        cotin[theirs(i), :] = cut(1 - core, i)

    def finish_parts(i):
        spart_copy(i).wait_recv()
        spart[half(i), :] = (
            spart[half(i), :].astype(f32) + srecv[half(i), :].astype(f32)
        ).astype(bf16)
        mpart_copy(i).wait_recv()
        mpart[half(i), :] = (
            mpart[half(i), :].astype(f32) + mrecv[half(i), :].astype(f32)
        ).astype(bf16)
        for copy in part_stores(i):
            copy.start()

    def gate(i):
        second_copy(i).wait_recv()
        both = jnp.concatenate([second[mine(i), :], second[theirs(i), :]], axis=0)
        gvalue[i] = dot_nn(both, wg[...])

    def up(i):
        both = jnp.concatenate([second[mine(i), :], second[theirs(i), :]], axis=0)
        up_value = dot_nn(both, wu[...])
        gate_value = gvalue[i]
        sigmoid = 1.0 / (1.0 + jnp.exp(-gate_value))
        swish = gate_value * sigmoid
        slope = sigmoid + swish * (1.0 - sigmoid)
        low = (swish * up_value).astype(bf16)
        hidden[mine(i), :] = low[:step_rows]
        hidden[theirs(i), :] = low[step_rows:]
        gvalue[i] = up_value * slope
        uvalue[i] = swish

    def backward(i):
        inward = jnp.concatenate([cotin[mine(i), :], cotin[theirs(i), :]], axis=0)
        hidden_back = dot_nt(inward, wd[...])
        gate_low = (hidden_back * gvalue[i]).astype(bf16)
        up_low = (hidden_back * uvalue[i]).astype(bf16)
        gback[mine(i), :] = gate_low[:step_rows]
        gback[theirs(i), :] = gate_low[step_rows:]
        uback[mine(i), :] = up_low[:step_rows]
        uback[theirs(i), :] = up_low[step_rows:]
        for copy in chunk_stores(i):
            copy.start()
        result = dot_nt(gate_low, wg[...]) + dot_nt(up_low, wu[...])
        ssend[half(i), :] = result[step_rows:].astype(bf16)
        spart_copy(i).start()
        spart[half(i), :] = result[:step_rows].astype(bf16)
        low = jnp.concatenate([hidden[mine(i), :], hidden[theirs(i), :]], axis=0)
        result = dot_nn(low, wd[...])
        msend[half(i), :] = result[step_rows:].astype(bf16)
        mpart_copy(i).start()
        mpart[half(i), :] = result[:step_rows].astype(bf16)

    def pass_on(n):
        for copy in sends[n]:
            copy.wait_recv()
        for copy in passes[n]:
            copy.start()

    def have(*pieces):
        for n in pieces:
            for copy in passes[n]:
                copy.wait_recv()

    def chunk_stores(i):
        rows = [(ref, out, at) for ref, out in ((gback, gback_out), (uback, uback_out)) for at in (mine(i), theirs(i))]
        return [
            pltpu.make_async_copy(ref.at[at, :], out.at[at, :], chunk_sem.at[n, i])
            for n, (ref, out, at) in enumerate(rows)
        ]

    def part_stores(i):
        return [
            pltpu.make_async_copy(ref.at[half(i), :], out.at[half(i), :], chunk_sem.at[n, i])
            for n, (ref, out) in enumerate(((spart, spart_out), (mpart, mpart_out)), 4)
        ]

    stores = []

    def store_all(*pairs):
        for source, target in pairs:
            copy = pltpu.make_async_copy(source, target, store_sem.at[len(stores)])
            copy.start()
            stores.append(copy)

    def run(action, start, stop):
        def body(i, _):
            action(i)
            return 0

        lax.fori_loop(start, stop, body, 0)

    half_steps = steps // 2
    pass_on(0)
    normalise(0)
    pass_on(1)
    gate(0)
    pass_on(2)

    def rest_of_half(i):
        normalise(i)
        gate(i)

    run(rest_of_half, 1, half_steps)
    pass_on(3)
    run(rest_of_half, half_steps, steps - 1)
    have(0, 1)
    run(up, 0, half_steps)
    have(2, 3)
    backward(0)
    normalise(steps - 1)
    gate(steps - 1)
    store_all((second, second_out), (cotin, cotin_out), (resid, resid_out), (square, square_out))
    store_all((own_tok, own_tok_out))
    run(up, half_steps, steps)
    store_all((hidden, hidden_out))

    def back_step(i):
        backward(i)
        finish_parts(i - 1)

    run(back_step, 1, steps)
    finish_parts(steps - 1)
    for copy in stores:
        copy.wait()

    def drain(i, _):
        for copy in (attn_copy, second_copy, spart_copy, mpart_copy, x_copy):
            copy(i).wait_send()
        for copy in [*chunk_stores(i), *part_stores(i)]:
            copy.wait()
        return 0

    lax.fori_loop(0, steps, drain, 0)
    for copies in sends + passes:
        for copy in copies:
            copy.wait_send()


def call_feed_forward(
    shards, lengths, mixed, out_whole, tokens, cotangent, gains, gate_whole, out_weight,
    gate_weight, up_weight, down_weight,
):
    slots, length, width = tokens.shape
    rows = slots * length
    qw = mixed.shape[1]
    ff = gate_weight.shape[1]
    steps = 2 * length // TILE
    shape = jax.ShapeDtypeStruct
    outs = (
        shape((rows, width), bf16), shape((rows, ff), bf16), shape((rows, ff), bf16),
        shape((rows, ff), bf16), shape((rows, width), bf16), shape((length, width), bf16),
        shape((length, width), bf16), shape((length, width), f32), shape((8, width), f32),
        shape((length, width), bf16),
    )
    half = pltpu.VMEM((length, width), bf16)
    return pl.pallas_call(
        functools.partial(feed_forward, shards),
        out_shape=outs,
        in_specs=[SMEM] + [HBM] * 10,
        out_specs=[HBM] * len(outs),
        scratch_shapes=[
            pltpu.VMEM((rows, qw), bf16),
            pltpu.VMEM((qw, width), bf16),
            pltpu.VMEM((slots, length, width), bf16),
            pltpu.VMEM((slots, length, width), bf16),
            pltpu.VMEM((16, width), f32),
            pltpu.VMEM((width, ff), bf16),
            pltpu.VMEM((width, ff), bf16),
            pltpu.VMEM((ff, width), bf16),
            *[pltpu.VMEM(out.shape, out.dtype) for out in outs],
            pltpu.VMEM((length, width), f32),
            *[half] * 8,
            pltpu.VMEM((steps, TILE, ff), f32),
            pltpu.VMEM((steps, TILE, ff), f32),
            pltpu.SemaphoreType.DMA((6,)),
            pltpu.SemaphoreType.DMA((2, shards)),
            pltpu.SemaphoreType.DMA((6,)),
            pltpu.SemaphoreType.DMA((6, steps)),
            pltpu.SemaphoreType.DMA((8, shards - 1)),
            pltpu.SemaphoreType.DMA((8, shards - 1)),
            pltpu.SemaphoreType.DMA((4, steps)),
            pltpu.SemaphoreType.DMA((4, steps)),
            pltpu.SemaphoreType.DMA((steps,)),
            pltpu.SemaphoreType.DMA((steps,)),
        ],
        compiler_params=pltpu.CompilerParams(
            collective_id=2, has_side_effects=True, vmem_limit_bytes=56 * 2**20
        ),
        name="feed_forward",
    )(
        lengths, mixed, out_whole, tokens, cotangent, gains, gate_whole, out_weight,
        gate_weight, up_weight, down_weight,
    )


def layer_backward(
    shards, contexts, lengths_ref, second_ref, gback_ref, uback_ref, cotin_ref, hidden_ref,
    spart_ref, mpart_ref, resid_ref, square_ref, mixed_ref, linv_ref, qs_ref, qraw_ref, kraw_ref,
    kv_ref, first_ref, wq_ref, wk_ref, wv_ref, wo_ref, wo_own_ref, gain_ref, own_tok_ref, head_gain_ref,
    inside_cos_ref, inside_sin_ref, start_ref,
    straight_out, turned_out, layer_out, tgrad_out, sums_out,
    second, gback, uback, cotin, hidden, spart, mpart, resid, square, dq, wq, wkv, wo, gains,
    unit_kv, unit_first, unit_kraw, unit_back, kv_grad, cosine, sine, xs, xm, outin,
    resback, part, part_core, part_x, part_z, fxrecv,
    piece, ysend, yrecv, zin, ztop, turned, sums, sums_circle, sums_line, acc_gain, acc_ff, acc_head,
    acc_square,
    load_sem, gather_sem, kv_sem, late_sem, store_sem, x_send, x_recv, core_send, core_recv, y_send, y_recv,
    g_send, z_recv, top_recv, res_send, res_recv, p_send, p_recv, s_send, s_recv,
):
    shard, context, tensor = place()
    rows, width = second.shape
    length = resid.shape[0]
    ff = gback.shape[1]
    qw, kw = wq.shape[1], wkv.shape[1] // 2
    head = head_gain_ref.shape[1]
    heads, kv_heads = qw // head, kw // head
    group = heads // kv_heads
    share = piece.shape[1]
    chunk_count, chunk = piece.shape[0], piece.shape[2]
    early = ysend.shape[1]
    half_contexts = contexts // 2
    root = contexts // 2
    turn_from, turn_to = 2 * ff // chunk, (3 * ff + qw) // chunk
    step_rows = TILE // 2
    steps = length // step_rows
    scale = head**-0.5
    core = tensor % 2
    chip = tensor // 2
    quarter = length // 4
    core_peer = (shard, context, tensor + 1 - 2 * core)
    x_peer = (shard, context, (tensor + 2) % 4)
    peers = [(lax.rem(shard + d, shards), context, tensor) for d in range(1, shards)]
    below = (shard, jnp.maximum(context - 1, 0), tensor)
    above = (shard, jnp.minimum(context + 1, contexts - 1), tensor)
    around = shards * 4
    index = shard * 4 + tensor
    places = [lax.rem(index + d, around) for d in range(1, around)]
    circle = [(at // 4, context, at % 4) for at in places]
    line = [(shard, lax.rem(context + d, contexts), tensor) for d in range(1, contexts)]
    barrier = greet([*circle, *line])

    pairs = [
        (spart_ref, spart), (second_ref, second), (gback_ref, gback), (uback_ref, uback),
        (cotin_ref, cotin), (hidden_ref, hidden), (mpart_ref, mpart), (resid_ref, resid),
        (gain_ref, gains), (linv_ref, dq), (square_ref, square), (wq_ref, wq),
        (wk_ref, wkv.at[:, :kw]), (wv_ref, wkv.at[:, kw:]),
    ]
    loads = [
        pltpu.make_async_copy(source, target, load_sem.at[n])
        for n, (source, target) in enumerate(pairs)
    ]
    loads += gather_loads(wo_own_ref, wo_ref, wo, shard, shards, 1, gather_sem)
    for copy in loads[:7]:
        copy.start()

    def mine(i):
        return rows_of(core * steps + i, step_rows)

    def theirs(i):
        return rows_of((1 - core) * steps + i, step_rows)

    def half(i):
        return rows_of(i, step_rows)

    def xs_copy(i):
        return remote(spart.at[half(i), :], xs.at[half(i), :], x_send.at[0, i], x_recv.at[0, i], x_peer)

    def xm_copy(i):
        return remote(mpart.at[half(i), :], xm.at[half(i), :], x_send.at[1, i], x_recv.at[1, i], x_peer)

    fsend, fxsend, frecv = part.at[0], part.at[1], xs

    def xf_copy(i):
        return remote(
            fxsend.at[half(i), :], fxrecv.at[half(i), :], x_send.at[2, i], x_recv.at[2, i], x_peer
        )

    def core_copy(kind, i, source, target):
        return remote(source, target, core_send.at[kind, i], core_recv.at[kind, i], core_peer)

    def outin_copy(i):
        return core_copy(0, i, outin.at[mine(i), :], outin.at[mine(i), :])

    def layer_copy(i):
        return core_copy(1, i, mpart.at[half(i), :], layer_out.at[core, half(i), :])

    def f_copy(i):
        return core_copy(2, i, fsend.at[half(i), :], frecv.at[half(i), :])

    def tgrad_copy(i):
        return core_copy(3, i, spart.at[half(i), :], tgrad_out.at[core, half(i), :])

    def layer_keep(i):
        return pltpu.make_async_copy(
            mpart.at[half(i), :], layer_out.at[core, half(i), :], store_sem.at[0, i]
        )

    def tgrad_keep(i):
        return pltpu.make_async_copy(
            spart.at[half(i), :], tgrad_out.at[core, half(i), :], store_sem.at[1, i]
        )

    def y_copy(d, k):
        return remote(
            ysend.at[d, k % early], yrecv.at[d, k], y_send.at[d, k], y_recv.at[d, k], peers[d]
        )

    def up_copy(k):
        return remote(piece.at[k], zin.at[k], g_send.at[k], z_recv.at[k], above)

    def down_copy(k):
        return remote(piece.at[k], zin.at[k], g_send.at[k], z_recv.at[k], below)

    def top_copy(k):
        return remote(piece.at[k], ztop.at[k], g_send.at[k], top_recv.at[k], below)

    def back_down_copy(k):
        return remote(zin.at[k], zin.at[k], res_send.at[0, k], res_recv.at[k], below)

    def back_up_copy(k):
        return remote(zin.at[k], zin.at[k], res_send.at[1, k], res_recv.at[k], above)

    def grad_copies(k):
        column = rows_of(jnp.where(k < turn_from, k, k - (turn_to - turn_from)), chunk)
        row = jnp.clip(k - turn_from, 0, turn_to - turn_from - 1)
        return (
            pltpu.make_async_copy(zin.at[k], straight_out.at[:, column], late_sem.at[k]),
            pltpu.make_async_copy(
                turned.at[row], turned_out.at[rows_of(row, chunk), :], late_sem.at[k]
            ),
        )

    def grad_keep(k, finish=False):
        straight_copy, turned_copy = grad_copies(k)
        aside = (k >= turn_from) & (k < turn_to)

        @pl.when(jnp.logical_not(aside))
        def _():
            straight_copy.wait() if finish else straight_copy.start()

        @pl.when(aside)
        def _():
            if not finish:
                turned[k - turn_from] = zin[k].astype(f32).T.astype(bf16)
            turned_copy.wait() if finish else turned_copy.start()

    def reduce_chunk(k):
        for d in range(shards - 1):
            y_copy(d, k).wait_recv()

        def total():
            result = piece[k].astype(f32)
            for d in range(shards - 1):
                result = result + yrecv[d, k].astype(f32)
            return result

        @pl.when((context == 0) | (context == contexts - 1))
        def _():
            piece[k] = total().astype(bf16)

        @pl.when((context > 0) & (context < root))
        def _():
            up_copy(k).wait_recv()
            piece[k] = (total() + zin[k].astype(f32)).astype(bf16)

        @pl.when((context > root) & (context < contexts - 1))
        def _():
            down_copy(k).wait_recv()
            piece[k] = (total() + zin[k].astype(f32)).astype(bf16)

        @pl.when(context < root)
        def _():
            up_copy(k).start()

        @pl.when(context == root + 1)
        def _():
            top_copy(k).start()

        @pl.when(context > root + 1)
        def _():
            down_copy(k).start()

        @pl.when(context == root)
        def _():
            up_copy(k).wait_recv()
            top_copy(k).wait_recv()
            zin[k] = (total() + zin[k].astype(f32) + ztop[k].astype(f32)).astype(bf16)
            back_down_copy(k).start()
            back_up_copy(k).start()
            grad_keep(k)

    def return_chunk(k):
        @pl.when(context < root)
        def _():
            back_down_copy(k).wait_recv()

            @pl.when(context > 0)
            def _():
                back_down_copy(k).start()

            grad_keep(k)

        @pl.when(context > root)
        def _():
            back_up_copy(k).wait_recv()

            @pl.when(context < contexts - 1)
            def _():
                back_up_copy(k).start()

            grad_keep(k)

    far = max(root, contexts - 1 - root)
    from_end = jnp.where(context <= root, context, contexts - 1 - context)
    hop = 2
    reduce_lag = hop * jnp.where(context == root, far, from_end)
    spare = 0
    at_end = (context == 0) | (context == contexts - 1)
    return_lag = hop * (far + jnp.abs(context - root)) + jnp.where(at_end, spare, 0)
    ticks = chunk_count + 2 * hop * far + spare

    def tick(t):
        k = t - reduce_lag

        @pl.when((k >= 0) & (k < chunk_count))
        def _():
            reduce_chunk(k)

        back = t - return_lag

        @pl.when((back >= 0) & (back < chunk_count) & (context != root))
        def _():
            return_chunk(back)

    def weight_grad(left, right, columns, first_chunk, count):
        for d in range(shards - 1):
            theirs_at = rows_of(lax.rem(shard + d + 1, shards), share)
            result = dot_tn(left[:, theirs_at], right[:, columns : columns + count * chunk])
            for n in range(count):
                k = first_chunk + n
                if k >= early:
                    y_copy(d, k - early).wait_send()
                ysend[d, k % early] = result[:, n * chunk : (n + 1) * chunk].astype(bf16)
                y_copy(d, k).start()
        result = dot_tn(left[:, rows_of(shard, share)], right[:, columns : columns + count * chunk])
        for n in range(count):
            piece[first_chunk + n] = result[:, n * chunk : (n + 1) * chunk].astype(bf16)

    def part_at(slot, block):
        return block if slot == 0 else contexts - 1 + block

    def part_core_copy(slot, block):
        at = part_at(slot, block)
        return remote(
            part.at[slot, pl.ds(0, length // 2), :], part_core.at[at], p_send.at[0, at],
            p_recv.at[0, at], core_peer,
        )

    def part_x_copy(slot, block):
        at = part_at(slot, block)
        return remote(
            part_core.at[at, rows_of(1 - chip, quarter), :], part_x.at[at], p_send.at[1, at],
            p_recv.at[1, at], x_peer,
        )

    def part_z_copy(slot, block):
        at = part_at(slot, block)
        return remote(part_x.at[at], part_z.at[at], p_send.at[2, at], p_recv.at[2, at], below)

    def part_make(slot, block):
        for q in range(4):
            result = dot_nt(unit_back[q * quarter : (q + 1) * quarter, :], wkv[...])
            place_at = jnp.where(core == q % 2, 2, 0) + q // 2
            part[slot, rows_of(place_at, quarter), :] = result.astype(bf16)
        part_core_copy(slot, block).start()

    def part_across(slot, block):
        part_core_copy(slot, block).wait_recv()
        at = part_at(slot, block)
        total = part[slot, length // 2 :, :].astype(f32) + part_core[at].astype(f32)
        part_core[at] = total.astype(bf16)
        part_x_copy(slot, block).start()
        part_core_copy(slot, block).wait_send()

    def part_down(slot, block, count):
        part_x_copy(slot, block).wait_recv()
        at = part_at(slot, block)
        total = part_core[at, rows_of(chip, quarter), :].astype(f32) + part_x[at].astype(f32)

        @pl.when(context == count - 1)
        def _():
            part_x[at] = total.astype(bf16)

        @pl.when(context < count - 1)
        def _():
            part_z_copy(slot, block).wait_recv()
            part_x[at] = (total + part_z[at].astype(f32)).astype(bf16)

        part_z_copy(slot, block).start()

    def unit_place(slot, block):
        return jnp.where(context < half_contexts, slot, block % 2)

    def unit_loads(slot, block):
        at = unit_place(slot, block)
        return [
            pltpu.make_async_copy(source.at[block, slot], target.at[at], kv_sem.at[n, at])
            for n, (source, target) in enumerate(
                ((kv_ref, unit_kv), (first_ref, unit_first), (kraw_ref, unit_kraw))
            )
        ]

    def start_unit(slot, block):
        for copy in unit_loads(slot, block):
            copy.start()

    acc_gain[...] = jnp.zeros_like(acc_gain)
    acc_ff[...] = jnp.zeros_like(acc_ff)
    acc_head[...] = jnp.zeros_like(acc_head)
    acc_square[...] = jnp.zeros_like(acc_square)
    loads[0].wait()
    pl.semaphore_wait(barrier, around + contexts - 2)
    alive = (context < half_contexts) | (core == 0)

    @pl.when(alive)
    def _():
        for i in range(steps):
            xs_copy(i).start()

    for n in range(1, 7):
        loads[n].wait()
    for copy in loads[7:]:
        copy.start()
    for i in range(steps):
        xm_copy(i).start()
    gate_chunks = ff // chunk
    out_chunks = qw // chunk
    query_chunk = 3 * gate_chunks + out_chunks
    weight_grad(second, gback, 0, 0, gate_chunks)
    weight_grad(second, uback, 0, gate_chunks, gate_chunks)
    weight_grad(cotin, hidden, 0, 2 * gate_chunks, gate_chunks)
    for n in range(7, len(loads)):
        loads[n].wait()
    qs, qraw, mixed = hidden.at[:, :qw], gback.at[:, :qw], uback.at[:, :qw]
    own_kback, own_vback = gback.at[:, qw : qw + kw], uback.at[:, qw : qw + kw]
    next_pairs = [(qs_ref, qs), (qraw_ref, qraw), (mixed_ref, mixed)]
    next_loads = [
        pltpu.make_async_copy(source, target, load_sem.at[n])
        for n, (source, target) in enumerate(next_pairs)
    ]
    for copy in next_loads:
        copy.start()
    start_unit(0, 0)

    def fold(values):
        return jnp.sum(values.reshape(values.shape[0] // 8, 8, values.shape[1]), axis=0)

    def norm_back(values, back, gain):
        inverse = lax.rsqrt(mean_square(values) + epsilon)
        normal = values * inverse
        scaled = back * gain
        inward = inverse * (scaled - normal * jnp.mean(normal * scaled, axis=-1, keepdims=True))
        return inward, back * normal

    def residual_step(i, _):
        @pl.when(alive)
        def _():
            xs_copy(i).wait_recv()

        back = spart[half(i), :].astype(f32)
        back += jnp.where(alive, xs[half(i), :].astype(f32), 0.0)
        inward, terms = norm_back(resid[half(i), :], back, gains[8:9, :])
        acc_ff[...] += fold(terms)
        total = cotin[mine(i), :].astype(f32) + inward
        resback[half(i), :] = total
        outin[mine(i), :] = total.astype(bf16)
        outin_copy(i).start()
        return 0

    tick_at = 0
    ready = 3 * gate_chunks

    def next_tick(count=1):
        nonlocal tick_at
        for _ in range(count):
            if tick_at < ready or (ready == chunk_count and tick_at < ticks):
                tick(tick_at)
                tick_at += 1

    for i, count in zip(range(steps), (2, 2, 2, 1)):
        residual_step(i, 0)
        next_tick(count)

    for i in range(steps):
        outin_copy(i).wait_recv()
    first = cotin
    first_loads = [
        pltpu.make_async_copy(
            first_ref.at[context, slot], first.at[slot * length : (slot + 1) * length, :],
            gather_sem.at[slot],
        )
        for slot in range(2)
    ]
    for copy in first_loads:
        copy.start()
    for copy in next_loads:
        copy.wait()
    dox = second

    def mixed_step(i, _):
        at = rows_of(i, TILE)
        back = dot_nt(outin[at, :], wo[...]).astype(bf16).astype(f32)
        lanes = lax.broadcasted_iota(jnp.int32, (TILE, head), 1)
        for h in range(heads):
            columns = slice(h * head, (h + 1) * head)
            low = (back[:, columns] * dq[at, columns]).astype(bf16)
            centre = jnp.sum(
                low.astype(f32) * mixed[at, columns].astype(f32), axis=-1, keepdims=True
            )
            high = centre.astype(bf16).astype(f32)
            extra = jnp.where(lanes == 0, -high, jnp.where(lanes == 1, high - centre, 0.0))
            dox[at, 2 * h * head : (2 * h + 1) * head] = low
            dox[at, (2 * h + 1) * head : (2 * h + 2) * head] = extra.astype(bf16)
        dq[at, :] = jnp.zeros((TILE, qw), f32)
        return 0

    lax.fori_loop(0, rows // TILE, mixed_step, 0)
    next_tick(2)
    ones = jnp.ones((length, head), bf16)

    def head_back(raw, back, gain, local):
        turned_back = back * cosine[local, :] - pltpu.roll(back, head // 2, 1) * sine[local, :]
        return norm_back(raw.astype(f32), turned_back, gain)

    kv_grad[...] = jnp.zeros_like(kv_grad)

    @pl.when(context >= half_contexts)
    def _():
        own_kback[length:, :] = jnp.zeros((length, kw), bf16)
        own_vback[length:, :] = jnp.zeros((length, kw), bf16)

    def block_back(slot, block, diagonal):
        lines = slice(slot * length, (slot + 1) * length)
        buffer = unit_place(slot, block)
        if diagonal:
            key_spots = lax.broadcasted_iota(jnp.int32, (length, length), 0)
            query_spots = lax.broadcasted_iota(jnp.int32, (length, length), 1)
            counted = key_spots <= query_spots

        def one_group(g, _):
            keys = unit_kv[buffer, :, rows_of(g, head)]
            values = unit_kv[buffer, :, rows_of(kv_heads + g, head)]
            widened = jnp.concatenate([values, ones], axis=1)
            key_back = jnp.zeros((length, head), f32)
            value_back = jnp.zeros((length, head), f32)
            for member in range(group):
                h = g * group + member
                columns = rows_of(h, head)
                queries = qs[lines, columns]
                inward = dox[lines, rows_of(h, 2 * head)]
                raised = jnp.exp2(dot_nt(keys, queries))
                if diagonal:
                    raised = jnp.where(counted, raised, 0.0)
                scores_back = (raised * dot_nt(widened, inward)).astype(bf16)
                value_back += dot_nn(raised.astype(bf16), inward[:, :head])
                key_back += dot_nn(scores_back, queries)
                dq[lines, columns] += dot_tn(scores_back, keys)
            raw_back, terms = head_back(
                unit_kraw[buffer, :, rows_of(g, head)], key_back * math.log(2.0),
                head_gain_ref[8:9, :], slice(None),
            )
            acc_head[1] += fold(terms)
            unit_back[:, rows_of(g, head)] = raw_back.astype(bf16)
            unit_back[:, rows_of(kv_heads + g, head)] = value_back.astype(bf16)
            return 0

        lax.fori_loop(0, kv_heads, one_group, 0)

        def grad_rows(n, _):
            at = rows_of(n, TILE)
            kv_grad[at, :] += dot_tn(unit_first[buffer, :, at], unit_back[...])
            return 0

        lax.fori_loop(0, width // TILE, grad_rows, 0)
        if diagonal:
            own_kback[lines, :] = unit_back[:, :kw]
            own_vback[lines, :] = unit_back[:, kw:]

    def next_units(slot, block):
        if slot == 0 and block < half_contexts:

            @pl.when(context < half_contexts)
            def _():
                start_unit(1, block)

        if block + 1 < contexts:
            more = block + 1 <= context
            if slot == 0:
                more = more & (context >= half_contexts)

            @pl.when(more)
            def _():
                start_unit(0, block + 1)

    for turn_at in range(contexts + 1):
        block, before = turn_at, turn_at - 1
        if block < contexts:
            turn(cosine, sine, start_ref, block, inside_cos_ref, inside_sin_ref)
        for slot, count in ((0, contexts), (1, half_contexts)):
            within = context < count
            if block < count:

                @pl.when((block <= context) & within)
                def _():
                    for copy in unit_loads(slot, block):
                        copy.wait()
                    next_units(slot, block)

                @pl.when((block == context) & within)
                def _():
                    block_back(slot, block, True)

                @pl.when((block < context) & within)
                def _():
                    block_back(slot, block, False)

            if 0 <= before < count - 1:

                @pl.when((before < context) & within)
                def _():
                    part_across(slot, before)

            if block < count - 1:

                @pl.when((block < context) & within)
                def _():
                    part_make(slot, block)

            gone = turn_at - 2 - (count - 1 - context)

            @pl.when((gone >= 0) & (gone < context) & within)
            def _():
                part_down(slot, gone, count)

        if turn_at == 0:
            weight_grad(outin, mixed, 0, 3 * gate_chunks, out_chunks)
            ready += out_chunks
        if turn_at < contexts:
            next_tick(3)
    for copy in first_loads:
        copy.wait()
    turn(cosine, sine, start_ref, context, inside_cos_ref, inside_sin_ref)

    def query_step(i, _):
        at = rows_of(i, TILE)
        local = rows_of(i % (length // TILE), TILE)
        for h in range(heads):
            columns = slice(h * head, (h + 1) * head)
            inward, terms = head_back(
                qraw[at, columns], dq[at, columns] * scale, head_gain_ref[0:1, :], local
            )
            acc_head[0] += fold(terms)
            qraw[at, columns] = inward.astype(bf16)
        return 0

    lax.fori_loop(0, rows // TILE, query_step, 0)
    next_tick()
    weight_grad(first, qraw, 0, query_chunk, out_chunks)
    key_chunk = query_chunk + out_chunks
    for n in range(2 * kw // chunk):
        k = key_chunk + n
        columns = slice(n * chunk, (n + 1) * chunk)
        for d in range(shards - 1):
            theirs_at = rows_of(lax.rem(shard + d + 1, shards), share)
            y_copy(d, k - early).wait_send()
            ysend[d, k % early] = kv_grad[theirs_at, columns].astype(bf16)
            y_copy(d, k).start()
        piece[k] = kv_grad[rows_of(shard, share), columns].astype(bf16)
    ready = chunk_count
    next_tick(2)
    _, short_length = slot_order(lengths_ref)

    @pl.when(alive)
    def _():
        for i in range(steps):
            xs_copy(i).wait_send()

    tok_load = pltpu.make_async_copy(own_tok_ref, spart, load_sem.at[0])
    tok_load.start()

    def layer_step(i, _):
        xm_copy(i).wait_recv()
        xm_copy(i).wait_send()
        mlp = mpart[half(i), :].astype(f32) + xm[half(i), :].astype(f32)
        layer = resid[half(i), :] + mlp
        mpart[half(i), :] = layer.astype(bf16)
        layer_copy(i).start()
        layer_keep(i).start()
        lines = lax.broadcasted_iota(jnp.int32, (step_rows, width), 0)
        limit = jnp.where(core == 0, 2**30, short_length)
        counted = lines + (context * length + i * step_rows) < limit
        acc_square[0] += fold(jnp.where(counted, layer * layer, 0.0))
        acc_square[1] += fold(jnp.where(counted, mlp * mlp, 0.0))
        return 0

    lax.fori_loop(0, steps, layer_step, 0)
    next_tick(3)

    @pl.when(context < contexts - 1)
    def _():
        part_z_copy(0, jnp.minimum(context, contexts - 2)).wait_recv()

    @pl.when(context < half_contexts - 1)
    def _():
        part_z_copy(1, jnp.minimum(context, max(half_contexts - 2, 0))).wait_recv()

    fown = resid

    def first_step(i, _):
        if i < steps:
            both = lambda ref: jnp.concatenate([ref[theirs(i), :], ref[mine(i), :]], axis=0)
            result = dot_nt(both(qraw), wq[...])
            result += dot_nt(both(own_kback), wkv[:, :kw])
            result += dot_nt(both(own_vback), wkv[:, kw:])

            def from_above(slot):
                at = jnp.where(
                    slot == 0,
                    jnp.minimum(context, contexts - 2),
                    contexts - 1 + jnp.minimum(context, max(half_contexts - 2, 0)),
                )
                last = jnp.where(slot == 0, contexts - 1, half_contexts - 1)
                come = (i == tensor) & (context < last)
                return jnp.where(come, part_z[at].astype(f32), 0.0)

            fsend[half(i), :] = (result[:step_rows] + from_above(1 - core)).astype(bf16)
            f_copy(i).start()
            fown[half(i), :] = result[step_rows:] + from_above(core)

        if i > 0:
            before = i - 1
            f_copy(before).wait_recv()
            total = fown[half(before), :] + frecv[half(before), :].astype(f32)
            fxsend[half(before), :] = total.astype(bf16)

            @pl.when(alive)
            def _():
                xf_copy(before).start()

        return 0

    for i in range(steps + 1):
        first_step(i, 0)
        next_tick(2 if i == 2 else 1 if i == 1 else 0)
    tok_load.wait()

    def tokens_step(i, _):
        @pl.when(alive)
        def _():
            xf_copy(i).wait_recv()

        back = fxsend[half(i), :].astype(f32)
        back += jnp.where(alive, fxrecv[half(i), :].astype(f32), 0.0)
        inward, terms = norm_back(spart[half(i), :].astype(f32), back, gains[0:1, :])
        acc_gain[...] += fold(terms)
        spart[half(i), :] = (resback[half(i), :] + inward).astype(bf16)
        tgrad_copy(i).start()
        tgrad_keep(i).start()
        return 0

    for i, count in zip(range(steps), (2, 1, 1, 4)):
        next_tick(count)
        tokens_step(i, 0)

    def total_of(values):
        return jnp.sum(jnp.sum(values, axis=0, keepdims=True), axis=1, keepdims=True)

    lanes = lax.broadcasted_iota(jnp.int32, (1, 128), 1)
    base = (shard * 2 + core) * 4
    squares = jnp.where(lanes == base, total_of(acc_square[0]), 0.0)
    squares += jnp.where(lanes == base + 1, total_of(square[...]), 0.0)
    squares += jnp.where(lanes == base + 2, total_of(acc_square[1]), 0.0)
    gain_row = 0.5 * jnp.sum(acc_gain[...], axis=0, keepdims=True)
    ff_row = 0.5 * jnp.sum(acc_ff[...], axis=0, keepdims=True)
    folds = width // 128
    sums[...] = jnp.zeros_like(sums)
    for n in range(folds):
        columns = slice(n * 128, (n + 1) * 128)
        sums[0, n : n + 1, :] = gain_row[:, columns]
        sums[0, folds + n : folds + n + 1, :] = ff_row[:, columns]
    sums[0, 2 * folds : 2 * folds + 1, :] = jnp.sum(acc_head[0], axis=0, keepdims=True)
    sums[0, 2 * folds + 1 : 2 * folds + 2, :] = jnp.sum(acc_head[1], axis=0, keepdims=True)
    sums[0, 2 * folds + 2 : 2 * folds + 3, :] = 0.5 * squares
    circle_hops = [
        remote(sums.at[0], sums_circle.at[index], s_send.at[d], s_recv.at[d], device)
        for d, device in enumerate(circle)
    ]
    for copy in circle_hops:
        copy.start()
    sums_circle[index] = sums[0]
    next_tick()
    for copy in circle_hops:
        copy.wait_recv()
    total = sums_circle[0]
    for n in range(1, around):
        total = total + sums_circle[n]
    sums[1] = total
    line_hops = [
        remote(
            sums.at[1], sums_line.at[context], s_send.at[around + d], s_recv.at[around + d], device
        )
        for d, device in enumerate(line)
    ]
    for copy in line_hops:
        copy.start()
    sums_line[context] = total

    def more_ticks(t, _):
        tick(t)
        return 0

    lax.fori_loop(tick_at, ticks, more_ticks, 0)
    for copy in line_hops:
        copy.wait_recv()
    total = sums_line[0]
    for n in range(1, contexts):
        total = total + sums_line[n]
    sums[2] = total
    sums_keep = pltpu.make_async_copy(sums.at[2], sums_out, store_sem.at[2, 0])
    sums_keep.start()
    for copy in [*circle_hops, *line_hops]:
        copy.wait_send()

    def drain_steps(i, _):
        for copy in (outin_copy, layer_copy, f_copy, tgrad_copy):
            copy(i).wait_send()
        layer_copy(i).wait_recv()
        tgrad_copy(i).wait_recv()

        @pl.when(alive)
        def _():
            xf_copy(i).wait_send()

        layer_keep(i).wait()
        tgrad_keep(i).wait()
        return 0

    lax.fori_loop(0, steps, drain_steps, 0)

    def drain_chunks(k, _):
        @pl.when(k >= chunk_count - early)
        def _():
            for d in range(shards - 1):
                y_copy(d, k).wait_send()

        @pl.when(context != root)
        def _():
            up_copy(k).wait_send()

        @pl.when((context <= root) & (context > 0))
        def _():
            back_down_copy(k).wait_send()

        @pl.when((context >= root) & (context < contexts - 1))
        def _():
            back_up_copy(k).wait_send()

        grad_keep(k, finish=True)
        return 0

    lax.fori_loop(0, chunk_count, drain_chunks, 0)
    for block in range(contexts - 1):
        for slot, count in ((0, contexts), (1, half_contexts)):
            if block < count - 1:

                @pl.when((block < context) & (context < count))
                def _():
                    part_x_copy(slot, block).wait_send()
                    part_z_copy(slot, block).wait_send()

    sums_keep.wait()


def call_layer_backward(shards, contexts, lengths, parts):
    (
        second, gback, uback, cotin, hidden, spart, mpart, resid, square, mixed, linv, qs, qraw,
        kraw, kv, first, wq, wk, wv, wo, out_weight, gains, own_tok, head_gains, *tables,
    ) = parts
    rows, width = second.shape
    length = resid.shape[0]
    ff, qw, kw = gback.shape[1], wq.shape[1], wk.shape[1]
    share = width // shards
    chunk = TILE // 2
    sum_rows = 2 * width // 128 + 8
    chunk_count = (3 * ff + 2 * qw + 2 * kw) // chunk
    early = 3 * ff // chunk
    steps = 2 * length // TILE
    units = contexts - 1 + max(contexts // 2 - 1, 1)
    head = head_gains.shape[1]
    slots = rows // length
    shape = jax.ShapeDtypeStruct
    outs = (
        shape((share, 2 * ff + qw + 2 * kw), bf16), shape((ff + qw, share), bf16),
        shape((slots, length, width), bf16), shape((slots, length, width), bf16),
        shape((sum_rows, 128), f32),
    )
    dma = pltpu.SemaphoreType.DMA

    def like(array):
        return pltpu.VMEM(array.shape, array.dtype)

    half = pltpu.VMEM((length, width), bf16)
    chunks = pltpu.VMEM((chunk_count, share, chunk), bf16)
    return pl.pallas_call(
        functools.partial(layer_backward, shards, contexts),
        out_shape=outs,
        in_specs=[SMEM] + [HBM] * 23 + [VMEM] * 4,
        out_specs=[HBM] * len(outs),
        scratch_shapes=[
            like(second), like(gback), like(uback), like(cotin), like(hidden), like(spart),
            like(mpart), like(resid), like(square), like(linv), like(wq),
            pltpu.VMEM((width, 2 * kw), bf16), like(wo), like(gains),
            pltpu.VMEM((2, length, 2 * kw), bf16), pltpu.VMEM((2, length, width), bf16),
            pltpu.VMEM((2, length, kw), bf16), pltpu.VMEM((length, 2 * kw), bf16),
            pltpu.VMEM((width, 2 * kw), f32),
            pltpu.VMEM((length, head), f32), pltpu.VMEM((length, head), f32),
            half, half, pltpu.VMEM((rows, width), bf16), pltpu.VMEM((length, width), f32),
            pltpu.VMEM((2, length, width), bf16),
            pltpu.VMEM((units, length // 2, width), bf16),
            pltpu.VMEM((units, length // 4, width), bf16),
            pltpu.VMEM((units, length // 4, width), bf16),
            half,
            chunks,
            pltpu.VMEM((shards - 1, early, share, chunk), bf16),
            pltpu.VMEM((shards - 1, chunk_count, share, chunk), bf16),
            chunks, chunks, pltpu.VMEM(((ff + qw) // chunk, chunk, share), bf16),
            pltpu.VMEM((3, sum_rows, 128), f32), pltpu.VMEM((4 * shards, sum_rows, 128), f32),
            pltpu.VMEM((contexts, sum_rows, 128), f32),
            pltpu.VMEM((8, width), f32), pltpu.VMEM((8, width), f32),
            pltpu.VMEM((2, 8, head), f32), pltpu.VMEM((2, 8, width), f32),
            dma((15,)), dma((shards,)), dma((3, 2)), dma((chunk_count,)), dma((3, steps)),
            dma((3, steps)), dma((3, steps)), dma((4, steps)), dma((4, steps)),
            dma((shards - 1, chunk_count)), dma((shards - 1, chunk_count)),
            dma((chunk_count,)), dma((chunk_count,)), dma((chunk_count,)),
            dma((2, chunk_count)), dma((chunk_count,)), dma((3, units)), dma((3, units)),
            dma((4 * shards + contexts,)), dma((4 * shards + contexts,)),
        ],
        compiler_params=pltpu.CompilerParams(
            collective_id=3, has_side_effects=True, vmem_limit_bytes=63 * 2**20
        ),
        name="layer_backward",
    )(lengths, *parts)


def local(
    tokens, lengths, cotangent, query_weight, key_weight, value_weight, out_weight, gate_weight,
    up_weight, down_weight, attention_gain, feedforward_gain, query_gain, key_gain,
):
    slots, length, width = tokens.shape
    shards, contexts = lax.axis_size("shard"), lax.axis_size("context")
    shard, context, _ = place()
    head = query_gain.shape[0]
    ff, qw, kw = gate_weight.shape[1], query_weight.shape[1], key_weight.shape[1]
    tables = [jnp.asarray(table) for table in rope_tables(length, contexts, head)]

    def packed(one, other):
        upper = lax.broadcasted_iota(jnp.int32, (16, one.shape[0]), 0) < 8
        return jnp.where(upper, one.astype(f32)[None], other.astype(f32)[None])

    gain_share = packed(attention_gain, feedforward_gain)
    head_gains = packed(query_gain, key_gain)
    (mixed, kv, qs, qraw, kraw, linv, first, wq, wk, wv, wo, wg, gains) = (
        call_attention_forward(
            shards, contexts, lengths, tokens, query_weight, key_weight, value_weight, out_weight,
            gate_weight, gain_share, head_gains, tables,
        )
    )
    (second, hidden, gback, uback, cotin, spart, mpart, resid, square, own_tok) = (
        call_feed_forward(
            shards, lengths, mixed, wo, tokens, cotangent, gains, wg, out_weight, gate_weight,
            up_weight, down_weight,
        )
    )
    straight, turned, layer, token_grads, sums = call_layer_backward(
        shards, contexts, lengths,
        (
            second, gback, uback, cotin, hidden, spart, mpart, resid, square, mixed, linv, qs,
            qraw, kraw, kv, first, wq, wk, wv, wo, out_weight, gains, own_tok, head_gains, *tables,
        ),
    )
    swapped = lengths[1] > lengths[0]

    def in_place(values):
        return jnp.where(swapped, values[::-1], values)

    ends = np.cumsum([ff, ff, qw, kw])
    gate_grad, up_grad, query_grad, key_grad, value_grad = (
        part.astype(f32) for part in jnp.split(straight, ends, axis=1)
    )
    down_grad, out_grad = (part.astype(f32) for part in jnp.split(turned, [ff], axis=0))
    folds = width // 128
    gain_grads = [
        lax.dynamic_slice_in_dim(
            sums[n * folds : (n + 1) * folds].reshape(width), shard * (width // shards),
            width // shards, 0,
        )
        for n in range(2)
    ]
    query_gain_grad, key_gain_grad, squares = sums[2 * folds : 2 * folds + 3]
    squares = lax.dynamic_slice_in_dim(squares, shard * slots * 4, slots * 4, 0)
    squares = in_place(squares.reshape(slots, 4)[:, :3])
    return (
        in_place(layer),
        in_place(token_grads.astype(f32)),
        query_grad,
        key_grad,
        value_grad,
        out_grad,
        gate_grad,
        up_grad,
        down_grad,
        gain_grads[0],
        gain_grads[1],
        query_gain_grad,
        key_gain_grad,
        jnp.sqrt(squares / (lengths.astype(f32)[:, None] * width)),
    )


def solution(mesh):
    placed = (
        P("shard", "context", None),
        P("shard"),
        P("shard", "context", None),
        P("shard", "tensor"),
        P("shard", "tensor"),
        P("shard", "tensor"),
        P("tensor", "shard"),
        P("shard", "tensor"),
        P("shard", "tensor"),
        P("tensor", "shard"),
        P("shard"),
        P("shard"),
        P(),
        P(),
    )
    return jax.shard_map(
        local,
        mesh=mesh,
        in_specs=placed,
        out_specs=(
            P("shard", "context", None),
            P("shard", "context", None),
            P("shard", "tensor"),
            P("shard", "tensor"),
            P("shard", "tensor"),
            P("tensor", "shard"),
            P("shard", "tensor"),
            P("shard", "tensor"),
            P("tensor", "shard"),
            P("shard"),
            P("shard"),
            P(),
            P(),
            P("shard", None),
        ),
        check_vma=False,
    )
```

```python
import functools
import math

import jax
import jax.numpy as jnp
import numpy as np
from jax import lax
from jax.experimental import pallas as pl
from jax.experimental.pallas import tpu as pltpu
from jax.sharding import PartitionSpec as P

epsilon = 1e-06
rope_base = 1000000.0
MESH = pl.DeviceIdType.MESH
f32 = jnp.float32
bf16 = jnp.bfloat16
HBM = pl.BlockSpec(memory_space=pl.ANY)
VMEM = pl.BlockSpec(memory_space=pltpu.VMEM)
SMEM = pl.BlockSpec(memory_space=pltpu.SMEM)
TILE = 256


def rows_of(index, size):
    if isinstance(index, int):
        return pl.ds(index * size, size)
    return pl.ds(pl.multiple_of(index * size, size), size)


def dot_nt(left, right):
    return lax.dot_general(left, right, (((1,), (1,)), ((), ())), preferred_element_type=f32)


def dot_tn(left, right):
    return lax.dot_general(left, right, (((0,), (0,)), ((), ())), preferred_element_type=f32)


def dot_nn(left, right):
    return jnp.dot(left, right, preferred_element_type=f32)


def mean_square(values):
    return jnp.mean(values * values, axis=-1, keepdims=True)


def place():
    return lax.axis_index("shard"), lax.axis_index("context"), lax.axis_index("tensor")


def greet(devices, extra=0):
    barrier = pltpu.get_barrier_semaphore()
    for device in devices:
        pl.semaphore_signal(barrier, inc=1, device_id=device, device_id_type=MESH)
    return barrier


def greet_line(barrier, shard, context, tensor, count):
    @pl.when(context > 0)
    def _():
        pl.semaphore_signal(
            barrier, inc=1, device_id=(shard, context - 1, tensor), device_id_type=MESH
        )

    @pl.when(context < count - 1)
    def _():
        pl.semaphore_signal(
            barrier, inc=1, device_id=(shard, context + 1, tensor), device_id_type=MESH
        )

    return jnp.minimum(context, 1) + jnp.minimum(count - 1 - context, 1)


def turn(cosine, sine, start_ref, block, inside_cos_ref, inside_sin_ref):
    head = cosine.shape[1]
    start_cos, start_sin = start_ref[block, 0:1, :], start_ref[block, 8:9, :]
    signs = jnp.where(lax.broadcasted_iota(jnp.int32, (1, head), 1) < head // 2, -1.0, 1.0)
    inside_cos, inside_sin = inside_cos_ref[...], inside_sin_ref[...]
    cosine[...] = start_cos * inside_cos - start_sin * inside_sin
    sine[...] = signs * (start_sin * inside_cos + start_cos * inside_sin)


def slot_order(lengths_ref):
    one, other = lengths_ref[0], lengths_ref[1]
    return jnp.where(other > one, 1, 0), jnp.minimum(one, other)


def gather_loads(share_ref, whole_ref, target, shard, shards, axis, sems):
    size = share_ref.shape[axis]
    copies = []
    for d in range(shards):
        at = rows_of(lax.rem(shard + d, shards), size)
        index = (slice(None), at) if axis == 1 else (at, slice(None))
        source = share_ref if d == 0 else whole_ref.at[index]
        copies.append(pltpu.make_async_copy(source, target.at[index], sems.at[d]))
    return copies


def remote(src, dst, send_sem, recv_sem, device):
    return pltpu.make_async_remote_copy(
        src_ref=src,
        dst_ref=dst,
        send_sem=send_sem,
        recv_sem=recv_sem,
        device_id=device,
        device_id_type=MESH,
    )


def rope_tables(length, contexts, head_size):
    half = head_size // 2
    speeds = np.tile(rope_base ** (-np.arange(half, dtype=np.float64) * 2.0 / head_size), 2)
    inside = np.arange(length, dtype=np.float64)[:, None] * speeds
    starts = np.arange(contexts, dtype=np.float64)[:, None] * length * speeds
    rows = np.stack([np.cos(starts), np.sin(starts)], axis=1)
    rows = np.repeat(rows, 8, axis=1)
    return (
        np.cos(inside).astype(np.float32),
        np.sin(inside).astype(np.float32),
        rows.astype(np.float32),
    )


def attention_forward(
    shards, contexts, lengths_ref, tok_ref, wq_ref, wk_ref, wv_ref, wo_ref, wg_ref, gain_ref,
    head_gain_ref, inside_cos_ref, inside_sin_ref, start_ref,
    mixed_out, kv_out, qs_out, qraw_out, kraw_out, linv_out, first_out, wq_out, wk_out, wv_out,
    wo_out, wg_out, gain_out,
    tok, first, wq, wk, wv, gains, kv, qs, qraw, kraw, acc, mixed, linv, cosine, sine,
    load_sem, own_sem, store_sem, unit_sem, wsend, wrecv, z_send, z_recv, x_send, x_recv,
    core_send, core_recv,
):
    shard, context, tensor = place()
    slots, length, width = tok.shape
    share = wq_ref.shape[0]
    query_width = wq.shape[1]
    key_width = wk.shape[1]
    head = head_gain_ref.shape[1]
    heads = query_width // head
    group = query_width // key_width
    half = contexts // 2
    quarter = length // 4
    score_scale = head**-0.5 * math.log2(math.e)
    core = tensor % 2
    core_peer = (shard, context, tensor + 1 - 2 * core)
    x_peer = (shard, context, (tensor + 2) % 4)
    above = (shard, jnp.minimum(context + 1, contexts - 1), tensor)
    peers = [(lax.rem(shard + d, shards), context, tensor) for d in range(1, shards)]
    barrier = greet([core_peer, x_peer, *peers])
    neighbours = greet_line(barrier, shard, context, tensor, contexts)

    load_tok = pltpu.make_async_copy(tok_ref, tok, load_sem)
    load_tok.start()
    mine = rows_of(shard, share)
    side = context % 2
    partner = (shard, context + 1 - 2 * side, tensor)
    weights = [
        (gain_ref, gains.at[:, mine]),
        (wk_ref, wk.at[mine, :]),
        (wv_ref, wv.at[mine, :]),
        (wq_ref, wq.at[mine, :]),
        (wg_ref.at[rows_of(side, share // 2), :], wg_out.at[rows_of(2 * shard + side, share // 2), :]),
        (wo_ref, wo_out.at[:, mine]),
    ]
    own = [
        pltpu.make_async_copy(source, target, own_sem.at[w])
        for w, (source, target) in enumerate(weights[:4])
    ]
    sends = [
        [
            remote(source, target, wsend.at[w, d], wrecv.at[w, d], peers[d])
            for d in range(shards - 1)
        ]
        for w, (source, target) in enumerate(weights)
    ]
    for copy in own:
        copy.start()
    pl.semaphore_wait(barrier, shards + 1 + neighbours)

    pair_copies = []
    for d in range(shards - 1):
        origin = lax.rem(shard + shards - d - 1, shards)
        rows = wg_out.at[rows_of(2 * origin + side, share // 2), :]
        pair_copies.append(remote(rows, rows, wsend.at[6, d], wrecv.at[6, d], partner))

    def send_weights(*places):
        for w in places:
            for copy in sends[w]:
                copy.start()

    def have_weights(*places):
        for w in places:
            for copy in sends[w]:
                copy.wait_recv()

    send_weights(0, 1, 2, 3, 4, 5)
    for slot in range(slots):
        for h in range(heads):
            acc[slot, h] = jnp.zeros((length, 2 * head), f32)
    load_tok.wait()
    for copy in own:
        copy.wait()
    have_weights(0)
    first_slot, short_length = slot_order(lengths_ref)
    head_gains = head_gain_ref[...].astype(f32)
    per_slot = length // TILE
    tiles = slots * per_slot

    first_gain = gains[...].astype(f32)[0:1, :]

    def norm_rows(i, _):
        slot = i // per_slot
        source = jnp.where(slot == 0, first_slot, 1 - first_slot)
        values = tok[source, rows_of(i % per_slot, TILE), :].astype(f32)
        scale = lax.rsqrt(mean_square(values) + epsilon)
        first[context, slot, rows_of(i % per_slot, TILE), :] = (
            values * scale * first_gain
        ).astype(bf16)
        return 0

    lax.fori_loop(0, tiles, norm_rows, 0)

    def part(block, slot, which):
        return first.at[block, slot, rows_of(which, quarter), :]

    def z_copy(block, slot):
        rows = part(block, slot, tensor)
        return remote(rows, rows, z_send.at[block, slot], z_recv.at[block, slot], above)

    def x_copy(block, slot):
        rows = part(block, slot, tensor)
        return remote(rows, rows, x_send.at[block, slot], x_recv.at[block, slot], x_peer)

    def core_copy(kind, block, slot):
        rows = part(block, slot, tensor if kind == 0 else (tensor + 2) % 4)
        return remote(
            rows, rows, core_send.at[kind, block, slot], core_recv.at[kind, block, slot], core_peer
        )

    def unit_copies(block, slot):
        return [
            pltpu.make_async_copy(
                source.at[block, slot], target.at[block, slot], unit_sem.at[n, block, slot]
            )
            for n, (source, target) in enumerate(
                ((first, first_out), (kv, kv_out), (kraw, kraw_out))
            )
        ]

    def go_up(block, slot):
        @pl.when(context < contexts - 1)
        def _():
            z_copy(block, slot).start()

    def stage_in(block, slot):
        z_copy(block, slot).wait_recv()
        go_up(block, slot)
        x_copy(block, slot).start()
        core_copy(0, block, slot).start()

    def stage_across(block, slot):
        x_copy(block, slot).wait_recv()
        core_copy(1, block, slot).start()

    def head_form(raw, gain, local):
        normal = raw * lax.rsqrt(mean_square(raw) + epsilon) * gain
        return normal * cosine[local, :] + pltpu.roll(normal, head // 2, 1) * sine[local, :]

    def make_keys(block, slot):
        turn(cosine, sine, start_ref, block, inside_cos_ref, inside_sin_ref)

        def rows(i, _):
            local = rows_of(i, TILE)
            values = first[block, slot, local, :]
            raw = dot_nn(values, wk[...])
            kraw[block, slot, local, :] = raw.astype(bf16)
            for g in range(key_width // head):
                columns = slice(g * head, (g + 1) * head)
                kv[block, slot, local, columns] = head_form(
                    raw[:, columns], head_gains[8:9, :], local
                ).astype(bf16)
            kv[block, slot, local, key_width:] = dot_nn(values, wv[...]).astype(bf16)
            return 0

        lax.fori_loop(0, per_slot, rows, 0)
        for copy in unit_copies(block, slot):
            copy.start()

    def stage_keys(block, slot):
        core_copy(0, block, slot).wait_recv()
        core_copy(1, block, slot).wait_recv()
        make_keys(block, slot)

    ones = jnp.ones((length, head), bf16)

    def attend(block, slot, diagonal):
        def one_head(h, _):
            columns = rows_of(h, head)
            keys = kv[block, slot, :, rows_of(h // group, head)]
            values = kv[block, slot, :, rows_of(key_width // head + h // group, head)]
            raised = jnp.exp2(dot_nt(qs[slot * length : (slot + 1) * length, columns], keys))
            spots = lax.broadcasted_iota(jnp.int32, (length, length), 1)
            if diagonal:
                lines = lax.broadcasted_iota(jnp.int32, (length, length), 0)
                raised = jnp.where(spots <= lines, raised, 0.0)
            if slot == 1:
                raised = jnp.where(spots + block * length < short_length, raised, 0.0)
            acc[slot, h] += dot_nn(
                raised.astype(bf16), jnp.concatenate([values, ones], axis=1)
            )
            return 0

        lax.fori_loop(0, heads, one_head, 0)

    units = [(r, slot) for r in range(1, contexts) for slot in range(slots)]

    def for_unit(n, action):
        if 0 <= n < len(units):
            back, slot = units[n]
            block = context - back

            @pl.when((block >= 0) if slot == 0 else ((block >= 0) & (block < half)))
            def _():
                action(block, slot)

    def for_own(action):
        action(context, 0)

        @pl.when(context < half)
        def _():
            action(context, 1)

    stores = []

    def store_all(*pairs):
        for source, target in pairs:
            copy = pltpu.make_async_copy(source, target, store_sem.at[len(stores)])
            copy.start()
            stores.append(copy)

    def make_queries():
        have_weights(3)
        store_all((wq, wq_out), (wk, wk_out), (wv, wv_out), (gains, gain_out))
        turn(cosine, sine, start_ref, context, inside_cos_ref, inside_sin_ref)

        def query_rows(i, _):
            place_rows = rows_of(i, TILE)
            local = rows_of(i % per_slot, TILE)
            raw = dot_nn(first[context, i // per_slot, local, :], wq[...])
            qraw[place_rows, :] = raw.astype(bf16)
            for h in range(heads):
                columns = slice(h * head, (h + 1) * head)
                qs[place_rows, columns] = (
                    head_form(raw[:, columns], head_gains[0:1, :], local) * score_scale
                ).astype(bf16)
            return 0

        lax.fori_loop(0, tiles, query_rows, 0)
        store_all((qs, qs_out), (qraw, qraw_out))

    def pass_on():
        have_weights(4)
        for copy in pair_copies:
            copy.start()

    def attend_own():
        for_own(lambda block, slot: attend(block, slot, True))

    actions = dict(
        i=stage_in, a=stage_across, k=stage_keys,
        t=lambda block, slot: attend(block, slot, False),
    )

    def steps(*names):
        for name in names:
            for_unit(int(name[1:]), actions[name[0]])

    for_own(go_up)
    steps("i0")
    have_weights(1, 2)
    steps("i1")
    make_keys(context, 0)
    make_keys(context, 1)
    steps("i2", "i3", "a0", "a1")
    make_queries()
    steps("a2", "k0", "i4", "a3", "k1")
    attend_own()
    steps("i5", "k2", "t0", "a4", "k3")
    pass_on()
    steps("t1", "t2", "k4", "t3", "a5", "t4")
    for n in range(6, len(units)):
        steps(f"i{n}", f"k{n - 1}", f"a{n}", f"t{n - 1}")
    steps(f"k{len(units) - 1}", f"t{len(units) - 1}")

    def finish(h, _):
        columns = rows_of(h, head)
        for slot in range(slots):
            lines = slice(slot * length, (slot + 1) * length)
            inverse = 1.0 / acc[slot, h, :, head:]
            mixed[lines, columns] = (acc[slot, h, :, :head] * inverse).astype(bf16)
            linv[lines, columns] = inverse
        return 0

    lax.fori_loop(0, heads, finish, 0)
    store_all((mixed, mixed_out), (linv, linv_out))

    def sent_up(block, slot):
        @pl.when(context < contexts - 1)
        def _():
            z_copy(block, slot).wait_send()

    def unit_done(block, slot):
        sent_up(block, slot)
        x_copy(block, slot).wait_send()
        core_copy(0, block, slot).wait_send()
        core_copy(1, block, slot).wait_send()
        for copy in unit_copies(block, slot):
            copy.wait()

    for_own(sent_up)
    for slot in range(slots):
        for copy in unit_copies(context, slot):
            copy.wait()
    for n in range(len(units)):
        for_unit(n, unit_done)
    have_weights(5)
    for copy in pair_copies:
        copy.wait_recv()
        copy.wait_send()
    for copies in sends:
        for copy in copies:
            copy.wait_send()
    for copy in stores:
        copy.wait()


def call_attention_forward(
    shards, contexts, lengths, tokens, query_weight, key_weight, value_weight, out_weight,
    gate_weight, gain_share, head_gains, tables,
):
    slots, length, width = tokens.shape
    rows = slots * length
    qw, kw, ff = query_weight.shape[1], key_weight.shape[1], gate_weight.shape[1]
    head = head_gains.shape[1]
    heads = qw // head
    n_weights = 6
    shape = jax.ShapeDtypeStruct
    dma = pltpu.SemaphoreType.DMA
    kv_shape = (contexts, slots, length, 2 * kw)
    kraw_shape = (contexts, slots, length, kw)
    first_shape = (contexts, slots, length, width)
    outs = (
        shape((rows, qw), bf16), shape(kv_shape, bf16), shape((rows, qw), bf16),
        shape((rows, qw), bf16), shape(kraw_shape, bf16), shape((rows, qw), f32),
        shape(first_shape, bf16), shape((width, qw), bf16), shape((width, kw), bf16),
        shape((width, kw), bf16), shape((qw, width), bf16), shape((width, ff), bf16),
        shape((16, width), bf16),
    )
    units = (contexts, slots)
    return pl.pallas_call(
        functools.partial(attention_forward, shards, contexts),
        out_shape=outs,
        in_specs=[SMEM] + [HBM] * 7 + [VMEM] * 4,
        out_specs=[HBM] * len(outs),
        scratch_shapes=[
            pltpu.VMEM((slots, length, width), bf16),
            pltpu.VMEM(first_shape, bf16),
            pltpu.VMEM((width, qw), bf16),
            pltpu.VMEM((width, kw), bf16),
            pltpu.VMEM((width, kw), bf16),
            pltpu.VMEM((16, width), bf16),
            pltpu.VMEM(kv_shape, bf16),
            pltpu.VMEM((rows, qw), bf16),
            pltpu.VMEM((rows, qw), bf16),
            pltpu.VMEM(kraw_shape, bf16),
            pltpu.VMEM((slots, heads, length, 2 * head), f32),
            pltpu.VMEM((rows, qw), bf16),
            pltpu.VMEM((rows, qw), f32),
            pltpu.VMEM((length, head), f32),
            pltpu.VMEM((length, head), f32),
            dma, dma((4,)), dma((8,)), dma((3, *units)),
            dma((n_weights + 1, shards - 1)), dma((n_weights + 1, shards - 1)),
            dma(units), dma(units), dma(units), dma(units), dma((2, *units)), dma((2, *units)),
        ],
        compiler_params=pltpu.CompilerParams(
            collective_id=1, has_side_effects=True, vmem_limit_bytes=60 * 2**20
        ),
        name="attention_forward",
    )(
        lengths, tokens, query_weight, key_weight, value_weight, out_weight, gate_weight,
        gain_share, head_gains, *tables,
    )


def feed_forward(
    shards, lengths_ref, mixed_ref, wo_ref, tok_ref, cot_ref, gain_ref, wg_ref, wo_own_ref,
    wg_own_ref, wu_ref, wd_ref,
    second_out, hidden_out, gback_out, uback_out, cotin_out, spart_out, mpart_out, resid_out,
    square_out, own_tok_out,
    mixed, wo, tok, cot, gains, wg, wu, wd, second, hidden, gback, uback, cotin, spart, mpart,
    resid, square, own_tok, apart, csend, crecv, xsend, xrecv, ssend, srecv, msend, mrecv, gvalue, uvalue,
    load_sem, gather_sem, store_sem, chunk_sem, wsend, wrecv, core_send, core_recv, x_send, x_recv,
):
    shard, context, tensor = place()
    slots, length, width = tok.shape
    share = wd_ref.shape[1]
    step_rows = TILE // 2
    steps = length // step_rows
    core = tensor % 2
    core_peer = (shard, context, tensor + 1 - 2 * core)
    x_peer = (shard, context, (tensor + 2) % 4)
    peers = [(lax.rem(shard + d, shards), context, tensor) for d in range(1, shards)]
    side = context % 2
    partner = (shard, context + 1 - 2 * side, tensor)
    barrier = greet([core_peer, x_peer, partner, *peers])
    loads = [
        pltpu.make_async_copy(source, target, load_sem.at[n])
        for n, (source, target) in enumerate(
            (
                (mixed_ref, mixed), (tok_ref, tok), (gain_ref, gains), (cot_ref, cot),
                (wu_ref, wu.at[rows_of(shard, share), :]),
                (wd_ref, wd.at[:, rows_of(shard, share)]),
            )
        )
    ]
    gathers = [
        gather_loads(own_ref, whole_ref, target, shard, shards, axis, gather_sem.at[n])
        for n, (own_ref, whole_ref, target, axis) in enumerate(
            (
                (wo_own_ref, wo_ref, wo, 1), (wg_own_ref, wg_ref, wg, 0),
            )
        )
    ]
    for copy in [loads[0], *gathers[0]]:
        copy.start()
    square[...] = jnp.zeros_like(square)
    pl.semaphore_wait(barrier, shards + 2)
    def piece_of(weight, ref, origin, piece):
        if weight == 0:
            size = share // 4
            return ref.at[rows_of((0 if origin is None else 4 * origin) + piece, size), :]
        rows = rows_of(piece, wd.shape[0] // 4)
        return ref.at[rows, :] if origin is None else ref.at[rows, rows_of(origin, share)]

    sends, passes = [], []
    for n in range(4):
        weight, piece = n // 2, 2 * side + n % 2
        source, target = ((wu_ref, wu), (wd_ref, wd))[weight]
        sends.append([])
        passes.append([])
        for d in range(shards - 1):
            sends[n].append(
                remote(
                    piece_of(weight, source, None, piece), piece_of(weight, target, shard, piece),
                    wsend.at[n, d], wrecv.at[n, d], peers[d],
                )
            )
            origin = lax.rem(shard + shards - d - 1, shards)
            place_at = piece_of(weight, target, origin, piece)
            passes[n].append(
                remote(place_at, place_at, wsend.at[4 + n, d], wrecv.at[4 + n, d], partner)
            )
    for copies in sends:
        for copy in copies:
            copy.start()
    for copy in [loads[0], *gathers[0]]:
        copy.wait()
    for copy in [*loads[1:], *gathers[1]]:
        copy.start()

    def mine(i):
        return rows_of(core * steps + i, step_rows)

    def theirs(i):
        return rows_of((1 - core) * steps + i, step_rows)

    def half(i):
        return rows_of(i, step_rows)

    def core_copy(kind, i, source, target):
        return remote(source, target, core_send.at[kind, i], core_recv.at[kind, i], core_peer)

    def attn_copy(i):
        return core_copy(0, i, csend.at[half(i), :], crecv.at[half(i), :])

    def second_copy(i):
        return core_copy(1, i, second.at[mine(i), :], second.at[mine(i), :])

    def spart_copy(i):
        return core_copy(2, i, ssend.at[half(i), :], srecv.at[half(i), :])

    def mpart_copy(i):
        return core_copy(3, i, msend.at[half(i), :], mrecv.at[half(i), :])

    def x_copy(i):
        return remote(
            xsend.at[half(i), :], xrecv.at[half(i), :], x_send.at[i], x_recv.at[i], x_peer
        )

    def project(i, _):
        @pl.when(i < steps)
        def _():
            both = jnp.concatenate([mixed[theirs(i), :], mixed[mine(i), :]], axis=0)
            result = dot_nn(both, wo[...])
            csend[half(i), :] = result[:step_rows].astype(bf16)
            attn_copy(i).start()
            apart[half(i), :] = result[step_rows:]

        @pl.when(i > 0)
        def _():
            before = i - 1
            attn_copy(before).wait_recv()
            total = apart[half(before), :] + crecv[half(before), :].astype(f32)
            xsend[half(before), :] = total.astype(bf16)
            x_copy(before).start()

        return 0

    lax.fori_loop(0, steps + 1, project, 0)
    for copy in [*loads[1:], *gathers[1]]:
        copy.wait()
    first_slot, short_length = slot_order(lengths_ref)
    second_gain = gains[...].astype(f32)[8:9, :]
    own_source = jnp.where(core == 0, first_slot, 1 - first_slot)

    def counted(slot, i):
        spots = context * length + i * step_rows
        lines = lax.broadcasted_iota(jnp.int32, (step_rows, width), 0) + spots
        limit = jnp.where(slot == 0, 2**30, short_length)
        return lines < limit

    def cut(slot, i):
        source = jnp.where(slot == 0, first_slot, 1 - first_slot)
        values = cot[source, half(i), :].astype(f32)
        return jnp.where(counted(slot, i), values, 0.0).astype(bf16)

    def normalise(i):
        x_copy(i).wait_recv()
        attn = xsend[half(i), :].astype(f32) + xrecv[half(i), :].astype(f32)
        attn_counted = jnp.where(counted(core, i), attn, 0.0)
        square[...] += jnp.sum(
            (attn_counted * attn_counted).reshape(step_rows // 8, 8, width), axis=0
        )
        own_tok[half(i), :] = tok[own_source, half(i), :]
        residual = own_tok[half(i), :].astype(f32) + attn
        resid[half(i), :] = residual
        scale = lax.rsqrt(mean_square(residual) + epsilon)
        second[mine(i), :] = (residual * scale * second_gain).astype(bf16)
        second_copy(i).start()
        cotin[mine(i), :] = cut(core, i)
        cotin[theirs(i), :] = cut(1 - core, i)

    def finish_parts(i):
        spart_copy(i).wait_recv()
        spart[half(i), :] = (
            spart[half(i), :].astype(f32) + srecv[half(i), :].astype(f32)
        ).astype(bf16)
        mpart_copy(i).wait_recv()
        mpart[half(i), :] = (
            mpart[half(i), :].astype(f32) + mrecv[half(i), :].astype(f32)
        ).astype(bf16)
        for copy in part_stores(i):
            copy.start()

    def gate(i):
        second_copy(i).wait_recv()
        both = jnp.concatenate([second[mine(i), :], second[theirs(i), :]], axis=0)
        gvalue[i] = dot_nn(both, wg[...])

    def up(i):
        both = jnp.concatenate([second[mine(i), :], second[theirs(i), :]], axis=0)
        up_value = dot_nn(both, wu[...])
        gate_value = gvalue[i]
        sigmoid = 1.0 / (1.0 + jnp.exp(-gate_value))
        swish = gate_value * sigmoid
        slope = sigmoid + swish * (1.0 - sigmoid)
        low = (swish * up_value).astype(bf16)
        hidden[mine(i), :] = low[:step_rows]
        hidden[theirs(i), :] = low[step_rows:]
        gvalue[i] = up_value * slope
        uvalue[i] = swish

    def backward(i):
        inward = jnp.concatenate([cotin[mine(i), :], cotin[theirs(i), :]], axis=0)
        hidden_back = dot_nt(inward, wd[...])
        gate_low = (hidden_back * gvalue[i]).astype(bf16)
        up_low = (hidden_back * uvalue[i]).astype(bf16)
        gback[mine(i), :] = gate_low[:step_rows]
        gback[theirs(i), :] = gate_low[step_rows:]
        uback[mine(i), :] = up_low[:step_rows]
        uback[theirs(i), :] = up_low[step_rows:]
        for copy in chunk_stores(i):
            copy.start()
        result = dot_nt(gate_low, wg[...]) + dot_nt(up_low, wu[...])
        ssend[half(i), :] = result[step_rows:].astype(bf16)
        spart_copy(i).start()
        spart[half(i), :] = result[:step_rows].astype(bf16)
        low = jnp.concatenate([hidden[mine(i), :], hidden[theirs(i), :]], axis=0)
        result = dot_nn(low, wd[...])
        msend[half(i), :] = result[step_rows:].astype(bf16)
        mpart_copy(i).start()
        mpart[half(i), :] = result[:step_rows].astype(bf16)

    def pass_on(n):
        for copy in sends[n]:
            copy.wait_recv()
        for copy in passes[n]:
            copy.start()

    def have(*pieces):
        for n in pieces:
            for copy in passes[n]:
                copy.wait_recv()

    def chunk_stores(i):
        rows = [(ref, out, at) for ref, out in ((gback, gback_out), (uback, uback_out)) for at in (mine(i), theirs(i))]
        return [
            pltpu.make_async_copy(ref.at[at, :], out.at[at, :], chunk_sem.at[n, i])
            for n, (ref, out, at) in enumerate(rows)
        ]

    def part_stores(i):
        return [
            pltpu.make_async_copy(ref.at[half(i), :], out.at[half(i), :], chunk_sem.at[n, i])
            for n, (ref, out) in enumerate(((spart, spart_out), (mpart, mpart_out)), 4)
        ]

    stores = []

    def store_all(*pairs):
        for source, target in pairs:
            copy = pltpu.make_async_copy(source, target, store_sem.at[len(stores)])
            copy.start()
            stores.append(copy)

    def run(action, start, stop):
        def body(i, _):
            action(i)
            return 0

        lax.fori_loop(start, stop, body, 0)

    half_steps = steps // 2
    pass_on(0)
    normalise(0)
    pass_on(1)
    gate(0)
    pass_on(2)

    def rest_of_half(i):
        normalise(i)
        gate(i)

    run(rest_of_half, 1, half_steps)
    pass_on(3)
    have(0, 1)
    up(0)
    run(rest_of_half, half_steps, steps - 1)
    run(up, 1, half_steps)
    have(2, 3)
    backward(0)
    normalise(steps - 1)
    gate(steps - 1)
    store_all((second, second_out), (cotin, cotin_out), (resid, resid_out), (square, square_out))
    store_all((own_tok, own_tok_out))
    run(up, half_steps, steps)
    store_all((hidden, hidden_out))

    def back_step(i):
        backward(i)
        finish_parts(i - 1)

    run(back_step, 1, steps)
    finish_parts(steps - 1)
    for copy in stores:
        copy.wait()

    def drain(i, _):
        for copy in (attn_copy, second_copy, spart_copy, mpart_copy, x_copy):
            copy(i).wait_send()
        for copy in [*chunk_stores(i), *part_stores(i)]:
            copy.wait()
        return 0

    lax.fori_loop(0, steps, drain, 0)
    for copies in sends + passes:
        for copy in copies:
            copy.wait_send()


def call_feed_forward(
    shards, lengths, mixed, out_whole, tokens, cotangent, gains, gate_whole, out_weight,
    gate_weight, up_weight, down_weight,
):
    slots, length, width = tokens.shape
    rows = slots * length
    qw = mixed.shape[1]
    ff = gate_weight.shape[1]
    steps = 2 * length // TILE
    shape = jax.ShapeDtypeStruct
    outs = (
        shape((rows, width), bf16), shape((rows, ff), bf16), shape((rows, ff), bf16),
        shape((rows, ff), bf16), shape((rows, width), bf16), shape((length, width), bf16),
        shape((length, width), bf16), shape((length, width), f32), shape((8, width), f32),
        shape((length, width), bf16),
    )
    half = pltpu.VMEM((length, width), bf16)
    return pl.pallas_call(
        functools.partial(feed_forward, shards),
        out_shape=outs,
        in_specs=[SMEM] + [HBM] * 10,
        out_specs=[HBM] * len(outs),
        scratch_shapes=[
            pltpu.VMEM((rows, qw), bf16),
            pltpu.VMEM((qw, width), bf16),
            pltpu.VMEM((slots, length, width), bf16),
            pltpu.VMEM((slots, length, width), bf16),
            pltpu.VMEM((16, width), bf16),
            pltpu.VMEM((width, ff), bf16),
            pltpu.VMEM((width, ff), bf16),
            pltpu.VMEM((ff, width), bf16),
            *[pltpu.VMEM(out.shape, out.dtype) for out in outs],
            pltpu.VMEM((length, width), f32),
            *[half] * 8,
            pltpu.VMEM((steps, TILE, ff), f32),
            pltpu.VMEM((steps, TILE, ff), f32),
            pltpu.SemaphoreType.DMA((6,)),
            pltpu.SemaphoreType.DMA((2, shards)),
            pltpu.SemaphoreType.DMA((6,)),
            pltpu.SemaphoreType.DMA((6, steps)),
            pltpu.SemaphoreType.DMA((8, shards - 1)),
            pltpu.SemaphoreType.DMA((8, shards - 1)),
            pltpu.SemaphoreType.DMA((4, steps)),
            pltpu.SemaphoreType.DMA((4, steps)),
            pltpu.SemaphoreType.DMA((steps,)),
            pltpu.SemaphoreType.DMA((steps,)),
        ],
        compiler_params=pltpu.CompilerParams(
            collective_id=2, has_side_effects=True, vmem_limit_bytes=56 * 2**20
        ),
        name="feed_forward",
    )(
        lengths, mixed, out_whole, tokens, cotangent, gains, gate_whole, out_weight,
        gate_weight, up_weight, down_weight,
    )


def gradient_places(contexts, steps):
    names = ["p0", "p1", "p2", *(f"res{n}" for n in range(steps)), "mixed", "m0", "out"]
    names += [*(f"m{n}" for n in range(1, contexts + 1)), "q", "qw"]
    names += [*(f"layer{n}" for n in range(steps)), "pz", *(f"first{n}" for n in range(steps + 1))]
    return [*names, *(f"tokb{n}" for n in range(steps)), "s1"]


def gradient_schedule(contexts, chunk_count, names):
    if contexts != 4 or chunk_count != 30:
        nothing = [[0] * len(names)] * contexts
        return nothing, nothing
    reduce_table = (
        (2, 3, 2, 0, 2, 0, 1, 3, 2, 0, 1, 2, 0, 0, 1, 0, 0, 2, 0, 3, 0, 0, 3, 0, 0, 1, 1, 1, 0, 0, 0),
        (1, 2, 0, 1, 2, 0, 1, 2, 0, 3, 4, 0, 0, 1, 0, 3, 0, 1, 0, 1, 0, 0, 0, 2, 0, 0, 1, 2, 3, 0, 0),
        (0, 0, 0, 0, 0, 2, 3, 2, 0, 2, 0, 3, 0, 0, 1, 1, 0, 0, 1, 0, 0, 5, 1, 3, 0, 1, 1, 1, 0, 1, 2),
        (2, 0, 0, 0, 2, 0, 2, 1, 3, 0, 3, 0, 1, 1, 0, 0, 2, 1, 0, 0, 0, 0, 0, 0, 4, 5, 0, 2, 1, 0, 0),
    )
    return_table = (
        (0, 0, 0, 1, 1, 0, 0, 1, 0, 2, 3, 1, 0, 0, 1, 1, 0, 0, 0, 0, 0, 0, 0, 2, 0, 0, 2, 2, 0, 0, 0),
        (0, 0, 0, 1, 1, 0, 2, 1, 1, 3, 3, 0, 0, 0, 0, 0, 0, 0, 1, 0, 0, 1, 1, 2, 0, 0, 0, 5, 1, 0, 3),
        (0, 0, 0, 0, 0, 0, 0, 0, 0, 0, 0, 0, 0, 0, 0, 0, 0, 0, 0, 0, 0, 0, 0, 0, 0, 0, 0, 0, 0, 0, 0),
        (0, 0, 0, 0, 0, 0, 0, 0, 0, 0, 0, 0, 0, 0, 0, 4, 0, 0, 1, 0, 0, 6, 0, 2, 0, 5, 1, 6, 0, 0, 2),
    )
    return reduce_table, return_table


def layer_backward(
    shards, contexts, lengths_ref, second_ref, gback_ref, uback_ref, cotin_ref, hidden_ref,
    spart_ref, mpart_ref, resid_ref, square_ref, mixed_ref, linv_ref, qs_ref, qraw_ref, kraw_ref,
    kv_ref, first_ref, wq_ref, wk_ref, wv_ref, wo_ref, wo_own_ref, gain_ref, own_tok_ref, head_gain_ref,
    inside_cos_ref, inside_sin_ref, start_ref,
    straight_out, turned_out, layer_out, tgrad_out, sums_out,
    second, gback, uback, cotin, hidden, spart, mpart, resid, square, dq, wq, wkv, wo, gains,
    unit_kv, unit_first, unit_kraw, unit_back, kv_grad, cosine, sine, xs, xm, outin,
    resback, part, part_core, part_x, part_z, fxrecv,
    piece, ysend, yrecv, zin, ztop, turned, sums, sums_circle, sums_line, acc_gain, acc_ff, acc_head,
    acc_square,
    load_sem, gather_sem, kv_sem, late_sem, store_sem, x_send, x_recv, core_send, core_recv, y_send, y_recv,
    g_send, z_recv, top_recv, res_send, res_recv, p_send, p_recv, s_send, s_recv,
):
    shard, context, tensor = place()
    rows, width = second.shape
    length = resid.shape[0]
    ff = gback.shape[1]
    qw, kw = wq.shape[1], wkv.shape[1] // 2
    head = head_gain_ref.shape[1]
    heads, kv_heads = qw // head, kw // head
    group = heads // kv_heads
    share = piece.shape[1]
    chunk_count, chunk = piece.shape[0], piece.shape[2]
    early = ysend.shape[1]
    half_contexts = contexts // 2
    root = contexts // 2
    turn_from, turn_to = 2 * ff // chunk, (3 * ff + qw) // chunk
    step_rows = TILE // 2
    steps = length // step_rows
    scale = head**-0.5
    core = tensor % 2
    chip = tensor // 2
    quarter = length // 4
    core_peer = (shard, context, tensor + 1 - 2 * core)
    x_peer = (shard, context, (tensor + 2) % 4)
    peers = [(lax.rem(shard + d, shards), context, tensor) for d in range(1, shards)]
    below = (shard, jnp.maximum(context - 1, 0), tensor)
    above = (shard, jnp.minimum(context + 1, contexts - 1), tensor)
    around = shards * 4
    index = shard * 4 + tensor
    places = [lax.rem(index + d, around) for d in range(1, around)]
    circle = [(at // 4, context, at % 4) for at in places]
    line = [(shard, lax.rem(context + d, contexts), tensor) for d in range(1, contexts)]
    barrier = greet([*circle, *line])

    pairs = [
        (spart_ref, spart), (second_ref, second), (gback_ref, gback), (uback_ref, uback),
        (cotin_ref, cotin), (hidden_ref, hidden), (mpart_ref, mpart), (resid_ref, resid),
        (gain_ref, gains), (linv_ref, dq), (square_ref, square), (wq_ref, wq),
        (wk_ref, wkv.at[:, :kw]), (wv_ref, wkv.at[:, kw:]),
    ]
    loads = [
        pltpu.make_async_copy(source, target, load_sem.at[n])
        for n, (source, target) in enumerate(pairs)
    ]
    loads += gather_loads(wo_own_ref, wo_ref, wo, shard, shards, 1, gather_sem)
    for copy in loads[:7]:
        copy.start()

    def mine(i):
        return rows_of(core * steps + i, step_rows)

    def theirs(i):
        return rows_of((1 - core) * steps + i, step_rows)

    def half(i):
        return rows_of(i, step_rows)

    def xs_copy(i):
        return remote(spart.at[half(i), :], xs.at[half(i), :], x_send.at[0, i], x_recv.at[0, i], x_peer)

    def xm_copy(i):
        return remote(mpart.at[half(i), :], xm.at[half(i), :], x_send.at[1, i], x_recv.at[1, i], x_peer)

    fsend, fxsend, frecv = part.at[0], part.at[1], xs

    def xf_copy(i):
        return remote(
            fxsend.at[half(i), :], fxrecv.at[half(i), :], x_send.at[2, i], x_recv.at[2, i], x_peer
        )

    def core_copy(kind, i, source, target):
        return remote(source, target, core_send.at[kind, i], core_recv.at[kind, i], core_peer)

    def outin_copy(i):
        return core_copy(0, i, outin.at[mine(i), :], outin.at[mine(i), :])

    def layer_copy(i):
        return core_copy(1, i, mpart.at[half(i), :], layer_out.at[core, half(i), :])

    def f_copy(i):
        return core_copy(2, i, fsend.at[half(i), :], frecv.at[half(i), :])

    def tgrad_copy(i):
        return core_copy(3, i, spart.at[half(i), :], tgrad_out.at[core, half(i), :])

    def layer_keep(i):
        return pltpu.make_async_copy(
            mpart.at[half(i), :], layer_out.at[core, half(i), :], store_sem.at[0, i]
        )

    def tgrad_keep(i):
        return pltpu.make_async_copy(
            spart.at[half(i), :], tgrad_out.at[core, half(i), :], store_sem.at[1, i]
        )

    def y_copy(d, k):
        return remote(
            ysend.at[d, k % early], yrecv.at[d, k], y_send.at[d, k], y_recv.at[d, k], peers[d]
        )

    def up_copy(k):
        return remote(piece.at[k], zin.at[k], g_send.at[k], z_recv.at[k], above)

    def down_copy(k):
        return remote(piece.at[k], zin.at[k], g_send.at[k], z_recv.at[k], below)

    def top_copy(k):
        return remote(piece.at[k], ztop.at[k], g_send.at[k], top_recv.at[k], below)

    def back_down_copy(k):
        return remote(zin.at[k], zin.at[k], res_send.at[0, k], res_recv.at[k], below)

    def back_up_copy(k):
        return remote(zin.at[k], zin.at[k], res_send.at[1, k], res_recv.at[k], above)

    def grad_copies(k):
        column = rows_of(jnp.where(k < turn_from, k, k - (turn_to - turn_from)), chunk)
        row = jnp.clip(k - turn_from, 0, turn_to - turn_from - 1)
        return (
            pltpu.make_async_copy(zin.at[k], straight_out.at[:, column], late_sem.at[k]),
            pltpu.make_async_copy(
                turned.at[row], turned_out.at[rows_of(row, chunk), :], late_sem.at[k]
            ),
        )

    def grad_keep(k, finish=False):
        straight_copy, turned_copy = grad_copies(k)
        aside = (k >= turn_from) & (k < turn_to)

        @pl.when(jnp.logical_not(aside))
        def _():
            straight_copy.wait() if finish else straight_copy.start()

        @pl.when(aside)
        def _():
            if not finish:
                turned[k - turn_from] = zin[k].astype(f32).T.astype(bf16)
            turned_copy.wait() if finish else turned_copy.start()

    def reduce_chunk(k):
        for d in range(shards - 1):
            y_copy(d, k).wait_recv()

        def total():
            result = piece[k].astype(f32)
            for d in range(shards - 1):
                result = result + yrecv[d, k].astype(f32)
            return result

        @pl.when((context == 0) | (context == contexts - 1))
        def _():
            piece[k] = total().astype(bf16)

        @pl.when((context > 0) & (context < root))
        def _():
            up_copy(k).wait_recv()
            piece[k] = (total() + zin[k].astype(f32)).astype(bf16)

        @pl.when((context > root) & (context < contexts - 1))
        def _():
            down_copy(k).wait_recv()
            piece[k] = (total() + zin[k].astype(f32)).astype(bf16)

        @pl.when(context < root)
        def _():
            up_copy(k).start()

        @pl.when(context == root + 1)
        def _():
            top_copy(k).start()

        @pl.when(context > root + 1)
        def _():
            down_copy(k).start()

        @pl.when(context == root)
        def _():
            up_copy(k).wait_recv()
            top_copy(k).wait_recv()
            zin[k] = (total() + zin[k].astype(f32) + ztop[k].astype(f32)).astype(bf16)
            back_down_copy(k).start()
            back_up_copy(k).start()
            grad_keep(k)

    def return_chunk(k):
        @pl.when(context < root)
        def _():
            back_down_copy(k).wait_recv()

            @pl.when(context > 0)
            def _():
                back_down_copy(k).start()

            grad_keep(k)

        @pl.when(context > root)
        def _():
            back_up_copy(k).wait_recv()

            @pl.when(context < contexts - 1)
            def _():
                back_up_copy(k).start()

            grad_keep(k)

    names = gradient_places(contexts, steps)
    reduce_table, return_table = gradient_schedule(contexts, chunk_count, names)

    def here(table, upto):
        total = 0
        for c in range(contexts):
            total += jnp.where(context == c, sum(table[c][:upto]), 0)
        return total

    def take_chunks(name):
        at = names.index(name)
        most = max(max(t[c][at] for c in range(contexts)) for t in (reduce_table, return_table))
        if most == 0:
            return
        reduced, reduced_next = here(reduce_table, at), here(reduce_table, at + 1)
        back, back_next = here(return_table, at), here(return_table, at + 1)

        def one(n, _):
            @pl.when(reduced + n < reduced_next)
            def _():
                reduce_chunk(reduced + n)

            @pl.when(back + n < back_next)
            def _():
                return_chunk(back + n)

            return 0

        lax.fori_loop(0, most, one, 0)

    def take_rest():
        reduced, back = here(reduce_table, len(names)), here(return_table, len(names))
        lag = 4 * jnp.abs(context - root)

        def give(k, _):
            @pl.when(context != root)
            def _():
                return_chunk(k)

            return 0

        def take(k, _):
            reduce_chunk(k)

            @pl.when((k - lag >= back) & (context != root))
            def _():
                return_chunk(k - lag)

            return 0

        lax.fori_loop(back, jnp.maximum(back, reduced - lag), give, 0)
        lax.fori_loop(reduced, chunk_count, take, 0)
        lax.fori_loop(jnp.maximum(back, chunk_count - lag), chunk_count, give, 0)

    def weight_grad(left, right, columns, first_chunk, count):
        for d in range(shards - 1):
            theirs_at = rows_of(lax.rem(shard + d + 1, shards), share)
            result = dot_tn(left[:, theirs_at], right[:, columns : columns + count * chunk])
            for n in range(count):
                k = first_chunk + n
                if k >= early:
                    y_copy(d, k - early).wait_send()
                ysend[d, k % early] = result[:, n * chunk : (n + 1) * chunk].astype(bf16)
                y_copy(d, k).start()
        result = dot_tn(left[:, rows_of(shard, share)], right[:, columns : columns + count * chunk])
        for n in range(count):
            piece[first_chunk + n] = result[:, n * chunk : (n + 1) * chunk].astype(bf16)

    def part_at(slot, block):
        return block if slot == 0 else contexts - 1 + block

    def part_core_copy(slot, block):
        at = part_at(slot, block)
        return remote(
            part.at[slot, pl.ds(0, length // 2), :], part_core.at[at], p_send.at[0, at],
            p_recv.at[0, at], core_peer,
        )

    def part_x_copy(slot, block):
        at = part_at(slot, block)
        return remote(
            part_core.at[at, rows_of(1 - chip, quarter), :], part_x.at[at], p_send.at[1, at],
            p_recv.at[1, at], x_peer,
        )

    def part_z_copy(slot, block):
        at = part_at(slot, block)
        return remote(part_x.at[at], part_z.at[at], p_send.at[2, at], p_recv.at[2, at], below)

    def part_make(slot, block):
        for pair in range(2):
            rows_at = slice(2 * pair * quarter, 2 * (pair + 1) * quarter)
            result = dot_nt(unit_back[rows_at, :], wkv[...]).astype(bf16)
            for side in range(2):
                place_at = jnp.where(core == side, 2, 0) + pair
                part[slot, rows_of(place_at, quarter), :] = result[
                    side * quarter : (side + 1) * quarter
                ]
        part_core_copy(slot, block).start()

    def part_across(slot, block):
        part_core_copy(slot, block).wait_recv()
        at = part_at(slot, block)
        total = part[slot, length // 2 :, :].astype(f32) + part_core[at].astype(f32)
        part_core[at] = total.astype(bf16)
        part_x_copy(slot, block).start()
        part_core_copy(slot, block).wait_send()

    def part_down(slot, block, count):
        part_x_copy(slot, block).wait_recv()
        at = part_at(slot, block)
        total = part_core[at, rows_of(chip, quarter), :].astype(f32) + part_x[at].astype(f32)

        @pl.when(context == count - 1)
        def _():
            part_x[at] = total.astype(bf16)

        @pl.when(context < count - 1)
        def _():
            part_z_copy(slot, block).wait_recv()
            part_x[at] = (total + part_z[at].astype(f32)).astype(bf16)

        part_z_copy(slot, block).start()

    def unit_place(slot, block):
        return jnp.where(context < half_contexts, slot, block % 2)

    def unit_loads(slot, block):
        at = unit_place(slot, block)
        return [
            pltpu.make_async_copy(source.at[block, slot], target.at[at], kv_sem.at[n, at])
            for n, (source, target) in enumerate(
                ((kv_ref, unit_kv), (first_ref, unit_first), (kraw_ref, unit_kraw))
            )
        ]

    def start_unit(slot, block):
        for copy in unit_loads(slot, block):
            copy.start()

    acc_gain[...] = jnp.zeros_like(acc_gain)
    acc_ff[...] = jnp.zeros_like(acc_ff)
    acc_head[...] = jnp.zeros_like(acc_head)
    acc_square[...] = jnp.zeros_like(acc_square)
    loads[0].wait()
    pl.semaphore_wait(barrier, around + contexts - 2)
    alive = (context < half_contexts) | (core == 0)

    @pl.when(alive)
    def _():
        for i in range(steps):
            xs_copy(i).start()

    for n in range(1, 3):
        loads[n].wait()
    gate_chunks = ff // chunk
    out_chunks = qw // chunk
    query_chunk = 3 * gate_chunks + out_chunks
    weight_grad(second, gback, 0, 0, gate_chunks)
    take_chunks("p0")
    loads[3].wait()
    weight_grad(second, uback, 0, gate_chunks, gate_chunks)
    take_chunks("p1")
    for n in range(4, 7):
        loads[n].wait()
    for copy in loads[7:]:
        copy.start()
    for i in range(steps):
        xm_copy(i).start()
    weight_grad(cotin, hidden, 0, 2 * gate_chunks, gate_chunks)
    take_chunks("p2")
    for n in range(7, len(loads)):
        loads[n].wait()
    both_gains = gains[...].astype(f32)
    head_gains = head_gain_ref[...].astype(f32)
    qs, qraw, mixed = hidden.at[:, :qw], gback.at[:, :qw], uback.at[:, :qw]
    own_kback, own_vback = gback.at[:, qw : qw + kw], uback.at[:, qw : qw + kw]
    next_pairs = [(qs_ref, qs), (qraw_ref, qraw), (mixed_ref, mixed)]
    next_loads = [
        pltpu.make_async_copy(source, target, load_sem.at[n])
        for n, (source, target) in enumerate(next_pairs)
    ]
    for copy in next_loads:
        copy.start()
    start_unit(0, 0)

    def fold(values):
        return jnp.sum(values.reshape(values.shape[0] // 8, 8, values.shape[1]), axis=0)

    def norm_back(values, back, gain):
        inverse = lax.rsqrt(mean_square(values) + epsilon)
        normal = values * inverse
        scaled = back * gain
        inward = inverse * (scaled - normal * jnp.mean(normal * scaled, axis=-1, keepdims=True))
        return inward, back * normal

    def residual_step(i, _):
        @pl.when(alive)
        def _():
            xs_copy(i).wait_recv()

        back = spart[half(i), :].astype(f32)
        back += jnp.where(alive, xs[half(i), :].astype(f32), 0.0)
        inward, terms = norm_back(resid[half(i), :], back, both_gains[8:9, :])
        acc_ff[...] += fold(terms)
        total = cotin[mine(i), :].astype(f32) + inward
        resback[half(i), :] = total
        outin[mine(i), :] = total.astype(bf16)
        outin_copy(i).start()
        return 0

    for i in range(steps):
        residual_step(i, 0)
        take_chunks(f"res{i}")
    for i in range(steps):
        outin_copy(i).wait_recv()
    first = cotin
    first_loads = [
        pltpu.make_async_copy(
            first_ref.at[context, slot], first.at[slot * length : (slot + 1) * length, :],
            gather_sem.at[slot],
        )
        for slot in range(2)
    ]
    for copy in first_loads:
        copy.start()
    for copy in next_loads:
        copy.wait()
    dox = second

    def mixed_step(i, _):
        at = rows_of(i, TILE)
        back = dot_nt(outin[at, :], wo[...]).astype(bf16).astype(f32)
        lanes = lax.broadcasted_iota(jnp.int32, (TILE, head), 1)
        for h in range(heads):
            columns = slice(h * head, (h + 1) * head)
            low = (back[:, columns] * dq[at, columns]).astype(bf16)
            centre = jnp.sum(
                low.astype(f32) * mixed[at, columns].astype(f32), axis=-1, keepdims=True
            )
            high = centre.astype(bf16).astype(f32)
            extra = jnp.where(lanes == 0, -high, jnp.where(lanes == 1, high - centre, 0.0))
            dox[at, 2 * h * head : (2 * h + 1) * head] = low
            dox[at, (2 * h + 1) * head : (2 * h + 2) * head] = extra.astype(bf16)
        dq[at, :] = jnp.zeros((TILE, qw), f32)
        return 0

    lax.fori_loop(0, rows // TILE, mixed_step, 0)
    take_chunks("mixed")
    ones = jnp.ones((length, head), bf16)

    def head_back(raw, back, gain, local):
        turned_back = back * cosine[local, :] - pltpu.roll(back, head // 2, 1) * sine[local, :]
        return norm_back(raw.astype(f32), turned_back, gain)

    kv_grad[...] = jnp.zeros_like(kv_grad)

    @pl.when(context >= half_contexts)
    def _():
        own_kback[length:, :] = jnp.zeros((length, kw), bf16)
        own_vback[length:, :] = jnp.zeros((length, kw), bf16)

    def block_back(slot, block, diagonal):
        lines = slice(slot * length, (slot + 1) * length)
        buffer = unit_place(slot, block)
        if diagonal:
            key_spots = lax.broadcasted_iota(jnp.int32, (length, length), 0)
            query_spots = lax.broadcasted_iota(jnp.int32, (length, length), 1)
            counted = key_spots <= query_spots

        def one_group(g, _):
            keys = unit_kv[buffer, :, rows_of(g, head)]
            values = unit_kv[buffer, :, rows_of(kv_heads + g, head)]
            widened = jnp.concatenate([values, ones], axis=1)
            key_back = jnp.zeros((length, head), f32)
            value_back = jnp.zeros((length, head), f32)
            for member in range(group):
                h = g * group + member
                columns = rows_of(h, head)
                queries = qs[lines, columns]
                inward = dox[lines, rows_of(h, 2 * head)]
                raised = jnp.exp2(dot_nt(keys, queries))
                if diagonal:
                    raised = jnp.where(counted, raised, 0.0)
                scores_back = (raised * dot_nt(widened, inward)).astype(bf16)
                value_back += dot_nn(raised.astype(bf16), inward[:, :head])
                key_back += dot_nn(scores_back, queries)
                dq[lines, columns] += dot_tn(scores_back, keys)
            raw_back, terms = head_back(
                unit_kraw[buffer, :, rows_of(g, head)], key_back * math.log(2.0),
                head_gains[8:9, :], slice(None),
            )
            acc_head[1] += fold(terms)
            unit_back[:, rows_of(g, head)] = raw_back.astype(bf16)
            unit_back[:, rows_of(kv_heads + g, head)] = value_back.astype(bf16)
            return 0

        lax.fori_loop(0, kv_heads, one_group, 0)

        def grad_rows(n, _):
            at = rows_of(n, TILE)
            kv_grad[at, :] += dot_tn(unit_first[buffer, :, at], unit_back[...])
            return 0

        lax.fori_loop(0, width // TILE, grad_rows, 0)
        if diagonal:
            own_kback[lines, :] = unit_back[:, :kw]
            own_vback[lines, :] = unit_back[:, kw:]

    def next_units(slot, block):
        if slot == 0 and block < half_contexts:

            @pl.when(context < half_contexts)
            def _():
                start_unit(1, block)

        if block + 1 < contexts:
            more = block + 1 <= context
            if slot == 0:
                more = more & (context >= half_contexts)

            @pl.when(more)
            def _():
                start_unit(0, block + 1)

    for turn_at in range(contexts + 1):
        block, before = turn_at, turn_at - 1
        if block < contexts:
            turn(cosine, sine, start_ref, block, inside_cos_ref, inside_sin_ref)
        for slot, count in ((0, contexts), (1, half_contexts)):
            within = context < count
            if block < count:

                @pl.when((block <= context) & within)
                def _():
                    for copy in unit_loads(slot, block):
                        copy.wait()
                    next_units(slot, block)

                @pl.when((block == context) & within)
                def _():
                    block_back(slot, block, True)

                @pl.when((block < context) & within)
                def _():
                    block_back(slot, block, False)

            if 0 <= before < count - 1:

                @pl.when((before < context) & within)
                def _():
                    part_across(slot, before)

            if block < count - 1:

                @pl.when((block < context) & within)
                def _():
                    part_make(slot, block)

            gone = turn_at - 2 - (count - 1 - context)

            @pl.when((gone >= 0) & (gone < context) & within)
            def _():
                part_down(slot, gone, count)

        take_chunks(f"m{turn_at}")
        if turn_at == 0:
            weight_grad(outin, mixed, 0, 3 * gate_chunks, out_chunks)
            take_chunks("out")
    for copy in first_loads:
        copy.wait()
    turn(cosine, sine, start_ref, context, inside_cos_ref, inside_sin_ref)

    def query_step(i, _):
        at = rows_of(i, TILE)
        local = rows_of(i % (length // TILE), TILE)
        for h in range(heads):
            columns = slice(h * head, (h + 1) * head)
            inward, terms = head_back(
                qraw[at, columns], dq[at, columns] * scale, head_gains[0:1, :], local
            )
            acc_head[0] += fold(terms)
            qraw[at, columns] = inward.astype(bf16)
        return 0

    lax.fori_loop(0, rows // TILE, query_step, 0)
    take_chunks("q")
    weight_grad(first, qraw, 0, query_chunk, out_chunks)
    key_chunk = query_chunk + out_chunks
    for n in range(2 * kw // chunk):
        k = key_chunk + n
        columns = slice(n * chunk, (n + 1) * chunk)
        for d in range(shards - 1):
            theirs_at = rows_of(lax.rem(shard + d + 1, shards), share)
            y_copy(d, k - early).wait_send()
            ysend[d, k % early] = kv_grad[theirs_at, columns].astype(bf16)
            y_copy(d, k).start()
        piece[k] = kv_grad[rows_of(shard, share), columns].astype(bf16)
    take_chunks("qw")
    _, short_length = slot_order(lengths_ref)

    @pl.when(alive)
    def _():
        for i in range(steps):
            xs_copy(i).wait_send()

    tok_load = pltpu.make_async_copy(own_tok_ref, spart, load_sem.at[0])
    tok_load.start()

    def layer_step(i, _):
        xm_copy(i).wait_recv()
        xm_copy(i).wait_send()
        mlp = mpart[half(i), :].astype(f32) + xm[half(i), :].astype(f32)
        layer = resid[half(i), :] + mlp
        mpart[half(i), :] = layer.astype(bf16)
        layer_copy(i).start()
        layer_keep(i).start()
        lines = lax.broadcasted_iota(jnp.int32, (step_rows, width), 0)
        limit = jnp.where(core == 0, 2**30, short_length)
        counted = lines + (context * length + i * step_rows) < limit
        acc_square[0] += fold(jnp.where(counted, layer * layer, 0.0))
        acc_square[1] += fold(jnp.where(counted, mlp * mlp, 0.0))
        return 0

    for i in range(steps):
        layer_step(i, 0)
        take_chunks(f"layer{i}")

    @pl.when(context < contexts - 1)
    def _():
        part_z_copy(0, jnp.minimum(context, contexts - 2)).wait_recv()

    @pl.when(context < half_contexts - 1)
    def _():
        part_z_copy(1, jnp.minimum(context, max(half_contexts - 2, 0))).wait_recv()

    take_chunks("pz")
    fown = resid

    def first_step(i, _):
        if i < steps:
            both = lambda ref: jnp.concatenate([ref[theirs(i), :], ref[mine(i), :]], axis=0)
            result = dot_nt(both(qraw), wq[...])
            result += dot_nt(both(own_kback), wkv[:, :kw])
            result += dot_nt(both(own_vback), wkv[:, kw:])

            def from_above(slot):
                at = jnp.where(
                    slot == 0,
                    jnp.minimum(context, contexts - 2),
                    contexts - 1 + jnp.minimum(context, max(half_contexts - 2, 0)),
                )
                last = jnp.where(slot == 0, contexts - 1, half_contexts - 1)
                come = (i == tensor) & (context < last)
                return jnp.where(come, part_z[at].astype(f32), 0.0)

            fsend[half(i), :] = (result[:step_rows] + from_above(1 - core)).astype(bf16)
            f_copy(i).start()
            fown[half(i), :] = result[step_rows:] + from_above(core)

        if i > 0:
            before = i - 1
            f_copy(before).wait_recv()
            total = fown[half(before), :] + frecv[half(before), :].astype(f32)
            fxsend[half(before), :] = total.astype(bf16)

            @pl.when(alive)
            def _():
                xf_copy(before).start()

        return 0

    for i in range(steps + 1):
        first_step(i, 0)
        take_chunks(f"first{i}")
    tok_load.wait()

    def tokens_step(i, _):
        @pl.when(alive)
        def _():
            xf_copy(i).wait_recv()

        back = fxsend[half(i), :].astype(f32)
        back += jnp.where(alive, fxrecv[half(i), :].astype(f32), 0.0)
        inward, terms = norm_back(spart[half(i), :].astype(f32), back, both_gains[0:1, :])
        acc_gain[...] += fold(terms)
        spart[half(i), :] = (resback[half(i), :] + inward).astype(bf16)
        tgrad_copy(i).start()
        tgrad_keep(i).start()
        return 0

    for i in range(steps):
        take_chunks(f"tokb{i}")
        tokens_step(i, 0)

    def total_of(values):
        return jnp.sum(jnp.sum(values, axis=0, keepdims=True), axis=1, keepdims=True)

    lanes = lax.broadcasted_iota(jnp.int32, (1, 128), 1)
    base = (shard * 2 + core) * 4
    squares = jnp.where(lanes == base, total_of(acc_square[0]), 0.0)
    squares += jnp.where(lanes == base + 1, total_of(square[...]), 0.0)
    squares += jnp.where(lanes == base + 2, total_of(acc_square[1]), 0.0)
    gain_row = 0.5 * jnp.sum(acc_gain[...], axis=0, keepdims=True)
    ff_row = 0.5 * jnp.sum(acc_ff[...], axis=0, keepdims=True)
    folds = width // 128
    sums[...] = jnp.zeros_like(sums)
    for n in range(folds):
        columns = slice(n * 128, (n + 1) * 128)
        sums[0, n : n + 1, :] = gain_row[:, columns]
        sums[0, folds + n : folds + n + 1, :] = ff_row[:, columns]
    sums[0, 2 * folds : 2 * folds + 1, :] = jnp.sum(acc_head[0], axis=0, keepdims=True)
    sums[0, 2 * folds + 1 : 2 * folds + 2, :] = jnp.sum(acc_head[1], axis=0, keepdims=True)
    sums[0, 2 * folds + 2 : 2 * folds + 3, :] = 0.5 * squares
    circle_hops = [
        remote(sums.at[0], sums_circle.at[index], s_send.at[d], s_recv.at[d], device)
        for d, device in enumerate(circle)
    ]
    for copy in circle_hops:
        copy.start()
    sums_circle[index] = sums[0]
    take_chunks("s1")
    for copy in circle_hops:
        copy.wait_recv()
    total = sums_circle[0]
    for n in range(1, around):
        total = total + sums_circle[n]
    sums[1] = total
    line_hops = [
        remote(
            sums.at[1], sums_line.at[context], s_send.at[around + d], s_recv.at[around + d], device
        )
        for d, device in enumerate(line)
    ]
    for copy in line_hops:
        copy.start()
    sums_line[context] = total

    take_rest()
    for copy in line_hops:
        copy.wait_recv()
    total = sums_line[0]
    for n in range(1, contexts):
        total = total + sums_line[n]
    sums[2] = total
    sums_keep = pltpu.make_async_copy(sums.at[2], sums_out, store_sem.at[2, 0])
    sums_keep.start()
    for copy in [*circle_hops, *line_hops]:
        copy.wait_send()

    def drain_steps(i, _):
        for copy in (outin_copy, layer_copy, f_copy, tgrad_copy):
            copy(i).wait_send()
        layer_copy(i).wait_recv()
        tgrad_copy(i).wait_recv()

        @pl.when(alive)
        def _():
            xf_copy(i).wait_send()

        layer_keep(i).wait()
        tgrad_keep(i).wait()
        return 0

    lax.fori_loop(0, steps, drain_steps, 0)

    def drain_chunks(k, _):
        @pl.when(k >= chunk_count - early)
        def _():
            for d in range(shards - 1):
                y_copy(d, k).wait_send()

        @pl.when(context != root)
        def _():
            up_copy(k).wait_send()

        @pl.when((context <= root) & (context > 0))
        def _():
            back_down_copy(k).wait_send()

        @pl.when((context >= root) & (context < contexts - 1))
        def _():
            back_up_copy(k).wait_send()

        grad_keep(k, finish=True)
        return 0

    lax.fori_loop(0, chunk_count, drain_chunks, 0)
    for block in range(contexts - 1):
        for slot, count in ((0, contexts), (1, half_contexts)):
            if block < count - 1:

                @pl.when((block < context) & (context < count))
                def _():
                    part_x_copy(slot, block).wait_send()
                    part_z_copy(slot, block).wait_send()

    sums_keep.wait()


def call_layer_backward(shards, contexts, lengths, parts):
    (
        second, gback, uback, cotin, hidden, spart, mpart, resid, square, mixed, linv, qs, qraw,
        kraw, kv, first, wq, wk, wv, wo, out_weight, gains, own_tok, head_gains, *tables,
    ) = parts
    rows, width = second.shape
    length = resid.shape[0]
    ff, qw, kw = gback.shape[1], wq.shape[1], wk.shape[1]
    share = width // shards
    chunk = TILE // 2
    sum_rows = 2 * width // 128 + 8
    chunk_count = (3 * ff + 2 * qw + 2 * kw) // chunk
    early = 3 * ff // chunk
    steps = 2 * length // TILE
    units = contexts - 1 + max(contexts // 2 - 1, 1)
    head = head_gains.shape[1]
    slots = rows // length
    shape = jax.ShapeDtypeStruct
    outs = (
        shape((share, 2 * ff + qw + 2 * kw), bf16), shape((ff + qw, share), bf16),
        shape((slots, length, width), bf16), shape((slots, length, width), bf16),
        shape((sum_rows, 128), f32),
    )
    dma = pltpu.SemaphoreType.DMA

    def like(array):
        return pltpu.VMEM(array.shape, array.dtype)

    half = pltpu.VMEM((length, width), bf16)
    chunks = pltpu.VMEM((chunk_count, share, chunk), bf16)
    return pl.pallas_call(
        functools.partial(layer_backward, shards, contexts),
        out_shape=outs,
        in_specs=[SMEM] + [HBM] * 23 + [VMEM] * 4,
        out_specs=[HBM] * len(outs),
        scratch_shapes=[
            like(second), like(gback), like(uback), like(cotin), like(hidden), like(spart),
            like(mpart), like(resid), like(square), like(linv), like(wq),
            pltpu.VMEM((width, 2 * kw), bf16), like(wo), like(gains),
            pltpu.VMEM((2, length, 2 * kw), bf16), pltpu.VMEM((2, length, width), bf16),
            pltpu.VMEM((2, length, kw), bf16), pltpu.VMEM((length, 2 * kw), bf16),
            pltpu.VMEM((width, 2 * kw), f32),
            pltpu.VMEM((length, head), f32), pltpu.VMEM((length, head), f32),
            half, half, pltpu.VMEM((rows, width), bf16), pltpu.VMEM((length, width), f32),
            pltpu.VMEM((2, length, width), bf16),
            pltpu.VMEM((units, length // 2, width), bf16),
            pltpu.VMEM((units, length // 4, width), bf16),
            pltpu.VMEM((units, length // 4, width), bf16),
            half,
            chunks,
            pltpu.VMEM((shards - 1, early, share, chunk), bf16),
            pltpu.VMEM((shards - 1, chunk_count, share, chunk), bf16),
            chunks, chunks, pltpu.VMEM(((ff + qw) // chunk, chunk, share), bf16),
            pltpu.VMEM((3, sum_rows, 128), f32), pltpu.VMEM((4 * shards, sum_rows, 128), f32),
            pltpu.VMEM((contexts, sum_rows, 128), f32),
            pltpu.VMEM((8, width), f32), pltpu.VMEM((8, width), f32),
            pltpu.VMEM((2, 8, head), f32), pltpu.VMEM((2, 8, width), f32),
            dma((15,)), dma((shards,)), dma((3, 2)), dma((chunk_count,)), dma((3, steps)),
            dma((3, steps)), dma((3, steps)), dma((4, steps)), dma((4, steps)),
            dma((shards - 1, chunk_count)), dma((shards - 1, chunk_count)),
            dma((chunk_count,)), dma((chunk_count,)), dma((chunk_count,)),
            dma((2, chunk_count)), dma((chunk_count,)), dma((3, units)), dma((3, units)),
            dma((4 * shards + contexts,)), dma((4 * shards + contexts,)),
        ],
        compiler_params=pltpu.CompilerParams(
            collective_id=3, has_side_effects=True, vmem_limit_bytes=63 * 2**20
        ),
        name="layer_backward",
    )(lengths, *parts)


def local(
    tokens, lengths, cotangent, query_weight, key_weight, value_weight, out_weight, gate_weight,
    up_weight, down_weight, attention_gain, feedforward_gain, query_gain, key_gain,
):
    slots, length, width = tokens.shape
    shards, contexts = lax.axis_size("shard"), lax.axis_size("context")
    shard, context, _ = place()
    head = query_gain.shape[0]
    ff, qw, kw = gate_weight.shape[1], query_weight.shape[1], key_weight.shape[1]
    tables = [jnp.asarray(table) for table in rope_tables(length, contexts, head)]

    def packed(one, other):
        upper = lax.broadcasted_iota(jnp.int32, (16, one.shape[0]), 0) < 8
        return jnp.where(upper, one[None], other[None])

    gain_share = packed(attention_gain, feedforward_gain)
    head_gains = packed(query_gain, key_gain)
    (mixed, kv, qs, qraw, kraw, linv, first, wq, wk, wv, wo, wg, gains) = (
        call_attention_forward(
            shards, contexts, lengths, tokens, query_weight, key_weight, value_weight, out_weight,
            gate_weight, gain_share, head_gains, tables,
        )
    )
    (second, hidden, gback, uback, cotin, spart, mpart, resid, square, own_tok) = (
        call_feed_forward(
            shards, lengths, mixed, wo, tokens, cotangent, gains, wg, out_weight, gate_weight,
            up_weight, down_weight,
        )
    )
    straight, turned, layer, token_grads, sums = call_layer_backward(
        shards, contexts, lengths,
        (
            second, gback, uback, cotin, hidden, spart, mpart, resid, square, mixed, linv, qs,
            qraw, kraw, kv, first, wq, wk, wv, wo, out_weight, gains, own_tok, head_gains, *tables,
        ),
    )
    swapped = lengths[1] > lengths[0]

    def in_place(values):
        return jnp.where(swapped, values[::-1], values)

    ends = np.cumsum([ff, ff, qw, kw])
    gate_grad, up_grad, query_grad, key_grad, value_grad = (
        part.astype(f32) for part in jnp.split(straight, ends, axis=1)
    )
    down_grad, out_grad = (part.astype(f32) for part in jnp.split(turned, [ff], axis=0))
    folds = width // 128
    gain_grads = [
        lax.dynamic_slice_in_dim(
            sums[n * folds : (n + 1) * folds].reshape(width), shard * (width // shards),
            width // shards, 0,
        )
        for n in range(2)
    ]
    query_gain_grad, key_gain_grad, squares = sums[2 * folds : 2 * folds + 3]
    squares = lax.dynamic_slice_in_dim(squares, shard * slots * 4, slots * 4, 0)
    squares = in_place(squares.reshape(slots, 4)[:, :3])
    return (
        in_place(layer),
        in_place(token_grads.astype(f32)),
        query_grad,
        key_grad,
        value_grad,
        out_grad,
        gate_grad,
        up_grad,
        down_grad,
        gain_grads[0],
        gain_grads[1],
        query_gain_grad,
        key_gain_grad,
        jnp.sqrt(squares / (lengths.astype(f32)[:, None] * width)),
    )


def solution(mesh):
    placed = (
        P("shard", "context", None),
        P("shard"),
        P("shard", "context", None),
        P("shard", "tensor"),
        P("shard", "tensor"),
        P("shard", "tensor"),
        P("tensor", "shard"),
        P("shard", "tensor"),
        P("shard", "tensor"),
        P("tensor", "shard"),
        P("shard"),
        P("shard"),
        P(),
        P(),
    )
    return jax.shard_map(
        local,
        mesh=mesh,
        in_specs=placed,
        out_specs=(
            P("shard", "context", None),
            P("shard", "context", None),
            P("shard", "tensor"),
            P("shard", "tensor"),
            P("shard", "tensor"),
            P("tensor", "shard"),
            P("shard", "tensor"),
            P("shard", "tensor"),
            P("tensor", "shard"),
            P("shard"),
            P("shard"),
            P(),
            P(),
            P("shard", None),
        ),
        check_vma=False,
    )
```

```python
import functools
import math

import jax
import jax.numpy as jnp
import numpy as np
from jax import lax
from jax.experimental import pallas as pl
from jax.experimental.pallas import tpu as pltpu
from jax.sharding import PartitionSpec as P

epsilon = 1e-06
rope_base = 1000000.0
MESH = pl.DeviceIdType.MESH
f32 = jnp.float32
bf16 = jnp.bfloat16
HBM = pl.BlockSpec(memory_space=pl.ANY)
VMEM = pl.BlockSpec(memory_space=pltpu.VMEM)
SMEM = pl.BlockSpec(memory_space=pltpu.SMEM)
TILE = 256
CHUNK = 128
GIVEN = 3


def rows_of(index, size):
    if isinstance(index, int):
        return pl.ds(index * size, size)
    return pl.ds(pl.multiple_of(index * size, size), size)


def dot_nt(left, right):
    return lax.dot_general(left, right, (((1,), (1,)), ((), ())), preferred_element_type=f32)


def dot_tn(left, right):
    return lax.dot_general(left, right, (((0,), (0,)), ((), ())), preferred_element_type=f32)


def dot_nn(left, right):
    return jnp.dot(left, right, preferred_element_type=f32)


def mean_square(values):
    return jnp.mean(values * values, axis=-1, keepdims=True)


def place():
    return lax.axis_index("shard"), lax.axis_index("context"), lax.axis_index("tensor")


def greet(devices, extra=0):
    barrier = pltpu.get_barrier_semaphore()
    for device in devices:
        pl.semaphore_signal(barrier, inc=1, device_id=device, device_id_type=MESH)
    return barrier


def greet_line(barrier, shard, context, tensor, count):
    @pl.when(context > 0)
    def _():
        pl.semaphore_signal(
            barrier, inc=1, device_id=(shard, context - 1, tensor), device_id_type=MESH
        )

    @pl.when(context < count - 1)
    def _():
        pl.semaphore_signal(
            barrier, inc=1, device_id=(shard, context + 1, tensor), device_id_type=MESH
        )

    return jnp.minimum(context, 1) + jnp.minimum(count - 1 - context, 1)


def turn(cosine, sine, start_ref, block, inside_cos_ref, inside_sin_ref):
    head = cosine.shape[1]
    start_cos, start_sin = start_ref[block, 0:1, :], start_ref[block, 8:9, :]
    signs = jnp.where(lax.broadcasted_iota(jnp.int32, (1, head), 1) < head // 2, -1.0, 1.0)
    inside_cos, inside_sin = inside_cos_ref[...], inside_sin_ref[...]
    cosine[...] = start_cos * inside_cos - start_sin * inside_sin
    sine[...] = signs * (start_sin * inside_cos + start_cos * inside_sin)


def slot_order(lengths_ref):
    one, other = lengths_ref[0], lengths_ref[1]
    return jnp.where(other > one, 1, 0), jnp.minimum(one, other)


def gather_loads(share_ref, whole_ref, target, shard, shards, axis, sems):
    size = share_ref.shape[axis]
    copies = []
    for d in range(shards):
        at = rows_of(lax.rem(shard + d, shards), size)
        index = (slice(None), at) if axis == 1 else (at, slice(None))
        source = share_ref if d == 0 else whole_ref.at[index]
        copies.append(pltpu.make_async_copy(source, target.at[index], sems.at[d]))
    return copies


def remote(src, dst, send_sem, recv_sem, device):
    return pltpu.make_async_remote_copy(
        src_ref=src,
        dst_ref=dst,
        send_sem=send_sem,
        recv_sem=recv_sem,
        device_id=device,
        device_id_type=MESH,
    )


def rope_tables(length, contexts, head_size):
    half = head_size // 2
    speeds = np.tile(rope_base ** (-np.arange(half, dtype=np.float64) * 2.0 / head_size), 2)
    inside = np.arange(length, dtype=np.float64)[:, None] * speeds
    starts = np.arange(contexts, dtype=np.float64)[:, None] * length * speeds
    rows = np.stack([np.cos(starts), np.sin(starts)], axis=1)
    rows = np.repeat(rows, 8, axis=1)
    return (
        np.cos(inside).astype(np.float32),
        np.sin(inside).astype(np.float32),
        rows.astype(np.float32),
    )


def attention_forward(
    shards, contexts, lengths_ref, tok_ref, wq_ref, wk_ref, wv_ref, wo_ref, wg_ref, gain_ref,
    head_gain_ref, inside_cos_ref, inside_sin_ref, start_ref,
    mixed_out, kv_out, qs_out, qraw_out, kraw_out, linv_out, first_out, wq_out, wk_out, wv_out,
    wo_out, wg_out, gain_out,
    tok, first, wq, wk, wv, gains, kv, qs, qraw, kraw, acc, mixed, linv, cosine, sine,
    load_sem, own_sem, store_sem, unit_sem, wsend, wrecv, z_send, z_recv, x_send, x_recv,
    core_send, core_recv,
):
    shard, context, tensor = place()
    slots, length, width = tok.shape
    share = wq_ref.shape[0]
    query_width = wq.shape[1]
    key_width = wk.shape[1]
    head = head_gain_ref.shape[1]
    heads = query_width // head
    group = query_width // key_width
    half = contexts // 2
    quarter = length // 4
    score_scale = head**-0.5 * math.log2(math.e)
    core = tensor % 2
    core_peer = (shard, context, tensor + 1 - 2 * core)
    x_peer = (shard, context, (tensor + 2) % 4)
    above = (shard, jnp.minimum(context + 1, contexts - 1), tensor)
    peers = [(lax.rem(shard + d, shards), context, tensor) for d in range(1, shards)]
    barrier = greet([core_peer, x_peer, *peers])
    neighbours = greet_line(barrier, shard, context, tensor, contexts)

    load_tok = pltpu.make_async_copy(tok_ref, tok, load_sem)
    load_tok.start()
    mine = rows_of(shard, share)
    side = context % 2
    partner = (shard, context + 1 - 2 * side, tensor)
    weights = [
        (gain_ref, gains.at[:, mine]),
        (wk_ref, wk.at[mine, :]),
        (wv_ref, wv.at[mine, :]),
        (wq_ref, wq.at[mine, :]),
        (wg_ref.at[rows_of(side, share // 2), :], wg_out.at[rows_of(2 * shard + side, share // 2), :]),
        (wo_ref, wo_out.at[:, mine]),
    ]
    own = [
        pltpu.make_async_copy(source, target, own_sem.at[w])
        for w, (source, target) in enumerate(weights[:4])
    ]
    sends = [
        [
            remote(source, target, wsend.at[w, d], wrecv.at[w, d], peers[d])
            for d in range(shards - 1)
        ]
        for w, (source, target) in enumerate(weights)
    ]
    for copy in own:
        copy.start()
    pl.semaphore_wait(barrier, shards + 1 + neighbours)

    pair_copies = []
    for d in range(shards - 1):
        origin = lax.rem(shard + shards - d - 1, shards)
        rows = wg_out.at[rows_of(2 * origin + side, share // 2), :]
        pair_copies.append(remote(rows, rows, wsend.at[6, d], wrecv.at[6, d], partner))

    def send_weights(*places):
        for w in places:
            for copy in sends[w]:
                copy.start()

    def have_weights(*places):
        for w in places:
            for copy in sends[w]:
                copy.wait_recv()

    send_weights(0, 1, 2, 3, 4, 5)
    for slot in range(slots):
        for h in range(heads):
            acc[slot, h] = jnp.zeros((length, 2 * head), f32)
    load_tok.wait()
    for copy in own:
        copy.wait()
    have_weights(0)
    first_slot, short_length = slot_order(lengths_ref)
    head_gains = head_gain_ref[...].astype(f32)
    per_slot = length // TILE
    tiles = slots * per_slot

    first_gain = gains[...].astype(f32)[0:1, :]

    def norm_rows(i, _):
        slot = i // per_slot
        source = jnp.where(slot == 0, first_slot, 1 - first_slot)
        values = tok[source, rows_of(i % per_slot, TILE), :].astype(f32)
        scale = lax.rsqrt(mean_square(values) + epsilon)
        first[context, slot, rows_of(i % per_slot, TILE), :] = (
            values * scale * first_gain
        ).astype(bf16)
        return 0

    lax.fori_loop(0, tiles, norm_rows, 0)

    def part(block, slot, which):
        return first.at[block, slot, rows_of(which, quarter), :]

    def z_copy(block, slot):
        rows = part(block, slot, tensor)
        return remote(rows, rows, z_send.at[block, slot], z_recv.at[block, slot], above)

    def x_copy(block, slot):
        rows = part(block, slot, tensor)
        return remote(rows, rows, x_send.at[block, slot], x_recv.at[block, slot], x_peer)

    def core_copy(kind, block, slot):
        rows = part(block, slot, tensor if kind == 0 else (tensor + 2) % 4)
        return remote(
            rows, rows, core_send.at[kind, block, slot], core_recv.at[kind, block, slot], core_peer
        )

    def unit_copies(block, slot):
        return [
            pltpu.make_async_copy(
                source.at[block, slot], target.at[block, slot], unit_sem.at[n, block, slot]
            )
            for n, (source, target) in enumerate(
                ((first, first_out), (kv, kv_out), (kraw, kraw_out))
            )
        ]

    def go_up(block, slot):
        @pl.when(context < contexts - 1)
        def _():
            z_copy(block, slot).start()

    def stage_in(block, slot):
        z_copy(block, slot).wait_recv()
        go_up(block, slot)
        x_copy(block, slot).start()
        core_copy(0, block, slot).start()

    def stage_across(block, slot):
        x_copy(block, slot).wait_recv()
        core_copy(1, block, slot).start()

    def head_form(raw, gain, local):
        normal = raw * lax.rsqrt(mean_square(raw) + epsilon) * gain
        return normal * cosine[local, :] + pltpu.roll(normal, head // 2, 1) * sine[local, :]

    def make_keys(block, slot):
        turn(cosine, sine, start_ref, block, inside_cos_ref, inside_sin_ref)

        def rows(i, _):
            local = rows_of(i, TILE)
            values = first[block, slot, local, :]
            raw = dot_nn(values, wk[...])
            kraw[block, slot, local, :] = raw.astype(bf16)
            for g in range(key_width // head):
                columns = slice(g * head, (g + 1) * head)
                kv[block, slot, local, columns] = head_form(
                    raw[:, columns], head_gains[8:9, :], local
                ).astype(bf16)
            kv[block, slot, local, key_width:] = dot_nn(values, wv[...]).astype(bf16)
            return 0

        lax.fori_loop(0, per_slot, rows, 0)
        for copy in unit_copies(block, slot):
            copy.start()

    def stage_keys(block, slot):
        core_copy(0, block, slot).wait_recv()
        core_copy(1, block, slot).wait_recv()
        make_keys(block, slot)

    ones = jnp.ones((length, head), bf16)

    def attend(block, slot, diagonal):
        def one_head(h, _):
            columns = rows_of(h, head)
            keys = kv[block, slot, :, rows_of(h // group, head)]
            values = kv[block, slot, :, rows_of(key_width // head + h // group, head)]
            raised = jnp.exp2(dot_nt(qs[slot * length : (slot + 1) * length, columns], keys))
            spots = lax.broadcasted_iota(jnp.int32, (length, length), 1)
            if diagonal:
                lines = lax.broadcasted_iota(jnp.int32, (length, length), 0)
                raised = jnp.where(spots <= lines, raised, 0.0)
            if slot == 1:
                raised = jnp.where(spots + block * length < short_length, raised, 0.0)
            acc[slot, h] += dot_nn(
                raised.astype(bf16), jnp.concatenate([values, ones], axis=1)
            )
            return 0

        lax.fori_loop(0, heads, one_head, 0)

    units = [(r, slot) for r in range(1, contexts) for slot in range(slots)]

    def for_unit(n, action):
        if 0 <= n < len(units):
            back, slot = units[n]
            block = context - back

            @pl.when((block >= 0) if slot == 0 else ((block >= 0) & (block < half)))
            def _():
                action(block, slot)

    def for_own(action):
        action(context, 0)

        @pl.when(context < half)
        def _():
            action(context, 1)

    stores = []

    def store_all(*pairs):
        for source, target in pairs:
            copy = pltpu.make_async_copy(source, target, store_sem.at[len(stores)])
            copy.start()
            stores.append(copy)

    def make_queries():
        have_weights(3)
        store_all((wq, wq_out), (wk, wk_out), (wv, wv_out), (gains, gain_out))
        turn(cosine, sine, start_ref, context, inside_cos_ref, inside_sin_ref)

        def query_rows(i, _):
            place_rows = rows_of(i, TILE)
            local = rows_of(i % per_slot, TILE)
            raw = dot_nn(first[context, i // per_slot, local, :], wq[...])
            qraw[place_rows, :] = raw.astype(bf16)
            for h in range(heads):
                columns = slice(h * head, (h + 1) * head)
                qs[place_rows, columns] = (
                    head_form(raw[:, columns], head_gains[0:1, :], local) * score_scale
                ).astype(bf16)
            return 0

        lax.fori_loop(0, tiles, query_rows, 0)
        store_all((qs, qs_out), (qraw, qraw_out))

    def pass_on():
        have_weights(4)
        for copy in pair_copies:
            copy.start()

    def attend_own():
        for_own(lambda block, slot: attend(block, slot, True))

    actions = dict(
        i=stage_in, a=stage_across, k=stage_keys,
        t=lambda block, slot: attend(block, slot, False),
    )

    def steps(*names):
        for name in names:
            for_unit(int(name[1:]), actions[name[0]])

    for_own(go_up)
    steps("i0")
    have_weights(1, 2)
    steps("i1")
    make_keys(context, 0)
    make_keys(context, 1)
    steps("i2", "i3", "a0", "a1")
    make_queries()
    steps("a2", "k0", "i4", "a3", "k1")
    attend_own()
    steps("i5", "k2", "t0", "a4", "k3")
    pass_on()
    steps("t1", "t2", "k4", "t3", "a5", "t4")
    for n in range(6, len(units)):
        steps(f"i{n}", f"k{n - 1}", f"a{n}", f"t{n - 1}")
    steps(f"k{len(units) - 1}", f"t{len(units) - 1}")

    def finish(h, _):
        columns = rows_of(h, head)
        for slot in range(slots):
            lines = slice(slot * length, (slot + 1) * length)
            inverse = 1.0 / acc[slot, h, :, head:]
            mixed[lines, columns] = (acc[slot, h, :, :head] * inverse).astype(bf16)
            linv[lines, columns] = inverse
        return 0

    lax.fori_loop(0, heads, finish, 0)
    store_all((mixed, mixed_out), (linv, linv_out))

    def sent_up(block, slot):
        @pl.when(context < contexts - 1)
        def _():
            z_copy(block, slot).wait_send()

    def unit_done(block, slot):
        sent_up(block, slot)
        x_copy(block, slot).wait_send()
        core_copy(0, block, slot).wait_send()
        core_copy(1, block, slot).wait_send()
        for copy in unit_copies(block, slot):
            copy.wait()

    for_own(sent_up)
    for slot in range(slots):
        for copy in unit_copies(context, slot):
            copy.wait()
    for n in range(len(units)):
        for_unit(n, unit_done)
    have_weights(5)
    for copy in pair_copies:
        copy.wait_recv()
        copy.wait_send()
    for copies in sends:
        for copy in copies:
            copy.wait_send()
    for copy in stores:
        copy.wait()


def call_attention_forward(
    shards, contexts, lengths, tokens, query_weight, key_weight, value_weight, out_weight,
    gate_weight, gain_share, head_gains, tables,
):
    slots, length, width = tokens.shape
    rows = slots * length
    qw, kw, ff = query_weight.shape[1], key_weight.shape[1], gate_weight.shape[1]
    head = head_gains.shape[1]
    heads = qw // head
    n_weights = 6
    shape = jax.ShapeDtypeStruct
    dma = pltpu.SemaphoreType.DMA
    kv_shape = (contexts, slots, length, 2 * kw)
    kraw_shape = (contexts, slots, length, kw)
    first_shape = (contexts, slots, length, width)
    outs = (
        shape((rows, qw), bf16), shape(kv_shape, bf16), shape((rows, qw), bf16),
        shape((rows, qw), bf16), shape(kraw_shape, bf16), shape((rows, qw), f32),
        shape(first_shape, bf16), shape((width, qw), bf16), shape((width, kw), bf16),
        shape((width, kw), bf16), shape((qw, width), bf16), shape((width, ff), bf16),
        shape((16, width), bf16),
    )
    units = (contexts, slots)
    return pl.pallas_call(
        functools.partial(attention_forward, shards, contexts),
        out_shape=outs,
        in_specs=[SMEM] + [HBM] * 7 + [VMEM] * 4,
        out_specs=[HBM] * len(outs),
        scratch_shapes=[
            pltpu.VMEM((slots, length, width), bf16),
            pltpu.VMEM(first_shape, bf16),
            pltpu.VMEM((width, qw), bf16),
            pltpu.VMEM((width, kw), bf16),
            pltpu.VMEM((width, kw), bf16),
            pltpu.VMEM((16, width), bf16),
            pltpu.VMEM(kv_shape, bf16),
            pltpu.VMEM((rows, qw), bf16),
            pltpu.VMEM((rows, qw), bf16),
            pltpu.VMEM(kraw_shape, bf16),
            pltpu.VMEM((slots, heads, length, 2 * head), f32),
            pltpu.VMEM((rows, qw), bf16),
            pltpu.VMEM((rows, qw), f32),
            pltpu.VMEM((length, head), f32),
            pltpu.VMEM((length, head), f32),
            dma, dma((4,)), dma((8,)), dma((3, *units)),
            dma((n_weights + 1, shards - 1)), dma((n_weights + 1, shards - 1)),
            dma(units), dma(units), dma(units), dma(units), dma((2, *units)), dma((2, *units)),
        ],
        compiler_params=pltpu.CompilerParams(
            collective_id=1, has_side_effects=True, vmem_limit_bytes=60 * 2**20
        ),
        name="attention_forward",
    )(
        lengths, tokens, query_weight, key_weight, value_weight, out_weight, gate_weight,
        gain_share, head_gains, *tables,
    )


def feed_forward(
    shards, lengths_ref, mixed_ref, wo_ref, tok_ref, cot_ref, gain_ref, wg_ref, wo_own_ref,
    wg_own_ref, wu_ref, wd_ref,
    second_out, hidden_out, gback_out, uback_out, cotin_out, spart_out, mpart_out, resid_out,
    square_out, own_tok_out, down_out,
    mixed, wo, tok, cot, gains, wg, wu, wd, second, hidden, gback, uback, cotin, spart, mpart,
    resid, square, own_tok, down, down_own, down_send, down_recv, apart, csend, crecv, xsend, xrecv, ssend, srecv, msend, mrecv, gvalue, uvalue,
    load_sem, gather_sem, store_sem, chunk_sem, wsend, wrecv, core_send, core_recv, x_send, x_recv,
):
    shard, context, tensor = place()
    slots, length, width = tok.shape
    share = wd_ref.shape[1]
    step_rows = TILE // 2
    steps = length // step_rows
    core = tensor % 2
    core_peer = (shard, context, tensor + 1 - 2 * core)
    x_peer = (shard, context, (tensor + 2) % 4)
    peers = [(lax.rem(shard + d, shards), context, tensor) for d in range(1, shards)]
    side = context % 2
    partner = (shard, context + 1 - 2 * side, tensor)
    barrier = greet([core_peer, x_peer, partner, *peers])
    loads = [
        pltpu.make_async_copy(source, target, load_sem.at[n])
        for n, (source, target) in enumerate(
            (
                (mixed_ref, mixed), (tok_ref, tok), (gain_ref, gains), (cot_ref, cot),
                (wu_ref, wu.at[rows_of(shard, share), :]),
                (wd_ref, wd.at[:, rows_of(shard, share)]),
            )
        )
    ]
    gathers = [
        gather_loads(own_ref, whole_ref, target, shard, shards, axis, gather_sem.at[n])
        for n, (own_ref, whole_ref, target, axis) in enumerate(
            (
                (wo_own_ref, wo_ref, wo, 1), (wg_own_ref, wg_ref, wg, 0),
            )
        )
    ]
    for copy in [loads[0], *gathers[0]]:
        copy.start()
    square[...] = jnp.zeros_like(square)
    pl.semaphore_wait(barrier, shards + 2)
    def piece_of(weight, ref, origin, piece):
        if weight == 0:
            size = share // 4
            return ref.at[rows_of((0 if origin is None else 4 * origin) + piece, size), :]
        rows = rows_of(piece, wd.shape[0] // 4)
        return ref.at[rows, :] if origin is None else ref.at[rows, rows_of(origin, share)]

    sends, passes = [], []
    for n in range(4):
        weight, piece = n // 2, 2 * side + n % 2
        source, target = ((wu_ref, wu), (wd_ref, wd))[weight]
        sends.append([])
        passes.append([])
        for d in range(shards - 1):
            sends[n].append(
                remote(
                    piece_of(weight, source, None, piece), piece_of(weight, target, shard, piece),
                    wsend.at[n, d], wrecv.at[n, d], peers[d],
                )
            )
            origin = lax.rem(shard + shards - d - 1, shards)
            place_at = piece_of(weight, target, origin, piece)
            passes[n].append(
                remote(place_at, place_at, wsend.at[4 + n, d], wrecv.at[4 + n, d], partner)
            )
    for copies in sends:
        for copy in copies:
            copy.start()
    for copy in [loads[0], *gathers[0]]:
        copy.wait()
    for copy in [*loads[1:], *gathers[1]]:
        copy.start()

    def mine(i):
        return rows_of(core * steps + i, step_rows)

    def theirs(i):
        return rows_of((1 - core) * steps + i, step_rows)

    def half(i):
        return rows_of(i, step_rows)

    def core_copy(kind, i, source, target):
        return remote(source, target, core_send.at[kind, i], core_recv.at[kind, i], core_peer)

    def attn_copy(i):
        return core_copy(0, i, csend.at[half(i), :], crecv.at[half(i), :])

    def second_copy(i):
        return core_copy(1, i, second.at[mine(i), :], second.at[mine(i), :])

    def spart_copy(i):
        return core_copy(2, i, ssend.at[half(i), :], srecv.at[half(i), :])

    def mpart_copy(i):
        return core_copy(3, i, msend.at[half(i), :], mrecv.at[half(i), :])

    def x_copy(i):
        return remote(
            xsend.at[half(i), :], xrecv.at[half(i), :], x_send.at[i], x_recv.at[i], x_peer
        )

    def project(i, _):
        @pl.when(i < steps)
        def _():
            both = jnp.concatenate([mixed[theirs(i), :], mixed[mine(i), :]], axis=0)
            result = dot_nn(both, wo[...])
            csend[half(i), :] = result[:step_rows].astype(bf16)
            attn_copy(i).start()
            apart[half(i), :] = result[step_rows:]

        @pl.when(i > 0)
        def _():
            before = i - 1
            attn_copy(before).wait_recv()
            total = apart[half(before), :] + crecv[half(before), :].astype(f32)
            xsend[half(before), :] = total.astype(bf16)
            x_copy(before).start()

        return 0

    lax.fori_loop(0, steps + 1, project, 0)
    for copy in [*loads[1:], *gathers[1]]:
        copy.wait()
    first_slot, short_length = slot_order(lengths_ref)
    second_gain = gains[...].astype(f32)[8:9, :]
    own_source = jnp.where(core == 0, first_slot, 1 - first_slot)

    def counted(slot, i):
        spots = context * length + i * step_rows
        lines = lax.broadcasted_iota(jnp.int32, (step_rows, width), 0) + spots
        limit = jnp.where(slot == 0, 2**30, short_length)
        return lines < limit

    def cut(slot, i):
        source = jnp.where(slot == 0, first_slot, 1 - first_slot)
        values = cot[source, half(i), :].astype(f32)
        return jnp.where(counted(slot, i), values, 0.0).astype(bf16)

    def normalise(i):
        x_copy(i).wait_recv()
        attn = xsend[half(i), :].astype(f32) + xrecv[half(i), :].astype(f32)
        attn_counted = jnp.where(counted(core, i), attn, 0.0)
        square[...] += jnp.sum(
            (attn_counted * attn_counted).reshape(step_rows // 8, 8, width), axis=0
        )
        own_tok[half(i), :] = tok[own_source, half(i), :]
        residual = own_tok[half(i), :].astype(f32) + attn
        resid[half(i), :] = residual
        scale = lax.rsqrt(mean_square(residual) + epsilon)
        second[mine(i), :] = (residual * scale * second_gain).astype(bf16)
        second_copy(i).start()
        cotin[mine(i), :] = cut(core, i)
        cotin[theirs(i), :] = cut(1 - core, i)

    def finish_parts(i):
        spart_copy(i).wait_recv()
        spart[half(i), :] = (
            spart[half(i), :].astype(f32) + srecv[half(i), :].astype(f32)
        ).astype(bf16)
        mpart_copy(i).wait_recv()
        mpart[half(i), :] = (
            mpart[half(i), :].astype(f32) + mrecv[half(i), :].astype(f32)
        ).astype(bf16)
        for copy in part_stores(i):
            copy.start()

    def gate(i):
        second_copy(i).wait_recv()
        both = jnp.concatenate([second[mine(i), :], second[theirs(i), :]], axis=0)
        gvalue[i] = dot_nn(both, wg[...])

    def up(i):
        both = jnp.concatenate([second[mine(i), :], second[theirs(i), :]], axis=0)
        up_value = dot_nn(both, wu[...])
        gate_value = gvalue[i]
        sigmoid = 1.0 / (1.0 + jnp.exp(-gate_value))
        swish = gate_value * sigmoid
        slope = sigmoid + swish * (1.0 - sigmoid)
        low = (swish * up_value).astype(bf16)
        hidden[mine(i), :] = low[:step_rows]
        hidden[theirs(i), :] = low[step_rows:]
        gvalue[i] = up_value * slope
        uvalue[i] = swish

    def backward(i):
        inward = jnp.concatenate([cotin[mine(i), :], cotin[theirs(i), :]], axis=0)
        hidden_back = dot_nt(inward, wd[...])
        gate_low = (hidden_back * gvalue[i]).astype(bf16)
        up_low = (hidden_back * uvalue[i]).astype(bf16)
        gback[mine(i), :] = gate_low[:step_rows]
        gback[theirs(i), :] = gate_low[step_rows:]
        uback[mine(i), :] = up_low[:step_rows]
        uback[theirs(i), :] = up_low[step_rows:]
        for copy in chunk_stores(i):
            copy.start()
        result = dot_nt(gate_low, wg[...]) + dot_nt(up_low, wu[...])
        ssend[half(i), :] = result[step_rows:].astype(bf16)
        spart_copy(i).start()
        spart[half(i), :] = result[:step_rows].astype(bf16)
        low = jnp.concatenate([hidden[mine(i), :], hidden[theirs(i), :]], axis=0)
        result = dot_nn(low, wd[...])
        msend[half(i), :] = result[step_rows:].astype(bf16)
        mpart_copy(i).start()
        mpart[half(i), :] = result[:step_rows].astype(bf16)

    def pass_on(n):
        for copy in sends[n]:
            copy.wait_recv()
        for copy in passes[n]:
            copy.start()

    def have(*pieces):
        for n in pieces:
            for copy in passes[n]:
                copy.wait_recv()

    def chunk_stores(i):
        rows = [(ref, out, at) for ref, out in ((gback, gback_out), (uback, uback_out)) for at in (mine(i), theirs(i))]
        return [
            pltpu.make_async_copy(ref.at[at, :], out.at[at, :], chunk_sem.at[n, i])
            for n, (ref, out, at) in enumerate(rows)
        ]

    def part_stores(i):
        return [
            pltpu.make_async_copy(ref.at[half(i), :], out.at[half(i), :], chunk_sem.at[n, i])
            for n, (ref, out) in enumerate(((spart, spart_out), (mpart, mpart_out)), 4)
        ]

    stores = []

    def store_all(*pairs):
        for source, target in pairs:
            copy = pltpu.make_async_copy(source, target, store_sem.at[len(stores)])
            copy.start()
            stores.append(copy)

    def run(action, start, stop):
        def body(i, _):
            action(i)
            return 0

        lax.fori_loop(start, stop, body, 0)

    half_steps = steps // 2
    pass_on(0)
    normalise(0)
    pass_on(1)
    gate(0)
    pass_on(2)

    def rest_of_half(i):
        normalise(i)
        gate(i)

    run(rest_of_half, 1, half_steps)
    pass_on(3)
    have(0, 1)
    up(0)
    run(rest_of_half, half_steps, steps - 1)
    run(up, 1, half_steps)
    have(2, 3)
    backward(0)
    normalise(steps - 1)
    gate(steps - 1)
    store_all((second, second_out), (cotin, cotin_out), (resid, resid_out), (square, square_out))
    store_all((own_tok, own_tok_out))
    run(up, half_steps, steps)
    store_all((hidden, hidden_out))
    given = down.shape[0]

    def down_copy(d, n):
        return remote(
            down_send.at[d, n], down_recv.at[d, n], wsend.at[8 + n, d], wrecv.at[8 + n, d],
            peers[d],
        )

    def down_grad(whose):
        return dot_tn(cotin[:, rows_of(whose, share)], hidden[:, : given * CHUNK])

    for d in range(shards - 1):
        result = down_grad(lax.rem(shard + d + 1, shards))
        for n in range(given):
            down_send[d, n] = result[:, n * CHUNK : (n + 1) * CHUNK].astype(bf16)
            down_copy(d, n).start()
    result = down_grad(shard)
    for n in range(given):
        down_own[n] = result[:, n * CHUNK : (n + 1) * CHUNK]

    def back_step(i):
        backward(i)
        finish_parts(i - 1)

    run(back_step, 1, steps)
    finish_parts(steps - 1)
    for n in range(given):
        total = down_own[n]
        for d in range(shards - 1):
            down_copy(d, n).wait_recv()
            total = total + down_recv[d, n].astype(f32)
        down[n] = total.astype(bf16)
    store_all((down, down_out))
    for d in range(shards - 1):
        for n in range(given):
            down_copy(d, n).wait_send()
    for copy in stores:
        copy.wait()

    def drain(i, _):
        for copy in (attn_copy, second_copy, spart_copy, mpart_copy, x_copy):
            copy(i).wait_send()
        for copy in [*chunk_stores(i), *part_stores(i)]:
            copy.wait()
        return 0

    lax.fori_loop(0, steps, drain, 0)
    for copies in sends + passes:
        for copy in copies:
            copy.wait_send()


def call_feed_forward(
    shards, lengths, mixed, out_whole, tokens, cotangent, gains, gate_whole, out_weight,
    gate_weight, up_weight, down_weight,
):
    slots, length, width = tokens.shape
    rows = slots * length
    qw = mixed.shape[1]
    ff = gate_weight.shape[1]
    steps = 2 * length // TILE
    shape = jax.ShapeDtypeStruct
    outs = (
        shape((rows, width), bf16), shape((rows, ff), bf16), shape((rows, ff), bf16),
        shape((rows, ff), bf16), shape((rows, width), bf16), shape((length, width), bf16),
        shape((length, width), bf16), shape((length, width), f32), shape((8, width), f32),
        shape((length, width), bf16), shape((GIVEN, down_weight.shape[1], CHUNK), bf16),
    )
    moved = pltpu.VMEM((shards - 1, GIVEN, down_weight.shape[1], CHUNK), bf16)
    half = pltpu.VMEM((length, width), bf16)
    return pl.pallas_call(
        functools.partial(feed_forward, shards),
        out_shape=outs,
        in_specs=[SMEM] + [HBM] * 10,
        out_specs=[HBM] * len(outs),
        scratch_shapes=[
            pltpu.VMEM((rows, qw), bf16),
            pltpu.VMEM((qw, width), bf16),
            pltpu.VMEM((slots, length, width), bf16),
            pltpu.VMEM((slots, length, width), bf16),
            pltpu.VMEM((16, width), bf16),
            pltpu.VMEM((width, ff), bf16),
            pltpu.VMEM((width, ff), bf16),
            pltpu.VMEM((ff, width), bf16),
            *[pltpu.VMEM(out.shape, out.dtype) for out in outs],
            pltpu.VMEM((GIVEN, down_weight.shape[1], CHUNK), f32), moved, moved,
            pltpu.VMEM((length, width), f32),
            *[half] * 8,
            pltpu.VMEM((steps, TILE, ff), f32),
            pltpu.VMEM((steps, TILE, ff), f32),
            pltpu.SemaphoreType.DMA((6,)),
            pltpu.SemaphoreType.DMA((2, shards)),
            pltpu.SemaphoreType.DMA((7,)),
            pltpu.SemaphoreType.DMA((6, steps)),
            pltpu.SemaphoreType.DMA((8 + GIVEN, shards - 1)),
            pltpu.SemaphoreType.DMA((8 + GIVEN, shards - 1)),
            pltpu.SemaphoreType.DMA((4, steps)),
            pltpu.SemaphoreType.DMA((4, steps)),
            pltpu.SemaphoreType.DMA((steps,)),
            pltpu.SemaphoreType.DMA((steps,)),
        ],
        compiler_params=pltpu.CompilerParams(
            collective_id=2, has_side_effects=True, vmem_limit_bytes=56 * 2**20
        ),
        name="feed_forward",
    )(
        lengths, mixed, out_whole, tokens, cotangent, gains, gate_whole, out_weight,
        gate_weight, up_weight, down_weight,
    )


def gradient_places(contexts, steps):
    names = ["p0", "p1", "p2", *(f"res{n}" for n in range(steps)), "mixed", "m0", "out"]
    names += [*(f"m{n}" for n in range(1, contexts + 1)), "q", "qw"]
    names += [*(f"layer{n}" for n in range(steps)), "pz", *(f"first{n}" for n in range(steps + 1))]
    return [*names, *(f"tokb{n}" for n in range(steps)), "s1"]


def gradient_schedule(contexts, chunk_count, names):
    if contexts != 4 or chunk_count != 30:
        nothing = [[0] * len(names)] * contexts
        return nothing, nothing
    reduce_table = (
        (1, 0, 0, 2, 3, 6, 3, 0, 2, 0, 0, 1, 1, 0, 0, 0, 1, 2, 0, 0, 0, 1, 0, 0, 1, 6, 0, 0, 0, 0, 0),
        (0, 3, 0, 0, 0, 0, 2, 2, 2, 3, 3, 0, 0, 1, 1, 1, 0, 0, 0, 1, 0, 0, 2, 1, 1, 1, 0, 0, 4, 1, 1),
        (0, 0, 0, 3, 2, 1, 1, 5, 2, 1, 3, 0, 0, 0, 0, 1, 0, 0, 0, 1, 0, 1, 0, 2, 0, 3, 0, 0, 2, 0, 2),
        (3, 1, 2, 0, 0, 1, 0, 4, 1, 3, 3, 1, 0, 0, 0, 1, 1, 1, 0, 0, 0, 0, 3, 1, 1, 0, 1, 0, 0, 0, 2),
    )
    return_table = (
        (0, 0, 0, 0, 0, 0, 0, 0, 0, 0, 0, 0, 1, 2, 1, 0, 1, 0, 0, 1, 1, 0, 1, 0, 5, 3, 1, 0, 4, 0, 5),
        (0, 0, 0, 0, 0, 0, 0, 0, 0, 0, 0, 0, 0, 0, 0, 0, 0, 0, 0, 0, 0, 0, 0, 0, 0, 0, 0, 0, 0, 0, 0),
        (0, 0, 0, 0, 1, 2, 0, 4, 0, 0, 3, 0, 5, 0, 0, 0, 0, 1, 0, 1, 0, 1, 0, 1, 1, 3, 0, 0, 1, 1, 1),
        (0, 0, 0, 0, 0, 0, 0, 0, 0, 4, 0, 0, 0, 0, 7, 1, 2, 0, 0, 1, 0, 0, 0, 0, 2, 0, 0, 3, 0, 1, 0),
    )
    return reduce_table, return_table


def layer_backward(
    shards, contexts, lengths_ref, second_ref, gback_ref, uback_ref, cotin_ref, hidden_ref,
    spart_ref, mpart_ref, resid_ref, square_ref, mixed_ref, linv_ref, qs_ref, qraw_ref, kraw_ref,
    kv_ref, first_ref, wq_ref, wk_ref, wv_ref, wo_ref, wo_own_ref, gain_ref, own_tok_ref, down_ref, head_gain_ref,
    inside_cos_ref, inside_sin_ref, start_ref,
    straight_out, turned_out, layer_out, tgrad_out, sums_out,
    second, gback, uback, cotin, hidden, spart, mpart, resid, square, dq, wq, wkv, wo, gains,
    unit_kv, unit_first, unit_kraw, unit_back, kv_grad, cosine, sine, xs, xm, outin,
    resback, part, part_core, part_x, part_z, fxrecv,
    piece, ysend, yrecv, zin, ztop, turned, sums, sums_circle, sums_line, acc_gain, acc_ff, acc_head,
    acc_square,
    load_sem, gather_sem, kv_sem, late_sem, store_sem, x_send, x_recv, core_send, core_recv, y_send, y_recv,
    g_send, z_recv, top_recv, res_send, res_recv, p_send, p_recv, s_send, s_recv,
):
    shard, context, tensor = place()
    rows, width = second.shape
    length = resid.shape[0]
    ff = gback.shape[1]
    qw, kw = wq.shape[1], wkv.shape[1] // 2
    head = head_gain_ref.shape[1]
    heads, kv_heads = qw // head, kw // head
    group = heads // kv_heads
    share = piece.shape[1]
    chunk_count, chunk = piece.shape[0], piece.shape[2]
    early = ysend.shape[1]
    half_contexts = contexts // 2
    root = (contexts - 1) // 2
    down_to, out_from, out_to = ff // chunk, 3 * ff // chunk, (3 * ff + qw) // chunk
    given = down_ref.shape[0]
    step_rows = TILE // 2
    steps = length // step_rows
    scale = head**-0.5
    core = tensor % 2
    chip = tensor // 2
    quarter = length // 4
    core_peer = (shard, context, tensor + 1 - 2 * core)
    x_peer = (shard, context, (tensor + 2) % 4)
    peers = [(lax.rem(shard + d, shards), context, tensor) for d in range(1, shards)]
    below = (shard, jnp.maximum(context - 1, 0), tensor)
    above = (shard, jnp.minimum(context + 1, contexts - 1), tensor)
    around = shards * 4
    index = shard * 4 + tensor
    places = [lax.rem(index + d, around) for d in range(1, around)]
    circle = [(at // 4, context, at % 4) for at in places]
    line = [(shard, lax.rem(context + d, contexts), tensor) for d in range(1, contexts)]
    barrier = greet([*circle, *line])

    pairs = [
        (spart_ref, spart), (cotin_ref, cotin), (hidden_ref, hidden),
        (down_ref, piece.at[pl.ds(0, down_ref.shape[0])]), (second_ref, second),
        (gback_ref, gback), (uback_ref, uback), (mpart_ref, mpart), (resid_ref, resid),
        (gain_ref, gains), (linv_ref, dq), (square_ref, square), (wq_ref, wq),
        (wk_ref, wkv.at[:, :kw]), (wv_ref, wkv.at[:, kw:]),
    ]
    loads = [
        pltpu.make_async_copy(source, target, load_sem.at[n])
        for n, (source, target) in enumerate(pairs)
    ]
    loads += gather_loads(wo_own_ref, wo_ref, wo, shard, shards, 1, gather_sem)
    for copy in loads[:8]:
        copy.start()

    def mine(i):
        return rows_of(core * steps + i, step_rows)

    def theirs(i):
        return rows_of((1 - core) * steps + i, step_rows)

    def half(i):
        return rows_of(i, step_rows)

    def xs_copy(i):
        return remote(spart.at[half(i), :], xs.at[half(i), :], x_send.at[0, i], x_recv.at[0, i], x_peer)

    def xm_copy(i):
        return remote(mpart.at[half(i), :], xm.at[half(i), :], x_send.at[1, i], x_recv.at[1, i], x_peer)

    fsend, fxsend, frecv = part.at[0], part.at[1], xs

    def xf_copy(i):
        return remote(
            fxsend.at[half(i), :], fxrecv.at[half(i), :], x_send.at[2, i], x_recv.at[2, i], x_peer
        )

    def core_copy(kind, i, source, target):
        return remote(source, target, core_send.at[kind, i], core_recv.at[kind, i], core_peer)

    def outin_copy(i):
        return core_copy(0, i, outin.at[mine(i), :], outin.at[mine(i), :])

    def layer_copy(i):
        return core_copy(1, i, mpart.at[half(i), :], layer_out.at[core, half(i), :])

    def f_copy(i):
        return core_copy(2, i, fsend.at[half(i), :], frecv.at[half(i), :])

    def tgrad_copy(i):
        return core_copy(3, i, spart.at[half(i), :], tgrad_out.at[core, half(i), :])

    def layer_keep(i):
        return pltpu.make_async_copy(
            mpart.at[half(i), :], layer_out.at[core, half(i), :], store_sem.at[0, i]
        )

    def tgrad_keep(i):
        return pltpu.make_async_copy(
            spart.at[half(i), :], tgrad_out.at[core, half(i), :], store_sem.at[1, i]
        )

    def y_copy(d, k):
        return remote(
            ysend.at[d, k % early], yrecv.at[d, k], y_send.at[d, k], y_recv.at[d, k], peers[d]
        )

    def up_copy(k):
        return remote(piece.at[k], zin.at[k], g_send.at[k], z_recv.at[k], above)

    def down_copy(k):
        return remote(piece.at[k], zin.at[k], g_send.at[k], z_recv.at[k], below)

    def top_copy(k):
        return remote(piece.at[k], ztop.at[k], g_send.at[k], top_recv.at[k], below)

    def back_down_copy(k):
        return remote(zin.at[k], zin.at[k], res_send.at[0, k], res_recv.at[k], below)

    def back_up_copy(k):
        return remote(zin.at[k], zin.at[k], res_send.at[1, k], res_recv.at[k], above)

    def turned_row(k):
        row = jnp.where(k < down_to, k, k - out_from + down_to)
        return jnp.clip(row, 0, down_to + out_to - out_from - 1)

    def grad_copies(k):
        early_columns = jnp.where(k < out_from, k - down_to, k - down_to - (out_to - out_from))
        column = rows_of(jnp.maximum(early_columns, 0), chunk)
        row = turned_row(k)
        return (
            pltpu.make_async_copy(zin.at[k], straight_out.at[:, column], late_sem.at[k]),
            pltpu.make_async_copy(
                turned.at[row], turned_out.at[rows_of(row, chunk), :], late_sem.at[k]
            ),
        )

    def grad_keep(k, finish=False):
        straight_copy, turned_copy = grad_copies(k)
        aside = (k < down_to) | ((k >= out_from) & (k < out_to))

        @pl.when(jnp.logical_not(aside))
        def _():
            straight_copy.wait() if finish else straight_copy.start()

        @pl.when(aside)
        def _():
            if not finish:
                turned[turned_row(k)] = zin[k].astype(f32).T.astype(bf16)
            turned_copy.wait() if finish else turned_copy.start()

    def reduce_chunk(k):
        @pl.when(k >= given)
        def _():
            for d in range(shards - 1):
                y_copy(d, k).wait_recv()

        def total():
            result = piece[k].astype(f32)
            for d in range(shards - 1):
                result += jnp.where(k >= given, yrecv[d, k].astype(f32), 0.0)
            return result

        @pl.when((context == 0) | (context == contexts - 1))
        def _():
            piece[k] = total().astype(bf16)

        @pl.when((context > 0) & (context < root))
        def _():
            up_copy(k).wait_recv()
            piece[k] = (total() + zin[k].astype(f32)).astype(bf16)

        @pl.when((context > root) & (context < contexts - 1))
        def _():
            down_copy(k).wait_recv()
            piece[k] = (total() + zin[k].astype(f32)).astype(bf16)

        @pl.when(context < root)
        def _():
            up_copy(k).start()

        @pl.when(context == root + 1)
        def _():
            top_copy(k).start()

        @pl.when(context > root + 1)
        def _():
            down_copy(k).start()

        @pl.when(context == root)
        def _():
            up_copy(k).wait_recv()
            top_copy(k).wait_recv()
            zin[k] = (total() + zin[k].astype(f32) + ztop[k].astype(f32)).astype(bf16)
            back_down_copy(k).start()
            back_up_copy(k).start()
            grad_keep(k)

    def return_chunk(k):
        @pl.when(context < root)
        def _():
            back_down_copy(k).wait_recv()

            @pl.when(context > 0)
            def _():
                back_down_copy(k).start()

            grad_keep(k)

        @pl.when(context > root)
        def _():
            back_up_copy(k).wait_recv()

            @pl.when(context < contexts - 1)
            def _():
                back_up_copy(k).start()

            grad_keep(k)

    names = gradient_places(contexts, steps)
    reduce_table, return_table = gradient_schedule(contexts, chunk_count, names)

    def here(table, upto):
        total = 0
        for c in range(contexts):
            total += jnp.where(context == c, sum(table[c][:upto]), 0)
        return total

    def take_chunks(name):
        at = names.index(name)
        most = max(max(t[c][at] for c in range(contexts)) for t in (reduce_table, return_table))
        if most == 0:
            return
        reduced, reduced_next = here(reduce_table, at), here(reduce_table, at + 1)
        back, back_next = here(return_table, at), here(return_table, at + 1)

        def one(n, _):
            @pl.when(reduced + n < reduced_next)
            def _():
                reduce_chunk(reduced + n)

            @pl.when(back + n < back_next)
            def _():
                return_chunk(back + n)

            return 0

        lax.fori_loop(0, most, one, 0)

    def take_rest():
        reduced, back = here(reduce_table, len(names)), here(return_table, len(names))
        lag = 4 * jnp.abs(context - root)

        def give(k, _):
            @pl.when(context != root)
            def _():
                return_chunk(k)

            return 0

        def take(k, _):
            reduce_chunk(k)

            @pl.when((k - lag >= back) & (context != root))
            def _():
                return_chunk(k - lag)

            return 0

        lax.fori_loop(back, jnp.maximum(back, reduced - lag), give, 0)
        lax.fori_loop(reduced, chunk_count, take, 0)
        lax.fori_loop(jnp.maximum(back, chunk_count - lag), chunk_count, give, 0)

    def weight_grad(left, right, columns, first_chunk, count):
        for d in range(shards - 1):
            theirs_at = rows_of(lax.rem(shard + d + 1, shards), share)
            result = dot_tn(left[:, theirs_at], right[:, columns : columns + count * chunk])
            for n in range(count):
                k = first_chunk + n
                if k - early >= given:
                    y_copy(d, k - early).wait_send()
                ysend[d, k % early] = result[:, n * chunk : (n + 1) * chunk].astype(bf16)
                y_copy(d, k).start()
        result = dot_tn(left[:, rows_of(shard, share)], right[:, columns : columns + count * chunk])
        for n in range(count):
            piece[first_chunk + n] = result[:, n * chunk : (n + 1) * chunk].astype(bf16)

    def part_at(slot, block):
        return block if slot == 0 else contexts - 1 + block

    def part_core_copy(slot, block):
        at = part_at(slot, block)
        return remote(
            part.at[slot, pl.ds(0, length // 2), :], part_core.at[at], p_send.at[0, at],
            p_recv.at[0, at], core_peer,
        )

    def part_x_copy(slot, block):
        at = part_at(slot, block)
        return remote(
            part_core.at[at, rows_of(1 - chip, quarter), :], part_x.at[at], p_send.at[1, at],
            p_recv.at[1, at], x_peer,
        )

    def part_z_copy(slot, block):
        at = part_at(slot, block)
        return remote(part_x.at[at], part_z.at[at], p_send.at[2, at], p_recv.at[2, at], below)

    def part_make(slot, block):
        for pair in range(2):
            rows_at = slice(2 * pair * quarter, 2 * (pair + 1) * quarter)
            result = dot_nt(unit_back[rows_at, :], wkv[...]).astype(bf16)
            for side in range(2):
                place_at = jnp.where(core == side, 2, 0) + pair
                part[slot, rows_of(place_at, quarter), :] = result[
                    side * quarter : (side + 1) * quarter
                ]
        part_core_copy(slot, block).start()

    def part_across(slot, block):
        part_core_copy(slot, block).wait_recv()
        at = part_at(slot, block)
        total = part[slot, length // 2 :, :].astype(f32) + part_core[at].astype(f32)
        part_core[at] = total.astype(bf16)
        part_x_copy(slot, block).start()
        part_core_copy(slot, block).wait_send()

    def part_down(slot, block, count):
        part_x_copy(slot, block).wait_recv()
        at = part_at(slot, block)
        total = part_core[at, rows_of(chip, quarter), :].astype(f32) + part_x[at].astype(f32)

        @pl.when(context == count - 1)
        def _():
            part_x[at] = total.astype(bf16)

        @pl.when(context < count - 1)
        def _():
            part_z_copy(slot, block).wait_recv()
            part_x[at] = (total + part_z[at].astype(f32)).astype(bf16)

        part_z_copy(slot, block).start()

    def unit_place(slot, block):
        return jnp.where(context < half_contexts, slot, block % 2)

    def unit_loads(slot, block):
        at = unit_place(slot, block)
        return [
            pltpu.make_async_copy(source.at[block, slot], target.at[at], kv_sem.at[n, at])
            for n, (source, target) in enumerate(
                ((kv_ref, unit_kv), (first_ref, unit_first), (kraw_ref, unit_kraw))
            )
        ]

    def start_unit(slot, block):
        for copy in unit_loads(slot, block):
            copy.start()

    acc_gain[...] = jnp.zeros_like(acc_gain)
    acc_ff[...] = jnp.zeros_like(acc_ff)
    acc_head[...] = jnp.zeros_like(acc_head)
    acc_square[...] = jnp.zeros_like(acc_square)
    loads[0].wait()
    pl.semaphore_wait(barrier, around + contexts - 2)
    alive = (context < half_contexts) | (core == 0)

    @pl.when(alive)
    def _():
        for i in range(steps):
            xs_copy(i).start()

    for n in range(1, 4):
        loads[n].wait()
    gate_chunks = ff // chunk
    out_chunks = qw // chunk
    query_chunk = 3 * gate_chunks + out_chunks
    weight_grad(cotin, hidden, given * chunk, given, down_to - given)
    take_chunks("p0")
    for n in range(4, 6):
        loads[n].wait()
    weight_grad(second, gback, 0, down_to, gate_chunks)
    take_chunks("p1")
    for n in range(6, 8):
        loads[n].wait()
    for copy in loads[8:]:
        copy.start()
    for i in range(steps):
        xm_copy(i).start()
    weight_grad(second, uback, 0, down_to + gate_chunks, gate_chunks)
    take_chunks("p2")
    for n in range(8, len(loads)):
        loads[n].wait()
    both_gains = gains[...].astype(f32)
    head_gains = head_gain_ref[...].astype(f32)
    qs, qraw, mixed = hidden.at[:, :qw], gback.at[:, :qw], uback.at[:, :qw]
    own_kback, own_vback = gback.at[:, qw : qw + kw], uback.at[:, qw : qw + kw]
    next_pairs = [(qs_ref, qs), (qraw_ref, qraw), (mixed_ref, mixed)]
    next_loads = [
        pltpu.make_async_copy(source, target, load_sem.at[n])
        for n, (source, target) in enumerate(next_pairs)
    ]
    for copy in next_loads:
        copy.start()
    start_unit(0, 0)

    def fold(values):
        return jnp.sum(values.reshape(values.shape[0] // 8, 8, values.shape[1]), axis=0)

    def norm_back(values, back, gain):
        inverse = lax.rsqrt(mean_square(values) + epsilon)
        normal = values * inverse
        scaled = back * gain
        inward = inverse * (scaled - normal * jnp.mean(normal * scaled, axis=-1, keepdims=True))
        return inward, back * normal

    def residual_step(i, _):
        @pl.when(alive)
        def _():
            xs_copy(i).wait_recv()

        back = spart[half(i), :].astype(f32)
        back += jnp.where(alive, xs[half(i), :].astype(f32), 0.0)
        inward, terms = norm_back(resid[half(i), :], back, both_gains[8:9, :])
        acc_ff[...] += fold(terms)
        total = cotin[mine(i), :].astype(f32) + inward
        resback[half(i), :] = total
        outin[mine(i), :] = total.astype(bf16)
        outin_copy(i).start()
        return 0

    for i in range(steps):
        residual_step(i, 0)
        take_chunks(f"res{i}")
    for i in range(steps):
        outin_copy(i).wait_recv()
    first = cotin
    first_loads = [
        pltpu.make_async_copy(
            first_ref.at[context, slot], first.at[slot * length : (slot + 1) * length, :],
            gather_sem.at[slot],
        )
        for slot in range(2)
    ]
    for copy in first_loads:
        copy.start()
    for copy in next_loads:
        copy.wait()
    dox = second

    def mixed_step(i, _):
        at = rows_of(i, TILE)
        back = dot_nt(outin[at, :], wo[...]).astype(bf16).astype(f32)
        lanes = lax.broadcasted_iota(jnp.int32, (TILE, head), 1)
        for h in range(heads):
            columns = slice(h * head, (h + 1) * head)
            low = (back[:, columns] * dq[at, columns]).astype(bf16)
            centre = jnp.sum(
                low.astype(f32) * mixed[at, columns].astype(f32), axis=-1, keepdims=True
            )
            high = centre.astype(bf16).astype(f32)
            extra = jnp.where(lanes == 0, -high, jnp.where(lanes == 1, high - centre, 0.0))
            dox[at, 2 * h * head : (2 * h + 1) * head] = low
            dox[at, (2 * h + 1) * head : (2 * h + 2) * head] = extra.astype(bf16)
        dq[at, :] = jnp.zeros((TILE, qw), f32)
        return 0

    lax.fori_loop(0, rows // TILE, mixed_step, 0)
    take_chunks("mixed")
    ones = jnp.ones((length, head), bf16)

    def head_back(raw, back, gain, local):
        turned_back = back * cosine[local, :] - pltpu.roll(back, head // 2, 1) * sine[local, :]
        return norm_back(raw.astype(f32), turned_back, gain)

    kv_grad[...] = jnp.zeros_like(kv_grad)

    @pl.when(context >= half_contexts)
    def _():
        own_kback[length:, :] = jnp.zeros((length, kw), bf16)
        own_vback[length:, :] = jnp.zeros((length, kw), bf16)

    def block_back(slot, block, diagonal):
        lines = slice(slot * length, (slot + 1) * length)
        buffer = unit_place(slot, block)
        if diagonal:
            key_spots = lax.broadcasted_iota(jnp.int32, (length, length), 0)
            query_spots = lax.broadcasted_iota(jnp.int32, (length, length), 1)
            counted = key_spots <= query_spots

        def one_group(g, _):
            keys = unit_kv[buffer, :, rows_of(g, head)]
            values = unit_kv[buffer, :, rows_of(kv_heads + g, head)]
            widened = jnp.concatenate([values, ones], axis=1)
            key_back = jnp.zeros((length, head), f32)
            value_back = jnp.zeros((length, head), f32)
            for member in range(group):
                h = g * group + member
                columns = rows_of(h, head)
                queries = qs[lines, columns]
                inward = dox[lines, rows_of(h, 2 * head)]
                raised = jnp.exp2(dot_nt(keys, queries))
                if diagonal:
                    raised = jnp.where(counted, raised, 0.0)
                scores_back = (raised * dot_nt(widened, inward)).astype(bf16)
                value_back += dot_nn(raised.astype(bf16), inward[:, :head])
                key_back += dot_nn(scores_back, queries)
                dq[lines, columns] += dot_tn(scores_back, keys)
            raw_back, terms = head_back(
                unit_kraw[buffer, :, rows_of(g, head)], key_back * math.log(2.0),
                head_gains[8:9, :], slice(None),
            )
            acc_head[1] += fold(terms)
            unit_back[:, rows_of(g, head)] = raw_back.astype(bf16)
            unit_back[:, rows_of(kv_heads + g, head)] = value_back.astype(bf16)
            return 0

        lax.fori_loop(0, kv_heads, one_group, 0)

        def grad_rows(n, _):
            at = rows_of(n, TILE)
            kv_grad[at, :] += dot_tn(unit_first[buffer, :, at], unit_back[...])
            return 0

        lax.fori_loop(0, width // TILE, grad_rows, 0)
        if diagonal:
            own_kback[lines, :] = unit_back[:, :kw]
            own_vback[lines, :] = unit_back[:, kw:]

    def next_units(slot, block):
        if slot == 0 and block < half_contexts:

            @pl.when(context < half_contexts)
            def _():
                start_unit(1, block)

        if block + 1 < contexts:
            more = block + 1 <= context
            if slot == 0:
                more = more & (context >= half_contexts)

            @pl.when(more)
            def _():
                start_unit(0, block + 1)

    for turn_at in range(contexts + 1):
        block, before = turn_at, turn_at - 1
        if block < contexts:
            turn(cosine, sine, start_ref, block, inside_cos_ref, inside_sin_ref)
        for slot, count in ((0, contexts), (1, half_contexts)):
            within = context < count
            if block < count:

                @pl.when((block <= context) & within)
                def _():
                    for copy in unit_loads(slot, block):
                        copy.wait()
                    next_units(slot, block)

                @pl.when((block == context) & within)
                def _():
                    block_back(slot, block, True)

                @pl.when((block < context) & within)
                def _():
                    block_back(slot, block, False)

            if 0 <= before < count - 1:

                @pl.when((before < context) & within)
                def _():
                    part_across(slot, before)

            if block < count - 1:

                @pl.when((block < context) & within)
                def _():
                    part_make(slot, block)

            gone = turn_at - 2 - (count - 1 - context)

            @pl.when((gone >= 0) & (gone < context) & within)
            def _():
                part_down(slot, gone, count)

        take_chunks(f"m{turn_at}")
        if turn_at == 0:
            weight_grad(outin, mixed, 0, 3 * gate_chunks, out_chunks)
            take_chunks("out")
    for copy in first_loads:
        copy.wait()
    turn(cosine, sine, start_ref, context, inside_cos_ref, inside_sin_ref)

    def query_step(i, _):
        at = rows_of(i, TILE)
        local = rows_of(i % (length // TILE), TILE)
        for h in range(heads):
            columns = slice(h * head, (h + 1) * head)
            inward, terms = head_back(
                qraw[at, columns], dq[at, columns] * scale, head_gains[0:1, :], local
            )
            acc_head[0] += fold(terms)
            qraw[at, columns] = inward.astype(bf16)
        return 0

    lax.fori_loop(0, rows // TILE, query_step, 0)
    take_chunks("q")
    weight_grad(first, qraw, 0, query_chunk, out_chunks)
    key_chunk = query_chunk + out_chunks
    for n in range(2 * kw // chunk):
        k = key_chunk + n
        columns = slice(n * chunk, (n + 1) * chunk)
        for d in range(shards - 1):
            theirs_at = rows_of(lax.rem(shard + d + 1, shards), share)
            if k - early >= given:
                y_copy(d, k - early).wait_send()
            ysend[d, k % early] = kv_grad[theirs_at, columns].astype(bf16)
            y_copy(d, k).start()
        piece[k] = kv_grad[rows_of(shard, share), columns].astype(bf16)
    take_chunks("qw")
    _, short_length = slot_order(lengths_ref)

    @pl.when(alive)
    def _():
        for i in range(steps):
            xs_copy(i).wait_send()

    tok_load = pltpu.make_async_copy(own_tok_ref, spart, load_sem.at[0])
    tok_load.start()

    def layer_step(i, _):
        xm_copy(i).wait_recv()
        xm_copy(i).wait_send()
        mlp = mpart[half(i), :].astype(f32) + xm[half(i), :].astype(f32)
        layer = resid[half(i), :] + mlp
        mpart[half(i), :] = layer.astype(bf16)
        layer_copy(i).start()
        layer_keep(i).start()
        lines = lax.broadcasted_iota(jnp.int32, (step_rows, width), 0)
        limit = jnp.where(core == 0, 2**30, short_length)
        counted = lines + (context * length + i * step_rows) < limit
        acc_square[0] += fold(jnp.where(counted, layer * layer, 0.0))
        acc_square[1] += fold(jnp.where(counted, mlp * mlp, 0.0))
        return 0

    for i in range(steps):
        layer_step(i, 0)
        take_chunks(f"layer{i}")

    @pl.when(context < contexts - 1)
    def _():
        part_z_copy(0, jnp.minimum(context, contexts - 2)).wait_recv()

    @pl.when(context < half_contexts - 1)
    def _():
        part_z_copy(1, jnp.minimum(context, max(half_contexts - 2, 0))).wait_recv()

    take_chunks("pz")
    fown = resid

    def first_step(i, _):
        if i < steps:
            both = lambda ref: jnp.concatenate([ref[theirs(i), :], ref[mine(i), :]], axis=0)
            result = dot_nt(both(qraw), wq[...])
            result += dot_nt(both(own_kback), wkv[:, :kw])
            result += dot_nt(both(own_vback), wkv[:, kw:])

            def from_above(slot):
                at = jnp.where(
                    slot == 0,
                    jnp.minimum(context, contexts - 2),
                    contexts - 1 + jnp.minimum(context, max(half_contexts - 2, 0)),
                )
                last = jnp.where(slot == 0, contexts - 1, half_contexts - 1)
                come = (i == tensor) & (context < last)
                return jnp.where(come, part_z[at].astype(f32), 0.0)

            fsend[half(i), :] = (result[:step_rows] + from_above(1 - core)).astype(bf16)
            f_copy(i).start()
            fown[half(i), :] = result[step_rows:] + from_above(core)

        if i > 0:
            before = i - 1
            f_copy(before).wait_recv()
            total = fown[half(before), :] + frecv[half(before), :].astype(f32)
            fxsend[half(before), :] = total.astype(bf16)

            @pl.when(alive)
            def _():
                xf_copy(before).start()

        return 0

    for i in range(steps + 1):
        first_step(i, 0)
        take_chunks(f"first{i}")
    tok_load.wait()

    def tokens_step(i, _):
        @pl.when(alive)
        def _():
            xf_copy(i).wait_recv()

        back = fxsend[half(i), :].astype(f32)
        back += jnp.where(alive, fxrecv[half(i), :].astype(f32), 0.0)
        inward, terms = norm_back(spart[half(i), :].astype(f32), back, both_gains[0:1, :])
        acc_gain[...] += fold(terms)
        spart[half(i), :] = (resback[half(i), :] + inward).astype(bf16)
        tgrad_copy(i).start()
        tgrad_keep(i).start()
        return 0

    for i in range(steps):
        take_chunks(f"tokb{i}")
        tokens_step(i, 0)

    def total_of(values):
        return jnp.sum(jnp.sum(values, axis=0, keepdims=True), axis=1, keepdims=True)

    lanes = lax.broadcasted_iota(jnp.int32, (1, 128), 1)
    base = (shard * 2 + core) * 4
    squares = jnp.where(lanes == base, total_of(acc_square[0]), 0.0)
    squares += jnp.where(lanes == base + 1, total_of(square[...]), 0.0)
    squares += jnp.where(lanes == base + 2, total_of(acc_square[1]), 0.0)
    gain_row = 0.5 * jnp.sum(acc_gain[...], axis=0, keepdims=True)
    ff_row = 0.5 * jnp.sum(acc_ff[...], axis=0, keepdims=True)
    folds = width // 128
    sums[...] = jnp.zeros_like(sums)
    for n in range(folds):
        columns = slice(n * 128, (n + 1) * 128)
        sums[0, n : n + 1, :] = gain_row[:, columns]
        sums[0, folds + n : folds + n + 1, :] = ff_row[:, columns]
    sums[0, 2 * folds : 2 * folds + 1, :] = jnp.sum(acc_head[0], axis=0, keepdims=True)
    sums[0, 2 * folds + 1 : 2 * folds + 2, :] = jnp.sum(acc_head[1], axis=0, keepdims=True)
    sums[0, 2 * folds + 2 : 2 * folds + 3, :] = 0.5 * squares
    circle_hops = [
        remote(sums.at[0], sums_circle.at[index], s_send.at[d], s_recv.at[d], device)
        for d, device in enumerate(circle)
    ]
    for copy in circle_hops:
        copy.start()
    sums_circle[index] = sums[0]
    take_chunks("s1")
    for copy in circle_hops:
        copy.wait_recv()
    total = sums_circle[0]
    for n in range(1, around):
        total = total + sums_circle[n]
    sums[1] = total
    line_hops = [
        remote(
            sums.at[1], sums_line.at[context], s_send.at[around + d], s_recv.at[around + d], device
        )
        for d, device in enumerate(line)
    ]
    for copy in line_hops:
        copy.start()
    sums_line[context] = total

    take_rest()
    for copy in line_hops:
        copy.wait_recv()
    total = sums_line[0]
    for n in range(1, contexts):
        total = total + sums_line[n]
    sums[2] = total
    sums_keep = pltpu.make_async_copy(sums.at[2], sums_out, store_sem.at[2, 0])
    sums_keep.start()
    for copy in [*circle_hops, *line_hops]:
        copy.wait_send()

    def drain_steps(i, _):
        for copy in (outin_copy, layer_copy, f_copy, tgrad_copy):
            copy(i).wait_send()
        layer_copy(i).wait_recv()
        tgrad_copy(i).wait_recv()

        @pl.when(alive)
        def _():
            xf_copy(i).wait_send()

        layer_keep(i).wait()
        tgrad_keep(i).wait()
        return 0

    lax.fori_loop(0, steps, drain_steps, 0)

    def drain_chunks(k, _):
        @pl.when(k >= chunk_count - early)
        def _():
            for d in range(shards - 1):
                y_copy(d, k).wait_send()

        @pl.when(context != root)
        def _():
            up_copy(k).wait_send()

        @pl.when((context <= root) & (context > 0))
        def _():
            back_down_copy(k).wait_send()

        @pl.when((context >= root) & (context < contexts - 1))
        def _():
            back_up_copy(k).wait_send()

        grad_keep(k, finish=True)
        return 0

    lax.fori_loop(0, chunk_count, drain_chunks, 0)
    for block in range(contexts - 1):
        for slot, count in ((0, contexts), (1, half_contexts)):
            if block < count - 1:

                @pl.when((block < context) & (context < count))
                def _():
                    part_x_copy(slot, block).wait_send()
                    part_z_copy(slot, block).wait_send()

    sums_keep.wait()


def call_layer_backward(shards, contexts, lengths, parts):
    (
        second, gback, uback, cotin, hidden, spart, mpart, resid, square, mixed, linv, qs, qraw,
        kraw, kv, first, wq, wk, wv, wo, out_weight, gains, own_tok, down, head_gains, *tables,
    ) = parts
    rows, width = second.shape
    length = resid.shape[0]
    ff, qw, kw = gback.shape[1], wq.shape[1], wk.shape[1]
    share = width // shards
    chunk = CHUNK
    sum_rows = 2 * width // 128 + 8
    chunk_count = (3 * ff + 2 * qw + 2 * kw) // chunk
    early = 3 * ff // chunk
    steps = 2 * length // TILE
    units = contexts - 1 + max(contexts // 2 - 1, 1)
    head = head_gains.shape[1]
    slots = rows // length
    shape = jax.ShapeDtypeStruct
    outs = (
        shape((share, 2 * ff + qw + 2 * kw), bf16), shape((ff + qw, share), bf16),
        shape((slots, length, width), bf16), shape((slots, length, width), bf16),
        shape((sum_rows, 128), f32),
    )
    dma = pltpu.SemaphoreType.DMA

    def like(array):
        return pltpu.VMEM(array.shape, array.dtype)

    half = pltpu.VMEM((length, width), bf16)
    chunks = pltpu.VMEM((chunk_count, share, chunk), bf16)
    return pl.pallas_call(
        functools.partial(layer_backward, shards, contexts),
        out_shape=outs,
        in_specs=[SMEM] + [HBM] * 24 + [VMEM] * 4,
        out_specs=[HBM] * len(outs),
        scratch_shapes=[
            like(second), like(gback), like(uback), like(cotin), like(hidden), like(spart),
            like(mpart), like(resid), like(square), like(linv), like(wq),
            pltpu.VMEM((width, 2 * kw), bf16), like(wo), like(gains),
            pltpu.VMEM((2, length, 2 * kw), bf16), pltpu.VMEM((2, length, width), bf16),
            pltpu.VMEM((2, length, kw), bf16), pltpu.VMEM((length, 2 * kw), bf16),
            pltpu.VMEM((width, 2 * kw), f32),
            pltpu.VMEM((length, head), f32), pltpu.VMEM((length, head), f32),
            half, half, pltpu.VMEM((rows, width), bf16), pltpu.VMEM((length, width), f32),
            pltpu.VMEM((2, length, width), bf16),
            pltpu.VMEM((units, length // 2, width), bf16),
            pltpu.VMEM((units, length // 4, width), bf16),
            pltpu.VMEM((units, length // 4, width), bf16),
            half,
            chunks,
            pltpu.VMEM((shards - 1, early, share, chunk), bf16),
            pltpu.VMEM((shards - 1, chunk_count, share, chunk), bf16),
            chunks, chunks, pltpu.VMEM(((ff + qw) // chunk, chunk, share), bf16),
            pltpu.VMEM((3, sum_rows, 128), f32), pltpu.VMEM((4 * shards, sum_rows, 128), f32),
            pltpu.VMEM((contexts, sum_rows, 128), f32),
            pltpu.VMEM((8, width), f32), pltpu.VMEM((8, width), f32),
            pltpu.VMEM((2, 8, head), f32), pltpu.VMEM((2, 8, width), f32),
            dma((16,)), dma((shards,)), dma((3, 2)), dma((chunk_count,)), dma((3, steps)),
            dma((3, steps)), dma((3, steps)), dma((4, steps)), dma((4, steps)),
            dma((shards - 1, chunk_count)), dma((shards - 1, chunk_count)),
            dma((chunk_count,)), dma((chunk_count,)), dma((chunk_count,)),
            dma((2, chunk_count)), dma((chunk_count,)), dma((3, units)), dma((3, units)),
            dma((4 * shards + contexts,)), dma((4 * shards + contexts,)),
        ],
        compiler_params=pltpu.CompilerParams(
            collective_id=3, has_side_effects=True, vmem_limit_bytes=63 * 2**20
        ),
        name="layer_backward",
    )(lengths, *parts)


def local(
    tokens, lengths, cotangent, query_weight, key_weight, value_weight, out_weight, gate_weight,
    up_weight, down_weight, attention_gain, feedforward_gain, query_gain, key_gain,
):
    slots, length, width = tokens.shape
    shards, contexts = lax.axis_size("shard"), lax.axis_size("context")
    shard, context, _ = place()
    head = query_gain.shape[0]
    ff, qw, kw = gate_weight.shape[1], query_weight.shape[1], key_weight.shape[1]
    tables = [jnp.asarray(table) for table in rope_tables(length, contexts, head)]

    def packed(one, other):
        upper = lax.broadcasted_iota(jnp.int32, (16, one.shape[0]), 0) < 8
        return jnp.where(upper, one[None], other[None])

    gain_share = packed(attention_gain, feedforward_gain)
    head_gains = packed(query_gain, key_gain)
    (mixed, kv, qs, qraw, kraw, linv, first, wq, wk, wv, wo, wg, gains) = (
        call_attention_forward(
            shards, contexts, lengths, tokens, query_weight, key_weight, value_weight, out_weight,
            gate_weight, gain_share, head_gains, tables,
        )
    )
    (second, hidden, gback, uback, cotin, spart, mpart, resid, square, own_tok, down) = (
        call_feed_forward(
            shards, lengths, mixed, wo, tokens, cotangent, gains, wg, out_weight, gate_weight,
            up_weight, down_weight,
        )
    )
    straight, turned, layer, token_grads, sums = call_layer_backward(
        shards, contexts, lengths,
        (
            second, gback, uback, cotin, hidden, spart, mpart, resid, square, mixed, linv, qs,
            qraw, kraw, kv, first, wq, wk, wv, wo, out_weight, gains, own_tok, down, head_gains, *tables,
        ),
    )
    swapped = lengths[1] > lengths[0]

    def in_place(values):
        return jnp.where(swapped, values[::-1], values)

    ends = np.cumsum([ff, ff, qw, kw])
    gate_grad, up_grad, query_grad, key_grad, value_grad = (
        part.astype(f32) for part in jnp.split(straight, ends, axis=1)
    )
    down_grad, out_grad = (part.astype(f32) for part in jnp.split(turned, [ff], axis=0))
    folds = width // 128
    gain_grads = [
        lax.dynamic_slice_in_dim(
            sums[n * folds : (n + 1) * folds].reshape(width), shard * (width // shards),
            width // shards, 0,
        )
        for n in range(2)
    ]
    query_gain_grad, key_gain_grad, squares = sums[2 * folds : 2 * folds + 3]
    squares = lax.dynamic_slice_in_dim(squares, shard * slots * 4, slots * 4, 0)
    squares = in_place(squares.reshape(slots, 4)[:, :3])
    return (
        in_place(layer),
        in_place(token_grads.astype(f32)),
        query_grad,
        key_grad,
        value_grad,
        out_grad,
        gate_grad,
        up_grad,
        down_grad,
        gain_grads[0],
        gain_grads[1],
        query_gain_grad,
        key_gain_grad,
        jnp.sqrt(squares / (lengths.astype(f32)[:, None] * width)),
    )


def solution(mesh):
    placed = (
        P("shard", "context", None),
        P("shard"),
        P("shard", "context", None),
        P("shard", "tensor"),
        P("shard", "tensor"),
        P("shard", "tensor"),
        P("tensor", "shard"),
        P("shard", "tensor"),
        P("shard", "tensor"),
        P("tensor", "shard"),
        P("shard"),
        P("shard"),
        P(),
        P(),
    )
    return jax.shard_map(
        local,
        mesh=mesh,
        in_specs=placed,
        out_specs=(
            P("shard", "context", None),
            P("shard", "context", None),
            P("shard", "tensor"),
            P("shard", "tensor"),
            P("shard", "tensor"),
            P("tensor", "shard"),
            P("shard", "tensor"),
            P("shard", "tensor"),
            P("tensor", "shard"),
            P("shard"),
            P("shard"),
            P(),
            P(),
            P("shard", None),
        ),
        check_vma=False,
    )
```

```python
import functools
import math

import jax
import jax.numpy as jnp
import numpy as np
from jax import lax
from jax.experimental import pallas as pl
from jax.experimental.pallas import tpu as pltpu
from jax.sharding import PartitionSpec as P

epsilon = 1e-06
rope_base = 1000000.0
MESH = pl.DeviceIdType.MESH
f32 = jnp.float32
bf16 = jnp.bfloat16
HBM = pl.BlockSpec(memory_space=pl.ANY)
VMEM = pl.BlockSpec(memory_space=pltpu.VMEM)
SMEM = pl.BlockSpec(memory_space=pltpu.SMEM)
TILE = 256
CHUNK = 128
GIVEN = 3


def rows_of(index, size):
    if isinstance(index, int):
        return pl.ds(index * size, size)
    return pl.ds(pl.multiple_of(index * size, size), size)


def dot_nt(left, right):
    return lax.dot_general(left, right, (((1,), (1,)), ((), ())), preferred_element_type=f32)


def dot_tn(left, right):
    return lax.dot_general(left, right, (((0,), (0,)), ((), ())), preferred_element_type=f32)


def dot_nn(left, right):
    return jnp.dot(left, right, preferred_element_type=f32)


def mean_square(values):
    return jnp.mean(values * values, axis=-1, keepdims=True)


def place():
    return lax.axis_index("shard"), lax.axis_index("context"), lax.axis_index("tensor")


def greet(devices, extra=0):
    barrier = pltpu.get_barrier_semaphore()
    for device in devices:
        pl.semaphore_signal(barrier, inc=1, device_id=device, device_id_type=MESH)
    return barrier


def greet_line(barrier, shard, context, tensor, count):
    @pl.when(context > 0)
    def _():
        pl.semaphore_signal(
            barrier, inc=1, device_id=(shard, context - 1, tensor), device_id_type=MESH
        )

    @pl.when(context < count - 1)
    def _():
        pl.semaphore_signal(
            barrier, inc=1, device_id=(shard, context + 1, tensor), device_id_type=MESH
        )

    return jnp.minimum(context, 1) + jnp.minimum(count - 1 - context, 1)


def turn(cosine, sine, start_ref, block, inside_cos_ref, inside_sin_ref):
    head = cosine.shape[1]
    start_cos, start_sin = start_ref[block, 0:1, :], start_ref[block, 8:9, :]
    signs = jnp.where(lax.broadcasted_iota(jnp.int32, (1, head), 1) < head // 2, -1.0, 1.0)
    inside_cos, inside_sin = inside_cos_ref[...], inside_sin_ref[...]
    cosine[...] = start_cos * inside_cos - start_sin * inside_sin
    sine[...] = signs * (start_sin * inside_cos + start_cos * inside_sin)


def slot_order(lengths_ref):
    one, other = lengths_ref[0], lengths_ref[1]
    return jnp.where(other > one, 1, 0), jnp.minimum(one, other)


def gather_loads(share_ref, whole_ref, target, shard, shards, axis, sems):
    size = share_ref.shape[axis]
    copies = []
    for d in range(shards):
        at = rows_of(lax.rem(shard + d, shards), size)
        index = (slice(None), at) if axis == 1 else (at, slice(None))
        source = share_ref if d == 0 else whole_ref.at[index]
        copies.append(pltpu.make_async_copy(source, target.at[index], sems.at[d]))
    return copies


def remote(src, dst, send_sem, recv_sem, device):
    return pltpu.make_async_remote_copy(
        src_ref=src,
        dst_ref=dst,
        send_sem=send_sem,
        recv_sem=recv_sem,
        device_id=device,
        device_id_type=MESH,
    )


def rope_tables(length, contexts, head_size):
    half = head_size // 2
    speeds = np.tile(rope_base ** (-np.arange(half, dtype=np.float64) * 2.0 / head_size), 2)
    inside = np.arange(length, dtype=np.float64)[:, None] * speeds
    starts = np.arange(contexts, dtype=np.float64)[:, None] * length * speeds
    rows = np.stack([np.cos(starts), np.sin(starts)], axis=1)
    rows = np.repeat(rows, 8, axis=1)
    return (
        np.cos(inside).astype(np.float32),
        np.sin(inside).astype(np.float32),
        rows.astype(np.float32),
    )


def attention_forward(
    shards, contexts, lengths_ref, tok_ref, wq_ref, wk_ref, wv_ref, wo_ref, wg_ref, gain_ref,
    head_gain_ref, inside_cos_ref, inside_sin_ref, start_ref,
    mixed_out, kv_out, qs_out, qraw_out, kraw_out, linv_out, first_out, wq_out, wk_out, wv_out,
    wo_out, wg_out, gain_out,
    tok, first, wq, wk, wv, gains, kv, qs, qraw, kraw, acc, mixed, linv, cosine, sine,
    load_sem, own_sem, store_sem, unit_sem, wsend, wrecv, z_send, z_recv, x_send, x_recv,
    core_send, core_recv,
):
    shard, context, tensor = place()
    slots, length, width = tok.shape
    share = wq_ref.shape[0]
    query_width = wq.shape[1]
    key_width = wk.shape[1]
    head = head_gain_ref.shape[1]
    heads = query_width // head
    group = query_width // key_width
    half = contexts // 2
    quarter = length // 4
    score_scale = head**-0.5 * math.log2(math.e)
    core = tensor % 2
    core_peer = (shard, context, tensor + 1 - 2 * core)
    x_peer = (shard, context, (tensor + 2) % 4)
    above = (shard, jnp.minimum(context + 1, contexts - 1), tensor)
    peers = [(lax.rem(shard + d, shards), context, tensor) for d in range(1, shards)]
    barrier = greet([core_peer, x_peer, *peers])
    neighbours = greet_line(barrier, shard, context, tensor, contexts)

    load_tok = pltpu.make_async_copy(tok_ref, tok, load_sem)
    load_tok.start()
    mine = rows_of(shard, share)
    side = context % 2
    partner = (shard, context + 1 - 2 * side, tensor)
    weights = [
        (gain_ref, gains.at[:, mine]),
        (wk_ref, wk.at[mine, :]),
        (wv_ref, wv.at[mine, :]),
        (wq_ref, wq.at[mine, :]),
        (wg_ref.at[rows_of(side, share // 2), :], wg_out.at[rows_of(2 * shard + side, share // 2), :]),
        (wo_ref, wo_out.at[:, mine]),
    ]
    own = [
        pltpu.make_async_copy(source, target, own_sem.at[w])
        for w, (source, target) in enumerate(weights[:4])
    ]
    sends = [
        [
            remote(source, target, wsend.at[w, d], wrecv.at[w, d], peers[d])
            for d in range(shards - 1)
        ]
        for w, (source, target) in enumerate(weights)
    ]
    for copy in own:
        copy.start()
    pl.semaphore_wait(barrier, shards + 1 + neighbours)

    pair_copies = []
    for d in range(shards - 1):
        origin = lax.rem(shard + shards - d - 1, shards)
        rows = wg_out.at[rows_of(2 * origin + side, share // 2), :]
        pair_copies.append(remote(rows, rows, wsend.at[6, d], wrecv.at[6, d], partner))

    def send_weights(*places):
        for w in places:
            for copy in sends[w]:
                copy.start()

    def have_weights(*places):
        for w in places:
            for copy in sends[w]:
                copy.wait_recv()

    send_weights(0, 1, 2, 3, 4, 5)
    for slot in range(slots):
        for h in range(heads):
            acc[slot, h] = jnp.zeros((length, 2 * head), f32)
    load_tok.wait()
    for copy in own:
        copy.wait()
    have_weights(0)
    first_slot, short_length = slot_order(lengths_ref)
    head_gains = head_gain_ref[...].astype(f32)
    per_slot = length // TILE
    tiles = slots * per_slot

    first_gain = gains[...].astype(f32)[0:1, :]

    def norm_rows(i, _):
        slot = i // per_slot
        source = jnp.where(slot == 0, first_slot, 1 - first_slot)
        values = tok[source, rows_of(i % per_slot, TILE), :].astype(f32)
        scale = lax.rsqrt(mean_square(values) + epsilon)
        first[context, slot, rows_of(i % per_slot, TILE), :] = (
            values * scale * first_gain
        ).astype(bf16)
        return 0

    lax.fori_loop(0, tiles, norm_rows, 0)

    def part(block, slot, which):
        return first.at[block, slot, rows_of(which, quarter), :]

    def z_copy(block, slot):
        rows = part(block, slot, tensor)
        return remote(rows, rows, z_send.at[block, slot], z_recv.at[block, slot], above)

    def x_copy(block, slot):
        rows = part(block, slot, tensor)
        return remote(rows, rows, x_send.at[block, slot], x_recv.at[block, slot], x_peer)

    def core_copy(kind, block, slot):
        rows = part(block, slot, tensor if kind == 0 else (tensor + 2) % 4)
        return remote(
            rows, rows, core_send.at[kind, block, slot], core_recv.at[kind, block, slot], core_peer
        )

    def unit_copies(block, slot):
        return [
            pltpu.make_async_copy(
                source.at[block, slot], target.at[block, slot], unit_sem.at[n, block, slot]
            )
            for n, (source, target) in enumerate(
                ((first, first_out), (kv, kv_out), (kraw, kraw_out))
            )
        ]

    def go_up(block, slot):
        @pl.when(context < contexts - 1)
        def _():
            z_copy(block, slot).start()

    def stage_in(block, slot):
        z_copy(block, slot).wait_recv()
        go_up(block, slot)
        x_copy(block, slot).start()
        core_copy(0, block, slot).start()

    def stage_across(block, slot):
        x_copy(block, slot).wait_recv()
        core_copy(1, block, slot).start()

    def head_form(raw, gain, local):
        normal = raw * lax.rsqrt(mean_square(raw) + epsilon) * gain
        return normal * cosine[local, :] + pltpu.roll(normal, head // 2, 1) * sine[local, :]

    def make_keys(block, slot):
        turn(cosine, sine, start_ref, block, inside_cos_ref, inside_sin_ref)

        def rows(i, _):
            local = rows_of(i, TILE)
            values = first[block, slot, local, :]
            raw = dot_nn(values, wk[...])
            kraw[block, slot, local, :] = raw.astype(bf16)
            for g in range(key_width // head):
                columns = slice(g * head, (g + 1) * head)
                kv[block, slot, local, columns] = head_form(
                    raw[:, columns], head_gains[8:9, :], local
                ).astype(bf16)
            kv[block, slot, local, key_width:] = dot_nn(values, wv[...]).astype(bf16)
            return 0

        lax.fori_loop(0, per_slot, rows, 0)
        for copy in unit_copies(block, slot):
            copy.start()

    def stage_keys(block, slot):
        core_copy(0, block, slot).wait_recv()
        core_copy(1, block, slot).wait_recv()
        make_keys(block, slot)

    ones = jnp.ones((length, head), bf16)

    def attend(block, slot, diagonal):
        def one_head(h, _):
            columns = rows_of(h, head)
            keys = kv[block, slot, :, rows_of(h // group, head)]
            values = kv[block, slot, :, rows_of(key_width // head + h // group, head)]
            raised = jnp.exp2(dot_nt(qs[slot * length : (slot + 1) * length, columns], keys))
            spots = lax.broadcasted_iota(jnp.int32, (length, length), 1)
            if diagonal:
                lines = lax.broadcasted_iota(jnp.int32, (length, length), 0)
                raised = jnp.where(spots <= lines, raised, 0.0)
            if slot == 1:
                raised = jnp.where(spots + block * length < short_length, raised, 0.0)
            acc[slot, h] += dot_nn(
                raised.astype(bf16), jnp.concatenate([values, ones], axis=1)
            )
            return 0

        lax.fori_loop(0, heads, one_head, 0)

    units = [(r, slot) for r in range(1, contexts) for slot in range(slots)]

    def for_unit(n, action):
        if 0 <= n < len(units):
            back, slot = units[n]
            block = context - back

            @pl.when((block >= 0) if slot == 0 else ((block >= 0) & (block < half)))
            def _():
                action(block, slot)

    def for_own(action):
        action(context, 0)

        @pl.when(context < half)
        def _():
            action(context, 1)

    stores = []

    def store_all(*pairs):
        for source, target in pairs:
            copy = pltpu.make_async_copy(source, target, store_sem.at[len(stores)])
            copy.start()
            stores.append(copy)

    def make_queries():
        have_weights(3)
        store_all((wq, wq_out), (wk, wk_out), (wv, wv_out), (gains, gain_out))
        turn(cosine, sine, start_ref, context, inside_cos_ref, inside_sin_ref)

        def query_rows(i, _):
            place_rows = rows_of(i, TILE)
            local = rows_of(i % per_slot, TILE)
            raw = dot_nn(first[context, i // per_slot, local, :], wq[...])
            qraw[place_rows, :] = raw.astype(bf16)
            for h in range(heads):
                columns = slice(h * head, (h + 1) * head)
                qs[place_rows, columns] = (
                    head_form(raw[:, columns], head_gains[0:1, :], local) * score_scale
                ).astype(bf16)
            return 0

        lax.fori_loop(0, tiles, query_rows, 0)
        store_all((qs, qs_out), (qraw, qraw_out))

    def pass_on():
        have_weights(4)
        for copy in pair_copies:
            copy.start()

    def attend_own():
        for_own(lambda block, slot: attend(block, slot, True))

    actions = dict(
        i=stage_in, a=stage_across, k=stage_keys,
        t=lambda block, slot: attend(block, slot, False),
    )

    def steps(*names):
        for name in names:
            for_unit(int(name[1:]), actions[name[0]])

    for_own(go_up)
    steps("i0")
    have_weights(1, 2)
    steps("i1")
    make_keys(context, 0)
    make_keys(context, 1)
    steps("i2", "i3", "a0", "a1")
    make_queries()
    steps("a2", "k0", "i4", "a3", "k1")
    attend_own()
    steps("i5", "k2", "t0", "a4", "k3")
    pass_on()
    steps("t1", "t2", "k4", "t3", "a5", "t4")
    for n in range(6, len(units)):
        steps(f"i{n}", f"k{n - 1}", f"a{n}", f"t{n - 1}")
    steps(f"k{len(units) - 1}", f"t{len(units) - 1}")

    def finish(h, _):
        columns = rows_of(h, head)
        for slot in range(slots):
            lines = slice(slot * length, (slot + 1) * length)
            inverse = 1.0 / acc[slot, h, :, head:]
            mixed[lines, columns] = (acc[slot, h, :, :head] * inverse).astype(bf16)
            linv[lines, columns] = inverse
        return 0

    lax.fori_loop(0, heads, finish, 0)
    store_all((mixed, mixed_out), (linv, linv_out))

    def sent_up(block, slot):
        @pl.when(context < contexts - 1)
        def _():
            z_copy(block, slot).wait_send()

    def unit_done(block, slot):
        sent_up(block, slot)
        x_copy(block, slot).wait_send()
        core_copy(0, block, slot).wait_send()
        core_copy(1, block, slot).wait_send()
        for copy in unit_copies(block, slot):
            copy.wait()

    for_own(sent_up)
    for slot in range(slots):
        for copy in unit_copies(context, slot):
            copy.wait()
    for n in range(len(units)):
        for_unit(n, unit_done)
    have_weights(5)
    for copy in pair_copies:
        copy.wait_recv()
        copy.wait_send()
    for copies in sends:
        for copy in copies:
            copy.wait_send()
    for copy in stores:
        copy.wait()


def call_attention_forward(
    shards, contexts, lengths, tokens, query_weight, key_weight, value_weight, out_weight,
    gate_weight, gain_share, head_gains, tables,
):
    slots, length, width = tokens.shape
    rows = slots * length
    qw, kw, ff = query_weight.shape[1], key_weight.shape[1], gate_weight.shape[1]
    head = head_gains.shape[1]
    heads = qw // head
    n_weights = 6
    shape = jax.ShapeDtypeStruct
    dma = pltpu.SemaphoreType.DMA
    kv_shape = (contexts, slots, length, 2 * kw)
    kraw_shape = (contexts, slots, length, kw)
    first_shape = (contexts, slots, length, width)
    outs = (
        shape((rows, qw), bf16), shape(kv_shape, bf16), shape((rows, qw), bf16),
        shape((rows, qw), bf16), shape(kraw_shape, bf16), shape((rows, qw), f32),
        shape(first_shape, bf16), shape((width, qw), bf16), shape((width, kw), bf16),
        shape((width, kw), bf16), shape((qw, width), bf16), shape((width, ff), bf16),
        shape((16, width), bf16),
    )
    units = (contexts, slots)
    return pl.pallas_call(
        functools.partial(attention_forward, shards, contexts),
        out_shape=outs,
        in_specs=[SMEM] + [HBM] * 7 + [VMEM] * 4,
        out_specs=[HBM] * len(outs),
        scratch_shapes=[
            pltpu.VMEM((slots, length, width), bf16),
            pltpu.VMEM(first_shape, bf16),
            pltpu.VMEM((width, qw), bf16),
            pltpu.VMEM((width, kw), bf16),
            pltpu.VMEM((width, kw), bf16),
            pltpu.VMEM((16, width), bf16),
            pltpu.VMEM(kv_shape, bf16),
            pltpu.VMEM((rows, qw), bf16),
            pltpu.VMEM((rows, qw), bf16),
            pltpu.VMEM(kraw_shape, bf16),
            pltpu.VMEM((slots, heads, length, 2 * head), f32),
            pltpu.VMEM((rows, qw), bf16),
            pltpu.VMEM((rows, qw), f32),
            pltpu.VMEM((length, head), f32),
            pltpu.VMEM((length, head), f32),
            dma, dma((4,)), dma((8,)), dma((3, *units)),
            dma((n_weights + 1, shards - 1)), dma((n_weights + 1, shards - 1)),
            dma(units), dma(units), dma(units), dma(units), dma((2, *units)), dma((2, *units)),
        ],
        compiler_params=pltpu.CompilerParams(
            collective_id=1, has_side_effects=True, vmem_limit_bytes=60 * 2**20
        ),
        name="attention_forward",
    )(
        lengths, tokens, query_weight, key_weight, value_weight, out_weight, gate_weight,
        gain_share, head_gains, *tables,
    )


def feed_forward(
    shards, lengths_ref, mixed_ref, wo_ref, tok_ref, cot_ref, gain_ref, wg_ref, wo_own_ref,
    wg_own_ref, wu_ref, wd_ref,
    second_out, hidden_out, gback_out, uback_out, cotin_out, spart_out, mpart_out, resid_out,
    square_out, own_tok_out, down_out,
    mixed, wo, tok, cot, gains, wg, wu, wd, second, hidden, gback, uback, cotin, spart, mpart,
    resid, square, own_tok, down, down_own, down_send, down_recv, apart, csend, crecv, xsend, xrecv, ssend, srecv, msend, mrecv, gvalue, uvalue,
    load_sem, gather_sem, store_sem, chunk_sem, wsend, wrecv, core_send, core_recv, x_send, x_recv,
):
    shard, context, tensor = place()
    slots, length, width = tok.shape
    share = wd_ref.shape[1]
    step_rows = TILE // 2
    steps = length // step_rows
    core = tensor % 2
    core_peer = (shard, context, tensor + 1 - 2 * core)
    x_peer = (shard, context, (tensor + 2) % 4)
    peers = [(lax.rem(shard + d, shards), context, tensor) for d in range(1, shards)]
    side = context % 2
    partner = (shard, context + 1 - 2 * side, tensor)
    barrier = greet([core_peer, x_peer, partner, *peers])
    loads = [
        pltpu.make_async_copy(source, target, load_sem.at[n])
        for n, (source, target) in enumerate(
            (
                (mixed_ref, mixed), (tok_ref, tok), (gain_ref, gains), (cot_ref, cot),
                (wu_ref, wu.at[rows_of(shard, share), :]),
                (wd_ref, wd.at[:, rows_of(shard, share)]),
            )
        )
    ]
    gathers = [
        gather_loads(own_ref, whole_ref, target, shard, shards, axis, gather_sem.at[n])
        for n, (own_ref, whole_ref, target, axis) in enumerate(
            (
                (wo_own_ref, wo_ref, wo, 1), (wg_own_ref, wg_ref, wg, 0),
            )
        )
    ]
    for copy in [loads[0], *gathers[0]]:
        copy.start()
    square[...] = jnp.zeros_like(square)
    pl.semaphore_wait(barrier, shards + 2)
    def piece_of(weight, ref, origin, piece):
        if weight == 0:
            size = share // 4
            return ref.at[rows_of((0 if origin is None else 4 * origin) + piece, size), :]
        rows = rows_of(piece, wd.shape[0] // 4)
        return ref.at[rows, :] if origin is None else ref.at[rows, rows_of(origin, share)]

    sends, passes = [], []
    for n in range(4):
        weight, piece = n // 2, 2 * side + n % 2
        source, target = ((wu_ref, wu), (wd_ref, wd))[weight]
        sends.append([])
        passes.append([])
        for d in range(shards - 1):
            sends[n].append(
                remote(
                    piece_of(weight, source, None, piece), piece_of(weight, target, shard, piece),
                    wsend.at[n, d], wrecv.at[n, d], peers[d],
                )
            )
            origin = lax.rem(shard + shards - d - 1, shards)
            place_at = piece_of(weight, target, origin, piece)
            passes[n].append(
                remote(place_at, place_at, wsend.at[4 + n, d], wrecv.at[4 + n, d], partner)
            )
    for copies in sends:
        for copy in copies:
            copy.start()
    for copy in [loads[0], *gathers[0]]:
        copy.wait()
    for copy in [*loads[1:], *gathers[1]]:
        copy.start()

    def mine(i):
        return rows_of(core * steps + i, step_rows)

    def theirs(i):
        return rows_of((1 - core) * steps + i, step_rows)

    def half(i):
        return rows_of(i, step_rows)

    def core_copy(kind, i, source, target):
        return remote(source, target, core_send.at[kind, i], core_recv.at[kind, i], core_peer)

    def attn_copy(i):
        return core_copy(0, i, csend.at[half(i), :], crecv.at[half(i), :])

    def second_copy(i):
        return core_copy(1, i, second.at[mine(i), :], second.at[mine(i), :])

    def spart_copy(i):
        return core_copy(2, i, ssend.at[half(i), :], srecv.at[half(i), :])

    def mpart_copy(i):
        return core_copy(3, i, msend.at[half(i), :], mrecv.at[half(i), :])

    def x_copy(i):
        return remote(
            xsend.at[half(i), :], xrecv.at[half(i), :], x_send.at[i], x_recv.at[i], x_peer
        )

    def project(i, _):
        @pl.when(i < steps)
        def _():
            both = jnp.concatenate([mixed[theirs(i), :], mixed[mine(i), :]], axis=0)
            result = dot_nn(both, wo[...])
            csend[half(i), :] = result[:step_rows].astype(bf16)
            attn_copy(i).start()
            apart[half(i), :] = result[step_rows:]

        @pl.when(i > 0)
        def _():
            before = i - 1
            attn_copy(before).wait_recv()
            total = apart[half(before), :] + crecv[half(before), :].astype(f32)
            xsend[half(before), :] = total.astype(bf16)
            x_copy(before).start()

        return 0

    lax.fori_loop(0, steps + 1, project, 0)
    for copy in [*loads[1:], *gathers[1]]:
        copy.wait()
    first_slot, short_length = slot_order(lengths_ref)
    second_gain = gains[...].astype(f32)[8:9, :]
    own_source = jnp.where(core == 0, first_slot, 1 - first_slot)

    def counted(slot, i):
        spots = context * length + i * step_rows
        lines = lax.broadcasted_iota(jnp.int32, (step_rows, width), 0) + spots
        limit = jnp.where(slot == 0, 2**30, short_length)
        return lines < limit

    def cut(slot, i):
        source = jnp.where(slot == 0, first_slot, 1 - first_slot)
        values = cot[source, half(i), :].astype(f32)
        return jnp.where(counted(slot, i), values, 0.0).astype(bf16)

    def normalise(i):
        x_copy(i).wait_recv()
        attn = xsend[half(i), :].astype(f32) + xrecv[half(i), :].astype(f32)
        attn_counted = jnp.where(counted(core, i), attn, 0.0)
        square[...] += jnp.sum(
            (attn_counted * attn_counted).reshape(step_rows // 8, 8, width), axis=0
        )
        own_tok[half(i), :] = tok[own_source, half(i), :]
        residual = own_tok[half(i), :].astype(f32) + attn
        resid[half(i), :] = residual
        scale = lax.rsqrt(mean_square(residual) + epsilon)
        second[mine(i), :] = (residual * scale * second_gain).astype(bf16)
        second_copy(i).start()
        cotin[mine(i), :] = cut(core, i)
        cotin[theirs(i), :] = cut(1 - core, i)

    def finish_parts(i):
        spart_copy(i).wait_recv()
        spart[half(i), :] = (
            spart[half(i), :].astype(f32) + srecv[half(i), :].astype(f32)
        ).astype(bf16)
        mpart_copy(i).wait_recv()
        mpart[half(i), :] = (
            mpart[half(i), :].astype(f32) + mrecv[half(i), :].astype(f32)
        ).astype(bf16)
        for copy in part_stores(i):
            copy.start()

    def gate(i):
        second_copy(i).wait_recv()
        both = jnp.concatenate([second[mine(i), :], second[theirs(i), :]], axis=0)
        gvalue[i] = dot_nn(both, wg[...])

    def up(i):
        both = jnp.concatenate([second[mine(i), :], second[theirs(i), :]], axis=0)
        up_value = dot_nn(both, wu[...])
        gate_value = gvalue[i]
        sigmoid = 1.0 / (1.0 + jnp.exp(-gate_value))
        swish = gate_value * sigmoid
        slope = sigmoid + swish * (1.0 - sigmoid)
        low = (swish * up_value).astype(bf16)
        hidden[mine(i), :] = low[:step_rows]
        hidden[theirs(i), :] = low[step_rows:]
        gvalue[i] = up_value * slope
        uvalue[i] = swish

    def backward(i):
        inward = jnp.concatenate([cotin[mine(i), :], cotin[theirs(i), :]], axis=0)
        hidden_back = dot_nt(inward, wd[...])
        gate_low = (hidden_back * gvalue[i]).astype(bf16)
        up_low = (hidden_back * uvalue[i]).astype(bf16)
        gback[mine(i), :] = gate_low[:step_rows]
        gback[theirs(i), :] = gate_low[step_rows:]
        uback[mine(i), :] = up_low[:step_rows]
        uback[theirs(i), :] = up_low[step_rows:]
        for copy in chunk_stores(i):
            copy.start()
        result = dot_nt(gate_low, wg[...]) + dot_nt(up_low, wu[...])
        ssend[half(i), :] = result[step_rows:].astype(bf16)
        spart_copy(i).start()
        spart[half(i), :] = result[:step_rows].astype(bf16)
        low = jnp.concatenate([hidden[mine(i), :], hidden[theirs(i), :]], axis=0)
        result = dot_nn(low, wd[...])
        msend[half(i), :] = result[step_rows:].astype(bf16)
        mpart_copy(i).start()
        mpart[half(i), :] = result[:step_rows].astype(bf16)

    def pass_on(n):
        for copy in sends[n]:
            copy.wait_recv()
        for copy in passes[n]:
            copy.start()

    def have(*pieces):
        for n in pieces:
            for copy in passes[n]:
                copy.wait_recv()

    def chunk_stores(i):
        rows = [(ref, out, at) for ref, out in ((gback, gback_out), (uback, uback_out)) for at in (mine(i), theirs(i))]
        return [
            pltpu.make_async_copy(ref.at[at, :], out.at[at, :], chunk_sem.at[n, i])
            for n, (ref, out, at) in enumerate(rows)
        ]

    def part_stores(i):
        return [
            pltpu.make_async_copy(ref.at[half(i), :], out.at[half(i), :], chunk_sem.at[n, i])
            for n, (ref, out) in enumerate(((spart, spart_out), (mpart, mpart_out)), 4)
        ]

    stores = []

    def store_all(*pairs):
        for source, target in pairs:
            copy = pltpu.make_async_copy(source, target, store_sem.at[len(stores)])
            copy.start()
            stores.append(copy)

    def run(action, start, stop):
        def body(i, _):
            action(i)
            return 0

        lax.fori_loop(start, stop, body, 0)

    half_steps = steps // 2
    pass_on(0)
    normalise(0)
    pass_on(1)
    gate(0)
    pass_on(2)

    def rest_of_half(i):
        normalise(i)
        gate(i)

    run(rest_of_half, 1, half_steps)
    pass_on(3)
    have(0, 1)
    up(0)
    run(rest_of_half, half_steps, steps - 1)
    run(up, 1, half_steps)
    have(2, 3)
    backward(0)
    normalise(steps - 1)
    gate(steps - 1)
    store_all((second, second_out), (cotin, cotin_out), (resid, resid_out), (square, square_out))
    store_all((own_tok, own_tok_out))
    run(up, half_steps, steps)
    store_all((hidden, hidden_out))
    given = down.shape[0]

    def down_copy(d, n):
        return remote(
            down_send.at[d, n], down_recv.at[d, n], wsend.at[8 + n, d], wrecv.at[8 + n, d],
            peers[d],
        )

    def down_grad(whose):
        return dot_tn(cotin[:, rows_of(whose, share)], hidden[:, : given * CHUNK])

    for d in range(shards - 1):
        result = down_grad(lax.rem(shard + d + 1, shards))
        for n in range(given):
            down_send[d, n] = result[:, n * CHUNK : (n + 1) * CHUNK].astype(bf16)
            down_copy(d, n).start()
    result = down_grad(shard)
    for n in range(given):
        down_own[n] = result[:, n * CHUNK : (n + 1) * CHUNK]

    def back_step(i):
        backward(i)
        finish_parts(i - 1)

    run(back_step, 1, steps)
    finish_parts(steps - 1)
    for n in range(given):
        total = down_own[n]
        for d in range(shards - 1):
            down_copy(d, n).wait_recv()
            total = total + down_recv[d, n].astype(f32)
        down[n] = total.astype(bf16)
    store_all((down, down_out))
    for d in range(shards - 1):
        for n in range(given):
            down_copy(d, n).wait_send()
    for copy in stores:
        copy.wait()

    def drain(i, _):
        for copy in (attn_copy, second_copy, spart_copy, mpart_copy, x_copy):
            copy(i).wait_send()
        for copy in [*chunk_stores(i), *part_stores(i)]:
            copy.wait()
        return 0

    lax.fori_loop(0, steps, drain, 0)
    for copies in sends + passes:
        for copy in copies:
            copy.wait_send()


def call_feed_forward(
    shards, lengths, mixed, out_whole, tokens, cotangent, gains, gate_whole, out_weight,
    gate_weight, up_weight, down_weight,
):
    slots, length, width = tokens.shape
    rows = slots * length
    qw = mixed.shape[1]
    ff = gate_weight.shape[1]
    steps = 2 * length // TILE
    shape = jax.ShapeDtypeStruct
    outs = (
        shape((rows, width), bf16), shape((rows, ff), bf16), shape((rows, ff), bf16),
        shape((rows, ff), bf16), shape((rows, width), bf16), shape((length, width), bf16),
        shape((length, width), bf16), shape((length, width), f32), shape((8, width), f32),
        shape((length, width), bf16), shape((GIVEN, down_weight.shape[1], CHUNK), bf16),
    )
    moved = pltpu.VMEM((shards - 1, GIVEN, down_weight.shape[1], CHUNK), bf16)
    half = pltpu.VMEM((length, width), bf16)
    return pl.pallas_call(
        functools.partial(feed_forward, shards),
        out_shape=outs,
        in_specs=[SMEM] + [HBM] * 10,
        out_specs=[HBM] * len(outs),
        scratch_shapes=[
            pltpu.VMEM((rows, qw), bf16),
            pltpu.VMEM((qw, width), bf16),
            pltpu.VMEM((slots, length, width), bf16),
            pltpu.VMEM((slots, length, width), bf16),
            pltpu.VMEM((16, width), bf16),
            pltpu.VMEM((width, ff), bf16),
            pltpu.VMEM((width, ff), bf16),
            pltpu.VMEM((ff, width), bf16),
            *[pltpu.VMEM(out.shape, out.dtype) for out in outs],
            pltpu.VMEM((GIVEN, down_weight.shape[1], CHUNK), f32), moved, moved,
            pltpu.VMEM((length, width), f32),
            *[half] * 8,
            pltpu.VMEM((steps, TILE, ff), f32),
            pltpu.VMEM((steps, TILE, ff), f32),
            pltpu.SemaphoreType.DMA((6,)),
            pltpu.SemaphoreType.DMA((2, shards)),
            pltpu.SemaphoreType.DMA((7,)),
            pltpu.SemaphoreType.DMA((6, steps)),
            pltpu.SemaphoreType.DMA((8 + GIVEN, shards - 1)),
            pltpu.SemaphoreType.DMA((8 + GIVEN, shards - 1)),
            pltpu.SemaphoreType.DMA((4, steps)),
            pltpu.SemaphoreType.DMA((4, steps)),
            pltpu.SemaphoreType.DMA((steps,)),
            pltpu.SemaphoreType.DMA((steps,)),
        ],
        compiler_params=pltpu.CompilerParams(
            collective_id=2, has_side_effects=True, vmem_limit_bytes=56 * 2**20
        ),
        name="feed_forward",
    )(
        lengths, mixed, out_whole, tokens, cotangent, gains, gate_whole, out_weight,
        gate_weight, up_weight, down_weight,
    )


def gradient_places(contexts, steps):
    names = ["p0", "p1", "p2", *(f"res{n}" for n in range(steps)), "mixed", "m0", "out"]
    names += [*(f"m{n}" for n in range(1, contexts + 1)), "q", "qw"]
    names += [*(f"layer{n}" for n in range(steps)), "pz", *(f"first{n}" for n in range(steps + 1))]
    return [*names, *(f"tokb{n}" for n in range(steps)), "s1"]


def gradient_schedule(contexts, chunk_count, names):
    if contexts != 4 or chunk_count != 30:
        nothing = [[0] * len(names)] * contexts
        return nothing, nothing
    reduce_table = (
        (1, 0, 0, 2, 3, 6, 3, 0, 2, 0, 0, 1, 1, 0, 0, 0, 1, 2, 0, 0, 0, 1, 0, 0, 1, 6, 0, 0, 0, 0, 0),
        (0, 3, 0, 0, 0, 0, 2, 2, 2, 3, 3, 0, 0, 1, 1, 1, 0, 0, 0, 1, 0, 0, 2, 1, 1, 1, 0, 0, 4, 1, 1),
        (0, 0, 0, 3, 2, 1, 1, 5, 2, 1, 3, 0, 0, 0, 0, 1, 0, 0, 0, 1, 0, 1, 0, 2, 0, 3, 0, 0, 2, 0, 2),
        (3, 1, 2, 0, 0, 1, 0, 4, 1, 3, 3, 1, 0, 0, 0, 1, 1, 1, 0, 0, 0, 0, 3, 1, 1, 0, 1, 0, 0, 0, 2),
    )
    return_table = (
        (0, 0, 0, 0, 0, 0, 0, 0, 0, 0, 0, 0, 1, 2, 1, 0, 1, 0, 0, 1, 1, 0, 1, 0, 5, 3, 1, 0, 4, 0, 5),
        (0, 0, 0, 0, 0, 0, 0, 0, 0, 0, 0, 0, 0, 0, 0, 0, 0, 0, 0, 0, 0, 0, 0, 0, 0, 0, 0, 0, 0, 0, 0),
        (0, 0, 0, 0, 1, 2, 0, 4, 0, 0, 3, 0, 5, 0, 0, 0, 0, 1, 0, 1, 0, 1, 0, 1, 1, 3, 0, 0, 1, 1, 1),
        (0, 0, 0, 0, 0, 0, 0, 0, 0, 4, 0, 0, 0, 0, 7, 1, 2, 0, 0, 1, 0, 0, 0, 0, 2, 0, 0, 3, 0, 1, 0),
    )
    return reduce_table, return_table


def layer_backward(
    shards, contexts, lengths_ref, second_ref, gback_ref, uback_ref, cotin_ref, hidden_ref,
    spart_ref, mpart_ref, resid_ref, square_ref, mixed_ref, linv_ref, qs_ref, qraw_ref, kraw_ref,
    kv_ref, first_ref, wq_ref, wk_ref, wv_ref, wo_ref, wo_own_ref, gain_ref, own_tok_ref, down_ref, head_gain_ref,
    inside_cos_ref, inside_sin_ref, start_ref,
    straight_out, turned_out, layer_out, tgrad_out, sums_out,
    second, gback, uback, cotin, hidden, spart, mpart, resid, square, dq, wq, wkv, wo, gains,
    unit_kv, unit_first, unit_kraw, unit_back, kv_grad, cosine, sine, xs, xm, outin,
    resback, part, part_core, part_x, part_z, fxrecv,
    piece, ysend, yrecv, zin, ztop, turned, sums, sums_circle, sums_line, acc_gain, acc_ff, acc_head,
    acc_square,
    load_sem, gather_sem, kv_sem, late_sem, store_sem, x_send, x_recv, core_send, core_recv, y_send, y_recv,
    g_send, z_recv, top_recv, res_send, res_recv, p_send, p_recv, s_send, s_recv,
):
    shard, context, tensor = place()
    rows, width = second.shape
    length = resid.shape[0]
    ff = gback.shape[1]
    qw, kw = wq.shape[1], wkv.shape[1] // 2
    head = head_gain_ref.shape[1]
    heads, kv_heads = qw // head, kw // head
    group = heads // kv_heads
    share = piece.shape[1]
    chunk_count, chunk = piece.shape[0], piece.shape[2]
    early = ysend.shape[1]
    half_contexts = contexts // 2
    root = (contexts - 1) // 2
    down_to, out_from, out_to = ff // chunk, 3 * ff // chunk, (3 * ff + qw) // chunk
    given = down_ref.shape[0]
    step_rows = TILE // 2
    steps = length // step_rows
    scale = head**-0.5
    core = tensor % 2
    chip = tensor // 2
    quarter = length // 4
    core_peer = (shard, context, tensor + 1 - 2 * core)
    x_peer = (shard, context, (tensor + 2) % 4)
    peers = [(lax.rem(shard + d, shards), context, tensor) for d in range(1, shards)]
    below = (shard, jnp.maximum(context - 1, 0), tensor)
    above = (shard, jnp.minimum(context + 1, contexts - 1), tensor)
    around = shards * 4
    index = shard * 4 + tensor
    places = [lax.rem(index + d, around) for d in range(1, around)]
    circle = [(at // 4, context, at % 4) for at in places]
    line = [(shard, lax.rem(context + d, contexts), tensor) for d in range(1, contexts)]
    barrier = greet([*circle, *line])

    pairs = [
        (spart_ref, spart), (cotin_ref, cotin), (hidden_ref, hidden),
        (down_ref, piece.at[pl.ds(0, down_ref.shape[0])]), (second_ref, second),
        (gback_ref, gback), (uback_ref, uback), (mpart_ref, mpart), (resid_ref, resid),
        (gain_ref, gains), (linv_ref, dq), (square_ref, square), (wq_ref, wq),
        (wk_ref, wkv.at[:, :kw]), (wv_ref, wkv.at[:, kw:]),
    ]
    loads = [
        pltpu.make_async_copy(source, target, load_sem.at[n])
        for n, (source, target) in enumerate(pairs)
    ]
    loads += gather_loads(wo_own_ref, wo_ref, wo, shard, shards, 1, gather_sem)
    for copy in loads[:8]:
        copy.start()

    def mine(i):
        return rows_of(core * steps + i, step_rows)

    def theirs(i):
        return rows_of((1 - core) * steps + i, step_rows)

    def half(i):
        return rows_of(i, step_rows)

    def xs_copy(i):
        return remote(spart.at[half(i), :], xs.at[half(i), :], x_send.at[0, i], x_recv.at[0, i], x_peer)

    def xm_copy(i):
        return remote(mpart.at[half(i), :], xm.at[half(i), :], x_send.at[1, i], x_recv.at[1, i], x_peer)

    fsend, fxsend, frecv = part.at[0], part.at[1], xs

    def xf_copy(i):
        return remote(
            fxsend.at[half(i), :], fxrecv.at[half(i), :], x_send.at[2, i], x_recv.at[2, i], x_peer
        )

    def core_copy(kind, i, source, target):
        return remote(source, target, core_send.at[kind, i], core_recv.at[kind, i], core_peer)

    def outin_copy(i):
        return core_copy(0, i, outin.at[mine(i), :], outin.at[mine(i), :])

    def layer_copy(i):
        return core_copy(1, i, mpart.at[half(i), :], layer_out.at[core, half(i), :])

    def f_copy(i):
        return core_copy(2, i, fsend.at[half(i), :], frecv.at[half(i), :])

    def tgrad_copy(i):
        return core_copy(3, i, spart.at[half(i), :], tgrad_out.at[core, half(i), :])

    def layer_keep(i):
        return pltpu.make_async_copy(
            mpart.at[half(i), :], layer_out.at[core, half(i), :], store_sem.at[0, i]
        )

    def tgrad_keep(i):
        return pltpu.make_async_copy(
            spart.at[half(i), :], tgrad_out.at[core, half(i), :], store_sem.at[1, i]
        )

    def y_copy(d, k):
        return remote(
            ysend.at[d, k % early], yrecv.at[d, k], y_send.at[d, k], y_recv.at[d, k], peers[d]
        )

    def up_copy(k):
        return remote(piece.at[k], zin.at[k], g_send.at[k], z_recv.at[k], above)

    def down_copy(k):
        return remote(piece.at[k], zin.at[k], g_send.at[k], z_recv.at[k], below)

    def top_copy(k):
        return remote(piece.at[k], ztop.at[k], g_send.at[k], top_recv.at[k], below)

    def back_down_copy(k):
        return remote(zin.at[k], zin.at[k], res_send.at[0, k], res_recv.at[k], below)

    def back_up_copy(k):
        return remote(zin.at[k], zin.at[k], res_send.at[1, k], res_recv.at[k], above)

    def turned_row(k):
        row = jnp.where(k < down_to, k, k - out_from + down_to)
        return jnp.clip(row, 0, down_to + out_to - out_from - 1)

    def grad_copies(k):
        early_columns = jnp.where(k < out_from, k - down_to, k - down_to - (out_to - out_from))
        column = rows_of(jnp.maximum(early_columns, 0), chunk)
        row = turned_row(k)
        return (
            pltpu.make_async_copy(zin.at[k], straight_out.at[:, column], late_sem.at[k]),
            pltpu.make_async_copy(
                turned.at[row], turned_out.at[rows_of(row, chunk), :], late_sem.at[k]
            ),
        )

    def grad_keep(k, finish=False):
        straight_copy, turned_copy = grad_copies(k)
        aside = (k < down_to) | ((k >= out_from) & (k < out_to))

        @pl.when(jnp.logical_not(aside))
        def _():
            straight_copy.wait() if finish else straight_copy.start()

        @pl.when(aside)
        def _():
            if not finish:
                turned[turned_row(k)] = zin[k].astype(f32).T.astype(bf16)
            turned_copy.wait() if finish else turned_copy.start()

    def reduce_chunk(k):
        @pl.when(k >= given)
        def _():
            for d in range(shards - 1):
                y_copy(d, k).wait_recv()

        def total():
            result = piece[k].astype(f32)
            for d in range(shards - 1):
                result += jnp.where(k >= given, yrecv[d, k].astype(f32), 0.0)
            return result

        @pl.when((context == 0) | (context == contexts - 1))
        def _():
            piece[k] = total().astype(bf16)

        @pl.when((context > 0) & (context < root))
        def _():
            up_copy(k).wait_recv()
            piece[k] = (total() + zin[k].astype(f32)).astype(bf16)

        @pl.when((context > root) & (context < contexts - 1))
        def _():
            down_copy(k).wait_recv()
            piece[k] = (total() + zin[k].astype(f32)).astype(bf16)

        @pl.when(context < root)
        def _():
            up_copy(k).start()

        @pl.when(context == root + 1)
        def _():
            top_copy(k).start()

        @pl.when(context > root + 1)
        def _():
            down_copy(k).start()

        @pl.when(context == root)
        def _():
            up_copy(k).wait_recv()
            top_copy(k).wait_recv()
            zin[k] = (total() + zin[k].astype(f32) + ztop[k].astype(f32)).astype(bf16)
            back_down_copy(k).start()
            back_up_copy(k).start()
            grad_keep(k)

    def return_chunk(k):
        @pl.when(context < root)
        def _():
            back_down_copy(k).wait_recv()

            @pl.when(context > 0)
            def _():
                back_down_copy(k).start()

            grad_keep(k)

        @pl.when(context > root)
        def _():
            back_up_copy(k).wait_recv()

            @pl.when(context < contexts - 1)
            def _():
                back_up_copy(k).start()

            grad_keep(k)

    names = gradient_places(contexts, steps)
    reduce_table, return_table = gradient_schedule(contexts, chunk_count, names)

    def here(table, upto):
        total = 0
        for c in range(contexts):
            total += jnp.where(context == c, sum(table[c][:upto]), 0)
        return total

    def take_chunks(name):
        at = names.index(name)
        most = max(max(t[c][at] for c in range(contexts)) for t in (reduce_table, return_table))
        if most == 0:
            return
        reduced, reduced_next = here(reduce_table, at), here(reduce_table, at + 1)
        back, back_next = here(return_table, at), here(return_table, at + 1)

        def one(n, _):
            @pl.when(reduced + n < reduced_next)
            def _():
                reduce_chunk(reduced + n)

            @pl.when(back + n < back_next)
            def _():
                return_chunk(back + n)

            return 0

        lax.fori_loop(0, most, one, 0)

    def take_rest():
        reduced, back = here(reduce_table, len(names)), here(return_table, len(names))
        lag = 4 * jnp.abs(context - root)

        def give(k, _):
            @pl.when(context != root)
            def _():
                return_chunk(k)

            return 0

        def take(k, _):
            reduce_chunk(k)

            @pl.when((k - lag >= back) & (context != root))
            def _():
                return_chunk(k - lag)

            return 0

        lax.fori_loop(back, jnp.maximum(back, reduced - lag), give, 0)
        lax.fori_loop(reduced, chunk_count, take, 0)
        lax.fori_loop(jnp.maximum(back, chunk_count - lag), chunk_count, give, 0)

    def weight_grad(left, right, columns, first_chunk, count):
        for d in range(shards - 1):
            theirs_at = rows_of(lax.rem(shard + d + 1, shards), share)
            result = dot_tn(left[:, theirs_at], right[:, columns : columns + count * chunk])
            for n in range(count):
                k = first_chunk + n
                if k - early >= given:
                    y_copy(d, k - early).wait_send()
                ysend[d, k % early] = result[:, n * chunk : (n + 1) * chunk].astype(bf16)
                y_copy(d, k).start()
        result = dot_tn(left[:, rows_of(shard, share)], right[:, columns : columns + count * chunk])
        for n in range(count):
            piece[first_chunk + n] = result[:, n * chunk : (n + 1) * chunk].astype(bf16)

    def part_at(slot, block):
        return block if slot == 0 else contexts - 1 + block

    def part_core_copy(slot, block):
        at = part_at(slot, block)
        return remote(
            part.at[slot, pl.ds(0, length // 2), :], part_core.at[at], p_send.at[0, at],
            p_recv.at[0, at], core_peer,
        )

    def part_x_copy(slot, block):
        at = part_at(slot, block)
        return remote(
            part_core.at[at, rows_of(1 - chip, quarter), :], part_x.at[at], p_send.at[1, at],
            p_recv.at[1, at], x_peer,
        )

    def part_z_copy(slot, block):
        at = part_at(slot, block)
        return remote(part_x.at[at], part_z.at[at], p_send.at[2, at], p_recv.at[2, at], below)

    def part_make(slot, block):
        for pair in range(2):
            rows_at = slice(2 * pair * quarter, 2 * (pair + 1) * quarter)
            result = dot_nt(unit_back[rows_at, :], wkv[...]).astype(bf16)
            for side in range(2):
                place_at = jnp.where(core == side, 2, 0) + pair
                part[slot, rows_of(place_at, quarter), :] = result[
                    side * quarter : (side + 1) * quarter
                ]
        part_core_copy(slot, block).start()

    def part_across(slot, block):
        part_core_copy(slot, block).wait_recv()
        at = part_at(slot, block)
        total = part[slot, length // 2 :, :].astype(f32) + part_core[at].astype(f32)
        part_core[at] = total.astype(bf16)
        part_x_copy(slot, block).start()
        part_core_copy(slot, block).wait_send()

    def part_down(slot, block, count):
        part_x_copy(slot, block).wait_recv()
        at = part_at(slot, block)
        total = part_core[at, rows_of(chip, quarter), :].astype(f32) + part_x[at].astype(f32)

        @pl.when(context == count - 1)
        def _():
            part_x[at] = total.astype(bf16)

        @pl.when(context < count - 1)
        def _():
            part_z_copy(slot, block).wait_recv()
            part_x[at] = (total + part_z[at].astype(f32)).astype(bf16)

        part_z_copy(slot, block).start()

    def unit_place(slot, block):
        return jnp.where(context < half_contexts, slot, block % 2)

    def unit_loads(slot, block):
        at = unit_place(slot, block)
        return [
            pltpu.make_async_copy(source.at[block, slot], target.at[at], kv_sem.at[n, at])
            for n, (source, target) in enumerate(
                ((kv_ref, unit_kv), (first_ref, unit_first), (kraw_ref, unit_kraw))
            )
        ]

    def start_unit(slot, block):
        for copy in unit_loads(slot, block):
            copy.start()

    acc_gain[...] = jnp.zeros_like(acc_gain)
    acc_ff[...] = jnp.zeros_like(acc_ff)
    acc_head[...] = jnp.zeros_like(acc_head)
    acc_square[...] = jnp.zeros_like(acc_square)
    loads[0].wait()
    pl.semaphore_wait(barrier, around + contexts - 2)
    alive = (context < half_contexts) | (core == 0)

    @pl.when(alive)
    def _():
        for i in range(steps):
            xs_copy(i).start()

    for n in range(1, 4):
        loads[n].wait()
    gate_chunks = ff // chunk
    out_chunks = qw // chunk
    query_chunk = 3 * gate_chunks + out_chunks
    weight_grad(cotin, hidden, given * chunk, given, down_to - given)
    take_chunks("p0")
    for n in range(4, 6):
        loads[n].wait()
    weight_grad(second, gback, 0, down_to, gate_chunks)
    take_chunks("p1")
    for n in range(6, 8):
        loads[n].wait()
    for copy in loads[8:]:
        copy.start()
    for i in range(steps):
        xm_copy(i).start()
    weight_grad(second, uback, 0, down_to + gate_chunks, gate_chunks)
    take_chunks("p2")
    for n in range(8, len(loads)):
        loads[n].wait()
    both_gains = gains[...].astype(f32)
    head_gains = head_gain_ref[...].astype(f32)
    qs, qraw, mixed = hidden.at[:, :qw], gback.at[:, :qw], uback.at[:, :qw]
    own_kback, own_vback = gback.at[:, qw : qw + kw], uback.at[:, qw : qw + kw]
    next_pairs = [(qs_ref, qs), (qraw_ref, qraw), (mixed_ref, mixed)]
    next_loads = [
        pltpu.make_async_copy(source, target, load_sem.at[n])
        for n, (source, target) in enumerate(next_pairs)
    ]
    for copy in next_loads:
        copy.start()
    start_unit(0, 0)

    def fold(values):
        return jnp.sum(values.reshape(values.shape[0] // 8, 8, values.shape[1]), axis=0)

    def norm_back(values, back, gain):
        inverse = lax.rsqrt(mean_square(values) + epsilon)
        normal = values * inverse
        scaled = back * gain
        inward = inverse * (scaled - normal * jnp.mean(normal * scaled, axis=-1, keepdims=True))
        return inward, back * normal

    def residual_step(i, _):
        @pl.when(alive)
        def _():
            xs_copy(i).wait_recv()

        back = spart[half(i), :].astype(f32)
        back += jnp.where(alive, xs[half(i), :].astype(f32), 0.0)
        inward, terms = norm_back(resid[half(i), :], back, both_gains[8:9, :])
        acc_ff[...] += fold(terms)
        total = cotin[mine(i), :].astype(f32) + inward
        resback[half(i), :] = total
        outin[mine(i), :] = total.astype(bf16)
        outin_copy(i).start()
        return 0

    for i in range(steps):
        residual_step(i, 0)
        take_chunks(f"res{i}")
    for i in range(steps):
        outin_copy(i).wait_recv()
    first = cotin
    first_loads = [
        pltpu.make_async_copy(
            first_ref.at[context, slot], first.at[slot * length : (slot + 1) * length, :],
            gather_sem.at[slot],
        )
        for slot in range(2)
    ]
    for copy in first_loads:
        copy.start()
    for copy in next_loads:
        copy.wait()
    dox = second

    def mixed_step(i, _):
        at = rows_of(i, TILE)
        back = dot_nt(outin[at, :], wo[...]).astype(bf16).astype(f32)
        lanes = lax.broadcasted_iota(jnp.int32, (TILE, head), 1)
        for h in range(heads):
            columns = slice(h * head, (h + 1) * head)
            low = (back[:, columns] * dq[at, columns]).astype(bf16)
            centre = jnp.sum(
                low.astype(f32) * mixed[at, columns].astype(f32), axis=-1, keepdims=True
            )
            high = centre.astype(bf16).astype(f32)
            extra = jnp.where(lanes == 0, -high, jnp.where(lanes == 1, high - centre, 0.0))
            dox[at, 2 * h * head : (2 * h + 1) * head] = low
            dox[at, (2 * h + 1) * head : (2 * h + 2) * head] = extra.astype(bf16)
        dq[at, :] = jnp.zeros((TILE, qw), f32)
        return 0

    lax.fori_loop(0, rows // TILE, mixed_step, 0)
    take_chunks("mixed")
    ones = jnp.ones((length, head), bf16)

    def head_back(raw, back, gain, local):
        turned_back = back * cosine[local, :] - pltpu.roll(back, head // 2, 1) * sine[local, :]
        return norm_back(raw.astype(f32), turned_back, gain)

    kv_grad[...] = jnp.zeros_like(kv_grad)

    @pl.when(context >= half_contexts)
    def _():
        own_kback[length:, :] = jnp.zeros((length, kw), bf16)
        own_vback[length:, :] = jnp.zeros((length, kw), bf16)

    def block_back(slot, block, diagonal):
        lines = slice(slot * length, (slot + 1) * length)
        buffer = unit_place(slot, block)
        if diagonal:
            key_spots = lax.broadcasted_iota(jnp.int32, (length, length), 0)
            query_spots = lax.broadcasted_iota(jnp.int32, (length, length), 1)
            counted = key_spots <= query_spots

        def one_group(g, _):
            keys = unit_kv[buffer, :, rows_of(g, head)]
            values = unit_kv[buffer, :, rows_of(kv_heads + g, head)]
            widened = jnp.concatenate([values, ones], axis=1)
            key_back = jnp.zeros((length, head), f32)
            value_back = jnp.zeros((length, head), f32)
            for member in range(group):
                h = g * group + member
                columns = rows_of(h, head)
                queries = qs[lines, columns]
                inward = dox[lines, rows_of(h, 2 * head)]
                raised = jnp.exp2(dot_nt(keys, queries))
                if diagonal:
                    raised = jnp.where(counted, raised, 0.0)
                scores_back = (raised * dot_nt(widened, inward)).astype(bf16)
                value_back += dot_nn(raised.astype(bf16), inward[:, :head])
                key_back += dot_nn(scores_back, queries)
                dq[lines, columns] += dot_tn(scores_back, keys)
            raw_back, terms = head_back(
                unit_kraw[buffer, :, rows_of(g, head)], key_back * math.log(2.0),
                head_gains[8:9, :], slice(None),
            )
            acc_head[1] += fold(terms)
            unit_back[:, rows_of(g, head)] = raw_back.astype(bf16)
            unit_back[:, rows_of(kv_heads + g, head)] = value_back.astype(bf16)
            return 0

        lax.fori_loop(0, kv_heads, one_group, 0)

        def grad_rows(n, _):
            at = rows_of(n, TILE)
            kv_grad[at, :] += dot_tn(unit_first[buffer, :, at], unit_back[...])
            return 0

        lax.fori_loop(0, width // TILE, grad_rows, 0)
        if diagonal:
            own_kback[lines, :] = unit_back[:, :kw]
            own_vback[lines, :] = unit_back[:, kw:]

    def next_units(slot, block):
        if slot == 0 and block < half_contexts:

            @pl.when(context < half_contexts)
            def _():
                start_unit(1, block)

        if block + 1 < contexts:
            more = block + 1 <= context
            if slot == 0:
                more = more & (context >= half_contexts)

            @pl.when(more)
            def _():
                start_unit(0, block + 1)

    for turn_at in range(contexts + 1):
        block, before = turn_at, turn_at - 1
        if block < contexts:
            turn(cosine, sine, start_ref, block, inside_cos_ref, inside_sin_ref)
        for slot, count in ((0, contexts), (1, half_contexts)):
            within = context < count
            if block < count:

                @pl.when((block <= context) & within)
                def _():
                    for copy in unit_loads(slot, block):
                        copy.wait()
                    next_units(slot, block)

                @pl.when((block == context) & within)
                def _():
                    block_back(slot, block, True)

                @pl.when((block < context) & within)
                def _():
                    block_back(slot, block, False)

            if 0 <= before < count - 1:

                @pl.when((before < context) & within)
                def _():
                    part_across(slot, before)

            if block < count - 1:

                @pl.when((block < context) & within)
                def _():
                    part_make(slot, block)

            gone = turn_at - 2 - (count - 1 - context)

            @pl.when((gone >= 0) & (gone < context) & within)
            def _():
                part_down(slot, gone, count)

        take_chunks(f"m{turn_at}")
        if turn_at == 0:
            weight_grad(outin, mixed, 0, 3 * gate_chunks, out_chunks)
            take_chunks("out")
    for copy in first_loads:
        copy.wait()
    turn(cosine, sine, start_ref, context, inside_cos_ref, inside_sin_ref)

    def query_step(i, _):
        at = rows_of(i, TILE)
        local = rows_of(i % (length // TILE), TILE)
        for h in range(heads):
            columns = slice(h * head, (h + 1) * head)
            inward, terms = head_back(
                qraw[at, columns], dq[at, columns] * scale, head_gains[0:1, :], local
            )
            acc_head[0] += fold(terms)
            qraw[at, columns] = inward.astype(bf16)
        return 0

    lax.fori_loop(0, rows // TILE, query_step, 0)
    take_chunks("q")
    weight_grad(first, qraw, 0, query_chunk, out_chunks)
    key_chunk = query_chunk + out_chunks
    for n in range(2 * kw // chunk):
        k = key_chunk + n
        columns = slice(n * chunk, (n + 1) * chunk)
        for d in range(shards - 1):
            theirs_at = rows_of(lax.rem(shard + d + 1, shards), share)
            if k - early >= given:
                y_copy(d, k - early).wait_send()
            ysend[d, k % early] = kv_grad[theirs_at, columns].astype(bf16)
            y_copy(d, k).start()
        piece[k] = kv_grad[rows_of(shard, share), columns].astype(bf16)
    take_chunks("qw")
    _, short_length = slot_order(lengths_ref)

    @pl.when(alive)
    def _():
        for i in range(steps):
            xs_copy(i).wait_send()

    tok_load = pltpu.make_async_copy(own_tok_ref, spart, load_sem.at[0])
    tok_load.start()

    def layer_step(i, _):
        xm_copy(i).wait_recv()
        xm_copy(i).wait_send()
        mlp = mpart[half(i), :].astype(f32) + xm[half(i), :].astype(f32)
        layer = resid[half(i), :] + mlp
        mpart[half(i), :] = layer.astype(bf16)
        layer_copy(i).start()
        layer_keep(i).start()
        lines = lax.broadcasted_iota(jnp.int32, (step_rows, width), 0)
        limit = jnp.where(core == 0, 2**30, short_length)
        counted = lines + (context * length + i * step_rows) < limit
        acc_square[0] += fold(jnp.where(counted, layer * layer, 0.0))
        acc_square[1] += fold(jnp.where(counted, mlp * mlp, 0.0))
        return 0

    for i in range(steps):
        layer_step(i, 0)
        take_chunks(f"layer{i}")

    @pl.when(context < contexts - 1)
    def _():
        part_z_copy(0, jnp.minimum(context, contexts - 2)).wait_recv()

    @pl.when(context < half_contexts - 1)
    def _():
        part_z_copy(1, jnp.minimum(context, max(half_contexts - 2, 0))).wait_recv()

    take_chunks("pz")
    fown = resid

    def first_step(i, _):
        if i < steps:
            both = lambda ref: jnp.concatenate([ref[theirs(i), :], ref[mine(i), :]], axis=0)
            result = dot_nt(both(qraw), wq[...])
            result += dot_nt(both(own_kback), wkv[:, :kw])
            result += dot_nt(both(own_vback), wkv[:, kw:])

            def from_above(slot):
                at = jnp.where(
                    slot == 0,
                    jnp.minimum(context, contexts - 2),
                    contexts - 1 + jnp.minimum(context, max(half_contexts - 2, 0)),
                )
                last = jnp.where(slot == 0, contexts - 1, half_contexts - 1)
                come = (i == tensor) & (context < last)
                return jnp.where(come, part_z[at].astype(f32), 0.0)

            fsend[half(i), :] = (result[:step_rows] + from_above(1 - core)).astype(bf16)
            f_copy(i).start()
            fown[half(i), :] = result[step_rows:] + from_above(core)

        if i > 0:
            before = i - 1
            f_copy(before).wait_recv()
            total = fown[half(before), :] + frecv[half(before), :].astype(f32)
            fxsend[half(before), :] = total.astype(bf16)

            @pl.when(alive)
            def _():
                xf_copy(before).start()

        return 0

    for i in range(steps + 1):
        first_step(i, 0)
        take_chunks(f"first{i}")
    tok_load.wait()

    def tokens_step(i, _):
        @pl.when(alive)
        def _():
            xf_copy(i).wait_recv()

        back = fxsend[half(i), :].astype(f32)
        back += jnp.where(alive, fxrecv[half(i), :].astype(f32), 0.0)
        inward, terms = norm_back(spart[half(i), :].astype(f32), back, both_gains[0:1, :])
        acc_gain[...] += fold(terms)
        spart[half(i), :] = (resback[half(i), :] + inward).astype(bf16)
        tgrad_copy(i).start()
        tgrad_keep(i).start()
        return 0

    for i in range(steps):
        take_chunks(f"tokb{i}")
        tokens_step(i, 0)

    def total_of(values):
        return jnp.sum(jnp.sum(values, axis=0, keepdims=True), axis=1, keepdims=True)

    lanes = lax.broadcasted_iota(jnp.int32, (1, 128), 1)
    base = (shard * 2 + core) * 4
    squares = jnp.where(lanes == base, total_of(acc_square[0]), 0.0)
    squares += jnp.where(lanes == base + 1, total_of(square[...]), 0.0)
    squares += jnp.where(lanes == base + 2, total_of(acc_square[1]), 0.0)
    gain_row = 0.5 * jnp.sum(acc_gain[...], axis=0, keepdims=True)
    ff_row = 0.5 * jnp.sum(acc_ff[...], axis=0, keepdims=True)
    folds = width // 128
    sums[...] = jnp.zeros_like(sums)
    for n in range(folds):
        columns = slice(n * 128, (n + 1) * 128)
        sums[0, n : n + 1, :] = gain_row[:, columns]
        sums[0, folds + n : folds + n + 1, :] = ff_row[:, columns]
    sums[0, 2 * folds : 2 * folds + 1, :] = jnp.sum(acc_head[0], axis=0, keepdims=True)
    sums[0, 2 * folds + 1 : 2 * folds + 2, :] = jnp.sum(acc_head[1], axis=0, keepdims=True)
    sums[0, 2 * folds + 2 : 2 * folds + 3, :] = 0.5 * squares
    circle_hops = [
        remote(sums.at[0], sums_circle.at[index], s_send.at[d], s_recv.at[d], device)
        for d, device in enumerate(circle)
    ]
    for copy in circle_hops:
        copy.start()
    sums_circle[index] = sums[0]
    take_chunks("s1")
    for copy in circle_hops:
        copy.wait_recv()
    total = sums_circle[0]
    for n in range(1, around):
        total = total + sums_circle[n]
    sums[1] = total
    line_hops = [
        remote(
            sums.at[1], sums_line.at[context], s_send.at[around + d], s_recv.at[around + d], device
        )
        for d, device in enumerate(line)
    ]
    for copy in line_hops:
        copy.start()
    sums_line[context] = total

    take_rest()
    for copy in line_hops:
        copy.wait_recv()
    total = sums_line[0]
    for n in range(1, contexts):
        total = total + sums_line[n]
    sums[2] = total
    sums_keep = pltpu.make_async_copy(sums.at[2], sums_out, store_sem.at[2, 0])
    sums_keep.start()
    for copy in [*circle_hops, *line_hops]:
        copy.wait_send()

    def drain_steps(i, _):
        for copy in (outin_copy, layer_copy, f_copy, tgrad_copy):
            copy(i).wait_send()
        layer_copy(i).wait_recv()
        tgrad_copy(i).wait_recv()

        @pl.when(alive)
        def _():
            xf_copy(i).wait_send()

        layer_keep(i).wait()
        tgrad_keep(i).wait()
        return 0

    lax.fori_loop(0, steps, drain_steps, 0)

    def drain_chunks(k, _):
        @pl.when(k >= chunk_count - early)
        def _():
            for d in range(shards - 1):
                y_copy(d, k).wait_send()

        @pl.when(context != root)
        def _():
            up_copy(k).wait_send()

        @pl.when((context <= root) & (context > 0))
        def _():
            back_down_copy(k).wait_send()

        @pl.when((context >= root) & (context < contexts - 1))
        def _():
            back_up_copy(k).wait_send()

        grad_keep(k, finish=True)
        return 0

    lax.fori_loop(0, chunk_count, drain_chunks, 0)
    for block in range(contexts - 1):
        for slot, count in ((0, contexts), (1, half_contexts)):
            if block < count - 1:

                @pl.when((block < context) & (context < count))
                def _():
                    part_x_copy(slot, block).wait_send()
                    part_z_copy(slot, block).wait_send()

    sums_keep.wait()


def call_layer_backward(shards, contexts, lengths, parts):
    (
        second, gback, uback, cotin, hidden, spart, mpart, resid, square, mixed, linv, qs, qraw,
        kraw, kv, first, wq, wk, wv, wo, out_weight, gains, own_tok, down, head_gains, *tables,
    ) = parts
    rows, width = second.shape
    length = resid.shape[0]
    ff, qw, kw = gback.shape[1], wq.shape[1], wk.shape[1]
    share = width // shards
    chunk = CHUNK
    sum_rows = 2 * width // 128 + 8
    chunk_count = (3 * ff + 2 * qw + 2 * kw) // chunk
    early = 3 * ff // chunk
    steps = 2 * length // TILE
    units = contexts - 1 + max(contexts // 2 - 1, 1)
    head = head_gains.shape[1]
    slots = rows // length
    shape = jax.ShapeDtypeStruct
    outs = (
        shape((share, 2 * ff + qw + 2 * kw), bf16), shape((ff + qw, share), bf16),
        shape((slots, length, width), bf16), shape((slots, length, width), bf16),
        shape((sum_rows, 128), f32),
    )
    dma = pltpu.SemaphoreType.DMA

    def like(array):
        return pltpu.VMEM(array.shape, array.dtype)

    half = pltpu.VMEM((length, width), bf16)
    chunks = pltpu.VMEM((chunk_count, share, chunk), bf16)
    return pl.pallas_call(
        functools.partial(layer_backward, shards, contexts),
        out_shape=outs,
        in_specs=[SMEM] + [HBM] * 24 + [VMEM] * 4,
        out_specs=[HBM] * len(outs),
        scratch_shapes=[
            like(second), like(gback), like(uback), like(cotin), like(hidden), like(spart),
            like(mpart), like(resid), like(square), like(linv), like(wq),
            pltpu.VMEM((width, 2 * kw), bf16), like(wo), like(gains),
            pltpu.VMEM((2, length, 2 * kw), bf16), pltpu.VMEM((2, length, width), bf16),
            pltpu.VMEM((2, length, kw), bf16), pltpu.VMEM((length, 2 * kw), bf16),
            pltpu.VMEM((width, 2 * kw), f32),
            pltpu.VMEM((length, head), f32), pltpu.VMEM((length, head), f32),
            half, half, pltpu.VMEM((rows, width), bf16), pltpu.VMEM((length, width), f32),
            pltpu.VMEM((2, length, width), bf16),
            pltpu.VMEM((units, length // 2, width), bf16),
            pltpu.VMEM((units, length // 4, width), bf16),
            pltpu.VMEM((units, length // 4, width), bf16),
            half,
            chunks,
            pltpu.VMEM((shards - 1, early, share, chunk), bf16),
            pltpu.VMEM((shards - 1, chunk_count, share, chunk), bf16),
            chunks, chunks, pltpu.VMEM(((ff + qw) // chunk, chunk, share), bf16),
            pltpu.VMEM((3, sum_rows, 128), f32), pltpu.VMEM((4 * shards, sum_rows, 128), f32),
            pltpu.VMEM((contexts, sum_rows, 128), f32),
            pltpu.VMEM((8, width), f32), pltpu.VMEM((8, width), f32),
            pltpu.VMEM((2, 8, head), f32), pltpu.VMEM((2, 8, width), f32),
            dma((16,)), dma((shards,)), dma((3, 2)), dma((chunk_count,)), dma((3, steps)),
            dma((3, steps)), dma((3, steps)), dma((4, steps)), dma((4, steps)),
            dma((shards - 1, chunk_count)), dma((shards - 1, chunk_count)),
            dma((chunk_count,)), dma((chunk_count,)), dma((chunk_count,)),
            dma((2, chunk_count)), dma((chunk_count,)), dma((3, units)), dma((3, units)),
            dma((4 * shards + contexts,)), dma((4 * shards + contexts,)),
        ],
        compiler_params=pltpu.CompilerParams(
            collective_id=3, has_side_effects=True, vmem_limit_bytes=63 * 2**20
        ),
        name="layer_backward",
    )(lengths, *parts)


def finish(
    shards, lengths_ref, straight_ref, down_ref, out_ref, token_ref, layer_ref, sums_ref,
    gate_out, up_out, query_out, key_out, value_out, down_out, out_out, token_out, layer_out,
    gain_out, head_out, root_out,
):
    at = 0
    for target in (gate_out, up_out, query_out, key_out, value_out):
        columns = target.shape[1]
        target[...] = straight_ref[:, at : at + columns].astype(f32)
        at += columns
    down_out[...] = down_ref[...].astype(f32)
    out_out[...] = out_ref[...].astype(f32)
    token_out[...] = token_ref[...].astype(f32)
    layer_out[...] = layer_ref[...]

    @pl.when(pl.program_id(0) == 0)
    def _():
        shard = lax.axis_index("shard")
        folds = (sums_ref.shape[0] - 8) // 2
        each = folds // shards

        def of_shard(pick):
            result = pick(0)
            for s in range(1, shards):
                result = jnp.where(shard == s, pick(s), result)
            return result

        for n in range(2):
            for fold in range(each):
                gain_out[n : n + 1, fold * 128 : (fold + 1) * 128] = of_shard(
                    lambda s: sums_ref[pl.ds(n * folds + s * each + fold, 1), :]
                )
        head_out[...] = sums_ref[2 * folds : 2 * folds + 2, :]
        first_slot, _ = slot_order(lengths_ref)
        squares = sums_ref[2 * folds + 2 : 2 * folds + 3, :]
        width = folds * 128

        def roots(slot):
            mine = of_shard(
                lambda s: squares if s + slot == 0 else pltpu.roll(squares, 128 - (2 * s + slot) * 4, 1)
            )
            return mine

        full, short = roots(0), roots(1)
        for slot in range(2):
            chosen = jnp.where(first_slot == slot, full, short)
            count = lengths_ref[slot].astype(f32) * width
            root_out[slot : slot + 1, :] = jnp.sqrt(chosen / count)


def call_finish(shards, lengths, straight, turned, token_grads, layer, sums, sizes):
    ff, qw, kw = sizes
    share = straight.shape[0]
    slots, length, width = layer.shape
    parts = 4
    per_slot = parts // slots

    def rows(count, columns, start=0):
        size = count // parts
        return pl.BlockSpec((size, columns), lambda i, _: (start // size + i, 0))

    def slot_in(i, lengths_ref):
        first_slot, _ = slot_order(lengths_ref)
        return (jnp.where(i // per_slot == first_slot, 0, 1), i % per_slot, 0)

    slot_block = (1, length // per_slot, width)
    slot_out = pl.BlockSpec(slot_block, lambda i, _: (i // per_slot, i % per_slot, 0))
    whole = lambda shape: pl.BlockSpec(shape, lambda i, _: (0, 0))
    shape = jax.ShapeDtypeStruct
    straight_widths = (ff, ff, qw, kw, kw)
    return pl.pallas_call(
        functools.partial(finish, shards),
        out_shape=(
            *(shape((share, columns), f32) for columns in straight_widths),
            shape((ff, share), f32), shape((qw, share), f32),
            shape(layer.shape, f32), shape(layer.shape, bf16),
            shape((2, share), f32), shape((2, 128), f32), shape((2, 128), f32),
        ),
        grid_spec=pltpu.PrefetchScalarGridSpec(
            num_scalar_prefetch=1,
            grid=(parts,),
            in_specs=[
                rows(share, straight.shape[1]), rows(ff, share), rows(qw, share, ff),
                pl.BlockSpec(slot_block, slot_in), pl.BlockSpec(slot_block, slot_in),
                whole(sums.shape),
            ],
            out_specs=(
                *(rows(share, columns) for columns in straight_widths),
                rows(ff, share), rows(qw, share), slot_out, slot_out,
                whole((2, share)), whole((2, 128)), whole((2, 128)),
            ),
        ),
        compiler_params=pltpu.CompilerParams(vmem_limit_bytes=63 * 2**20),
        name="finish",
    )(lengths, straight, turned, turned, token_grads, layer, sums)


def local(
    tokens, lengths, cotangent, query_weight, key_weight, value_weight, out_weight, gate_weight,
    up_weight, down_weight, attention_gain, feedforward_gain, query_gain, key_gain,
):
    slots, length, width = tokens.shape
    shards, contexts = lax.axis_size("shard"), lax.axis_size("context")
    head = query_gain.shape[0]
    ff, qw, kw = gate_weight.shape[1], query_weight.shape[1], key_weight.shape[1]
    tables = [jnp.asarray(table) for table in rope_tables(length, contexts, head)]

    def packed(one, other):
        upper = lax.broadcasted_iota(jnp.int32, (16, one.shape[0]), 0) < 8
        return jnp.where(upper, one[None], other[None])

    gain_share = packed(attention_gain, feedforward_gain)
    head_gains = packed(query_gain, key_gain)
    (mixed, kv, qs, qraw, kraw, linv, first, wq, wk, wv, wo, wg, gains) = (
        call_attention_forward(
            shards, contexts, lengths, tokens, query_weight, key_weight, value_weight, out_weight,
            gate_weight, gain_share, head_gains, tables,
        )
    )
    (second, hidden, gback, uback, cotin, spart, mpart, resid, square, own_tok, down) = (
        call_feed_forward(
            shards, lengths, mixed, wo, tokens, cotangent, gains, wg, out_weight, gate_weight,
            up_weight, down_weight,
        )
    )
    straight, turned, layer, token_grads, sums = call_layer_backward(
        shards, contexts, lengths,
        (
            second, gback, uback, cotin, hidden, spart, mpart, resid, square, mixed, linv, qs,
            qraw, kraw, kv, first, wq, wk, wv, wo, out_weight, gains, own_tok, down, head_gains, *tables,
        ),
    )
    (
        gate_grad, up_grad, query_grad, key_grad, value_grad, down_grad, out_grad, tokens_grad,
        layer_out, gain_grads, head_gain_grads, root_means,
    ) = call_finish(
        shards, lengths, straight, turned, token_grads, layer, sums, (ff, qw, kw)
    )
    return (
        layer_out,
        tokens_grad,
        query_grad,
        key_grad,
        value_grad,
        out_grad,
        gate_grad,
        up_grad,
        down_grad,
        gain_grads[0],
        gain_grads[1],
        head_gain_grads[0],
        head_gain_grads[1],
        root_means[:, :3],
    )


def solution(mesh):
    placed = (
        P("shard", "context", None),
        P("shard"),
        P("shard", "context", None),
        P("shard", "tensor"),
        P("shard", "tensor"),
        P("shard", "tensor"),
        P("tensor", "shard"),
        P("shard", "tensor"),
        P("shard", "tensor"),
        P("tensor", "shard"),
        P("shard"),
        P("shard"),
        P(),
        P(),
    )
    return jax.shard_map(
        local,
        mesh=mesh,
        in_specs=placed,
        out_specs=(
            P("shard", "context", None),
            P("shard", "context", None),
            P("shard", "tensor"),
            P("shard", "tensor"),
            P("shard", "tensor"),
            P("tensor", "shard"),
            P("shard", "tensor"),
            P("shard", "tensor"),
            P("tensor", "shard"),
            P("shard"),
            P("shard"),
            P(),
            P(),
            P("shard", None),
        ),
        check_vma=False,
    )
```

```python
import functools
import math

import jax
import jax.numpy as jnp
import numpy as np
from jax import lax
from jax.experimental import pallas as pl
from jax.experimental.pallas import tpu as pltpu
from jax.sharding import PartitionSpec as P

epsilon = 1e-06
rope_base = 1000000.0
MESH = pl.DeviceIdType.MESH
f32 = jnp.float32
bf16 = jnp.bfloat16
HBM = pl.BlockSpec(memory_space=pl.ANY)
VMEM = pl.BlockSpec(memory_space=pltpu.VMEM)
SMEM = pl.BlockSpec(memory_space=pltpu.SMEM)
TILE = 256
CHUNK = 128
GIVEN = 3


def rows_of(index, size):
    if isinstance(index, int):
        return pl.ds(index * size, size)
    return pl.ds(pl.multiple_of(index * size, size), size)


def dot_nt(left, right):
    return lax.dot_general(left, right, (((1,), (1,)), ((), ())), preferred_element_type=f32)


def dot_tn(left, right):
    return lax.dot_general(left, right, (((0,), (0,)), ((), ())), preferred_element_type=f32)


def dot_nn(left, right):
    return jnp.dot(left, right, preferred_element_type=f32)


def mean_square(values):
    return jnp.mean(values * values, axis=-1, keepdims=True)


def place():
    return lax.axis_index("shard"), lax.axis_index("context"), lax.axis_index("tensor")


def greet(devices, extra=0):
    barrier = pltpu.get_barrier_semaphore()
    for device in devices:
        pl.semaphore_signal(barrier, inc=1, device_id=device, device_id_type=MESH)
    return barrier


def greet_line(barrier, shard, context, tensor, count):
    @pl.when(context > 0)
    def _():
        pl.semaphore_signal(
            barrier, inc=1, device_id=(shard, context - 1, tensor), device_id_type=MESH
        )

    @pl.when(context < count - 1)
    def _():
        pl.semaphore_signal(
            barrier, inc=1, device_id=(shard, context + 1, tensor), device_id_type=MESH
        )

    return jnp.minimum(context, 1) + jnp.minimum(count - 1 - context, 1)


def turn(cosine, sine, start_ref, block, inside_cos_ref, inside_sin_ref):
    head = cosine.shape[1]
    start_cos, start_sin = start_ref[block, 0:1, :], start_ref[block, 8:9, :]
    signs = jnp.where(lax.broadcasted_iota(jnp.int32, (1, head), 1) < head // 2, -1.0, 1.0)
    inside_cos, inside_sin = inside_cos_ref[...], inside_sin_ref[...]
    cosine[...] = start_cos * inside_cos - start_sin * inside_sin
    sine[...] = signs * (start_sin * inside_cos + start_cos * inside_sin)


def slot_order(lengths_ref):
    one, other = lengths_ref[0], lengths_ref[1]
    return jnp.where(other > one, 1, 0), jnp.minimum(one, other)


def gather_loads(share_ref, whole_ref, target, shard, shards, axis, sems):
    size = share_ref.shape[axis]
    copies = []
    for d in range(shards):
        at = rows_of(lax.rem(shard + d, shards), size)
        index = (slice(None), at) if axis == 1 else (at, slice(None))
        source = share_ref if d == 0 else whole_ref.at[index]
        copies.append(pltpu.make_async_copy(source, target.at[index], sems.at[d]))
    return copies


def remote(src, dst, send_sem, recv_sem, device):
    return pltpu.make_async_remote_copy(
        src_ref=src,
        dst_ref=dst,
        send_sem=send_sem,
        recv_sem=recv_sem,
        device_id=device,
        device_id_type=MESH,
    )


def rope_tables(length, contexts, head_size):
    half = head_size // 2
    speeds = np.tile(rope_base ** (-np.arange(half, dtype=np.float64) * 2.0 / head_size), 2)
    inside = np.arange(length, dtype=np.float64)[:, None] * speeds
    starts = np.arange(contexts, dtype=np.float64)[:, None] * length * speeds
    rows = np.stack([np.cos(starts), np.sin(starts)], axis=1)
    rows = np.repeat(rows, 8, axis=1)
    return (
        np.cos(inside).astype(np.float32),
        np.sin(inside).astype(np.float32),
        rows.astype(np.float32),
    )


def attention_forward(
    shards, contexts, lengths_ref, tok_ref, wq_ref, wk_ref, wv_ref, wo_ref, wg_ref, gain_ref,
    head_gain_ref, inside_cos_ref, inside_sin_ref, start_ref,
    mixed_out, kv_out, qs_out, qraw_out, kraw_out, linv_out, first_out, wq_out, wk_out, wv_out,
    wo_out, wg_out, gain_out,
    tok, first, wq, wk, wv, gains, kv, qs, qraw, kraw, acc, mixed, linv, cosine, sine,
    load_sem, own_sem, store_sem, unit_sem, wsend, wrecv, z_send, z_recv, x_send, x_recv,
    core_send, core_recv,
):
    shard, context, tensor = place()
    slots, length, width = tok.shape
    share = wq_ref.shape[0]
    query_width = wq.shape[1]
    key_width = wk.shape[1]
    head = head_gain_ref.shape[1]
    heads = query_width // head
    group = query_width // key_width
    half = contexts // 2
    quarter = length // 4
    score_scale = head**-0.5 * math.log2(math.e)
    core = tensor % 2
    core_peer = (shard, context, tensor + 1 - 2 * core)
    x_peer = (shard, context, (tensor + 2) % 4)
    above = (shard, jnp.minimum(context + 1, contexts - 1), tensor)
    peers = [(lax.rem(shard + d, shards), context, tensor) for d in range(1, shards)]
    barrier = greet([core_peer, x_peer, *peers])
    neighbours = greet_line(barrier, shard, context, tensor, contexts)

    load_tok = pltpu.make_async_copy(tok_ref, tok, load_sem)
    load_tok.start()
    mine = rows_of(shard, share)
    side = context % 2
    partner = (shard, context + 1 - 2 * side, tensor)
    weights = [
        (gain_ref, gains.at[:, mine]),
        (wk_ref, wk.at[mine, :]),
        (wv_ref, wv.at[mine, :]),
        (wq_ref, wq.at[mine, :]),
        (wg_ref.at[rows_of(side, share // 2), :], wg_out.at[rows_of(2 * shard + side, share // 2), :]),
        (wo_ref, wo_out.at[:, mine]),
    ]
    own = [
        pltpu.make_async_copy(source, target, own_sem.at[w])
        for w, (source, target) in enumerate(weights[:4])
    ]
    sends = [
        [
            remote(source, target, wsend.at[w, d], wrecv.at[w, d], peers[d])
            for d in range(shards - 1)
        ]
        for w, (source, target) in enumerate(weights)
    ]
    for copy in own:
        copy.start()
    pl.semaphore_wait(barrier, shards + 1 + neighbours)

    pair_copies = []
    for d in range(shards - 1):
        origin = lax.rem(shard + shards - d - 1, shards)
        rows = wg_out.at[rows_of(2 * origin + side, share // 2), :]
        pair_copies.append(remote(rows, rows, wsend.at[6, d], wrecv.at[6, d], partner))

    def send_weights(*places):
        for w in places:
            for copy in sends[w]:
                copy.start()

    def have_weights(*places):
        for w in places:
            for copy in sends[w]:
                copy.wait_recv()

    send_weights(0, 1, 2, 3, 4, 5)
    for slot in range(slots):
        for h in range(heads):
            acc[slot, h] = jnp.zeros((length, 2 * head), f32)
    load_tok.wait()
    for copy in own:
        copy.wait()
    have_weights(0)
    first_slot, short_length = slot_order(lengths_ref)
    head_gains = head_gain_ref[...].astype(f32)
    per_slot = length // TILE
    tiles = slots * per_slot

    first_gain = gains[...].astype(f32)[0:1, :]

    def norm_rows(i, _):
        slot = i // per_slot
        source = jnp.where(slot == 0, first_slot, 1 - first_slot)
        values = tok[source, rows_of(i % per_slot, TILE), :].astype(f32)
        scale = lax.rsqrt(mean_square(values) + epsilon)
        first[context, slot, rows_of(i % per_slot, TILE), :] = (
            values * scale * first_gain
        ).astype(bf16)
        return 0

    lax.fori_loop(0, tiles, norm_rows, 0)

    def part(block, slot, which):
        return first.at[block, slot, rows_of(which, quarter), :]

    def z_copy(block, slot):
        rows = part(block, slot, tensor)
        return remote(rows, rows, z_send.at[block, slot], z_recv.at[block, slot], above)

    def x_copy(block, slot):
        rows = part(block, slot, tensor)
        return remote(rows, rows, x_send.at[block, slot], x_recv.at[block, slot], x_peer)

    def core_copy(kind, block, slot):
        rows = part(block, slot, tensor if kind == 0 else (tensor + 2) % 4)
        return remote(
            rows, rows, core_send.at[kind, block, slot], core_recv.at[kind, block, slot], core_peer
        )

    def unit_copies(block, slot):
        return [
            pltpu.make_async_copy(
                source.at[block, slot], target.at[block, slot], unit_sem.at[n, block, slot]
            )
            for n, (source, target) in enumerate(
                ((first, first_out), (kv, kv_out), (kraw, kraw_out))
            )
        ]

    def go_up(block, slot):
        @pl.when(context < contexts - 1)
        def _():
            z_copy(block, slot).start()

    def stage_in(block, slot):
        z_copy(block, slot).wait_recv()
        go_up(block, slot)
        x_copy(block, slot).start()
        core_copy(0, block, slot).start()

    def stage_across(block, slot):
        x_copy(block, slot).wait_recv()
        core_copy(1, block, slot).start()

    def head_form(raw, gain, local):
        normal = raw * lax.rsqrt(mean_square(raw) + epsilon) * gain
        return normal * cosine[local, :] + pltpu.roll(normal, head // 2, 1) * sine[local, :]

    def make_keys(block, slot):
        turn(cosine, sine, start_ref, block, inside_cos_ref, inside_sin_ref)

        def rows(i, _):
            local = rows_of(i, TILE)
            values = first[block, slot, local, :]
            raw = dot_nn(values, wk[...])
            kraw[block, slot, local, :] = raw.astype(bf16)
            for g in range(key_width // head):
                columns = slice(g * head, (g + 1) * head)
                kv[block, slot, local, columns] = head_form(
                    raw[:, columns], head_gains[8:9, :], local
                ).astype(bf16)
            kv[block, slot, local, key_width:] = dot_nn(values, wv[...]).astype(bf16)
            return 0

        lax.fori_loop(0, per_slot, rows, 0)
        for copy in unit_copies(block, slot):
            copy.start()

    def stage_keys(block, slot):
        core_copy(0, block, slot).wait_recv()
        core_copy(1, block, slot).wait_recv()
        make_keys(block, slot)

    ones = jnp.ones((length, head), bf16)

    def attend(block, slot, diagonal):
        def one_head(h, _):
            columns = rows_of(h, head)
            keys = kv[block, slot, :, rows_of(h // group, head)]
            values = kv[block, slot, :, rows_of(key_width // head + h // group, head)]
            raised = jnp.exp2(dot_nt(qs[slot * length : (slot + 1) * length, columns], keys))
            spots = lax.broadcasted_iota(jnp.int32, (length, length), 1)
            if diagonal:
                lines = lax.broadcasted_iota(jnp.int32, (length, length), 0)
                raised = jnp.where(spots <= lines, raised, 0.0)
            if slot == 1:
                raised = jnp.where(spots + block * length < short_length, raised, 0.0)
            acc[slot, h] += dot_nn(
                raised.astype(bf16), jnp.concatenate([values, ones], axis=1)
            )
            return 0

        lax.fori_loop(0, heads, one_head, 0)

    units = [(r, slot) for r in range(1, contexts) for slot in range(slots)]

    def for_unit(n, action):
        if 0 <= n < len(units):
            back, slot = units[n]
            block = context - back

            @pl.when((block >= 0) if slot == 0 else ((block >= 0) & (block < half)))
            def _():
                action(block, slot)

    def for_own(action):
        action(context, 0)

        @pl.when(context < half)
        def _():
            action(context, 1)

    stores = []

    def store_all(*pairs):
        for source, target in pairs:
            copy = pltpu.make_async_copy(source, target, store_sem.at[len(stores)])
            copy.start()
            stores.append(copy)

    def make_queries():
        have_weights(3)
        store_all((wq, wq_out), (wk, wk_out), (wv, wv_out), (gains, gain_out))
        turn(cosine, sine, start_ref, context, inside_cos_ref, inside_sin_ref)

        def query_rows(i, _):
            place_rows = rows_of(i, TILE)
            local = rows_of(i % per_slot, TILE)
            raw = dot_nn(first[context, i // per_slot, local, :], wq[...])
            qraw[place_rows, :] = raw.astype(bf16)
            for h in range(heads):
                columns = slice(h * head, (h + 1) * head)
                qs[place_rows, columns] = (
                    head_form(raw[:, columns], head_gains[0:1, :], local) * score_scale
                ).astype(bf16)
            return 0

        lax.fori_loop(0, tiles, query_rows, 0)
        store_all((qs, qs_out), (qraw, qraw_out))

    def pass_on():
        have_weights(4)
        for copy in pair_copies:
            copy.start()

    def attend_own():
        for_own(lambda block, slot: attend(block, slot, True))

    actions = dict(
        i=stage_in, a=stage_across, k=stage_keys,
        t=lambda block, slot: attend(block, slot, False),
    )

    def steps(*names):
        for name in names:
            for_unit(int(name[1:]), actions[name[0]])

    for_own(go_up)
    steps("i0")
    have_weights(1, 2)
    steps("i1")
    make_keys(context, 0)
    make_keys(context, 1)
    steps("i2", "i3", "a0", "a1")
    make_queries()
    steps("a2", "k0", "i4", "a3", "k1")
    attend_own()
    steps("i5", "k2", "t0", "a4", "k3")
    pass_on()
    steps("t1", "t2", "k4", "t3", "a5", "t4")
    for n in range(6, len(units)):
        steps(f"i{n}", f"k{n - 1}", f"a{n}", f"t{n - 1}")
    steps(f"k{len(units) - 1}", f"t{len(units) - 1}")

    def finish(h, _):
        columns = rows_of(h, head)
        for slot in range(slots):
            lines = slice(slot * length, (slot + 1) * length)
            inverse = 1.0 / acc[slot, h, :, head:]
            mixed[lines, columns] = (acc[slot, h, :, :head] * inverse).astype(bf16)
            linv[lines, columns] = inverse
        return 0

    lax.fori_loop(0, heads, finish, 0)
    store_all((mixed, mixed_out), (linv, linv_out))

    def sent_up(block, slot):
        @pl.when(context < contexts - 1)
        def _():
            z_copy(block, slot).wait_send()

    def unit_done(block, slot):
        sent_up(block, slot)
        x_copy(block, slot).wait_send()
        core_copy(0, block, slot).wait_send()
        core_copy(1, block, slot).wait_send()
        for copy in unit_copies(block, slot):
            copy.wait()

    for_own(sent_up)
    for slot in range(slots):
        for copy in unit_copies(context, slot):
            copy.wait()
    for n in range(len(units)):
        for_unit(n, unit_done)
    have_weights(5)
    for copy in pair_copies:
        copy.wait_recv()
        copy.wait_send()
    for copies in sends:
        for copy in copies:
            copy.wait_send()
    for copy in stores:
        copy.wait()


def call_attention_forward(
    shards, contexts, lengths, tokens, query_weight, key_weight, value_weight, out_weight,
    gate_weight, gain_share, head_gains, tables,
):
    slots, length, width = tokens.shape
    rows = slots * length
    qw, kw, ff = query_weight.shape[1], key_weight.shape[1], gate_weight.shape[1]
    head = head_gains.shape[1]
    heads = qw // head
    n_weights = 6
    shape = jax.ShapeDtypeStruct
    dma = pltpu.SemaphoreType.DMA
    kv_shape = (contexts, slots, length, 2 * kw)
    kraw_shape = (contexts, slots, length, kw)
    first_shape = (contexts, slots, length, width)
    outs = (
        shape((rows, qw), bf16), shape(kv_shape, bf16), shape((rows, qw), bf16),
        shape((rows, qw), bf16), shape(kraw_shape, bf16), shape((rows, qw), f32),
        shape(first_shape, bf16), shape((width, qw), bf16), shape((width, kw), bf16),
        shape((width, kw), bf16), shape((qw, width), bf16), shape((width, ff), bf16),
        shape((16, width), bf16),
    )
    units = (contexts, slots)
    return pl.pallas_call(
        functools.partial(attention_forward, shards, contexts),
        out_shape=outs,
        in_specs=[SMEM] + [HBM] * 7 + [VMEM] * 4,
        out_specs=[HBM] * len(outs),
        scratch_shapes=[
            pltpu.VMEM((slots, length, width), bf16),
            pltpu.VMEM(first_shape, bf16),
            pltpu.VMEM((width, qw), bf16),
            pltpu.VMEM((width, kw), bf16),
            pltpu.VMEM((width, kw), bf16),
            pltpu.VMEM((16, width), bf16),
            pltpu.VMEM(kv_shape, bf16),
            pltpu.VMEM((rows, qw), bf16),
            pltpu.VMEM((rows, qw), bf16),
            pltpu.VMEM(kraw_shape, bf16),
            pltpu.VMEM((slots, heads, length, 2 * head), f32),
            pltpu.VMEM((rows, qw), bf16),
            pltpu.VMEM((rows, qw), f32),
            pltpu.VMEM((length, head), f32),
            pltpu.VMEM((length, head), f32),
            dma, dma((4,)), dma((8,)), dma((3, *units)),
            dma((n_weights + 1, shards - 1)), dma((n_weights + 1, shards - 1)),
            dma(units), dma(units), dma(units), dma(units), dma((2, *units)), dma((2, *units)),
        ],
        compiler_params=pltpu.CompilerParams(
            collective_id=1, has_side_effects=True, vmem_limit_bytes=60 * 2**20
        ),
        name="attention_forward",
    )(
        lengths, tokens, query_weight, key_weight, value_weight, out_weight, gate_weight,
        gain_share, head_gains, *tables,
    )


def feed_forward(
    shards, lengths_ref, mixed_ref, wo_ref, tok_ref, cot_ref, gain_ref, wg_ref, wo_own_ref,
    wg_own_ref, wu_ref, wd_ref,
    second_out, hidden_out, gback_out, uback_out, cotin_out, spart_out, mpart_out, resid_out,
    square_out, own_tok_out, down_out,
    mixed, wo, tok, cot, gains, wg, wu, wd, second, hidden, gback, uback, cotin, spart, mpart,
    resid, square, own_tok, down, down_own, down_send, down_recv, apart, csend, crecv, xsend, xrecv, ssend, srecv, msend, mrecv, gvalue, uvalue,
    load_sem, gather_sem, store_sem, chunk_sem, wsend, wrecv, core_send, core_recv, x_send, x_recv,
):
    shard, context, tensor = place()
    slots, length, width = tok.shape
    share = wd_ref.shape[1]
    step_rows = TILE // 2
    steps = length // step_rows
    core = tensor % 2
    core_peer = (shard, context, tensor + 1 - 2 * core)
    x_peer = (shard, context, (tensor + 2) % 4)
    peers = [(lax.rem(shard + d, shards), context, tensor) for d in range(1, shards)]
    side = context % 2
    partner = (shard, context + 1 - 2 * side, tensor)
    barrier = greet([core_peer, x_peer, partner, *peers])
    loads = [
        pltpu.make_async_copy(source, target, load_sem.at[n])
        for n, (source, target) in enumerate(
            (
                (mixed_ref, mixed), (tok_ref, tok), (gain_ref, gains), (cot_ref, cot),
                (wu_ref, wu.at[rows_of(shard, share), :]),
                (wd_ref, wd.at[:, rows_of(shard, share)]),
            )
        )
    ]
    gathers = [
        gather_loads(own_ref, whole_ref, target, shard, shards, axis, gather_sem.at[n])
        for n, (own_ref, whole_ref, target, axis) in enumerate(
            (
                (wo_own_ref, wo_ref, wo, 1), (wg_own_ref, wg_ref, wg, 0),
            )
        )
    ]
    for copy in [loads[0], *gathers[0]]:
        copy.start()
    square[...] = jnp.zeros_like(square)
    pl.semaphore_wait(barrier, shards + 2)
    def piece_of(weight, ref, origin, piece):
        if weight == 0:
            size = share // 4
            return ref.at[rows_of((0 if origin is None else 4 * origin) + piece, size), :]
        rows = rows_of(piece, wd.shape[0] // 4)
        return ref.at[rows, :] if origin is None else ref.at[rows, rows_of(origin, share)]

    sends, passes = [], []
    for n in range(4):
        weight, piece = n // 2, 2 * side + n % 2
        source, target = ((wu_ref, wu), (wd_ref, wd))[weight]
        sends.append([])
        passes.append([])
        for d in range(shards - 1):
            sends[n].append(
                remote(
                    piece_of(weight, source, None, piece), piece_of(weight, target, shard, piece),
                    wsend.at[n, d], wrecv.at[n, d], peers[d],
                )
            )
            origin = lax.rem(shard + shards - d - 1, shards)
            place_at = piece_of(weight, target, origin, piece)
            passes[n].append(
                remote(place_at, place_at, wsend.at[4 + n, d], wrecv.at[4 + n, d], partner)
            )
    for copies in sends:
        for copy in copies:
            copy.start()
    for copy in [loads[0], *gathers[0]]:
        copy.wait()
    for copy in [*loads[1:], *gathers[1]]:
        copy.start()

    def mine(i):
        return rows_of(core * steps + i, step_rows)

    def theirs(i):
        return rows_of((1 - core) * steps + i, step_rows)

    def half(i):
        return rows_of(i, step_rows)

    def core_copy(kind, i, source, target):
        return remote(source, target, core_send.at[kind, i], core_recv.at[kind, i], core_peer)

    def attn_copy(i):
        return core_copy(0, i, csend.at[half(i), :], crecv.at[half(i), :])

    def second_copy(i):
        return core_copy(1, i, second.at[mine(i), :], second.at[mine(i), :])

    def spart_copy(i):
        return core_copy(2, i, ssend.at[half(i), :], srecv.at[half(i), :])

    def mpart_copy(i):
        return core_copy(3, i, msend.at[half(i), :], mrecv.at[half(i), :])

    def x_copy(i):
        return remote(
            xsend.at[half(i), :], xrecv.at[half(i), :], x_send.at[i], x_recv.at[i], x_peer
        )

    def project(i, _):
        @pl.when(i < steps)
        def _():
            both = jnp.concatenate([mixed[theirs(i), :], mixed[mine(i), :]], axis=0)
            result = dot_nn(both, wo[...])
            csend[half(i), :] = result[:step_rows].astype(bf16)
            attn_copy(i).start()
            apart[half(i), :] = result[step_rows:]

        @pl.when(i > 0)
        def _():
            before = i - 1
            attn_copy(before).wait_recv()
            total = apart[half(before), :] + crecv[half(before), :].astype(f32)
            xsend[half(before), :] = total.astype(bf16)
            x_copy(before).start()

        return 0

    lax.fori_loop(0, steps + 1, project, 0)
    for copy in [*loads[1:], *gathers[1]]:
        copy.wait()
    first_slot, short_length = slot_order(lengths_ref)
    second_gain = gains[...].astype(f32)[8:9, :]
    own_source = jnp.where(core == 0, first_slot, 1 - first_slot)

    def counted(slot, i):
        spots = context * length + i * step_rows
        lines = lax.broadcasted_iota(jnp.int32, (step_rows, width), 0) + spots
        limit = jnp.where(slot == 0, 2**30, short_length)
        return lines < limit

    def cut(slot, i):
        source = jnp.where(slot == 0, first_slot, 1 - first_slot)
        values = cot[source, half(i), :].astype(f32)
        return jnp.where(counted(slot, i), values, 0.0).astype(bf16)

    def normalise(i):
        x_copy(i).wait_recv()
        attn = xsend[half(i), :].astype(f32) + xrecv[half(i), :].astype(f32)
        attn_counted = jnp.where(counted(core, i), attn, 0.0)
        square[...] += jnp.sum(
            (attn_counted * attn_counted).reshape(step_rows // 8, 8, width), axis=0
        )
        own_tok[half(i), :] = tok[own_source, half(i), :]
        residual = own_tok[half(i), :].astype(f32) + attn
        resid[half(i), :] = residual
        scale = lax.rsqrt(mean_square(residual) + epsilon)
        second[mine(i), :] = (residual * scale * second_gain).astype(bf16)
        second_copy(i).start()
        cotin[mine(i), :] = cut(core, i)
        cotin[theirs(i), :] = cut(1 - core, i)

    def finish_parts(i):
        spart_copy(i).wait_recv()
        spart[half(i), :] = (
            spart[half(i), :].astype(f32) + srecv[half(i), :].astype(f32)
        ).astype(bf16)
        mpart_copy(i).wait_recv()
        mpart[half(i), :] = (
            mpart[half(i), :].astype(f32) + mrecv[half(i), :].astype(f32)
        ).astype(bf16)
        for copy in part_stores(i):
            copy.start()

    def gate(i):
        second_copy(i).wait_recv()
        both = jnp.concatenate([second[mine(i), :], second[theirs(i), :]], axis=0)
        gvalue[i] = dot_nn(both, wg[...])

    def up(i):
        both = jnp.concatenate([second[mine(i), :], second[theirs(i), :]], axis=0)
        up_value = dot_nn(both, wu[...])
        gate_value = gvalue[i]
        sigmoid = 1.0 / (1.0 + jnp.exp(-gate_value))
        swish = gate_value * sigmoid
        slope = sigmoid + swish * (1.0 - sigmoid)
        low = (swish * up_value).astype(bf16)
        hidden[mine(i), :] = low[:step_rows]
        hidden[theirs(i), :] = low[step_rows:]
        gvalue[i] = up_value * slope
        uvalue[i] = swish

    def backward(i):
        inward = jnp.concatenate([cotin[mine(i), :], cotin[theirs(i), :]], axis=0)
        hidden_back = dot_nt(inward, wd[...])
        gate_low = (hidden_back * gvalue[i]).astype(bf16)
        up_low = (hidden_back * uvalue[i]).astype(bf16)
        gback[mine(i), :] = gate_low[:step_rows]
        gback[theirs(i), :] = gate_low[step_rows:]
        uback[mine(i), :] = up_low[:step_rows]
        uback[theirs(i), :] = up_low[step_rows:]
        for copy in chunk_stores(i):
            copy.start()
        result = dot_nt(gate_low, wg[...]) + dot_nt(up_low, wu[...])
        ssend[half(i), :] = result[step_rows:].astype(bf16)
        spart_copy(i).start()
        spart[half(i), :] = result[:step_rows].astype(bf16)
        low = jnp.concatenate([hidden[mine(i), :], hidden[theirs(i), :]], axis=0)
        result = dot_nn(low, wd[...])
        msend[half(i), :] = result[step_rows:].astype(bf16)
        mpart_copy(i).start()
        mpart[half(i), :] = result[:step_rows].astype(bf16)

    def pass_on(n):
        for copy in sends[n]:
            copy.wait_recv()
        for copy in passes[n]:
            copy.start()

    def have(*pieces):
        for n in pieces:
            for copy in passes[n]:
                copy.wait_recv()

    def chunk_stores(i):
        rows = [(ref, out, at) for ref, out in ((gback, gback_out), (uback, uback_out)) for at in (mine(i), theirs(i))]
        return [
            pltpu.make_async_copy(ref.at[at, :], out.at[at, :], chunk_sem.at[n, i])
            for n, (ref, out, at) in enumerate(rows)
        ]

    def part_stores(i):
        return [
            pltpu.make_async_copy(ref.at[half(i), :], out.at[half(i), :], chunk_sem.at[n, i])
            for n, (ref, out) in enumerate(((spart, spart_out), (mpart, mpart_out)), 4)
        ]

    stores = []

    def store_all(*pairs):
        for source, target in pairs:
            copy = pltpu.make_async_copy(source, target, store_sem.at[len(stores)])
            copy.start()
            stores.append(copy)

    def run(action, start, stop):
        def body(i, _):
            action(i)
            return 0

        lax.fori_loop(start, stop, body, 0)

    half_steps = steps // 2
    pass_on(0)
    normalise(0)
    pass_on(1)
    gate(0)
    pass_on(2)

    def rest_of_half(i):
        normalise(i)
        gate(i)

    run(rest_of_half, 1, half_steps)
    pass_on(3)
    have(0, 1)
    up(0)
    run(rest_of_half, half_steps, steps - 1)
    run(up, 1, half_steps)
    have(2, 3)
    backward(0)
    normalise(steps - 1)
    gate(steps - 1)
    store_all((second, second_out), (cotin, cotin_out), (resid, resid_out), (square, square_out))
    store_all((own_tok, own_tok_out))
    run(up, half_steps, steps)
    store_all((hidden, hidden_out))
    given = down.shape[0]

    def down_copy(d, n):
        return remote(
            down_send.at[d, n], down_recv.at[d, n], wsend.at[8 + n, d], wrecv.at[8 + n, d],
            peers[d],
        )

    def down_grad(whose):
        return dot_tn(cotin[:, rows_of(whose, share)], hidden[:, : given * CHUNK])

    for d in range(shards - 1):
        result = down_grad(lax.rem(shard + d + 1, shards))
        for n in range(given):
            down_send[d, n] = result[:, n * CHUNK : (n + 1) * CHUNK].astype(bf16)
            down_copy(d, n).start()
    result = down_grad(shard)
    for n in range(given):
        down_own[n] = result[:, n * CHUNK : (n + 1) * CHUNK]

    def back_step(i):
        backward(i)
        finish_parts(i - 1)

    run(back_step, 1, steps)
    finish_parts(steps - 1)
    for n in range(given):
        total = down_own[n]
        for d in range(shards - 1):
            down_copy(d, n).wait_recv()
            total = total + down_recv[d, n].astype(f32)
        down[n] = total.astype(bf16)
    store_all((down, down_out))
    for d in range(shards - 1):
        for n in range(given):
            down_copy(d, n).wait_send()
    for copy in stores:
        copy.wait()

    def drain(i, _):
        for copy in (attn_copy, second_copy, spart_copy, mpart_copy, x_copy):
            copy(i).wait_send()
        for copy in [*chunk_stores(i), *part_stores(i)]:
            copy.wait()
        return 0

    lax.fori_loop(0, steps, drain, 0)
    for copies in sends + passes:
        for copy in copies:
            copy.wait_send()


def call_feed_forward(
    shards, lengths, mixed, out_whole, tokens, cotangent, gains, gate_whole, out_weight,
    gate_weight, up_weight, down_weight,
):
    slots, length, width = tokens.shape
    rows = slots * length
    qw = mixed.shape[1]
    ff = gate_weight.shape[1]
    steps = 2 * length // TILE
    shape = jax.ShapeDtypeStruct
    outs = (
        shape((rows, width), bf16), shape((rows, ff), bf16), shape((rows, ff), bf16),
        shape((rows, ff), bf16), shape((rows, width), bf16), shape((length, width), bf16),
        shape((length, width), bf16), shape((length, width), f32), shape((8, width), f32),
        shape((length, width), bf16), shape((GIVEN, down_weight.shape[1], CHUNK), bf16),
    )
    moved = pltpu.VMEM((shards - 1, GIVEN, down_weight.shape[1], CHUNK), bf16)
    half = pltpu.VMEM((length, width), bf16)
    return pl.pallas_call(
        functools.partial(feed_forward, shards),
        out_shape=outs,
        in_specs=[SMEM] + [HBM] * 10,
        out_specs=[HBM] * len(outs),
        scratch_shapes=[
            pltpu.VMEM((rows, qw), bf16),
            pltpu.VMEM((qw, width), bf16),
            pltpu.VMEM((slots, length, width), bf16),
            pltpu.VMEM((slots, length, width), bf16),
            pltpu.VMEM((16, width), bf16),
            pltpu.VMEM((width, ff), bf16),
            pltpu.VMEM((width, ff), bf16),
            pltpu.VMEM((ff, width), bf16),
            *[pltpu.VMEM(out.shape, out.dtype) for out in outs],
            pltpu.VMEM((GIVEN, down_weight.shape[1], CHUNK), f32), moved, moved,
            pltpu.VMEM((length, width), f32),
            *[half] * 8,
            pltpu.VMEM((steps, TILE, ff), f32),
            pltpu.VMEM((steps, TILE, ff), f32),
            pltpu.SemaphoreType.DMA((6,)),
            pltpu.SemaphoreType.DMA((2, shards)),
            pltpu.SemaphoreType.DMA((7,)),
            pltpu.SemaphoreType.DMA((6, steps)),
            pltpu.SemaphoreType.DMA((8 + GIVEN, shards - 1)),
            pltpu.SemaphoreType.DMA((8 + GIVEN, shards - 1)),
            pltpu.SemaphoreType.DMA((4, steps)),
            pltpu.SemaphoreType.DMA((4, steps)),
            pltpu.SemaphoreType.DMA((steps,)),
            pltpu.SemaphoreType.DMA((steps,)),
        ],
        compiler_params=pltpu.CompilerParams(
            collective_id=2, has_side_effects=True, vmem_limit_bytes=56 * 2**20
        ),
        name="feed_forward",
    )(
        lengths, mixed, out_whole, tokens, cotangent, gains, gate_whole, out_weight,
        gate_weight, up_weight, down_weight,
    )


def gradient_places(contexts, steps):
    names = ["p0", "p1", "p2", *(f"res{n}" for n in range(steps)), "mixed", "m0", "out"]
    names += [*(f"m{n}" for n in range(1, contexts + 1)), "q", "qw"]
    names += [*(f"layer{n}" for n in range(steps)), "pz", *(f"first{n}" for n in range(steps + 1))]
    return [*names, *(f"tokb{n}" for n in range(steps)), "s1"]


def gradient_schedule(contexts, chunk_count, names):
    if contexts != 4 or chunk_count != 30:
        nothing = [[0] * len(names)] * contexts
        return nothing, nothing
    reduce_table = (
        (1, 0, 0, 2, 3, 6, 3, 0, 2, 0, 0, 1, 1, 0, 0, 0, 1, 2, 0, 0, 0, 1, 0, 0, 1, 6, 0, 0, 0, 0, 0),
        (0, 3, 0, 0, 0, 0, 2, 2, 2, 3, 3, 0, 0, 1, 1, 1, 0, 0, 0, 1, 0, 0, 2, 1, 1, 1, 0, 0, 4, 1, 1),
        (0, 0, 0, 3, 2, 1, 1, 5, 2, 1, 3, 0, 0, 0, 0, 1, 0, 0, 0, 1, 0, 1, 0, 2, 0, 3, 0, 0, 2, 0, 2),
        (3, 1, 2, 0, 0, 1, 0, 4, 1, 3, 3, 1, 0, 0, 0, 1, 1, 1, 0, 0, 0, 0, 3, 1, 1, 0, 1, 0, 0, 0, 2),
    )
    return_table = (
        (0, 0, 0, 0, 0, 0, 0, 0, 0, 0, 0, 0, 1, 2, 1, 0, 1, 0, 0, 1, 1, 0, 1, 0, 5, 3, 1, 0, 4, 0, 5),
        (0, 0, 0, 0, 0, 0, 0, 0, 0, 0, 0, 0, 0, 0, 0, 0, 0, 0, 0, 0, 0, 0, 0, 0, 0, 0, 0, 0, 0, 0, 0),
        (0, 0, 0, 0, 1, 2, 0, 4, 0, 0, 3, 0, 5, 0, 0, 0, 0, 1, 0, 1, 0, 1, 0, 1, 1, 3, 0, 0, 1, 1, 1),
        (0, 0, 0, 0, 0, 0, 0, 0, 0, 4, 0, 0, 0, 0, 7, 1, 2, 0, 0, 1, 0, 0, 0, 0, 2, 0, 0, 3, 0, 1, 0),
    )
    return reduce_table, return_table


def layer_backward(
    shards, contexts, lengths_ref, second_ref, gback_ref, uback_ref, cotin_ref, hidden_ref,
    spart_ref, mpart_ref, resid_ref, square_ref, mixed_ref, linv_ref, qs_ref, qraw_ref, kraw_ref,
    kv_ref, first_ref, wq_ref, wk_ref, wv_ref, wo_ref, wo_own_ref, gain_ref, own_tok_ref, down_ref, head_gain_ref,
    inside_cos_ref, inside_sin_ref, start_ref,
    straight_out, turned_out, layer_out, tgrad_out, sums_out,
    second, gback, uback, cotin, hidden, spart, mpart, resid, square, dq, wq, wkv, wo, gains,
    unit_kv, unit_first, unit_kraw, unit_back, kv_grad, cosine, sine, xs, xm, outin,
    resback, part, part_core, part_x, part_z, fxrecv,
    piece, ysend, yrecv, zin, ztop, turned, sums, sums_circle, sums_line, acc_gain, acc_ff, acc_head,
    acc_square,
    load_sem, gather_sem, kv_sem, late_sem, store_sem, x_send, x_recv, core_send, core_recv, y_send, y_recv,
    g_send, z_recv, top_recv, res_send, res_recv, p_send, p_recv, s_send, s_recv,
):
    shard, context, tensor = place()
    rows, width = second.shape
    length = resid.shape[0]
    ff = gback.shape[1]
    qw, kw = wq.shape[1], wkv.shape[1] // 2
    head = head_gain_ref.shape[1]
    heads, kv_heads = qw // head, kw // head
    group = heads // kv_heads
    share = piece.shape[1]
    chunk_count, chunk = piece.shape[0], piece.shape[2]
    early = ysend.shape[1]
    half_contexts = contexts // 2
    root = (contexts - 1) // 2
    down_to, out_from, out_to = ff // chunk, 3 * ff // chunk, (3 * ff + qw) // chunk
    given = down_ref.shape[0]
    step_rows = TILE // 2
    steps = length // step_rows
    scale = head**-0.5
    core = tensor % 2
    chip = tensor // 2
    quarter = length // 4
    core_peer = (shard, context, tensor + 1 - 2 * core)
    x_peer = (shard, context, (tensor + 2) % 4)
    peers = [(lax.rem(shard + d, shards), context, tensor) for d in range(1, shards)]
    below = (shard, jnp.maximum(context - 1, 0), tensor)
    above = (shard, jnp.minimum(context + 1, contexts - 1), tensor)
    around = shards * 4
    index = shard * 4 + tensor
    places = [lax.rem(index + d, around) for d in range(1, around)]
    circle = [(at // 4, context, at % 4) for at in places]
    line = [(shard, lax.rem(context + d, contexts), tensor) for d in range(1, contexts)]
    barrier = greet([*circle, *line])

    pairs = [
        (spart_ref, spart), (cotin_ref, cotin), (hidden_ref, hidden),
        (down_ref, piece.at[pl.ds(0, down_ref.shape[0])]), (second_ref, second),
        (gback_ref, gback), (uback_ref, uback), (mpart_ref, mpart), (resid_ref, resid),
        (gain_ref, gains), (linv_ref, dq), (square_ref, square), (wq_ref, wq),
        (wk_ref, wkv.at[:, :kw]), (wv_ref, wkv.at[:, kw:]),
    ]
    loads = [
        pltpu.make_async_copy(source, target, load_sem.at[n])
        for n, (source, target) in enumerate(pairs)
    ]
    loads += gather_loads(wo_own_ref, wo_ref, wo, shard, shards, 1, gather_sem)
    for copy in loads[:8]:
        copy.start()

    def mine(i):
        return rows_of(core * steps + i, step_rows)

    def theirs(i):
        return rows_of((1 - core) * steps + i, step_rows)

    def half(i):
        return rows_of(i, step_rows)

    def xs_copy(i):
        return remote(spart.at[half(i), :], xs.at[half(i), :], x_send.at[0, i], x_recv.at[0, i], x_peer)

    def xm_copy(i):
        return remote(mpart.at[half(i), :], xm.at[half(i), :], x_send.at[1, i], x_recv.at[1, i], x_peer)

    fsend, fxsend, frecv = part.at[0], part.at[1], xs

    def xf_copy(i):
        return remote(
            fxsend.at[half(i), :], fxrecv.at[half(i), :], x_send.at[2, i], x_recv.at[2, i], x_peer
        )

    def core_copy(kind, i, source, target):
        return remote(source, target, core_send.at[kind, i], core_recv.at[kind, i], core_peer)

    def outin_copy(i):
        return core_copy(0, i, outin.at[mine(i), :], outin.at[mine(i), :])

    def layer_copy(i):
        return core_copy(1, i, mpart.at[half(i), :], layer_out.at[core, half(i), :])

    def f_copy(i):
        return core_copy(2, i, fsend.at[half(i), :], frecv.at[half(i), :])

    def tgrad_copy(i):
        return core_copy(3, i, spart.at[half(i), :], tgrad_out.at[core, half(i), :])

    def layer_keep(i):
        return pltpu.make_async_copy(
            mpart.at[half(i), :], layer_out.at[core, half(i), :], store_sem.at[0, i]
        )

    def tgrad_keep(i):
        return pltpu.make_async_copy(
            spart.at[half(i), :], tgrad_out.at[core, half(i), :], store_sem.at[1, i]
        )

    def y_copy(d, k):
        return remote(
            ysend.at[d, k % early], yrecv.at[d, k], y_send.at[d, k], y_recv.at[d, k], peers[d]
        )

    def up_copy(k):
        return remote(piece.at[k], zin.at[k], g_send.at[k], z_recv.at[k], above)

    def down_copy(k):
        return remote(piece.at[k], zin.at[k], g_send.at[k], z_recv.at[k], below)

    def top_copy(k):
        return remote(piece.at[k], ztop.at[k], g_send.at[k], top_recv.at[k], below)

    def back_down_copy(k):
        return remote(zin.at[k], zin.at[k], res_send.at[0, k], res_recv.at[k], below)

    def back_up_copy(k):
        return remote(zin.at[k], zin.at[k], res_send.at[1, k], res_recv.at[k], above)

    def turned_row(k):
        row = jnp.where(k < down_to, k, k - out_from + down_to)
        return jnp.clip(row, 0, down_to + out_to - out_from - 1)

    def grad_copies(k):
        early_columns = jnp.where(k < out_from, k - down_to, k - down_to - (out_to - out_from))
        column = rows_of(jnp.maximum(early_columns, 0), chunk)
        row = turned_row(k)
        return (
            pltpu.make_async_copy(zin.at[k], straight_out.at[:, column], late_sem.at[k]),
            pltpu.make_async_copy(
                turned.at[row], turned_out.at[rows_of(row, chunk), :], late_sem.at[k]
            ),
        )

    def grad_keep(k, finish=False):
        straight_copy, turned_copy = grad_copies(k)
        aside = (k < down_to) | ((k >= out_from) & (k < out_to))

        @pl.when(jnp.logical_not(aside))
        def _():
            straight_copy.wait() if finish else straight_copy.start()

        @pl.when(aside)
        def _():
            if not finish:
                turned[turned_row(k)] = zin[k].astype(f32).T.astype(bf16)
            turned_copy.wait() if finish else turned_copy.start()

    def reduce_chunk(k):
        @pl.when(k >= given)
        def _():
            for d in range(shards - 1):
                y_copy(d, k).wait_recv()

        def total():
            result = piece[k].astype(f32)
            for d in range(shards - 1):
                result += jnp.where(k >= given, yrecv[d, k].astype(f32), 0.0)
            return result

        @pl.when((context == 0) | (context == contexts - 1))
        def _():
            piece[k] = total().astype(bf16)

        @pl.when((context > 0) & (context < root))
        def _():
            up_copy(k).wait_recv()
            piece[k] = (total() + zin[k].astype(f32)).astype(bf16)

        @pl.when((context > root) & (context < contexts - 1))
        def _():
            down_copy(k).wait_recv()
            piece[k] = (total() + zin[k].astype(f32)).astype(bf16)

        @pl.when(context < root)
        def _():
            up_copy(k).start()

        @pl.when(context == root + 1)
        def _():
            top_copy(k).start()

        @pl.when(context > root + 1)
        def _():
            down_copy(k).start()

        @pl.when(context == root)
        def _():
            up_copy(k).wait_recv()
            top_copy(k).wait_recv()
            zin[k] = (total() + zin[k].astype(f32) + ztop[k].astype(f32)).astype(bf16)
            back_down_copy(k).start()
            back_up_copy(k).start()
            grad_keep(k)

    def return_chunk(k):
        @pl.when(context < root)
        def _():
            back_down_copy(k).wait_recv()

            @pl.when(context > 0)
            def _():
                back_down_copy(k).start()

            grad_keep(k)

        @pl.when(context > root)
        def _():
            back_up_copy(k).wait_recv()

            @pl.when(context < contexts - 1)
            def _():
                back_up_copy(k).start()

            grad_keep(k)

    names = gradient_places(contexts, steps)
    reduce_table, return_table = gradient_schedule(contexts, chunk_count, names)

    def here(table, upto):
        total = 0
        for c in range(contexts):
            total += jnp.where(context == c, sum(table[c][:upto]), 0)
        return total

    def take_chunks(name):
        at = names.index(name)
        most = max(max(t[c][at] for c in range(contexts)) for t in (reduce_table, return_table))
        if most == 0:
            return
        reduced, reduced_next = here(reduce_table, at), here(reduce_table, at + 1)
        back, back_next = here(return_table, at), here(return_table, at + 1)

        def one(n, _):
            @pl.when(reduced + n < reduced_next)
            def _():
                reduce_chunk(reduced + n)

            @pl.when(back + n < back_next)
            def _():
                return_chunk(back + n)

            return 0

        lax.fori_loop(0, most, one, 0)

    def take_rest():
        reduced, back = here(reduce_table, len(names)), here(return_table, len(names))
        lag = 4 * jnp.abs(context - root)

        def give(k, _):
            @pl.when(context != root)
            def _():
                return_chunk(k)

            return 0

        def take(k, _):
            reduce_chunk(k)

            @pl.when((k - lag >= back) & (context != root))
            def _():
                return_chunk(k - lag)

            return 0

        lax.fori_loop(back, jnp.maximum(back, reduced - lag), give, 0)
        lax.fori_loop(reduced, chunk_count, take, 0)
        lax.fori_loop(jnp.maximum(back, chunk_count - lag), chunk_count, give, 0)

    def weight_grad(left, right, columns, first_chunk, count):
        for d in range(shards - 1):
            theirs_at = rows_of(lax.rem(shard + d + 1, shards), share)
            result = dot_tn(left[:, theirs_at], right[:, columns : columns + count * chunk])
            for n in range(count):
                k = first_chunk + n
                if k - early >= given:
                    y_copy(d, k - early).wait_send()
                ysend[d, k % early] = result[:, n * chunk : (n + 1) * chunk].astype(bf16)
                y_copy(d, k).start()
        result = dot_tn(left[:, rows_of(shard, share)], right[:, columns : columns + count * chunk])
        for n in range(count):
            piece[first_chunk + n] = result[:, n * chunk : (n + 1) * chunk].astype(bf16)

    def part_at(slot, block):
        return block if slot == 0 else contexts - 1 + block

    def part_core_copy(slot, block):
        at = part_at(slot, block)
        return remote(
            part.at[slot, pl.ds(0, length // 2), :], part_core.at[at], p_send.at[0, at],
            p_recv.at[0, at], core_peer,
        )

    def part_x_copy(slot, block):
        at = part_at(slot, block)
        return remote(
            part_core.at[at, rows_of(1 - chip, quarter), :], part_x.at[at], p_send.at[1, at],
            p_recv.at[1, at], x_peer,
        )

    def part_z_copy(slot, block):
        at = part_at(slot, block)
        return remote(part_x.at[at], part_z.at[at], p_send.at[2, at], p_recv.at[2, at], below)

    def part_make(slot, block):
        for pair in range(2):
            rows_at = slice(2 * pair * quarter, 2 * (pair + 1) * quarter)
            result = dot_nt(unit_back[rows_at, :], wkv[...]).astype(bf16)
            for side in range(2):
                place_at = jnp.where(core == side, 2, 0) + pair
                part[slot, rows_of(place_at, quarter), :] = result[
                    side * quarter : (side + 1) * quarter
                ]
        part_core_copy(slot, block).start()

    def part_across(slot, block):
        part_core_copy(slot, block).wait_recv()
        at = part_at(slot, block)
        total = part[slot, length // 2 :, :].astype(f32) + part_core[at].astype(f32)
        part_core[at] = total.astype(bf16)
        part_x_copy(slot, block).start()
        part_core_copy(slot, block).wait_send()

    def part_down(slot, block, count):
        part_x_copy(slot, block).wait_recv()
        at = part_at(slot, block)
        total = part_core[at, rows_of(chip, quarter), :].astype(f32) + part_x[at].astype(f32)

        @pl.when(context == count - 1)
        def _():
            part_x[at] = total.astype(bf16)

        @pl.when(context < count - 1)
        def _():
            part_z_copy(slot, block).wait_recv()
            part_x[at] = (total + part_z[at].astype(f32)).astype(bf16)

        part_z_copy(slot, block).start()

    def unit_place(slot, block):
        return jnp.where(context < half_contexts, slot, block % 2)

    def unit_loads(slot, block):
        at = unit_place(slot, block)
        return [
            pltpu.make_async_copy(source.at[block, slot], target.at[at], kv_sem.at[n, at])
            for n, (source, target) in enumerate(
                ((kv_ref, unit_kv), (first_ref, unit_first), (kraw_ref, unit_kraw))
            )
        ]

    def start_unit(slot, block):
        for copy in unit_loads(slot, block):
            copy.start()

    acc_gain[...] = jnp.zeros_like(acc_gain)
    acc_ff[...] = jnp.zeros_like(acc_ff)
    acc_head[...] = jnp.zeros_like(acc_head)
    acc_square[...] = jnp.zeros_like(acc_square)
    loads[0].wait()
    pl.semaphore_wait(barrier, around + contexts - 2)
    alive = (context < half_contexts) | (core == 0)

    @pl.when(alive)
    def _():
        for i in range(steps):
            xs_copy(i).start()

    for n in range(1, 4):
        loads[n].wait()
    gate_chunks = ff // chunk
    out_chunks = qw // chunk
    query_chunk = 3 * gate_chunks + out_chunks
    weight_grad(cotin, hidden, given * chunk, given, down_to - given)
    take_chunks("p0")
    for n in range(4, 6):
        loads[n].wait()
    weight_grad(second, gback, 0, down_to, gate_chunks)
    take_chunks("p1")
    for n in range(6, 8):
        loads[n].wait()
    for copy in loads[8:]:
        copy.start()
    for i in range(steps):
        xm_copy(i).start()
    weight_grad(second, uback, 0, down_to + gate_chunks, gate_chunks)
    take_chunks("p2")
    for n in range(8, len(loads)):
        loads[n].wait()
    both_gains = gains[...].astype(f32)
    head_gains = head_gain_ref[...].astype(f32)
    qs, qraw, mixed = hidden.at[:, :qw], gback.at[:, :qw], uback.at[:, :qw]
    own_kback, own_vback = gback.at[:, qw : qw + kw], uback.at[:, qw : qw + kw]
    next_pairs = [(qs_ref, qs), (qraw_ref, qraw), (mixed_ref, mixed)]
    next_loads = [
        pltpu.make_async_copy(source, target, load_sem.at[n])
        for n, (source, target) in enumerate(next_pairs)
    ]
    for copy in next_loads:
        copy.start()
    start_unit(0, 0)

    def fold(values):
        return jnp.sum(values.reshape(values.shape[0] // 8, 8, values.shape[1]), axis=0)

    def norm_back(values, back, gain):
        inverse = lax.rsqrt(mean_square(values) + epsilon)
        normal = values * inverse
        scaled = back * gain
        inward = inverse * (scaled - normal * jnp.mean(normal * scaled, axis=-1, keepdims=True))
        return inward, back * normal

    def residual_step(i, _):
        @pl.when(alive)
        def _():
            xs_copy(i).wait_recv()

        back = spart[half(i), :].astype(f32)
        back += jnp.where(alive, xs[half(i), :].astype(f32), 0.0)
        inward, terms = norm_back(resid[half(i), :], back, both_gains[8:9, :])
        acc_ff[...] += fold(terms)
        total = cotin[mine(i), :].astype(f32) + inward
        resback[half(i), :] = total
        outin[mine(i), :] = total.astype(bf16)
        outin_copy(i).start()
        return 0

    for i in range(steps):
        residual_step(i, 0)
        take_chunks(f"res{i}")
    for i in range(steps):
        outin_copy(i).wait_recv()
    first = cotin
    first_loads = [
        pltpu.make_async_copy(
            first_ref.at[context, slot], first.at[slot * length : (slot + 1) * length, :],
            gather_sem.at[slot],
        )
        for slot in range(2)
    ]
    for copy in first_loads:
        copy.start()
    for copy in next_loads:
        copy.wait()
    dox = second

    def mixed_step(i, _):
        at = rows_of(i, TILE)
        back = dot_nt(outin[at, :], wo[...]).astype(bf16).astype(f32)
        lanes = lax.broadcasted_iota(jnp.int32, (TILE, head), 1)
        for h in range(heads):
            columns = slice(h * head, (h + 1) * head)
            low = (back[:, columns] * dq[at, columns]).astype(bf16)
            centre = jnp.sum(
                low.astype(f32) * mixed[at, columns].astype(f32), axis=-1, keepdims=True
            )
            high = centre.astype(bf16).astype(f32)
            extra = jnp.where(lanes == 0, -high, jnp.where(lanes == 1, high - centre, 0.0))
            dox[at, 2 * h * head : (2 * h + 1) * head] = low
            dox[at, (2 * h + 1) * head : (2 * h + 2) * head] = extra.astype(bf16)
        dq[at, :] = jnp.zeros((TILE, qw), f32)
        return 0

    lax.fori_loop(0, rows // TILE, mixed_step, 0)
    take_chunks("mixed")
    ones = jnp.ones((length, head), bf16)

    def head_back(raw, back, gain, local):
        turned_back = back * cosine[local, :] - pltpu.roll(back, head // 2, 1) * sine[local, :]
        return norm_back(raw.astype(f32), turned_back, gain)

    kv_grad[...] = jnp.zeros_like(kv_grad)

    @pl.when(context >= half_contexts)
    def _():
        own_kback[length:, :] = jnp.zeros((length, kw), bf16)
        own_vback[length:, :] = jnp.zeros((length, kw), bf16)

    def block_back(slot, block, diagonal):
        lines = slice(slot * length, (slot + 1) * length)
        buffer = unit_place(slot, block)
        if diagonal:
            key_spots = lax.broadcasted_iota(jnp.int32, (length, length), 0)
            query_spots = lax.broadcasted_iota(jnp.int32, (length, length), 1)
            counted = key_spots <= query_spots

        def one_group(g, _):
            keys = unit_kv[buffer, :, rows_of(g, head)]
            values = unit_kv[buffer, :, rows_of(kv_heads + g, head)]
            widened = jnp.concatenate([values, ones], axis=1)
            key_back = jnp.zeros((length, head), f32)
            value_back = jnp.zeros((length, head), f32)
            for member in range(group):
                h = g * group + member
                columns = rows_of(h, head)
                queries = qs[lines, columns]
                inward = dox[lines, rows_of(h, 2 * head)]
                raised = jnp.exp2(dot_nt(keys, queries))
                if diagonal:
                    raised = jnp.where(counted, raised, 0.0)
                scores_back = (raised * dot_nt(widened, inward)).astype(bf16)
                value_back += dot_nn(raised.astype(bf16), inward[:, :head])
                key_back += dot_nn(scores_back, queries)
                dq[lines, columns] += dot_tn(scores_back, keys)
            raw_back, terms = head_back(
                unit_kraw[buffer, :, rows_of(g, head)], key_back * math.log(2.0),
                head_gains[8:9, :], slice(None),
            )
            acc_head[1] += fold(terms)
            unit_back[:, rows_of(g, head)] = raw_back.astype(bf16)
            unit_back[:, rows_of(kv_heads + g, head)] = value_back.astype(bf16)
            return 0

        lax.fori_loop(0, kv_heads, one_group, 0)

        def grad_rows(n, _):
            at = rows_of(n, TILE)
            kv_grad[at, :] += dot_tn(unit_first[buffer, :, at], unit_back[...])
            return 0

        lax.fori_loop(0, width // TILE, grad_rows, 0)
        if diagonal:
            own_kback[lines, :] = unit_back[:, :kw]
            own_vback[lines, :] = unit_back[:, kw:]

    def next_units(slot, block):
        if slot == 0 and block < half_contexts:

            @pl.when(context < half_contexts)
            def _():
                start_unit(1, block)

        if block + 1 < contexts:
            more = block + 1 <= context
            if slot == 0:
                more = more & (context >= half_contexts)

            @pl.when(more)
            def _():
                start_unit(0, block + 1)

    for turn_at in range(contexts + 1):
        block, before = turn_at, turn_at - 1
        if block < contexts:
            turn(cosine, sine, start_ref, block, inside_cos_ref, inside_sin_ref)
        for slot, count in ((0, contexts), (1, half_contexts)):
            within = context < count
            if block < count:

                @pl.when((block <= context) & within)
                def _():
                    for copy in unit_loads(slot, block):
                        copy.wait()
                    next_units(slot, block)

                @pl.when((block == context) & within)
                def _():
                    block_back(slot, block, True)

                @pl.when((block < context) & within)
                def _():
                    block_back(slot, block, False)

            if 0 <= before < count - 1:

                @pl.when((before < context) & within)
                def _():
                    part_across(slot, before)

            if block < count - 1:

                @pl.when((block < context) & within)
                def _():
                    part_make(slot, block)

            gone = turn_at - 2 - (count - 1 - context)

            @pl.when((gone >= 0) & (gone < context) & within)
            def _():
                part_down(slot, gone, count)

        take_chunks(f"m{turn_at}")
        if turn_at == 0:
            weight_grad(outin, mixed, 0, 3 * gate_chunks, out_chunks)
            take_chunks("out")
    for copy in first_loads:
        copy.wait()
    turn(cosine, sine, start_ref, context, inside_cos_ref, inside_sin_ref)

    def query_step(i, _):
        at = rows_of(i, TILE)
        local = rows_of(i % (length // TILE), TILE)
        for h in range(heads):
            columns = slice(h * head, (h + 1) * head)
            inward, terms = head_back(
                qraw[at, columns], dq[at, columns] * scale, head_gains[0:1, :], local
            )
            acc_head[0] += fold(terms)
            qraw[at, columns] = inward.astype(bf16)
        return 0

    lax.fori_loop(0, rows // TILE, query_step, 0)
    take_chunks("q")
    weight_grad(first, qraw, 0, query_chunk, out_chunks)
    key_chunk = query_chunk + out_chunks
    for n in range(2 * kw // chunk):
        k = key_chunk + n
        columns = slice(n * chunk, (n + 1) * chunk)
        for d in range(shards - 1):
            theirs_at = rows_of(lax.rem(shard + d + 1, shards), share)
            if k - early >= given:
                y_copy(d, k - early).wait_send()
            ysend[d, k % early] = kv_grad[theirs_at, columns].astype(bf16)
            y_copy(d, k).start()
        piece[k] = kv_grad[rows_of(shard, share), columns].astype(bf16)
    take_chunks("qw")
    _, short_length = slot_order(lengths_ref)

    @pl.when(alive)
    def _():
        for i in range(steps):
            xs_copy(i).wait_send()

    tok_load = pltpu.make_async_copy(own_tok_ref, spart, load_sem.at[0])
    tok_load.start()

    def layer_step(i, _):
        xm_copy(i).wait_recv()
        xm_copy(i).wait_send()
        mlp = mpart[half(i), :].astype(f32) + xm[half(i), :].astype(f32)
        layer = resid[half(i), :] + mlp
        mpart[half(i), :] = layer.astype(bf16)
        layer_copy(i).start()
        layer_keep(i).start()
        lines = lax.broadcasted_iota(jnp.int32, (step_rows, width), 0)
        limit = jnp.where(core == 0, 2**30, short_length)
        counted = lines + (context * length + i * step_rows) < limit
        acc_square[0] += fold(jnp.where(counted, layer * layer, 0.0))
        acc_square[1] += fold(jnp.where(counted, mlp * mlp, 0.0))
        return 0

    for i in range(steps):
        layer_step(i, 0)
        take_chunks(f"layer{i}")

    @pl.when(context < contexts - 1)
    def _():
        part_z_copy(0, jnp.minimum(context, contexts - 2)).wait_recv()

    @pl.when(context < half_contexts - 1)
    def _():
        part_z_copy(1, jnp.minimum(context, max(half_contexts - 2, 0))).wait_recv()

    take_chunks("pz")
    fown = resid

    def first_step(i, _):
        if i < steps:
            both = lambda ref: jnp.concatenate([ref[theirs(i), :], ref[mine(i), :]], axis=0)
            result = dot_nt(both(qraw), wq[...])
            result += dot_nt(both(own_kback), wkv[:, :kw])
            result += dot_nt(both(own_vback), wkv[:, kw:])

            def from_above(slot):
                at = jnp.where(
                    slot == 0,
                    jnp.minimum(context, contexts - 2),
                    contexts - 1 + jnp.minimum(context, max(half_contexts - 2, 0)),
                )
                last = jnp.where(slot == 0, contexts - 1, half_contexts - 1)
                come = (i == tensor) & (context < last)
                return jnp.where(come, part_z[at].astype(f32), 0.0)

            fsend[half(i), :] = (result[:step_rows] + from_above(1 - core)).astype(bf16)
            f_copy(i).start()
            fown[half(i), :] = result[step_rows:] + from_above(core)

        if i > 0:
            before = i - 1
            f_copy(before).wait_recv()
            total = fown[half(before), :] + frecv[half(before), :].astype(f32)
            fxsend[half(before), :] = total.astype(bf16)

            @pl.when(alive)
            def _():
                xf_copy(before).start()

        return 0

    for i in range(steps + 1):
        first_step(i, 0)
        take_chunks(f"first{i}")
    tok_load.wait()

    def tokens_step(i, _):
        @pl.when(alive)
        def _():
            xf_copy(i).wait_recv()

        back = fxsend[half(i), :].astype(f32)
        back += jnp.where(alive, fxrecv[half(i), :].astype(f32), 0.0)
        inward, terms = norm_back(spart[half(i), :].astype(f32), back, both_gains[0:1, :])
        acc_gain[...] += fold(terms)
        spart[half(i), :] = (resback[half(i), :] + inward).astype(bf16)
        tgrad_copy(i).start()
        tgrad_keep(i).start()
        return 0

    for i in range(steps):
        take_chunks(f"tokb{i}")
        tokens_step(i, 0)

    def total_of(values):
        return jnp.sum(jnp.sum(values, axis=0, keepdims=True), axis=1, keepdims=True)

    lanes = lax.broadcasted_iota(jnp.int32, (1, 128), 1)
    base = (shard * 2 + core) * 4
    squares = jnp.where(lanes == base, total_of(acc_square[0]), 0.0)
    squares += jnp.where(lanes == base + 1, total_of(square[...]), 0.0)
    squares += jnp.where(lanes == base + 2, total_of(acc_square[1]), 0.0)
    gain_row = 0.5 * jnp.sum(acc_gain[...], axis=0, keepdims=True)
    ff_row = 0.5 * jnp.sum(acc_ff[...], axis=0, keepdims=True)
    folds = width // 128
    sums[...] = jnp.zeros_like(sums)
    for n in range(folds):
        columns = slice(n * 128, (n + 1) * 128)
        sums[0, n : n + 1, :] = gain_row[:, columns]
        sums[0, folds + n : folds + n + 1, :] = ff_row[:, columns]
    sums[0, 2 * folds : 2 * folds + 1, :] = jnp.sum(acc_head[0], axis=0, keepdims=True)
    sums[0, 2 * folds + 1 : 2 * folds + 2, :] = jnp.sum(acc_head[1], axis=0, keepdims=True)
    sums[0, 2 * folds + 2 : 2 * folds + 3, :] = 0.5 * squares
    circle_hops = [
        remote(sums.at[0], sums_circle.at[index], s_send.at[d], s_recv.at[d], device)
        for d, device in enumerate(circle)
    ]
    for copy in circle_hops:
        copy.start()
    sums_circle[index] = sums[0]
    take_chunks("s1")
    for copy in circle_hops:
        copy.wait_recv()
    total = sums_circle[0]
    for n in range(1, around):
        total = total + sums_circle[n]
    sums[1] = total
    line_hops = [
        remote(
            sums.at[1], sums_line.at[context], s_send.at[around + d], s_recv.at[around + d], device
        )
        for d, device in enumerate(line)
    ]
    for copy in line_hops:
        copy.start()
    sums_line[context] = total

    take_rest()
    for copy in line_hops:
        copy.wait_recv()
    total = sums_line[0]
    for n in range(1, contexts):
        total = total + sums_line[n]
    sums[2] = total
    sums_keep = pltpu.make_async_copy(sums.at[2], sums_out, store_sem.at[2, 0])
    sums_keep.start()
    for copy in [*circle_hops, *line_hops]:
        copy.wait_send()

    def drain_steps(i, _):
        for copy in (outin_copy, layer_copy, f_copy, tgrad_copy):
            copy(i).wait_send()
        layer_copy(i).wait_recv()
        tgrad_copy(i).wait_recv()

        @pl.when(alive)
        def _():
            xf_copy(i).wait_send()

        layer_keep(i).wait()
        tgrad_keep(i).wait()
        return 0

    lax.fori_loop(0, steps, drain_steps, 0)

    def drain_chunks(k, _):
        @pl.when(k >= chunk_count - early)
        def _():
            for d in range(shards - 1):
                y_copy(d, k).wait_send()

        @pl.when(context != root)
        def _():
            up_copy(k).wait_send()

        @pl.when((context <= root) & (context > 0))
        def _():
            back_down_copy(k).wait_send()

        @pl.when((context >= root) & (context < contexts - 1))
        def _():
            back_up_copy(k).wait_send()

        grad_keep(k, finish=True)
        return 0

    lax.fori_loop(0, chunk_count, drain_chunks, 0)
    for block in range(contexts - 1):
        for slot, count in ((0, contexts), (1, half_contexts)):
            if block < count - 1:

                @pl.when((block < context) & (context < count))
                def _():
                    part_x_copy(slot, block).wait_send()
                    part_z_copy(slot, block).wait_send()

    sums_keep.wait()


def call_layer_backward(shards, contexts, lengths, parts):
    (
        second, gback, uback, cotin, hidden, spart, mpart, resid, square, mixed, linv, qs, qraw,
        kraw, kv, first, wq, wk, wv, wo, out_weight, gains, own_tok, down, head_gains, *tables,
    ) = parts
    rows, width = second.shape
    length = resid.shape[0]
    ff, qw, kw = gback.shape[1], wq.shape[1], wk.shape[1]
    share = width // shards
    chunk = CHUNK
    sum_rows = 2 * width // 128 + 8
    chunk_count = (3 * ff + 2 * qw + 2 * kw) // chunk
    early = 3 * ff // chunk
    steps = 2 * length // TILE
    units = contexts - 1 + max(contexts // 2 - 1, 1)
    head = head_gains.shape[1]
    slots = rows // length
    shape = jax.ShapeDtypeStruct
    outs = (
        shape((share, 2 * ff + qw + 2 * kw), bf16), shape((ff + qw, share), bf16),
        shape((slots, length, width), bf16), shape((slots, length, width), bf16),
        shape((sum_rows, 128), f32),
    )
    dma = pltpu.SemaphoreType.DMA

    def like(array):
        return pltpu.VMEM(array.shape, array.dtype)

    half = pltpu.VMEM((length, width), bf16)
    chunks = pltpu.VMEM((chunk_count, share, chunk), bf16)
    return pl.pallas_call(
        functools.partial(layer_backward, shards, contexts),
        out_shape=outs,
        in_specs=[SMEM] + [HBM] * 24 + [VMEM] * 4,
        out_specs=[HBM] * len(outs),
        scratch_shapes=[
            like(second), like(gback), like(uback), like(cotin), like(hidden), like(spart),
            like(mpart), like(resid), like(square), like(linv), like(wq),
            pltpu.VMEM((width, 2 * kw), bf16), like(wo), like(gains),
            pltpu.VMEM((2, length, 2 * kw), bf16), pltpu.VMEM((2, length, width), bf16),
            pltpu.VMEM((2, length, kw), bf16), pltpu.VMEM((length, 2 * kw), bf16),
            pltpu.VMEM((width, 2 * kw), f32),
            pltpu.VMEM((length, head), f32), pltpu.VMEM((length, head), f32),
            half, half, pltpu.VMEM((rows, width), bf16), pltpu.VMEM((length, width), f32),
            pltpu.VMEM((2, length, width), bf16),
            pltpu.VMEM((units, length // 2, width), bf16),
            pltpu.VMEM((units, length // 4, width), bf16),
            pltpu.VMEM((units, length // 4, width), bf16),
            half,
            chunks,
            pltpu.VMEM((shards - 1, early, share, chunk), bf16),
            pltpu.VMEM((shards - 1, chunk_count, share, chunk), bf16),
            chunks, chunks, pltpu.VMEM(((ff + qw) // chunk, chunk, share), bf16),
            pltpu.VMEM((3, sum_rows, 128), f32), pltpu.VMEM((4 * shards, sum_rows, 128), f32),
            pltpu.VMEM((contexts, sum_rows, 128), f32),
            pltpu.VMEM((8, width), f32), pltpu.VMEM((8, width), f32),
            pltpu.VMEM((2, 8, head), f32), pltpu.VMEM((2, 8, width), f32),
            dma((16,)), dma((shards,)), dma((3, 2)), dma((chunk_count,)), dma((3, steps)),
            dma((3, steps)), dma((3, steps)), dma((4, steps)), dma((4, steps)),
            dma((shards - 1, chunk_count)), dma((shards - 1, chunk_count)),
            dma((chunk_count,)), dma((chunk_count,)), dma((chunk_count,)),
            dma((2, chunk_count)), dma((chunk_count,)), dma((3, units)), dma((3, units)),
            dma((4 * shards + contexts,)), dma((4 * shards + contexts,)),
        ],
        compiler_params=pltpu.CompilerParams(
            collective_id=3, has_side_effects=True, vmem_limit_bytes=63 * 2**20
        ),
        name="layer_backward",
    )(lengths, *parts)


def finish(
    shards, lengths_ref, straight_ref, down_ref, out_ref, token_ref, layer_ref, sums_ref,
    gate_out, up_out, query_out, key_out, value_out, down_out, out_out, token_out, layer_out,
    gain_out, ff_gain_out, query_gain_out, key_gain_out, root_out,
):
    at = 0
    for target in (gate_out, up_out, query_out, key_out, value_out):
        columns = target.shape[1]
        target[...] = straight_ref[:, at : at + columns].astype(f32)
        at += columns
    down_out[...] = down_ref[...].astype(f32)
    out_out[...] = out_ref[...].astype(f32)
    token_out[...] = token_ref[...].astype(f32)
    layer_out[...] = layer_ref[...]

    @pl.when(pl.program_id(0) == 0)
    def _():
        shard = lax.axis_index("shard")
        folds = (sums_ref.shape[0] - 8) // 2
        each = folds // shards

        def of_shard(pick):
            result = pick(0)
            for s in range(1, shards):
                result = jnp.where(shard == s, pick(s), result)
            return result

        for n, target in enumerate((gain_out, ff_gain_out)):
            for fold in range(each):
                target[:, fold * 128 : (fold + 1) * 128] = of_shard(
                    lambda s: sums_ref[pl.ds(n * folds + s * each + fold, 1), :]
                )
        query_gain_out[...] = sums_ref[2 * folds : 2 * folds + 1, :]
        key_gain_out[...] = sums_ref[2 * folds + 1 : 2 * folds + 2, :]
        first_slot, _ = slot_order(lengths_ref)
        squares = sums_ref[2 * folds + 2 : 2 * folds + 3, :]
        width = folds * 128

        def roots(slot):
            mine = of_shard(
                lambda s: squares if s + slot == 0 else pltpu.roll(squares, 128 - (2 * s + slot) * 4, 1)
            )
            return mine

        full, short = roots(0), roots(1)
        for slot in range(2):
            chosen = jnp.where(first_slot == slot, full, short)
            count = lengths_ref[slot].astype(f32) * width
            root_out[slot : slot + 1, :] = jnp.sqrt(chosen / count)[:, :3]


def call_finish(shards, lengths, straight, turned, token_grads, layer, sums, sizes):
    ff, qw, kw = sizes
    share = straight.shape[0]
    slots, length, width = layer.shape
    parts = 4
    per_slot = parts // slots

    def rows(count, columns, start=0):
        size = count // parts
        return pl.BlockSpec((size, columns), lambda i, _: (start // size + i, 0))

    def slot_in(i, lengths_ref):
        first_slot, _ = slot_order(lengths_ref)
        return (jnp.where(i // per_slot == first_slot, 0, 1), i % per_slot, 0)

    slot_block = (1, length // per_slot, width)
    slot_out = pl.BlockSpec(slot_block, lambda i, _: (i // per_slot, i % per_slot, 0))
    whole = lambda shape: pl.BlockSpec(shape, lambda i, _: (0, 0))
    shape = jax.ShapeDtypeStruct
    smalls = ((1, share), (1, share), (1, 128), (1, 128), (2, 3))
    straight_widths = (ff, ff, qw, kw, kw)
    return pl.pallas_call(
        functools.partial(finish, shards),
        out_shape=(
            *(shape((share, columns), f32) for columns in straight_widths),
            shape((ff, share), f32), shape((qw, share), f32),
            shape(layer.shape, f32), shape(layer.shape, bf16),
            *(shape(small, f32) for small in smalls),
        ),
        grid_spec=pltpu.PrefetchScalarGridSpec(
            num_scalar_prefetch=1,
            grid=(parts,),
            in_specs=[
                rows(share, straight.shape[1]), rows(ff, share), rows(qw, share, ff),
                pl.BlockSpec(slot_block, slot_in), pl.BlockSpec(slot_block, slot_in),
                whole(sums.shape),
            ],
            out_specs=(
                *(rows(share, columns) for columns in straight_widths),
                rows(ff, share), rows(qw, share), slot_out, slot_out,
                *(whole(small) for small in smalls),
            ),
        ),
        compiler_params=pltpu.CompilerParams(vmem_limit_bytes=63 * 2**20),
        name="finish",
    )(lengths, straight, turned, turned, token_grads, layer, sums)


def local(
    tokens, lengths, cotangent, query_weight, key_weight, value_weight, out_weight, gate_weight,
    up_weight, down_weight, attention_gain, feedforward_gain, query_gain, key_gain,
):
    slots, length, width = tokens.shape
    shards, contexts = lax.axis_size("shard"), lax.axis_size("context")
    head = query_gain.shape[0]
    ff, qw, kw = gate_weight.shape[1], query_weight.shape[1], key_weight.shape[1]
    tables = [jnp.asarray(table) for table in rope_tables(length, contexts, head)]

    def packed(one, other):
        upper = lax.broadcasted_iota(jnp.int32, (16, one.shape[0]), 0) < 8
        return jnp.where(upper, one[None], other[None])

    gain_share = packed(attention_gain, feedforward_gain)
    head_gains = packed(query_gain, key_gain)
    (mixed, kv, qs, qraw, kraw, linv, first, wq, wk, wv, wo, wg, gains) = (
        call_attention_forward(
            shards, contexts, lengths, tokens, query_weight, key_weight, value_weight, out_weight,
            gate_weight, gain_share, head_gains, tables,
        )
    )
    (second, hidden, gback, uback, cotin, spart, mpart, resid, square, own_tok, down) = (
        call_feed_forward(
            shards, lengths, mixed, wo, tokens, cotangent, gains, wg, out_weight, gate_weight,
            up_weight, down_weight,
        )
    )
    straight, turned, layer, token_grads, sums = call_layer_backward(
        shards, contexts, lengths,
        (
            second, gback, uback, cotin, hidden, spart, mpart, resid, square, mixed, linv, qs,
            qraw, kraw, kv, first, wq, wk, wv, wo, out_weight, gains, own_tok, down, head_gains, *tables,
        ),
    )
    (
        gate_grad, up_grad, query_grad, key_grad, value_grad, down_grad, out_grad, tokens_grad,
        layer_out, *gain_grads, root_means,
    ) = call_finish(
        shards, lengths, straight, turned, token_grads, layer, sums, (ff, qw, kw)
    )
    return (
        layer_out,
        tokens_grad,
        query_grad,
        key_grad,
        value_grad,
        out_grad,
        gate_grad,
        up_grad,
        down_grad,
        *(grad.reshape(grad.shape[1]) for grad in gain_grads),
        root_means,
    )


def solution(mesh):
    placed = (
        P("shard", "context", None),
        P("shard"),
        P("shard", "context", None),
        P("shard", "tensor"),
        P("shard", "tensor"),
        P("shard", "tensor"),
        P("tensor", "shard"),
        P("shard", "tensor"),
        P("shard", "tensor"),
        P("tensor", "shard"),
        P("shard"),
        P("shard"),
        P(),
        P(),
    )
    return jax.shard_map(
        local,
        mesh=mesh,
        in_specs=placed,
        out_specs=(
            P("shard", "context", None),
            P("shard", "context", None),
            P("shard", "tensor"),
            P("shard", "tensor"),
            P("shard", "tensor"),
            P("tensor", "shard"),
            P("shard", "tensor"),
            P("shard", "tensor"),
            P("tensor", "shard"),
            P("shard"),
            P("shard"),
            P(),
            P(),
            P("shard", None),
        ),
        check_vma=False,
    )
```
